32 devices in a mesh: tp: 4 (over z), cp: 8 (over y, x, core).
Axes of the slice: x: 2, y: 2, z: 4, core: 2. Of those that a mesh axis runs over, the one named last changes fastest.
Arguments:
- layer_input: bfloat16 [1024, 1, 2048], P('cp'), may hold values from -6 to 6
- segment_ids: int32 [1024, 1], P('cp'), may hold values from 0 to 6, as said below
- qkv_weight: bfloat16 [2048, 3, 2048], P(None, None, 'tp'), may hold values from -0.125 to 0.125
- out_weight: bfloat16 [2048, 2048], P('tp'), may hold values from -0.125 to 0.125
- up_weight: bfloat16 [2048, 8192], P(None, 'tp'), may hold values from -0.125 to 0.125
- down_weight: bfloat16 [8192, 2048], P('tp'), may hold values from -0.0625 to 0.0625
- input_gain: float32 [2048], replicated, may hold values from 0.5 to 1.5
- heads_gain: float32 [2048], P('tp'), may hold values from 0.5 to 1.5
- middle_gain: float32 [2048], replicated, may hold values from 0.5 to 1.5
- hidden_gain: float32 [8192], P('tp'), may hold values from 0.5 to 1.5
- cotangent: bfloat16 [1024, 1, 2048], P('cp'), may hold values from -6 to 6
Outputs:
- layer_output: bfloat16 [1024, 1, 2048], P('cp')
- grad_input: bfloat16 [1024, 1, 2048], P('cp')
- grad_qkv: float32 [2048, 3, 2048], P('cp', None, 'tp')
- grad_out: float32 [2048, 2048], P(('tp', 'cp'))
- grad_up: float32 [2048, 8192], P('cp', 'tp')
- grad_down: float32 [8192, 2048], P(('tp', 'cp'))
- grad_input_gain: float32 [2048], P('cp')
- grad_heads_gain: float32 [2048], P(('tp', 'cp'))
- grad_middle_gain: float32 [2048], P('cp')
- grad_hidden_gain: float32 [8192], P(('tp', 'cp'))
The draws below stay inside these ranges and needn't reach their ends.
Inputs may be any that keep to these rules, and one draw needn't show every extreme that they name: `segment_ids`: along the positions of a row the ids never fall; the first position has id 0 and the last id 6.
All inputs are finite; a program needn't handle non-finite values.
Results may differ from the reference program's by a relative error of at most 0.025.
Values may be sent and summed in bfloat16 or wider, within the bound.
No kernel may reach another device: no remote copies, remote signals or barrier semaphores. Data moves between devices by JAX's collectives and lax.ppermute only.
A program may use at most 192 MiB of HBM per device.

```python
from functools import partial
import jax
import jax.numpy as jnp
from jax import lax

HEADS = 32
HD = 64
D = 2048
FF = 8192
ROWS = 1
ROW_DEV = 128
LENGTH = 1024


def draw_segment_ids(key, part):
    key = jax.random.fold_in(key, 7)
    early_key, late_key = jax.random.split(key)
    early = jax.random.randint(early_key, (3, ROWS), 1, ROW_DEV)
    late = jax.random.randint(late_key, (3, ROWS), LENGTH - ROW_DEV + 1, LENGTH)
    cuts = jnp.concatenate([early, late], axis=0)
    position = jnp.arange(LENGTH, dtype=jnp.int32)[:, None, None]
    return jnp.sum((position >= cuts[None]).astype(jnp.int32), axis=1)


def level_of(rng, dims, cuts, low, largest):
    level = 1.0
    for dim, parts in cuts:
        draws = jax.random.uniform(jax.random.fold_in(jax.random.fold_in(rng, 6), dim), (parts,), jnp.float32, low / len(cuts), largest / len(cuts))
        level = level * jnp.repeat(jnp.exp(draws), dims[dim] // parts).reshape((-1,) + (1,) * (len(dims) - 1 - dim))
    return level


def normal_values(stream_key, extent, scale, most, cuts=(), kind=jnp.bfloat16):
    array = jax.random.normal(stream_key, extent, jnp.float32) * scale
    if len(cuts) > 0:
        array = level_of(stream_key, extent, cuts, -0.22, 0.18) * array
    return jnp.clip(array, min=-most, max=most).astype(kind)


def setup_inputs(seed: int = 0) -> dict:
    splits = jax.random.split(jax.random.key(seed), 12)
    return {
        "layer_input": normal_values(splits[0], (LENGTH, ROWS, D), 1.0, 6.0, ((0, 8),)),
        "segment_ids": draw_segment_ids(jax.random.fold_in(splits[11], 71), 0),
        "qkv_weight": normal_values(splits[2], (D, 3, D), D ** -0.5, 0.125, ((2, 4),)),
        "out_weight": normal_values(splits[3], (D, D), D ** -0.5, 0.125, ((0, 4),)),
        "up_weight": normal_values(splits[4], (D, FF), D ** -0.5, 0.125, ((1, 4),)),
        "down_weight": normal_values(splits[5], (FF, D), FF ** -0.5, 0.0625, ((0, 4),)),
        "input_gain": jnp.clip(jax.random.uniform(splits[6], (D,), jnp.float32, 0.5, 1.5), 0.5, 1.5),
        "heads_gain": jnp.clip(0.5 + 1.0 * jax.random.uniform(splits[7], (D,), jnp.float32) ** level_of(splits[7], (D,), ((0, 4),), -0.2, 0.2), 0.5, 1.5),
        "middle_gain": jnp.clip(jax.random.uniform(splits[8], (D,), jnp.float32, 0.5, 1.5), 0.5, 1.5),
        "hidden_gain": jnp.clip(0.5 + 1.0 * jax.random.uniform(splits[9], (FF,), jnp.float32) ** level_of(splits[9], (FF,), ((0, 4),), -0.2, 0.2), 0.5, 1.5),
        "cotangent": normal_values(splits[10], (LENGTH, ROWS, D), 1.0, 6.0, ((0, 8),)),
    }


eps = 1e-05
scale_base = 512.0
masked_score = -1e+30

@jax.custom_vjp
def low(v):
    return lax.optimization_barrier(v.astype(jnp.bfloat16)).astype(jnp.float32)

@jax.custom_vjp
def low_back(v):
    return v

def low_keep(v):
    return (low(v), None)

def low_pass(kept, grad):
    return (grad,)

def back_keep(v):
    return (v, None)

def back_low(kept, grad):
    return (low(grad),)
low.defvjp(low_keep, low_pass)
low_back.defvjp(back_keep, back_low)

def layer_norm(vector, gain):
    center = lax.optimization_barrier(jnp.mean(vector, axis=-1, keepdims=True))
    shifted = vector - center
    spread = lax.optimization_barrier(jnp.mean(shifted * shifted, axis=-1, keepdims=True))
    return shifted * lax.rsqrt(spread + eps) * gain

def xpos_tables(positions, half):
    column = jnp.arange(half, dtype=jnp.float32)
    frequency = 10000.0 ** (-column / half)
    zeta = (2.0 * column + 0.8 * half) / (2.8 * half)
    places = positions.astype(jnp.float32)[..., None, None]
    angle = places * frequency
    return (jnp.cos(angle), jnp.sin(angle), zeta ** (places / scale_base))

def turn(vector, cosine, sine, factor):
    paired = vector.reshape(vector.shape[:-1] + (vector.shape[-1] // 2, 2))
    first_half = paired[..., 0]
    second_half = paired[..., 1]
    turned = jnp.stack([(first_half * cosine - second_half * sine) * factor, (first_half * sine + second_half * cosine) * factor], axis=-1)
    return turned.reshape(vector.shape)

def attend_block(item, key_block, value_block, key_seg):
    queries, query_seg, query_start = item
    size = queries.shape[0]
    query_index = query_start + jnp.arange(size, dtype=jnp.int32)
    key_index = jnp.arange(key_block.shape[0], dtype=jnp.int32)
    allowed = (key_index[None, :] <= query_index[:, None]) & (query_seg[:, None] == key_seg[None, :])
    scores = low_back(jnp.einsum('qhd,khd->qhk', queries, key_block, precision=lax.Precision.HIGHEST) * HD ** (-0.5))
    scores = jnp.where(allowed[:, None, :], scores, masked_score)
    top = lax.optimization_barrier(jnp.max(scores, axis=-1, keepdims=True))
    exponent = jnp.where(allowed[:, None, :], jnp.exp(scores - top), 0.0)
    probability = exponent / lax.optimization_barrier(jnp.sum(exponent, axis=-1, keepdims=True))
    return jnp.einsum('qhk,khd->qhd', low(probability), value_block, precision=lax.Precision.HIGHEST)

def attend_row(item):
    queries, key_block, value_block, seg_row = item
    block = min(512, LENGTH)
    blocks = LENGTH // block
    starts = jnp.arange(blocks, dtype=jnp.int32) * block
    step = jax.checkpoint(partial(attend_block, key_block=key_block, value_block=value_block, key_seg=seg_row))
    mixed = lax.map(step, (queries.reshape(blocks, block, HEADS, HD), seg_row.reshape(blocks, block), starts))
    return mixed.reshape(queries.shape)

def layer(stream, qkv_weight, out_weight, up_weight, down_weight, input_gain, heads_gain, middle_gain, hidden_gain, segment_ids, cosine, sine, factor):
    high = lax.Precision.HIGHEST
    normed_in = low(layer_norm(stream, input_gain))
    qkv = low_back(jnp.einsum('lrd,dce->lrce', normed_in, qkv_weight, precision=high))
    head_shape = (LENGTH, ROWS, HEADS, HD)
    queries = low(turn(qkv[:, :, 0].reshape(head_shape), cosine, sine, factor))
    key_all = low(turn(qkv[:, :, 1].reshape(head_shape), cosine, sine, 1.0 / factor))
    value_all = low(qkv[:, :, 2].reshape(head_shape))
    mixed = lax.map(jax.checkpoint(attend_row), (jnp.moveaxis(queries, 1, 0), jnp.moveaxis(key_all, 1, 0), jnp.moveaxis(value_all, 1, 0), segment_ids.T))
    attended = low_back(jnp.moveaxis(mixed, 0, 1).reshape(LENGTH, ROWS, D))
    normed_heads = low(layer_norm(attended, heads_gain))
    middle = stream + low_back(jnp.einsum('lrd,de->lre', normed_heads, out_weight, precision=high))
    normed_mid = low(layer_norm(middle, middle_gain))
    hidden = low_back(jnp.einsum('lrd,df->lrf', normed_mid, up_weight, precision=high))
    normed_hidden = low(layer_norm(jax.nn.gelu(hidden, approximate=False), hidden_gain))
    return middle + jnp.einsum('lrf,fd->lrd', normed_hidden, down_weight, precision=high)

def reference(layer_input, segment_ids, qkv_weight, out_weight, up_weight, down_weight, input_gain, heads_gain, middle_gain, hidden_gain, cotangent):
    position = jnp.arange(LENGTH, dtype=jnp.int32)[:, None]
    previous = jnp.concatenate([segment_ids[:1], segment_ids[:-1]], axis=0)
    boundary = jnp.where((segment_ids != previous) | (position == 0), position, 0)
    places = position - lax.cummax(boundary, axis=0)
    cosine, sine, factor = xpos_tables(places, HD // 2)

    def forward(*params):
        return layer(*params, segment_ids, cosine, sine, factor)
    primals = tuple((v.astype(jnp.float32) for v in (layer_input, qkv_weight, out_weight, up_weight, down_weight, input_gain, heads_gain, middle_gain, hidden_gain)))
    result, pullback = jax.vjp(forward, *primals)
    grads = pullback(cotangent.astype(jnp.float32))
    return (result.astype(jnp.bfloat16), grads[0].astype(jnp.bfloat16), grads[1], grads[2], grads[3], grads[4], grads[5], grads[6], grads[7], grads[8])
```

```python
import jax
import jax.numpy as jnp
from jax import lax
from jax.sharding import PartitionSpec as P

HD = 64
D = 2048
FF = 8192

eps = 1e-05
scale_base = 512.0
masked_score = -1e30
f32 = jnp.float32
bf16 = jnp.bfloat16


def dot(a, b):
    return jnp.dot(a, b, preferred_element_type=f32)


def dot_t(a, b):
    return lax.dot_general(a, b, (((1,), (1,)), ((), ())), preferred_element_type=f32)


def t_dot(a, b):
    return lax.dot_general(a, b, (((0,), (0,)), ((), ())), preferred_element_type=f32)


def pairs(count, k):
    return [(i, i ^ k) for i in range(count)]


def swap_tp(value, k):
    return lax.ppermute(value, "tp", pairs(lax.axis_size("tp"), k))


def tp_order(value):
    count, me = lax.axis_size("tp"), lax.axis_index("tp")
    part = value.shape[0] // count
    return jnp.concatenate(
        [lax.dynamic_slice_in_dim(value, (me ^ k) * part, part, 0) for k in range(count)], axis=0
    )


def tp_scatter_sum(partial_sum):
    count = lax.axis_size("tp")
    part = partial_sum.shape[0] // count
    low = partial_sum.astype(bf16)
    total = partial_sum[:part]
    for k in range(1, count):
        total = total + swap_tp(low[k * part : (k + 1) * part], k).astype(f32)
    return total


def tp_gather(block):
    count = lax.axis_size("tp")
    return jnp.concatenate([block] + [swap_tp(block, k) for k in range(1, count)], axis=0)


def tp_sum(value):
    total = value
    for k in range(1, lax.axis_size("tp")):
        total = total + swap_tp(value, k)
    return total


def tp_token_sum(value):
    count = lax.axis_size("tp")
    blocks = value.reshape(value.shape[0], count, -1)
    total = blocks
    for k in range(1, count):
        got = swap_tp(blocks, k)
        total = total + jnp.stack([got[:, j ^ k] for j in range(count)], axis=1)
    return total.reshape(value.shape)


def cp_columns(value):
    return lax.all_to_all(value, "cp", split_axis=1, concat_axis=0, tiled=True)


def cp_gather(value):
    return lax.all_gather(value, "cp", axis=0, tiled=True)


def xpos_tables(positions):
    column = jnp.arange(HD // 2, dtype=f32)
    frequency = 10000.0 ** (-column / (HD // 2))
    zeta = (2.0 * column + 0.4 * HD) / (1.4 * HD)
    places = positions.astype(f32)[:, None]
    angle = places * frequency
    return (jnp.cos(angle), jnp.sin(angle), zeta ** (places / scale_base))


def turn(vector, cosine, sine, factor):
    paired = vector.reshape(vector.shape[:-1] + (HD // 2, 2))
    first, second = paired[..., 0], paired[..., 1]
    cosine, sine, factor = cosine[:, None], sine[:, None], factor[:, None]
    turned = jnp.stack(
        [(first * cosine - second * sine) * factor, (first * sine + second * cosine) * factor],
        axis=-1,
    )
    return turned.reshape(vector.shape)


def norm_rows(vector):
    center = jnp.mean(vector, axis=-1, keepdims=True)
    shifted = vector - center
    scaling = lax.rsqrt(jnp.mean(shifted * shifted, axis=-1, keepdims=True) + eps)
    return (shifted * scaling, scaling)


def norm_back(grad_result, gain, normed, scaling):
    grad_normed = grad_result * gain
    first = jnp.mean(grad_normed, axis=-1, keepdims=True)
    cross = jnp.mean(grad_normed * normed, axis=-1, keepdims=True)
    return scaling * (grad_normed - first - normed * cross)


def attend(queries, keys, values, allowed):
    scores = jnp.einsum("qhd,khd->hqk", queries, keys, preferred_element_type=f32) * HD**-0.5
    scores = jnp.where(allowed[None], scores, masked_score)
    top = jnp.max(scores, axis=-1, keepdims=True)
    exponent = jnp.where(allowed[None], jnp.exp(scores - top), 0.0)
    total = jnp.sum(exponent, axis=-1, keepdims=True)
    probability = (exponent / total).astype(bf16)
    mixed = jnp.einsum("hqk,khd->qhd", probability, values, preferred_element_type=f32)
    return (mixed, top + jnp.log(total))


def attend_back(queries, keys, values, allowed, lse, grad, delta):
    scores = jnp.einsum("qhd,khd->hqk", queries, keys, preferred_element_type=f32) * HD**-0.5
    probability = jnp.where(allowed[None], jnp.exp(scores - lse), 0.0)
    grad_prob = jnp.einsum("qhd,khd->hqk", grad, values, preferred_element_type=f32)
    grad_scores = (probability * (grad_prob - delta.T[:, :, None])).astype(bf16)
    grad_q = jnp.einsum("hqk,khd->qhd", grad_scores, keys, preferred_element_type=f32) * HD**-0.5
    grad_k = jnp.einsum("hqk,qhd->khd", grad_scores, queries, preferred_element_type=f32) * HD**-0.5
    grad_v = jnp.einsum(
        "hqk,qhd->khd", probability.astype(bf16), grad, preferred_element_type=f32
    )
    return (grad_q, grad_k, grad_v)


def body(
    layer_input,
    segment_ids,
    qkv_weight,
    out_weight,
    up_weight,
    down_weight,
    input_gain,
    heads_gain,
    middle_gain,
    hidden_gain,
    cotangent,
):
    local_len, row_count, width = layer_input.shape
    tp_count, cp_count = lax.axis_size("tp"), lax.axis_size("cp")
    me_tp, me_cp = lax.axis_index("tp"), lax.axis_index("cp")
    part = local_len // tp_count
    head_width = qkv_weight.shape[2]
    heads = head_width // HD
    by_head = heads % cp_count == 0
    own_heads = heads // cp_count if by_head else heads
    weight3 = jnp.transpose(qkv_weight, (1, 0, 2))

    x = tp_order(layer_input.reshape(local_len, width))
    gy = tp_order(cotangent.reshape(local_len, width))
    seg = tp_order(segment_ids)[:, 0]
    natural = tp_order(jnp.arange(local_len, dtype=jnp.int32))
    position = me_cp * local_len + natural
    position_all = (jnp.arange(cp_count, dtype=jnp.int32)[:, None] * local_len + natural).reshape(-1)

    stream = x.astype(f32)
    normed_one, scaling_one = norm_rows(stream)
    a = (normed_one * input_gain).astype(bf16)
    a_all = cp_gather(a)
    cosine, sine, factor = xpos_tables(position)
    raw_q = dot(a, weight3[0]).reshape(local_len, heads, HD)
    raw_k = dot(a, weight3[1]).reshape(local_len, heads, HD)
    raw_v = dot(a, weight3[2]).reshape(local_len, heads, HD)
    q = turn(raw_q, cosine, sine, factor).astype(bf16)
    k = turn(raw_k, cosine, sine, 1.0 / factor).astype(bf16)
    v = raw_v.astype(bf16)
    if by_head:
        extra = jnp.broadcast_to(seg.astype(bf16)[:, None, None], (local_len, cp_count, 16))
        sent = jnp.concatenate(
            [t.reshape(local_len, cp_count, own_heads * HD) for t in (q, k, v)] + [extra], axis=-1
        )
        got = lax.all_to_all(sent, "cp", split_axis=1, concat_axis=0, tiled=True)[:, 0]
        span = own_heads * HD
        q_all, k_all, v_all = (
            got[:, i * span : (i + 1) * span].reshape(-1, own_heads, HD) for i in range(3)
        )
        seg_all = got[:, 3 * span]
        seg_q, position_q = seg_all, position_all
    else:
        q_all, k_all, v_all = q, cp_gather(k), cp_gather(v)
        seg_all = cp_gather(seg.astype(bf16))
        seg_q, position_q = seg.astype(bf16), position
    allowed = (position_all[None, :] <= position_q[:, None]) & (seg_q[:, None] == seg_all[None, :])
    mixed, lse = attend(q_all, k_all, v_all, allowed)
    if by_head:
        attended = lax.all_to_all(
            mixed.astype(bf16).reshape(cp_count * local_len, own_heads * HD),
            "cp", split_axis=0, concat_axis=1, tiled=True,
        ).astype(f32)
    else:
        attended = mixed.reshape(local_len, head_width)

    sums = tp_token_sum(jnp.stack([jnp.sum(attended, axis=1), jnp.sum(attended * attended, axis=1)]))
    center = sums[0] / width
    scaling_h = lax.rsqrt(sums[1] / width - center * center + eps)[:, None]
    normed_h = (attended - center[:, None]) * scaling_h
    z = (normed_h * heads_gain).astype(bf16)
    gain_row = tp_sum(jnp.dot(heads_gain, out_weight.astype(f32)))
    branch = tp_scatter_sum(dot(z, out_weight))
    x1 = stream[:part] + branch
    normed_two, scaling_two = norm_rows(x1)
    u = tp_gather((normed_two * middle_gain).astype(bf16))

    grad_hid = dot_t(gy, down_weight)
    grad_normed = grad_hid * hidden_gain
    hidden = dot(u, up_weight)
    cdf = 0.5 * (1.0 + lax.erf(hidden * (0.5**0.5)))
    act = hidden * cdf
    slope = cdf + hidden * jnp.exp(-0.5 * hidden * hidden) * 0.3989422804014327
    sums = tp_token_sum(
        jnp.stack(
            [
                jnp.sum(act, axis=1),
                jnp.sum(act * act, axis=1),
                jnp.sum(grad_normed, axis=1),
                jnp.sum(grad_normed * act, axis=1),
            ]
        )
    )
    center = sums[0] / FF
    scaling_f = lax.rsqrt(sums[1] / FF - center * center + eps)
    first = sums[2] / FF
    cross = scaling_f * (sums[3] / FF - center * first)
    normed_f = (act - center[:, None]) * scaling_f[:, None]
    z2 = (normed_f * hidden_gain).astype(bf16)
    grad_act = scaling_f[:, None] * (grad_normed - first[:, None] - normed_f * cross[:, None])
    gh = (grad_act * slope).astype(bf16)
    hidden_gain_sum = jnp.sum(grad_hid * normed_f, axis=0)
    gu = tp_scatter_sum(dot_t(gh, up_weight))
    gx1 = gy[:part].astype(f32) + norm_back(gu, middle_gain, normed_two, scaling_two)
    middle_gain_sum = jnp.sum(gu * normed_two, axis=0)
    gb_own = gx1.astype(bf16)
    gb_f = gb_own.astype(f32)
    first = jnp.sum(gb_f * gain_row, axis=1) / width
    cross = jnp.sum(gb_f * branch, axis=1) / width
    gb = tp_gather(gb_own)
    stats = tp_gather(jnp.stack([first, cross], axis=1))

    gz = dot_t(gb, out_weight)
    heads_gain_sum = jnp.sum(gz * normed_h, axis=0)
    go = (scaling_h * (gz * heads_gain - stats[:, :1] - normed_h * stats[:, 1:])).astype(bf16)
    if by_head:
        grad_mixed = cp_columns(go).reshape(-1, own_heads, HD)
    else:
        grad_mixed = go.reshape(local_len, heads, HD)
    delta = jnp.sum(grad_mixed.astype(f32) * mixed, axis=-1)
    gq, gk, gv = attend_back(q_all, k_all, v_all, allowed, lse, grad_mixed, delta)
    if by_head:
        cos_all, sin_all, factor_all = xpos_tables(position_all)
    else:
        cos_all, sin_all, factor_all = cosine, sine, factor
        gk = lax.psum_scatter(gk.astype(bf16), "cp", scatter_dimension=0, tiled=True).astype(f32)
        gv = lax.psum_scatter(gv.astype(bf16), "cp", scatter_dimension=0, tiled=True).astype(f32)
    gq = turn(gq, cos_all, -sin_all, factor_all)
    gk = turn(gk, cos_all, -sin_all, 1.0 / factor_all)
    grads = jnp.stack([gq, gk, gv], axis=1).astype(bf16)
    if by_head:
        grads_own = grads.reshape(-1, 3 * own_heads * HD)
        grads = lax.all_to_all(
            grads.reshape(-1, 3, own_heads * HD), "cp", split_axis=0, concat_axis=2, tiled=True
        )
    else:
        grads = grads.reshape(local_len, 3, head_width)
        grads_own = lax.all_to_all(grads, "cp", split_axis=2, concat_axis=0, tiled=True)
        grads_own = grads_own.reshape(-1, 3 * head_width // cp_count)
    ga = (
        dot_t(grads[:, 0], weight3[0]) + dot_t(grads[:, 1], weight3[1]) + dot_t(grads[:, 2], weight3[2])
    )
    ga = tp_scatter_sum(ga)
    input_gain_sum = jnp.sum(ga * normed_one[:part], axis=0)
    grad_in = gx1 + norm_back(ga, input_gain, normed_one[:part], scaling_one[:part])

    y = (x1 + tp_scatter_sum(dot(z2, down_weight))).astype(bf16)
    layer_output = tp_order(tp_gather(y)).reshape(layer_input.shape)
    grad_input = tp_order(tp_gather(grad_in.astype(bf16))).reshape(layer_input.shape)

    grad_down = t_dot(cp_columns(z2), cp_gather(gy))
    grad_up = t_dot(cp_columns(u), cp_gather(gh))
    grad_out = t_dot(cp_columns(z), cp_gather(gb))
    grad_qkv = t_dot(a_all, grads_own).astype(bf16)
    grad_qkv = lax.all_to_all(
        grad_qkv.reshape(width, 3, head_width // cp_count), "cp", split_axis=0, concat_axis=2, tiled=True
    ).astype(f32)

    def cp_sum_own(vector):
        return jnp.sum(lax.all_to_all(vector.reshape(cp_count, -1), "cp", 0, 0, tiled=True), axis=0)

    def both_sum_own(vector):
        return tp_sum(cp_sum_own(vector))

    return (
        layer_output,
        grad_input,
        grad_qkv,
        grad_out,
        grad_up,
        grad_down,
        both_sum_own(input_gain_sum),
        cp_sum_own(heads_gain_sum),
        both_sum_own(middle_gain_sum),
        cp_sum_own(hidden_gain_sum),
    )


def solution(mesh):
    placed = (
        P("cp", None, None),
        P("cp", None),
        P(None, None, "tp"),
        P("tp", None),
        P(None, "tp"),
        P("tp", None),
        P(),
        P("tp"),
        P(),
        P("tp"),
        P("cp", None, None),
    )
    return jax.shard_map(
        body,
        mesh=mesh,
        in_specs=placed,
        out_specs=(
            P("cp", None, None),
            P("cp", None, None),
            P("cp", None, "tp"),
            P(("tp", "cp"), None),
            P("cp", "tp"),
            P(("tp", "cp"), None),
            P("cp"),
            P(("tp", "cp")),
            P("cp"),
            P(("tp", "cp")),
        ),
        check_vma=False,
    )
```

```python
import functools

import jax
import jax.numpy as jnp
import numpy as np
from jax import lax
from jax.experimental import pallas as pl
from jax.experimental.pallas import tpu as pltpu
from jax.sharding import PartitionSpec as P

HD = 64
D = 2048
FF = 8192

eps = 1e-05
scale_base = 512.0
masked_score = -1e30
f32 = jnp.float32
bf16 = jnp.bfloat16


def dot(a, b):
    return jnp.dot(a, b, preferred_element_type=f32)


def dot_t(a, b):
    return lax.dot_general(a, b, (((1,), (1,)), ((), ())), preferred_element_type=f32)


def t_dot(a, b):
    return lax.dot_general(a, b, (((0,), (0,)), ((), ())), preferred_element_type=f32)


def pairs(count, k):
    return [(i, i ^ k) for i in range(count)]


def swap_tp(value, k):
    return lax.ppermute(value, "tp", pairs(lax.axis_size("tp"), k))


def tp_order(value):
    count, me = lax.axis_size("tp"), lax.axis_index("tp")
    part = value.shape[0] // count
    return jnp.concatenate(
        [lax.dynamic_slice_in_dim(value, (me ^ k) * part, part, 0) for k in range(count)], axis=0
    )


def tp_scatter_sum(partial_sum):
    count = lax.axis_size("tp")
    part = partial_sum.shape[0] // count
    low = partial_sum.astype(bf16)
    total = partial_sum[:part]
    for k in range(1, count):
        total = total + swap_tp(low[k * part : (k + 1) * part], k).astype(f32)
    return total


def tp_gather(block):
    count = lax.axis_size("tp")
    return jnp.concatenate([block] + [swap_tp(block, k) for k in range(1, count)], axis=0)


def tp_sum(value):
    total = value
    for k in range(1, lax.axis_size("tp")):
        total = total + swap_tp(value, k)
    return total


def tp_token_sum(value):
    count = lax.axis_size("tp")
    blocks = value.reshape(value.shape[0], count, -1)
    total = blocks
    for k in range(1, count):
        got = swap_tp(blocks, k)
        total = total + jnp.stack([got[:, j ^ k] for j in range(count)], axis=1)
    return total.reshape(value.shape)


def cp_columns(value):
    return lax.all_to_all(value, "cp", split_axis=1, concat_axis=0, tiled=True)


def cp_gather(value):
    return lax.all_gather(value, "cp", axis=0, tiled=True)


def xpos_tables(positions):
    column = jnp.arange(HD // 2, dtype=f32)
    frequency = 10000.0 ** (-column / (HD // 2))
    zeta = (2.0 * column + 0.4 * HD) / (1.4 * HD)
    places = positions.astype(f32)[:, None]
    angle = places * frequency
    return (jnp.cos(angle), jnp.sin(angle), zeta ** (places / scale_base))


def turn(vector, cosine, sine, factor):
    paired = vector.reshape(vector.shape[:-1] + (HD // 2, 2))
    first, second = paired[..., 0], paired[..., 1]
    cosine, sine, factor = cosine[:, None], sine[:, None], factor[:, None]
    turned = jnp.stack(
        [(first * cosine - second * sine) * factor, (first * sine + second * cosine) * factor],
        axis=-1,
    )
    return turned.reshape(vector.shape)


def norm_rows(vector):
    center = jnp.mean(vector, axis=-1, keepdims=True)
    shifted = vector - center
    scaling = lax.rsqrt(jnp.mean(shifted * shifted, axis=-1, keepdims=True) + eps)
    return (shifted * scaling, scaling)


def norm_back(grad_result, gain, normed, scaling):
    grad_normed = grad_result * gain
    first = jnp.mean(grad_normed, axis=-1, keepdims=True)
    cross = jnp.mean(grad_normed * normed, axis=-1, keepdims=True)
    return scaling * (grad_normed - first - normed * cross)


def attend(queries, keys, values, allowed):
    scores = jnp.einsum("qhd,khd->hqk", queries, keys, preferred_element_type=f32) * HD**-0.5
    scores = jnp.where(allowed[None], scores, masked_score)
    top = jnp.max(scores, axis=-1, keepdims=True)
    exponent = jnp.where(allowed[None], jnp.exp(scores - top), 0.0)
    total = jnp.sum(exponent, axis=-1, keepdims=True)
    probability = (exponent / total).astype(bf16)
    mixed = jnp.einsum("hqk,khd->qhd", probability, values, preferred_element_type=f32)
    return (mixed, top + jnp.log(total))


def attend_back(queries, keys, values, allowed, lse, grad, delta):
    scores = jnp.einsum("qhd,khd->hqk", queries, keys, preferred_element_type=f32) * HD**-0.5
    probability = jnp.where(allowed[None], jnp.exp(scores - lse), 0.0)
    grad_prob = jnp.einsum("qhd,khd->hqk", grad, values, preferred_element_type=f32)
    grad_scores = (probability * (grad_prob - delta.T[:, :, None])).astype(bf16)
    grad_q = jnp.einsum("hqk,khd->qhd", grad_scores, keys, preferred_element_type=f32) * HD**-0.5
    grad_k = jnp.einsum("hqk,qhd->khd", grad_scores, queries, preferred_element_type=f32) * HD**-0.5
    grad_v = jnp.einsum(
        "hqk,qhd->khd", probability.astype(bf16), grad, preferred_element_type=f32
    )
    return (grad_q, grad_k, grad_v)


def body_general(
    layer_input,
    segment_ids,
    qkv_weight,
    out_weight,
    up_weight,
    down_weight,
    input_gain,
    heads_gain,
    middle_gain,
    hidden_gain,
    cotangent,
):
    local_len, row_count, width = layer_input.shape
    tp_count, cp_count = lax.axis_size("tp"), lax.axis_size("cp")
    me_tp, me_cp = lax.axis_index("tp"), lax.axis_index("cp")
    part = local_len // tp_count
    head_width = qkv_weight.shape[2]
    heads = head_width // HD
    by_head = heads % cp_count == 0
    own_heads = heads // cp_count if by_head else heads
    weight3 = jnp.transpose(qkv_weight, (1, 0, 2))

    x = tp_order(layer_input.reshape(local_len, width))
    gy = tp_order(cotangent.reshape(local_len, width))
    seg = tp_order(segment_ids)[:, 0]
    natural = tp_order(jnp.arange(local_len, dtype=jnp.int32))
    position = me_cp * local_len + natural
    position_all = (jnp.arange(cp_count, dtype=jnp.int32)[:, None] * local_len + natural).reshape(-1)

    stream = x.astype(f32)
    normed_one, scaling_one = norm_rows(stream)
    a = (normed_one * input_gain).astype(bf16)
    a_all = cp_gather(a)
    cosine, sine, factor = xpos_tables(position)
    raw_q = dot(a, weight3[0]).reshape(local_len, heads, HD)
    raw_k = dot(a, weight3[1]).reshape(local_len, heads, HD)
    raw_v = dot(a, weight3[2]).reshape(local_len, heads, HD)
    q = turn(raw_q, cosine, sine, factor).astype(bf16)
    k = turn(raw_k, cosine, sine, 1.0 / factor).astype(bf16)
    v = raw_v.astype(bf16)
    if by_head:
        extra = jnp.broadcast_to(seg.astype(bf16)[:, None, None], (local_len, cp_count, 16))
        sent = jnp.concatenate(
            [t.reshape(local_len, cp_count, own_heads * HD) for t in (q, k, v)] + [extra], axis=-1
        )
        got = lax.all_to_all(sent, "cp", split_axis=1, concat_axis=0, tiled=True)[:, 0]
        span = own_heads * HD
        q_all, k_all, v_all = (
            got[:, i * span : (i + 1) * span].reshape(-1, own_heads, HD) for i in range(3)
        )
        seg_all = got[:, 3 * span]
        seg_q, position_q = seg_all, position_all
    else:
        q_all, k_all, v_all = q, cp_gather(k), cp_gather(v)
        seg_all = cp_gather(seg.astype(bf16))
        seg_q, position_q = seg.astype(bf16), position
    allowed = (position_all[None, :] <= position_q[:, None]) & (seg_q[:, None] == seg_all[None, :])
    mixed, lse = attend(q_all, k_all, v_all, allowed)
    if by_head:
        attended = lax.all_to_all(
            mixed.astype(bf16).reshape(cp_count * local_len, own_heads * HD),
            "cp", split_axis=0, concat_axis=1, tiled=True,
        ).astype(f32)
    else:
        attended = mixed.reshape(local_len, head_width)

    sums = tp_token_sum(jnp.stack([jnp.sum(attended, axis=1), jnp.sum(attended * attended, axis=1)]))
    center = sums[0] / width
    scaling_h = lax.rsqrt(sums[1] / width - center * center + eps)[:, None]
    normed_h = (attended - center[:, None]) * scaling_h
    z = (normed_h * heads_gain).astype(bf16)
    gain_row = tp_sum(jnp.dot(heads_gain, out_weight.astype(f32)))
    branch = tp_scatter_sum(dot(z, out_weight))
    x1 = stream[:part] + branch
    normed_two, scaling_two = norm_rows(x1)
    u = tp_gather((normed_two * middle_gain).astype(bf16))

    grad_hid = dot_t(gy, down_weight)
    grad_normed = grad_hid * hidden_gain
    hidden = dot(u, up_weight)
    cdf = 0.5 * (1.0 + lax.erf(hidden * (0.5**0.5)))
    act = hidden * cdf
    slope = cdf + hidden * jnp.exp(-0.5 * hidden * hidden) * 0.3989422804014327
    sums = tp_token_sum(
        jnp.stack(
            [
                jnp.sum(act, axis=1),
                jnp.sum(act * act, axis=1),
                jnp.sum(grad_normed, axis=1),
                jnp.sum(grad_normed * act, axis=1),
            ]
        )
    )
    center = sums[0] / FF
    scaling_f = lax.rsqrt(sums[1] / FF - center * center + eps)
    first = sums[2] / FF
    cross = scaling_f * (sums[3] / FF - center * first)
    normed_f = (act - center[:, None]) * scaling_f[:, None]
    z2 = (normed_f * hidden_gain).astype(bf16)
    grad_act = scaling_f[:, None] * (grad_normed - first[:, None] - normed_f * cross[:, None])
    gh = (grad_act * slope).astype(bf16)
    hidden_gain_sum = jnp.sum(grad_hid * normed_f, axis=0)
    gu = tp_scatter_sum(dot_t(gh, up_weight))
    gx1 = gy[:part].astype(f32) + norm_back(gu, middle_gain, normed_two, scaling_two)
    middle_gain_sum = jnp.sum(gu * normed_two, axis=0)
    gb_own = gx1.astype(bf16)
    gb_f = gb_own.astype(f32)
    first = jnp.sum(gb_f * gain_row, axis=1) / width
    cross = jnp.sum(gb_f * branch, axis=1) / width
    gb = tp_gather(gb_own)
    stats = tp_gather(jnp.stack([first, cross], axis=1))

    gz = dot_t(gb, out_weight)
    heads_gain_sum = jnp.sum(gz * normed_h, axis=0)
    go = (scaling_h * (gz * heads_gain - stats[:, :1] - normed_h * stats[:, 1:])).astype(bf16)
    if by_head:
        grad_mixed = cp_columns(go).reshape(-1, own_heads, HD)
    else:
        grad_mixed = go.reshape(local_len, heads, HD)
    delta = jnp.sum(grad_mixed.astype(f32) * mixed, axis=-1)
    gq, gk, gv = attend_back(q_all, k_all, v_all, allowed, lse, grad_mixed, delta)
    if by_head:
        cos_all, sin_all, factor_all = xpos_tables(position_all)
    else:
        cos_all, sin_all, factor_all = cosine, sine, factor
        gk = lax.psum_scatter(gk.astype(bf16), "cp", scatter_dimension=0, tiled=True).astype(f32)
        gv = lax.psum_scatter(gv.astype(bf16), "cp", scatter_dimension=0, tiled=True).astype(f32)
    gq = turn(gq, cos_all, -sin_all, factor_all)
    gk = turn(gk, cos_all, -sin_all, 1.0 / factor_all)
    grads = jnp.stack([gq, gk, gv], axis=1).astype(bf16)
    if by_head:
        grads_own = grads.reshape(-1, 3 * own_heads * HD)
        grads = lax.all_to_all(
            grads.reshape(-1, 3, own_heads * HD), "cp", split_axis=0, concat_axis=2, tiled=True
        )
    else:
        grads = grads.reshape(local_len, 3, head_width)
        grads_own = lax.all_to_all(grads, "cp", split_axis=2, concat_axis=0, tiled=True)
        grads_own = grads_own.reshape(-1, 3 * head_width // cp_count)
    ga = (
        dot_t(grads[:, 0], weight3[0]) + dot_t(grads[:, 1], weight3[1]) + dot_t(grads[:, 2], weight3[2])
    )
    ga = tp_scatter_sum(ga)
    input_gain_sum = jnp.sum(ga * normed_one[:part], axis=0)
    grad_in = gx1 + norm_back(ga, input_gain, normed_one[:part], scaling_one[:part])

    y = (x1 + tp_scatter_sum(dot(z2, down_weight))).astype(bf16)
    layer_output = tp_order(tp_gather(y)).reshape(layer_input.shape)
    grad_input = tp_order(tp_gather(grad_in.astype(bf16))).reshape(layer_input.shape)

    grad_down = t_dot(cp_columns(z2), cp_gather(gy))
    grad_up = t_dot(cp_columns(u), cp_gather(gh))
    grad_out = t_dot(cp_columns(z), cp_gather(gb))
    grad_qkv = t_dot(a_all, grads_own).astype(bf16)
    grad_qkv = lax.all_to_all(
        grad_qkv.reshape(width, 3, head_width // cp_count), "cp", split_axis=0, concat_axis=2, tiled=True
    ).astype(f32)

    def cp_sum_own(vector):
        return jnp.sum(lax.all_to_all(vector.reshape(cp_count, -1), "cp", 0, 0, tiled=True), axis=0)

    def both_sum_own(vector):
        return tp_sum(cp_sum_own(vector))

    return (
        layer_output,
        grad_input,
        grad_qkv,
        grad_out,
        grad_up,
        grad_down,
        both_sum_own(input_gain_sum),
        cp_sum_own(heads_gain_sum),
        both_sum_own(middle_gain_sum),
        cp_sum_own(hidden_gain_sum),
    )


INTERPRET = False


def params(megabytes):
    return pltpu.CompilerParams(vmem_limit_bytes=megabytes * 1024 * 1024)


def shape(dims, kind):
    return jax.ShapeDtypeStruct(dims, kind)


def whole():
    return pl.BlockSpec(memory_space=pltpu.VMEM)


def scalars():
    return pl.BlockSpec(memory_space=pltpu.SMEM)


def call(kernel, outs, args, specs=None, out_specs=None, grid=None, scratch=(), mb=32, flops=0, after=()):
    specs = list(specs) if specs is not None else [whole() for _ in args]
    count = len(args)
    extra = len(after)

    def run(*refs):
        kernel(*refs[:count], *refs[count + extra :])

    moved = sum(int(np.prod(t.shape)) * t.dtype.itemsize for t in list(args) + list(outs))
    options = {} if grid is None else {"grid": grid}
    return pl.pallas_call(
        run,
        out_shape=tuple(outs),
        in_specs=specs + [pl.BlockSpec(memory_space=pl.ANY)] * extra,
        out_specs=tuple(out_specs) if out_specs is not None else tuple(whole() for _ in outs),
        scratch_shapes=list(scratch),
        compiler_params=params(mb),
        cost_estimate=pl.CostEstimate(flops=flops, bytes_accessed=moved, transcendentals=0),
        interpret=INTERPRET,
        **options,
    )(*args, *after)


def fixed(dims):
    return pl.BlockSpec(dims, lambda i: (0,) * len(dims))


def split_low(value):
    high = value.astype(bf16)
    return high, (value - high.astype(f32)).astype(bf16)


def lanes_of(columns, rows):
    lane = lax.broadcasted_iota(jnp.int32, (rows, 128), 1)
    out = jnp.zeros((rows, 128), f32)
    for i, column in enumerate(columns):
        out = jnp.where(lane == i, column.astype(f32), out)
    return out


def pair_sum(block, i):
    return block[:, i : i + 1].astype(f32) + block[:, i + 1 : i + 2].astype(f32)


def own_order(me, part, index):
    return ((index // part) ^ me) * part + index % part


def block_at(me, k, part):
    return pl.ds(pl.multiple_of((me ^ k) * part, part), part)


def swap_pairs(value, axis):
    size = value.shape[axis]
    place = lax.broadcasted_iota(jnp.int32, value.shape, axis)
    return jnp.where(
        place % 2 == 0, pltpu.roll(value, size - 1, axis), pltpu.roll(value, 1, axis)
    )


def tables(local_len, cp_count):
    column = np.arange(HD) // 2
    frequency = 10000.0 ** (-column / (HD // 2))
    zeta = (2.0 * column + 0.4 * HD) / (1.4 * HD)

    def of(places):
        angle = places[:, None] * frequency
        factor = zeta ** (places[:, None] / scale_base)
        return np.stack([np.cos(angle), np.sin(angle), factor, 1.0 / factor]).astype(np.float32)

    return of(np.arange(local_len)), of(np.arange(cp_count) * local_len)


def project_kernel(parts, ids, x, seg, gain, weight, inner, base, a, out, tab):
    step = pl.program_id(0)
    me, mine = ids[0], ids[1]
    rows, width = x.shape
    part = rows // parts
    heads = out.shape[0]

    @pl.when(step == 0)
    def _():
        for k in range(parts):
            block = x[block_at(me, k, part), :].astype(f32)
            normed, _ = norm_rows(block)
            a[k * part : (k + 1) * part, :] = (normed * gain[...]).astype(bf16)
            for kind in range(4):
                tab[kind, k * part : (k + 1) * part, :] = inner[kind, block_at(me, k, part), :]
        place = lax.broadcasted_iota(jnp.int32, (rows, rows), 1)
        source = lax.broadcasted_iota(jnp.int32, (rows, rows), 0)
        moved = (own_order(me, part, place) == source).astype(bf16)
        ids_row = jnp.broadcast_to(seg[...].astype(f32), (16, rows)).astype(bf16)
        ordered = dot(ids_row, moved).astype(bf16)
        for j in range(heads):
            out[j, 3 * HD : 3 * HD + 16, :] = ordered

    acc = dot(a[...], weight[0])
    here = [base[kind, pl.ds(mine, 1), :] for kind in range(4)]
    cosine = tab[0] * here[0] - tab[1] * here[1]
    sine = tab[1] * here[0] + tab[0] * here[1]
    factor = jnp.where(step == 0, tab[2] * here[2], tab[3] * here[3])
    lane = lax.broadcasted_iota(jnp.int32, cosine.shape, 1)
    sine = jnp.where(lane % 2 == 0, -sine, sine)
    cosine = jnp.where(step == 2, 1.0, cosine * factor)
    sine = jnp.where(step == 2, 0.0, sine * factor)
    for i in range(acc.shape[1] // 128):
        piece = acc[:, i * 128 : (i + 1) * 128]
        turned = (piece * cosine + swap_pairs(piece, 1) * sine).T.astype(bf16)
        for h in range(128 // HD):
            out[i * (128 // HD) + h, pl.ds(pl.multiple_of(step * HD, HD), HD), :] = turned[
                h * HD : (h + 1) * HD
            ]


def gather_heads(got, keys, ids_col, values=None):
    for j in range(got.shape[0]):
        rows = slice(j * got.shape[2], (j + 1) * got.shape[2])
        both = jnp.concatenate([got[j, HD : 3 * HD, :].astype(f32)], axis=0).T
        keys[rows, :] = both[:, :HD].astype(bf16)
        if values is not None:
            values[rows, :] = both[:, HD:].astype(bf16)
        ids_col[rows, :] = got[j, 3 * HD : 3 * HD + 16, :].astype(f32).T


def visible_scores(me, part, scores, ids_col, ids_row, count, first, group):
    same = ids_col[0:count, 0:1] == ids_row
    length = group
    key = lax.broadcasted_iota(jnp.int32, (length, length), 0)
    query = lax.broadcasted_iota(jnp.int32, (length, length), 1)
    rows = first
    own = lambda index: (index // rows) * rows + own_order(me, part, index % rows)
    earlier = own(key) <= own(query)
    if count > length:
        earlier = jnp.concatenate([jnp.ones((count - length, length), jnp.bool_), earlier], axis=0)
    return same & earlier


def attend_kernel(parts, ids, got, out, mixed, lse, keys, ids_col):
    me = ids[0]
    blocks, _, rows = got.shape
    part = rows // parts
    gather_heads(got, keys, ids_col)
    group = 2 if blocks % 2 == 0 else 1
    width = group * rows
    for i in range(blocks // group):
        mine = range(i * group, (i + 1) * group)
        query = jnp.concatenate([got[j, :HD, :] for j in mine], axis=1) * bf16(HD**-0.5)
        ids_row = jnp.concatenate([got[j, 3 * HD : 3 * HD + 1, :] for j in mine], axis=1).astype(f32)
        count = (i + 1) * width
        scores = dot(keys[0:count, :], query)
        allowed = visible_scores(me, part, scores, ids_col, ids_row, count, rows, width)
        scores = jnp.where(allowed, scores, masked_score)
        top = jnp.max(scores, axis=0, keepdims=True)
        exponent = jnp.exp(scores - top)
        total = jnp.sum(exponent, axis=0, keepdims=True)
        value = jnp.concatenate([got[j, 2 * HD : 3 * HD, :] for j in range((i + 1) * group)], axis=1)
        result = dot(value, exponent.astype(bf16)) / total
        mixed[:, i * width : (i + 1) * width] = result
        lse[:, i * width : (i + 1) * width] = top + jnp.log(total)
        for n, j in enumerate(mine):
            out[j] = result[:, n * rows : (n + 1) * rows].astype(bf16)


def store_pieces(total, own, pieces, part, extra=None):
    own[:, : total.shape[1]] = total[:part]
    for k, piece in enumerate(pieces, 1):
        piece[:, : total.shape[1]] = total[k * part : (k + 1) * part].astype(bf16)
    if extra is not None:
        own[:, total.shape[1] :] = extra[:part]
        for k, piece in enumerate(pieces, 1):
            piece[:, total.shape[1] :] = extra[k * part : (k + 1) * part].astype(bf16)


def out_kernel(parts, att, gain, weight, own, *pieces):
    blocks, _, rows = att.shape
    part = rows // parts
    value = jnp.concatenate([att[j].astype(f32) for j in range(blocks)], axis=0).T
    high, low = split_low(jnp.mean(value, axis=1, keepdims=True))
    centred = value - (high.astype(f32) + low.astype(f32))
    square = split_low(jnp.sum(centred * centred, axis=1, keepdims=True))
    total = dot((centred * gain[...]).astype(bf16), weight[...])
    store_pieces(total, own, pieces, part, lanes_of([high, low, *square], rows))


def middle_kernel(parts, head_width, ids, own, *refs):
    got, refs = refs[: parts - 1], refs[parts - 1 :]
    gain_rows, refs = refs[:parts], refs[parts:]
    x, gain, x1, u = refs
    part, width = x1.shape
    blocks = [own] + list(got)
    means = [pair_sum(b[:, width:], 0) for b in blocks]
    squares = [pair_sum(b[:, width:], 2) for b in blocks]
    mean = sum(means) / parts
    spread = sum(squares) + head_width * sum((m - mean) * (m - mean) for m in means)
    scaling = lax.rsqrt(spread / width + eps)
    total = sum(b[:, :width].astype(f32) for b in blocks)
    for m, row in zip(means, gain_rows):
        total = total + (m - mean) * row[...]
    value = x[block_at(ids[0], 0, part), :].astype(f32) + total * scaling
    x1[...] = value
    normed, _ = norm_rows(value)
    u[:, :width] = (normed * gain[...]).astype(bf16)
    u[:, width:] = lanes_of([*split_low(mean), *split_low(scaling)], part).astype(bf16)


def grad_hidden_kernel(parts, ids, gy, weight, heads_gain, out_weight, grad, gain_row, ordered):
    rows = gy.shape[0]
    part = rows // parts

    @pl.when(pl.program_id(0) == 0)
    def _():
        for k in range(parts):
            ordered[k * part : (k + 1) * part, :] = gy[block_at(ids[0], k, part), :]
        high, low = split_low(heads_gain[...])
        row = lax.broadcasted_iota(jnp.int32, (16, heads_gain.shape[1]), 0)
        both = jnp.where(row == 0, high.astype(f32), jnp.where(row == 1, low.astype(f32), 0.0))
        product = dot(both.astype(bf16), out_weight[...])
        gain_row[...] = product[0:1] + product[1:2]

    grad[...] = dot_t(ordered[...], weight[...])


def up_kernel(parts, own, *refs):
    got, refs = refs[: parts - 1], refs[parts - 1 :]
    weight, grad, gain, act, slope, u, stats, rows_u, sums = refs
    step = pl.program_id(0)
    part = own.shape[0]
    rows, width = rows_u.shape

    @pl.when(step == 0)
    def _():
        for k, block in enumerate([own] + list(got)):
            rows_u[k * part : (k + 1) * part, :] = block[:, :width]
        wide = u.shape[2]
        for j in range(u.shape[0]):
            u[j] = rows_u[:, j * wide : (j + 1) * wide]
        sums[...] = jnp.zeros_like(sums)

    hidden = dot(rows_u[...], weight[...])
    cdf = 0.5 * (1.0 + lax.erf(hidden * (0.5**0.5)))
    value = hidden * cdf
    act[...] = value
    slope[...] = cdf + hidden * jnp.exp(-0.5 * hidden * hidden) * 0.3989422804014327
    grad_normed = grad[...] * gain[...]
    columns = [value, value * value, grad_normed, grad_normed * value]
    sums[...] += lanes_of([jnp.sum(c, axis=1, keepdims=True) for c in columns], rows)

    @pl.when(step == pl.num_programs(0) - 1)
    def _():
        stats[...] = sums[...].T[:8, :]


def swap_lane_blocks(value, k, part):
    lanes = value.shape[1]
    lane = lax.broadcasted_iota(jnp.int32, value.shape, 1)
    distance = 1
    while distance <= k:
        if k & distance:
            move = distance * part
            value = jnp.where(
                (lane // move) % 2 == 0,
                pltpu.roll(value, lanes - move, 1),
                pltpu.roll(value, move, 1),
            )
        distance *= 2
    return value


def hidden_back_kernel(parts, full, own, *refs):
    got, refs = refs[: parts - 1], refs[parts - 1 :]
    act, slope, grad, gain, weight, gh, z2, gain_sum, own_out = refs[:9]
    pieces, (acc, cols) = refs[9 : 9 + parts - 1], refs[9 + parts - 1 :]
    step = pl.program_id(0)
    rows = act.shape[0]
    part = rows // parts

    @pl.when(step == 0)
    def _():
        total = own[...]
        for k, block in enumerate(got, 1):
            total = total + swap_lane_blocks(block[...], k, part)
        mean = total[0:1] / full
        scaling = lax.rsqrt(total[1:2] / full - mean * mean + eps)
        first = total[2:3] / full
        cross = scaling * (total[3:4] / full - mean * first)
        row = lax.broadcasted_iota(jnp.int32, (rows, rows), 0)
        table = jnp.zeros((rows, rows), f32)
        for i, value in enumerate([mean, scaling, first, cross]):
            table = jnp.where(row == i, value, table)
        cols[...] = table.T
        acc[...] = jnp.zeros_like(acc)

    mean, scaling, first, cross = (cols[:, i : i + 1] for i in range(4))
    normed = (act[...] - mean) * scaling
    low = (normed * gain[...]).astype(bf16)
    wide = z2.shape[2]
    for j in range(z2.shape[0]):
        z2[j] = low[:, j * wide : (j + 1) * wide]
    gain_sum[...] = jnp.sum(grad[...] * normed, axis=0, keepdims=True)
    value = (scaling * (grad[...] * gain[...] - first - normed * cross) * slope[...]).astype(bf16)
    gh[...] = value
    acc[...] += dot_t(value, weight[...])

    @pl.when(step == pl.num_programs(0) - 1)
    def _():
        store_pieces(acc[...], own_out, pieces, part)


def down_kernel(parts, z2, weight, own_out, *refs):
    pieces, (acc,) = refs[: parts - 1], refs[parts - 1 :]
    step = pl.program_id(0)

    @pl.when(step == 0)
    def _():
        acc[...] = jnp.zeros_like(acc)

    wide = z2.shape[2]
    for j in range(z2.shape[0]):
        acc[...] += dot(z2[j], weight[j * wide : (j + 1) * wide, :])

    @pl.when(step == pl.num_programs(0) - 1)
    def _():
        store_pieces(acc[...], own_out, pieces, acc.shape[0] // parts)


def middle_back_kernel(parts, ids, own, *refs):
    got, refs = refs[: parts - 1], refs[parts - 1 :]
    gain_rows, refs = refs[:parts], refs[parts:]
    x, x1, gy, gain, gx1, gb, gain_sum = refs
    part, width = x1.shape
    here = block_at(ids[0], 0, part)
    grad = own[...]
    for block in got:
        grad = grad + block[...].astype(f32)
    value = x1[...]
    normed, scaling = norm_rows(value)
    result = gy[here, :].astype(f32) + norm_back(grad, gain[...], normed, scaling)
    gx1[...] = result
    gain_sum[...] = jnp.sum(grad * normed, axis=0, keepdims=True)
    low = result.astype(bf16)
    gb[:, :width] = low
    low = low.astype(f32)
    gain_row = sum(row[...] for row in gain_rows)
    first = jnp.sum(low * gain_row, axis=1, keepdims=True) / width
    cross = jnp.sum(low * (value - x[here, :].astype(f32)), axis=1, keepdims=True) / width
    gb[:, width:] = lanes_of([*split_low(first), *split_low(cross)], part).astype(bf16)


def heads_back_kernel(parts, own, *refs):
    got, refs = refs[: parts - 1], refs[parts - 1 :]
    stats, refs = refs[:parts], refs[parts:]
    att, gain, weight, sent, gb, gain_sum = refs
    blocks, _, rows = att.shape
    part, width = own.shape[0], gb.shape[1]
    for k, block in enumerate([own] + list(got)):
        gb[k * part : (k + 1) * part, :] = block[:, :width]
    columns = jnp.concatenate([b[:, width:].astype(f32) for b in [own] + list(got)], axis=0).T
    first = columns[0:1] + columns[1:2]
    cross = columns[2:3] + columns[3:4]
    columns = jnp.concatenate([b[:, width:].astype(f32) for b in stats], axis=0).T
    mean = columns[0:1] + columns[1:2]
    scaling = columns[2:3] + columns[3:4]
    grad = dot_t(weight[...], gb[...])
    value = jnp.concatenate([att[j].astype(f32) for j in range(blocks)], axis=0)
    normed = (value - mean) * scaling
    gain_col = jnp.broadcast_to(gain[...], (8, gain.shape[1])).T[:, 0:1]
    gain_sum[...] = jnp.sum((grad * normed).T, axis=0, keepdims=True)
    go = (scaling * (grad * gain_col - first - normed * cross)).astype(bf16)
    z = (normed * gain_col).astype(bf16)
    for j in range(blocks):
        sent[j, :HD, :] = go[j * HD : (j + 1) * HD]
        sent[j, HD:, :] = z[j * HD : (j + 1) * HD]


def turn_back(grad, table, base, j, inverse):
    here = [base[kind, :, j : j + 1] for kind in range(4)]
    cosine = table[0] * here[0] - table[1] * here[1]
    sine = table[1] * here[0] + table[0] * here[1]
    factor = table[3] * here[3] if inverse else table[2] * here[2]
    row = lax.broadcasted_iota(jnp.int32, grad.shape, 0)
    sine = jnp.where(row % 2 == 0, sine, -sine)
    return (grad * cosine + swap_pairs(grad, 0) * sine) * factor


def attend_back_kernel(parts, ids, got, grads, mixed, lse, inner, base, out, keys, values, ids_col, gk, gv):
    me = ids[0]
    blocks, _, rows = got.shape
    part = rows // parts
    gather_heads(got, keys, ids_col, values)
    gk[...] = jnp.zeros_like(gk)
    gv[...] = jnp.zeros_like(gv)
    table = []
    for kind in range(4):
        ordered = jnp.concatenate(
            [inner[kind, block_at(me, k, part), :] for k in range(parts)], axis=0
        )
        table.append(ordered.T[:HD])
    group = 2 if blocks % 2 == 0 else 1
    width = group * rows
    for i in range(blocks // group):
        mine = range(i * group, (i + 1) * group)
        query = jnp.concatenate([got[j, :HD, :] for j in mine], axis=1) * bf16(HD**-0.5)
        ids_row = jnp.concatenate([got[j, 3 * HD : 3 * HD + 1, :] for j in mine], axis=1).astype(f32)
        go = jnp.concatenate([grads[j, :HD, :] for j in mine], axis=1)
        span = slice(i * width, (i + 1) * width)
        delta = jnp.sum(go.astype(f32) * mixed[:, span], axis=0, keepdims=True)
        count = (i + 1) * width
        scores = dot(keys[0:count, :], query)
        allowed = visible_scores(me, part, scores, ids_col, ids_row, count, rows, width)
        probability = jnp.where(allowed, jnp.exp(jnp.minimum(scores - lse[:, span], 0.5)), 0.0)
        grad_prob = dot(values[0:count, :], go)
        grad_scores = (probability * (grad_prob - delta)).astype(bf16)
        gv[:, 0:count] += dot_t(go, probability.astype(bf16))
        gk[:, 0:count] += dot_t(query, grad_scores)
        key = jnp.concatenate([got[j, HD : 2 * HD, :] for j in range((i + 1) * group)], axis=1)
        gq = dot(key, grad_scores) * HD**-0.5
        for n, j in enumerate(mine):
            piece = turn_back(gq[:, n * rows : (n + 1) * rows], table, base, j, False)
            out[j, :HD, :] = piece.astype(bf16)
    for j in range(blocks):
        span = slice(j * rows, (j + 1) * rows)
        out[j, HD : 2 * HD, :] = turn_back(gk[:, span], table, base, j, True).astype(bf16)
        out[j, 2 * HD :, :] = gv[:, span].astype(bf16)


def input_back_kernel(parts, got, weight, own_out, *refs):
    pieces, (acc,) = refs[: parts - 1], refs[parts - 1 :]
    step = pl.program_id(0)

    @pl.when(step == 0)
    def _():
        acc[...] = jnp.zeros_like(acc)

    here = pl.ds(pl.multiple_of(step * HD, HD), HD)
    grad = jnp.concatenate([got[j, here, :].astype(f32) for j in range(got.shape[0])], axis=0).T
    acc[...] += dot_t(grad.astype(bf16), weight[0])

    @pl.when(step == pl.num_programs(0) - 1)
    def _():
        store_pieces(acc[...], own_out, pieces, acc.shape[0] // parts)


def final_kernel(parts, ids, own, *refs):
    got, refs = refs[: parts - 1], refs[parts - 1 :]
    x, gx1, gain, out, gain_sum = refs
    part = gx1.shape[0]
    grad = own[...]
    for block in got:
        grad = grad + block[...].astype(f32)
    normed, scaling = norm_rows(x[block_at(ids[0], 0, part), :].astype(f32))
    out[...] = (gx1[...] + norm_back(grad, gain[...], normed, scaling)).astype(bf16)
    gain_sum[...] = jnp.sum(grad * normed, axis=0, keepdims=True)


def output_kernel(own, *refs):
    got, (x1, out) = refs[:-2], refs[-2:]
    total = own[...] + x1[...]
    for block in got:
        total = total + block[...].astype(f32)
    out[...] = total.astype(bf16)


def natural_kernel(ids, *refs):
    blocks, out = refs[:-1], refs[-1]
    part = blocks[0].shape[0]
    for k, block in enumerate(blocks):
        out[block_at(ids[0], k, part), :] = block[...]


def columns_grad_kernel(parts, reorder, ids, left, right, out, acc_left):
    @pl.when(pl.program_id(0) == 0)
    def _():
        blocks, rows, _ = left.shape
        part = rows // parts
        for j in range(blocks):
            for k in range(parts):
                if reorder:
                    to = pl.ds(pl.multiple_of(j * rows + (ids[0] ^ k) * part, part), part)
                else:
                    to = slice(j * rows + k * part, j * rows + (k + 1) * part)
                acc_left[to, :] = left[j, k * part : (k + 1) * part, :]

    out[...] = t_dot(acc_left[...], right[...])


def rows_grad_kernel(first, left, right, out):
    value = jnp.concatenate([left[j, first:, :] for j in range(left.shape[0])], axis=1)
    out[...] = dot(value, right[...])


def grad_qkv_kernel(left, right, out):
    value = jnp.concatenate([left[j] for j in range(left.shape[0])], axis=1)
    out[0] = dot(value, right[...]).astype(bf16)


def grad_qkv_place_kernel(got, out):
    for c in range(3):
        value = jnp.concatenate(
            [got[j, c * HD : (c + 1) * HD, :].astype(f32) for j in range(got.shape[0])], axis=0
        )
        out[c] = value.T


def body(
    layer_input,
    segment_ids,
    qkv_weight,
    out_weight,
    up_weight,
    down_weight,
    input_gain,
    heads_gain,
    middle_gain,
    hidden_gain,
    cotangent,
):
    rows, row_count, width = layer_input.shape
    T, C = lax.axis_size("tp"), lax.axis_size("cp")
    part = rows // T
    head_width = qkv_weight.shape[2]
    if head_width // HD != C or row_count != 1 or rows != 128 or part % 16 != 0:
        return body_general(
            layer_input, segment_ids, qkv_weight, out_weight, up_weight, down_weight,
            input_gain, heads_gain, middle_gain, hidden_gain, cotangent,
        )
    tokens = rows * C
    hidden = up_weight.shape[1]
    wide = width // C
    high = hidden // C
    ids = jnp.stack([lax.axis_index("tp"), lax.axis_index("cp")]).astype(jnp.int32)
    x = layer_input.reshape(rows, width)
    gy = cotangent.reshape(rows, width)
    weight3 = jnp.transpose(qkv_weight, (1, 0, 2))
    gain_in, gain_mid = input_gain.reshape(1, -1), middle_gain.reshape(1, -1)
    gain_heads, gain_hid = heads_gain.reshape(1, -1), hidden_gain.reshape(1, -1)
    inner, base = tables(rows, C)
    inner2 = jnp.asarray(np.concatenate([inner, inner], axis=2))
    base2 = jnp.asarray(np.concatenate([base, base], axis=2))
    base_t = np.zeros((4, HD, 128), np.float32)
    base_t[:, :, :C] = np.transpose(base, (0, 2, 1))
    base_t = jnp.asarray(base_t)
    wide_part = width + 128

    def piece_shapes(columns):
        return [shape((part, columns), f32)] + [shape((part, columns), bf16)] * (T - 1)

    def exchange(pieces):
        return [swap_tp(piece, k) for k, piece in enumerate(pieces, 1)]

    def spread(block):
        return [swap_tp(block, k) for k in range(1, T)]

    def to_cp(value):
        return lax.all_to_all(value, "cp", 0, 0, tiled=True)

    gy_all = cp_gather(gy)
    a, sent = call(
        functools.partial(project_kernel, T),
        [shape((rows, width), bf16), shape((C, 3 * HD + 16, rows), bf16)],
        [ids, x, segment_ids.reshape(1, rows), gain_in, weight3, inner2, base2],
        [scalars(), fixed((rows, width)), fixed((1, rows)), fixed((1, width)),
         pl.BlockSpec((1, width, head_width), lambda i: (i, 0, 0)), fixed((4, rows, 128)), fixed((4, C, 128))],
        [fixed((rows, width)), fixed((C, 3 * HD + 16, rows))],
        grid=(3,), scratch=[pltpu.VMEM((4, rows, 128), f32)],
        flops=2 * rows * width * 3 * head_width,
    )
    a_all = cp_gather(a)
    got = to_cp(sent)
    step = 512
    grad_hid, gain_row = call(
        functools.partial(grad_hidden_kernel, T),
        [shape((rows, hidden), f32), shape((1, width), f32)],
        [ids, gy, down_weight, gain_heads, out_weight],
        [scalars(), fixed((rows, width)), pl.BlockSpec((step, width), lambda i: (i, 0)),
         fixed((1, head_width)), fixed((head_width, width))],
        [pl.BlockSpec((rows, step), lambda i: (0, i)), fixed((1, width))],
        grid=(hidden // step,), scratch=[pltpu.VMEM((rows, width), bf16)],
        flops=2 * rows * width * hidden, after=[sent],
    )
    gain_rows = [gain_row] + spread(gain_row)
    back, mixed, lse = call(
        functools.partial(attend_kernel, T),
        [shape((C, HD, rows), bf16), shape((HD, tokens), f32), shape((1, tokens), f32)],
        [ids, got], [scalars(), whole()],
        scratch=[pltpu.VMEM((tokens, HD), bf16), pltpu.VMEM((tokens, 16), f32)],
        flops=4 * tokens * tokens * HD,
    )
    att = to_cp(back)

    own, *pieces = call(
        functools.partial(out_kernel, T), piece_shapes(wide_part), [att, gain_heads, out_weight],
        flops=2 * rows * width * head_width,
    )
    x1, u_own = call(
        functools.partial(middle_kernel, T, head_width),
        [shape((part, width), f32), shape((part, wide_part), bf16)],
        [ids, own, *exchange(pieces), *gain_rows, x, gain_mid],
        [scalars()] + [whole()] * (2 * T + 2),
    )
    u_blocks = [u_own] + spread(u_own)

    act, slope, u_cols, stats = call(
        functools.partial(up_kernel, T),
        [shape((rows, hidden), f32), shape((rows, hidden), f32), shape((C, rows, wide), bf16), shape((8, rows), f32)],
        [*u_blocks, up_weight, grad_hid, gain_hid],
        [fixed((part, wide_part))] * T
        + [pl.BlockSpec((width, step), lambda i: (0, i)), pl.BlockSpec((rows, step), lambda i: (0, i)),
           pl.BlockSpec((1, step), lambda i: (0, i))],
        [pl.BlockSpec((rows, step), lambda i: (0, i)), pl.BlockSpec((rows, step), lambda i: (0, i)),
         fixed((C, rows, wide)), fixed((8, rows))],
        grid=(hidden // step,), scratch=[pltpu.VMEM((rows, width), bf16), pltpu.VMEM((rows, 128), f32)],
        flops=2 * rows * width * hidden,
    )
    gh, z2, hidden_gain_sum, own, *pieces = call(
        functools.partial(hidden_back_kernel, T, FF),
        [shape((rows, hidden), bf16), shape((C, rows, high), bf16), shape((1, hidden), f32)] + piece_shapes(width),
        [stats, *spread(stats), act, slope, grad_hid, gain_hid, up_weight],
        [fixed((8, rows))] * T
        + [pl.BlockSpec((rows, step), lambda i: (0, i))] * 3
        + [pl.BlockSpec((1, step), lambda i: (0, i)), pl.BlockSpec((width, step), lambda i: (0, i))],
        [pl.BlockSpec((rows, step), lambda i: (0, i)),
         pl.BlockSpec((step // high, rows, high), lambda i: (i, 0, 0)),
         pl.BlockSpec((1, step), lambda i: (0, i))] + [fixed((part, width))] * T,
        grid=(hidden // step,), scratch=[pltpu.VMEM((rows, width), f32), pltpu.VMEM((rows, rows), f32)],
        flops=2 * rows * width * hidden,
    )
    gh_all = cp_gather(gh)
    gu_got = exchange(pieces)
    y_own, *y_pieces = call(
        functools.partial(down_kernel, T), piece_shapes(width), [z2, down_weight],
        [pl.BlockSpec((step // high, rows, high), lambda i: (i, 0, 0)), pl.BlockSpec((step, width), lambda i: (i, 0))],
        [fixed((part, width))] * T,
        grid=(hidden // step,), scratch=[pltpu.VMEM((rows, width), f32)],
        flops=2 * rows * width * hidden, after=[own],
    )
    gx1, gb_own, middle_gain_sum = call(
        functools.partial(middle_back_kernel, T),
        [shape((part, width), f32), shape((part, wide_part), bf16), shape((1, width), f32)],
        [ids, own, *gu_got, *gain_rows, x, x1, gy, gain_mid],
        [scalars()] + [whole()] * (2 * T + 4),
    )
    gb_blocks = [gb_own] + spread(gb_own)

    sent, gb, heads_gain_sum = call(
        functools.partial(heads_back_kernel, T),
        [shape((C, 2 * HD, rows), bf16), shape((rows, width), bf16), shape((1, head_width), f32)],
        [*gb_blocks, *u_blocks, att, gain_heads, out_weight],
        flops=2 * rows * width * head_width,
    )
    gb_all = cp_gather(gb)
    grads = to_cp(sent)
    (gq_sent,) = call(
        functools.partial(attend_back_kernel, T), [shape((C, 3 * HD, rows), bf16)],
        [ids, got, grads, mixed, lse, inner2, base_t], [scalars()] + [whole()] * 6,
        scratch=[pltpu.VMEM((tokens, HD), bf16), pltpu.VMEM((tokens, HD), bf16), pltpu.VMEM((tokens, 16), f32),
                 pltpu.VMEM((HD, tokens), f32), pltpu.VMEM((HD, tokens), f32)],
        flops=10 * tokens * tokens * HD,
    )
    gq = to_cp(gq_sent)
    own, *pieces = call(
        functools.partial(input_back_kernel, T), piece_shapes(width), [gq, weight3],
        [fixed((C, 3 * HD, rows)), pl.BlockSpec((1, width, head_width), lambda i: (i, 0, 0))],
        [fixed((part, width))] * T,
        grid=(3,), scratch=[pltpu.VMEM((rows, width), f32)],
        flops=2 * rows * width * 3 * head_width,
    )
    grad_in, input_gain_sum = call(
        functools.partial(final_kernel, T),
        [shape((part, width), bf16), shape((1, width), f32)],
        [ids, own, *exchange(pieces), x, gx1, gain_in],
        [scalars()] + [whole()] * (T + 3),
    )
    grad_blocks = [grad_in] + spread(grad_in)
    (grad_input,) = call(
        natural_kernel, [shape((rows, width), bf16)], [ids, *grad_blocks], [scalars()] + [whole()] * T
    )

    (y_low,) = call(output_kernel, [shape((part, width), bf16)], [y_own, *exchange(y_pieces), x1])
    y_blocks = [y_low] + spread(y_low)
    (layer_output,) = call(
        natural_kernel, [shape((rows, width), bf16)], [ids, *y_blocks], [scalars()] + [whole()] * T
    )

    def columns_grad(left, right, reorder):
        own_columns = left.shape[2]
        return call(
            functools.partial(columns_grad_kernel, T, reorder),
            [shape((own_columns, right.shape[1]), f32)], [ids, left, right],
            [scalars(), fixed(left.shape), pl.BlockSpec((tokens, step), lambda i: (0, i))],
            [pl.BlockSpec((own_columns, step), lambda i: (0, i))],
            grid=(right.shape[1] // step,), scratch=[pltpu.VMEM((tokens, own_columns), bf16)],
            flops=2 * tokens * own_columns * right.shape[1],
        )[0]

    grad_down = columns_grad(to_cp(z2), gy_all, True)
    grad_up = columns_grad(to_cp(u_cols), gh_all, False)
    (grad_out,) = call(
        functools.partial(rows_grad_kernel, HD), [shape((HD, width), f32)], [grads, gb_all],
        [fixed(grads.shape), pl.BlockSpec((tokens, step), lambda i: (0, i))],
        [pl.BlockSpec((HD, step), lambda i: (0, i))], grid=(width // step,),
        flops=2 * tokens * HD * width,
    )
    (grad_qkv,) = call(
        grad_qkv_kernel, [shape((C, 3 * HD, wide), bf16)], [gq_sent, a_all],
        [fixed(gq_sent.shape), pl.BlockSpec((tokens, wide), lambda i: (0, i))],
        [pl.BlockSpec((1, 3 * HD, wide), lambda i: (i, 0, 0))], grid=(C,),
        flops=2 * tokens * 3 * HD * width,
    )
    (grad_qkv,) = call(grad_qkv_place_kernel, [shape((3, wide, head_width), f32)], [to_cp(grad_qkv)])

    by_cp = jnp.concatenate([heads_gain_sum.reshape(C, -1), hidden_gain_sum.reshape(C, -1)], axis=1)
    by_cp = jnp.sum(to_cp(by_cp), axis=0)
    by_all = jnp.concatenate([input_gain_sum.reshape(C, -1), middle_gain_sum.reshape(C, -1)], axis=1)
    by_all = jnp.broadcast_to(by_all[None], (T, C, 2 * wide)).reshape(T * C, 2 * wide)
    by_all = jnp.sum(lax.all_to_all(by_all, ("tp", "cp"), 0, 0, tiled=True), axis=0)
    return (
        layer_output.reshape(layer_input.shape),
        grad_input.reshape(layer_input.shape),
        jnp.transpose(grad_qkv, (1, 0, 2)),
        grad_out,
        grad_up,
        grad_down,
        by_all[:wide],
        by_cp[: head_width // C],
        by_all[wide:],
        by_cp[head_width // C :],
    )


def solution(mesh):
    placed = (
        P("cp", None, None),
        P("cp", None),
        P(None, None, "tp"),
        P("tp", None),
        P(None, "tp"),
        P("tp", None),
        P(),
        P("tp"),
        P(),
        P("tp"),
        P("cp", None, None),
    )
    return jax.shard_map(
        body,
        mesh=mesh,
        in_specs=placed,
        out_specs=(
            P("cp", None, None),
            P("cp", None, None),
            P("cp", None, "tp"),
            P(("tp", "cp"), None),
            P("cp", "tp"),
            P(("tp", "cp"), None),
            P("cp"),
            P(("tp", "cp")),
            P("cp"),
            P(("tp", "cp")),
        ),
        check_vma=False,
    )
```

```python
import functools

import jax
import jax.numpy as jnp
import numpy as np
from jax import lax
from jax.experimental import pallas as pl
from jax.experimental.pallas import tpu as pltpu
from jax.sharding import PartitionSpec as P

HD = 64
D = 2048
FF = 8192

eps = 1e-05
scale_base = 512.0
masked_score = -1e30
f32 = jnp.float32
bf16 = jnp.bfloat16


def dot(a, b):
    return jnp.dot(a, b, preferred_element_type=f32)


def dot_t(a, b):
    return lax.dot_general(a, b, (((1,), (1,)), ((), ())), preferred_element_type=f32)


def t_dot(a, b):
    return lax.dot_general(a, b, (((0,), (0,)), ((), ())), preferred_element_type=f32)


def pairs(count, k):
    return [(i, i ^ k) for i in range(count)]


def swap_tp(value, k):
    return lax.ppermute(value, "tp", pairs(lax.axis_size("tp"), k))


def tp_order(value):
    count, me = lax.axis_size("tp"), lax.axis_index("tp")
    part = value.shape[0] // count
    return jnp.concatenate(
        [lax.dynamic_slice_in_dim(value, (me ^ k) * part, part, 0) for k in range(count)], axis=0
    )


def tp_scatter_sum(partial_sum):
    count = lax.axis_size("tp")
    part = partial_sum.shape[0] // count
    low = partial_sum.astype(bf16)
    total = partial_sum[:part]
    for k in range(1, count):
        total = total + swap_tp(low[k * part : (k + 1) * part], k).astype(f32)
    return total


def tp_gather(block):
    count = lax.axis_size("tp")
    return jnp.concatenate([block] + [swap_tp(block, k) for k in range(1, count)], axis=0)


def tp_sum(value):
    total = value
    for k in range(1, lax.axis_size("tp")):
        total = total + swap_tp(value, k)
    return total


def tp_token_sum(value):
    count = lax.axis_size("tp")
    blocks = value.reshape(value.shape[0], count, -1)
    total = blocks
    for k in range(1, count):
        got = swap_tp(blocks, k)
        total = total + jnp.stack([got[:, j ^ k] for j in range(count)], axis=1)
    return total.reshape(value.shape)


def cp_columns(value):
    return lax.all_to_all(value, "cp", split_axis=1, concat_axis=0, tiled=True)


def cp_gather(value):
    return lax.all_gather(value, "cp", axis=0, tiled=True)


def xpos_tables(positions):
    column = jnp.arange(HD // 2, dtype=f32)
    frequency = 10000.0 ** (-column / (HD // 2))
    zeta = (2.0 * column + 0.4 * HD) / (1.4 * HD)
    places = positions.astype(f32)[:, None]
    angle = places * frequency
    return (jnp.cos(angle), jnp.sin(angle), zeta ** (places / scale_base))


def turn(vector, cosine, sine, factor):
    paired = vector.reshape(vector.shape[:-1] + (HD // 2, 2))
    first, second = paired[..., 0], paired[..., 1]
    cosine, sine, factor = cosine[:, None], sine[:, None], factor[:, None]
    turned = jnp.stack(
        [(first * cosine - second * sine) * factor, (first * sine + second * cosine) * factor],
        axis=-1,
    )
    return turned.reshape(vector.shape)


def norm_rows(vector):
    center = jnp.mean(vector, axis=-1, keepdims=True)
    shifted = vector - center
    scaling = lax.rsqrt(jnp.mean(shifted * shifted, axis=-1, keepdims=True) + eps)
    return (shifted * scaling, scaling)


def norm_back(grad_result, gain, normed, scaling):
    grad_normed = grad_result * gain
    first = jnp.mean(grad_normed, axis=-1, keepdims=True)
    cross = jnp.mean(grad_normed * normed, axis=-1, keepdims=True)
    return scaling * (grad_normed - first - normed * cross)


def attend(queries, keys, values, allowed):
    scores = jnp.einsum("qhd,khd->hqk", queries, keys, preferred_element_type=f32) * HD**-0.5
    scores = jnp.where(allowed[None], scores, masked_score)
    top = jnp.max(scores, axis=-1, keepdims=True)
    exponent = jnp.where(allowed[None], jnp.exp(scores - top), 0.0)
    total = jnp.sum(exponent, axis=-1, keepdims=True)
    probability = (exponent / total).astype(bf16)
    mixed = jnp.einsum("hqk,khd->qhd", probability, values, preferred_element_type=f32)
    return (mixed, top + jnp.log(total))


def attend_back(queries, keys, values, allowed, lse, grad, delta):
    scores = jnp.einsum("qhd,khd->hqk", queries, keys, preferred_element_type=f32) * HD**-0.5
    probability = jnp.where(allowed[None], jnp.exp(scores - lse), 0.0)
    grad_prob = jnp.einsum("qhd,khd->hqk", grad, values, preferred_element_type=f32)
    grad_scores = (probability * (grad_prob - delta.T[:, :, None])).astype(bf16)
    grad_q = jnp.einsum("hqk,khd->qhd", grad_scores, keys, preferred_element_type=f32) * HD**-0.5
    grad_k = jnp.einsum("hqk,qhd->khd", grad_scores, queries, preferred_element_type=f32) * HD**-0.5
    grad_v = jnp.einsum(
        "hqk,qhd->khd", probability.astype(bf16), grad, preferred_element_type=f32
    )
    return (grad_q, grad_k, grad_v)


def body_general(
    layer_input,
    segment_ids,
    qkv_weight,
    out_weight,
    up_weight,
    down_weight,
    input_gain,
    heads_gain,
    middle_gain,
    hidden_gain,
    cotangent,
):
    local_len, row_count, width = layer_input.shape
    tp_count, cp_count = lax.axis_size("tp"), lax.axis_size("cp")
    me_tp, me_cp = lax.axis_index("tp"), lax.axis_index("cp")
    part = local_len // tp_count
    head_width = qkv_weight.shape[2]
    heads = head_width // HD
    by_head = heads % cp_count == 0
    own_heads = heads // cp_count if by_head else heads
    weight3 = jnp.transpose(qkv_weight, (1, 0, 2))

    x = tp_order(layer_input.reshape(local_len, width))
    gy = tp_order(cotangent.reshape(local_len, width))
    seg = tp_order(segment_ids)[:, 0]
    natural = tp_order(jnp.arange(local_len, dtype=jnp.int32))
    position = me_cp * local_len + natural
    position_all = (jnp.arange(cp_count, dtype=jnp.int32)[:, None] * local_len + natural).reshape(-1)

    stream = x.astype(f32)
    normed_one, scaling_one = norm_rows(stream)
    a = (normed_one * input_gain).astype(bf16)
    a_all = cp_gather(a)
    cosine, sine, factor = xpos_tables(position)
    raw_q = dot(a, weight3[0]).reshape(local_len, heads, HD)
    raw_k = dot(a, weight3[1]).reshape(local_len, heads, HD)
    raw_v = dot(a, weight3[2]).reshape(local_len, heads, HD)
    q = turn(raw_q, cosine, sine, factor).astype(bf16)
    k = turn(raw_k, cosine, sine, 1.0 / factor).astype(bf16)
    v = raw_v.astype(bf16)
    if by_head:
        extra = jnp.broadcast_to(seg.astype(bf16)[:, None, None], (local_len, cp_count, 16))
        sent = jnp.concatenate(
            [t.reshape(local_len, cp_count, own_heads * HD) for t in (q, k, v)] + [extra], axis=-1
        )
        got = lax.all_to_all(sent, "cp", split_axis=1, concat_axis=0, tiled=True)[:, 0]
        span = own_heads * HD
        q_all, k_all, v_all = (
            got[:, i * span : (i + 1) * span].reshape(-1, own_heads, HD) for i in range(3)
        )
        seg_all = got[:, 3 * span]
        seg_q, position_q = seg_all, position_all
    else:
        q_all, k_all, v_all = q, cp_gather(k), cp_gather(v)
        seg_all = cp_gather(seg.astype(bf16))
        seg_q, position_q = seg.astype(bf16), position
    allowed = (position_all[None, :] <= position_q[:, None]) & (seg_q[:, None] == seg_all[None, :])
    mixed, lse = attend(q_all, k_all, v_all, allowed)
    if by_head:
        attended = lax.all_to_all(
            mixed.astype(bf16).reshape(cp_count * local_len, own_heads * HD),
            "cp", split_axis=0, concat_axis=1, tiled=True,
        ).astype(f32)
    else:
        attended = mixed.reshape(local_len, head_width)

    sums = tp_token_sum(jnp.stack([jnp.sum(attended, axis=1), jnp.sum(attended * attended, axis=1)]))
    center = sums[0] / width
    scaling_h = lax.rsqrt(sums[1] / width - center * center + eps)[:, None]
    normed_h = (attended - center[:, None]) * scaling_h
    z = (normed_h * heads_gain).astype(bf16)
    gain_row = tp_sum(jnp.dot(heads_gain, out_weight.astype(f32)))
    branch = tp_scatter_sum(dot(z, out_weight))
    x1 = stream[:part] + branch
    normed_two, scaling_two = norm_rows(x1)
    u = tp_gather((normed_two * middle_gain).astype(bf16))

    grad_hid = dot_t(gy, down_weight)
    grad_normed = grad_hid * hidden_gain
    hidden = dot(u, up_weight)
    cdf = 0.5 * (1.0 + lax.erf(hidden * (0.5**0.5)))
    act = hidden * cdf
    slope = cdf + hidden * jnp.exp(-0.5 * hidden * hidden) * 0.3989422804014327
    sums = tp_token_sum(
        jnp.stack(
            [
                jnp.sum(act, axis=1),
                jnp.sum(act * act, axis=1),
                jnp.sum(grad_normed, axis=1),
                jnp.sum(grad_normed * act, axis=1),
            ]
        )
    )
    center = sums[0] / FF
    scaling_f = lax.rsqrt(sums[1] / FF - center * center + eps)
    first = sums[2] / FF
    cross = scaling_f * (sums[3] / FF - center * first)
    normed_f = (act - center[:, None]) * scaling_f[:, None]
    z2 = (normed_f * hidden_gain).astype(bf16)
    grad_act = scaling_f[:, None] * (grad_normed - first[:, None] - normed_f * cross[:, None])
    gh = (grad_act * slope).astype(bf16)
    hidden_gain_sum = jnp.sum(grad_hid * normed_f, axis=0)
    gu = tp_scatter_sum(dot_t(gh, up_weight))
    gx1 = gy[:part].astype(f32) + norm_back(gu, middle_gain, normed_two, scaling_two)
    middle_gain_sum = jnp.sum(gu * normed_two, axis=0)
    gb_own = gx1.astype(bf16)
    gb_f = gb_own.astype(f32)
    first = jnp.sum(gb_f * gain_row, axis=1) / width
    cross = jnp.sum(gb_f * branch, axis=1) / width
    gb = tp_gather(gb_own)
    stats = tp_gather(jnp.stack([first, cross], axis=1))

    gz = dot_t(gb, out_weight)
    heads_gain_sum = jnp.sum(gz * normed_h, axis=0)
    go = (scaling_h * (gz * heads_gain - stats[:, :1] - normed_h * stats[:, 1:])).astype(bf16)
    if by_head:
        grad_mixed = cp_columns(go).reshape(-1, own_heads, HD)
    else:
        grad_mixed = go.reshape(local_len, heads, HD)
    delta = jnp.sum(grad_mixed.astype(f32) * mixed, axis=-1)
    gq, gk, gv = attend_back(q_all, k_all, v_all, allowed, lse, grad_mixed, delta)
    if by_head:
        cos_all, sin_all, factor_all = xpos_tables(position_all)
    else:
        cos_all, sin_all, factor_all = cosine, sine, factor
        gk = lax.psum_scatter(gk.astype(bf16), "cp", scatter_dimension=0, tiled=True).astype(f32)
        gv = lax.psum_scatter(gv.astype(bf16), "cp", scatter_dimension=0, tiled=True).astype(f32)
    gq = turn(gq, cos_all, -sin_all, factor_all)
    gk = turn(gk, cos_all, -sin_all, 1.0 / factor_all)
    grads = jnp.stack([gq, gk, gv], axis=1).astype(bf16)
    if by_head:
        grads_own = grads.reshape(-1, 3 * own_heads * HD)
        grads = lax.all_to_all(
            grads.reshape(-1, 3, own_heads * HD), "cp", split_axis=0, concat_axis=2, tiled=True
        )
    else:
        grads = grads.reshape(local_len, 3, head_width)
        grads_own = lax.all_to_all(grads, "cp", split_axis=2, concat_axis=0, tiled=True)
        grads_own = grads_own.reshape(-1, 3 * head_width // cp_count)
    ga = (
        dot_t(grads[:, 0], weight3[0]) + dot_t(grads[:, 1], weight3[1]) + dot_t(grads[:, 2], weight3[2])
    )
    ga = tp_scatter_sum(ga)
    input_gain_sum = jnp.sum(ga * normed_one[:part], axis=0)
    grad_in = gx1 + norm_back(ga, input_gain, normed_one[:part], scaling_one[:part])

    y = (x1 + tp_scatter_sum(dot(z2, down_weight))).astype(bf16)
    layer_output = tp_order(tp_gather(y)).reshape(layer_input.shape)
    grad_input = tp_order(tp_gather(grad_in.astype(bf16))).reshape(layer_input.shape)

    grad_down = t_dot(cp_columns(z2), cp_gather(gy))
    grad_up = t_dot(cp_columns(u), cp_gather(gh))
    grad_out = t_dot(cp_columns(z), cp_gather(gb))
    grad_qkv = t_dot(a_all, grads_own).astype(bf16)
    grad_qkv = lax.all_to_all(
        grad_qkv.reshape(width, 3, head_width // cp_count), "cp", split_axis=0, concat_axis=2, tiled=True
    ).astype(f32)

    def cp_sum_own(vector):
        return jnp.sum(lax.all_to_all(vector.reshape(cp_count, -1), "cp", 0, 0, tiled=True), axis=0)

    def both_sum_own(vector):
        return tp_sum(cp_sum_own(vector))

    return (
        layer_output,
        grad_input,
        grad_qkv,
        grad_out,
        grad_up,
        grad_down,
        both_sum_own(input_gain_sum),
        cp_sum_own(heads_gain_sum),
        both_sum_own(middle_gain_sum),
        cp_sum_own(hidden_gain_sum),
    )


INTERPRET = False


def params(megabytes):
    return pltpu.CompilerParams(vmem_limit_bytes=megabytes * 1024 * 1024)


def shape(dims, kind):
    return jax.ShapeDtypeStruct(dims, kind)


def whole():
    return pl.BlockSpec(memory_space=pltpu.VMEM)


def scalars():
    return pl.BlockSpec(memory_space=pltpu.SMEM)


class Pin:
    def __init__(self, value):
        self.value = value


class Far(Pin):
    def __init__(self, value, dims=None, block=None):
        super().__init__(value)
        self.dims = tuple(value.shape) if dims is None else dims
        self.block = block


class Near:
    def __init__(self, value):
        self.value = value


class Fetched:
    def __init__(self, ref, copy):
        self.ref, self.copy, self.shape = ref, copy, ref.shape

    def ready(self):
        if self.copy is not None:
            self.copy.wait()
            self.copy = None

    def __getitem__(self, index):
        self.ready()
        return self.ref[index]


def pinned(value):
    return value if INTERPRET else pltpu.with_memory_space_constraint(value, pltpu.HBM)


def call(
    kernel, outs, args, specs=None, out_specs=None, grid=None, scratch=(), mb=8, flops=0, after=(), carry=(), prefetch=0
):
    specs = list(specs) if specs is not None else [whole() for _ in args]
    out_specs = list(out_specs) if out_specs is not None else [whole() for _ in outs]
    count, extra, kept, made = len(args), len(after), len(carry), len(outs)
    anywhere = pl.BlockSpec(memory_space=pl.ANY)
    far_in = [i for i, t in enumerate(args) if isinstance(t, Far)]
    far_out = [i for i, t in enumerate(outs) if isinstance(t, Far)]
    for i in far_in:
        specs[i] = anywhere
    for i in far_out:
        out_specs[i] = anywhere
    moving = [pltpu.VMEM(args[i].dims, args[i].value.dtype) for i in far_in]
    moving += [pltpu.VMEM(outs[i].dims, outs[i].value.dtype) for i in far_out]
    moving += [pltpu.SemaphoreType.DMA] * (len(far_in) + len(far_out))
    own_scratch = len(scratch)

    def run(*refs):
        ins = list(refs[:count])
        results = refs[count + extra + kept :]
        products = list(results[:made])
        rest = results[made + kept :]
        slots, sems = rest[own_scratch : own_scratch + len(far_in) + len(far_out)], rest[own_scratch + len(far_in) + len(far_out) :]
        for i, slot, sem in zip(far_in, slots, sems):
            source = refs[i]
            if args[i].block is not None:
                source = source.at[args[i].block(refs[0])]
            copy = pltpu.make_async_copy(source, slot, sem)
            copy.start()
            ins[i] = Fetched(slot, copy)
        for i, slot in zip(far_out, slots[len(far_in) :]):
            products[i] = slot
        kernel(*ins, *products, *rest[:own_scratch])
        for i in far_in:
            ins[i].ready()
        copies = [
            pltpu.make_async_copy(slot, results[i], sem)
            for i, slot, sem in zip(far_out, slots[len(far_in) :], sems[len(far_in) :])
        ]
        for copy in copies:
            copy.start()
        for copy in copies:
            copy.wait()

    def plain(value):
        return value.value if isinstance(value, (Pin, Near)) else value

    def result(value):
        dims = plain(value)
        if INTERPRET or value is dims:
            return dims
        return (pltpu.HBM if isinstance(value, Pin) else pltpu.VMEM)(dims.shape, dims.dtype)

    moved = sum(int(np.prod(plain(t).shape)) * plain(t).dtype.itemsize for t in list(args) + list(outs))
    where = dict(
        in_specs=specs + [anywhere] * (extra + kept),
        out_specs=tuple(out_specs + [anywhere] * kept),
        scratch_shapes=list(scratch) + moving,
    )
    if prefetch:
        where["in_specs"] = where["in_specs"][prefetch:]
        where = {"grid_spec": pltpu.PrefetchScalarGridSpec(num_scalar_prefetch=prefetch, grid=grid, **where)}
    elif grid is not None:
        where["grid"] = grid
    return pl.pallas_call(
        run,
        out_shape=tuple(result(t) for t in outs) + tuple(result(Pin(shape(t.shape, t.dtype))) for t in carry),
        input_output_aliases={count + extra + i: made + i for i in range(kept)},
        compiler_params=params(mb),
        cost_estimate=pl.CostEstimate(flops=5000000000, bytes_accessed=0, transcendentals=0),
        interpret=INTERPRET,
        **where,
    )(*[pinned(t.value) if isinstance(t, Pin) else t for t in list(args) + list(after)], *[pinned(t) for t in carry])


def bring(items, ids, after=()):
    def kernel(ids, *refs):
        sources, slots, sems = refs[: len(items)], refs[len(items) : 2 * len(items)], refs[2 * len(items) :]
        copies = []
        for (_, _, block), source, slot, sem in zip(items, sources, slots, sems):
            copies.append(pltpu.make_async_copy(source if block is None else source.at[block(ids)], slot, sem))
        for copy in copies:
            copy.start()
        for copy in copies:
            copy.wait()

    return call(
        kernel,
        [Near(shape(dims, array.dtype)) for array, dims, _ in items],
        [ids] + [Pin(array) for array, _, _ in items],
        [scalars()] + [pl.BlockSpec(memory_space=pl.ANY)] * len(items),
        scratch=[pltpu.SemaphoreType.DMA] * len(items), after=after, mb=2,
    )


def fixed(dims):
    return pl.BlockSpec(dims, lambda i: (0,) * len(dims))


def split_low(value):
    high = value.astype(bf16)
    return high, (value - high.astype(f32)).astype(bf16)


def lanes_of(columns, rows):
    lane = lax.broadcasted_iota(jnp.int32, (rows, 128), 1)
    out = jnp.zeros((rows, 128), f32)
    for i, column in enumerate(columns):
        out = jnp.where(lane == i, column.astype(f32), out)
    return out


def pair_sum(block, i):
    return block[:, i : i + 1].astype(f32) + block[:, i + 1 : i + 2].astype(f32)


def own_order(me, part, index):
    return ((index // part) ^ me) * part + index % part


def block_at(me, k, part):
    return pl.ds(pl.multiple_of((me ^ k) * part, part), part)


def swap_pairs(value, axis):
    size = value.shape[axis]
    place = lax.broadcasted_iota(jnp.int32, value.shape, axis)
    return jnp.where(
        place % 2 == 0, pltpu.roll(value, size - 1, axis), pltpu.roll(value, 1, axis)
    )


def tables(local_len, cp_count):
    column = np.arange(HD) // 2
    frequency = 10000.0 ** (-column / (HD // 2))
    zeta = (2.0 * column + 0.4 * HD) / (1.4 * HD)

    def of(places):
        angle = places[:, None] * frequency
        factor = zeta ** (places[:, None] / scale_base)
        return np.stack([np.cos(angle), np.sin(angle), factor, 1.0 / factor]).astype(np.float32)

    return of(np.arange(local_len)), of(np.arange(cp_count) * local_len)


def project_kernel(parts, ids, x, gy, seg, gain, weight, inner, base, a, gy_out, out, tab):
    step = pl.program_id(0)
    me, mine = ids[0], ids[1]
    rows, width = x.shape
    part = rows // parts
    heads = out.shape[0]

    @pl.when(step == 0)
    def _():
        for k in range(parts):
            block = x[block_at(me, k, part), :].astype(f32)
            normed, _ = norm_rows(block)
            a[k * part : (k + 1) * part, :] = (normed * gain[...]).astype(bf16)
            gy_out[k * part : (k + 1) * part, :] = gy[block_at(me, k, part), :]
            for kind in range(4):
                tab[kind, k * part : (k + 1) * part, :] = inner[kind, block_at(me, k, part), :]
        place = lax.broadcasted_iota(jnp.int32, (rows, rows), 1)
        source = lax.broadcasted_iota(jnp.int32, (rows, rows), 0)
        moved = (own_order(me, part, place) == source).astype(bf16)
        ids_row = jnp.broadcast_to(seg[...].astype(f32), (16, rows)).astype(bf16)
        ordered = dot(ids_row, moved).astype(bf16)
        for j in range(heads):
            out[j, 3 * HD : 3 * HD + 16, :] = ordered

    acc = dot(a[...], weight[0])
    here = [base[kind, pl.ds(mine, 1), :] for kind in range(4)]
    cosine = tab[0] * here[0] - tab[1] * here[1]
    sine = tab[1] * here[0] + tab[0] * here[1]
    factor = jnp.where(step == 0, tab[2] * here[2], tab[3] * here[3])
    lane = lax.broadcasted_iota(jnp.int32, cosine.shape, 1)
    sine = jnp.where(lane % 2 == 0, -sine, sine)
    cosine = jnp.where(step == 2, 1.0, cosine * factor)
    sine = jnp.where(step == 2, 0.0, sine * factor)
    for i in range(acc.shape[1] // 128):
        piece = acc[:, i * 128 : (i + 1) * 128]
        turned = (piece * cosine + swap_pairs(piece, 1) * sine).T.astype(bf16)
        for h in range(128 // HD):
            out[i * (128 // HD) + h, pl.ds(pl.multiple_of(step * HD, HD), HD), :] = turned[
                h * HD : (h + 1) * HD
            ]


def gather_heads(got, keys, ids_col, values=None):
    for j in range(got.shape[0]):
        rows = slice(j * got.shape[2], (j + 1) * got.shape[2])
        both = jnp.concatenate([got[j, HD : 3 * HD, :].astype(f32)], axis=0).T
        keys[rows, :] = both[:, :HD].astype(bf16)
        if values is not None:
            values[rows, :] = both[:, HD:].astype(bf16)
        ids_col[rows, :] = got[j, 3 * HD : 3 * HD + 16, :].astype(f32).T


def visible_scores(me, part, scores, ids_col, ids_row, count, first, group):
    same = ids_col[0:count, 0:1] == ids_row
    length = group
    key = lax.broadcasted_iota(jnp.int32, (length, length), 0)
    query = lax.broadcasted_iota(jnp.int32, (length, length), 1)
    rows = first
    own = lambda index: (index // rows) * rows + own_order(me, part, index % rows)
    earlier = own(key) <= own(query)
    if count > length:
        earlier = jnp.concatenate([jnp.ones((count - length, length), jnp.bool_), earlier], axis=0)
    return same & earlier


def attend_kernel(parts, ids, got, out, mixed, lse, kept, keys, ids_col):
    me = ids[0]
    kept[...] = got[...]
    blocks, _, rows = got.shape
    part = rows // parts
    gather_heads(got, keys, ids_col)
    group = 2 if blocks % 2 == 0 else 1
    width = group * rows
    for i in range(blocks // group):
        mine = range(i * group, (i + 1) * group)
        query = jnp.concatenate([got[j, :HD, :] for j in mine], axis=1) * bf16(HD**-0.5)
        ids_row = jnp.concatenate([got[j, 3 * HD : 3 * HD + 1, :] for j in mine], axis=1).astype(f32)
        count = (i + 1) * width
        scores = dot(keys[0:count, :], query)
        allowed = visible_scores(me, part, scores, ids_col, ids_row, count, rows, width)
        scores = jnp.where(allowed, scores, masked_score)
        top = jnp.max(scores, axis=0, keepdims=True)
        exponent = jnp.exp(scores - top)
        total = jnp.sum(exponent, axis=0, keepdims=True)
        value = jnp.concatenate([got[j, 2 * HD : 3 * HD, :] for j in range((i + 1) * group)], axis=1)
        result = dot(value, exponent.astype(bf16)) / total
        mixed[:, i * width : (i + 1) * width] = result
        lse[:, i * width : (i + 1) * width] = top + jnp.log(total)
        for n, j in enumerate(mine):
            out[j] = result[:, n * rows : (n + 1) * rows].astype(bf16)


def store_pieces(total, own, pieces, part, extra=None):
    own[:, : total.shape[1]] = total[:part]
    for k, piece in enumerate(pieces, 1):
        piece[:, : total.shape[1]] = total[k * part : (k + 1) * part].astype(bf16)
    if extra is not None:
        own[:, total.shape[1] :] = extra[:part]
        for k, piece in enumerate(pieces, 1):
            piece[:, total.shape[1] :] = extra[k * part : (k + 1) * part].astype(bf16)


def fold_row(row, part):
    block = jnp.concatenate([row[:, i : i + 128] for i in range(0, row.shape[1], 128)], axis=0)
    return jnp.concatenate(split_low(block), axis=0)


def unfold_row(block):
    half = block.shape[0] // 2
    total = block[:half].astype(f32) + block[half:].astype(f32)
    return jnp.concatenate([total[i : i + 1] for i in range(half)], axis=1)


def out_kernel(parts, att, gain, weight, own, *refs):
    pieces, kept = refs[:-1], refs[-1]
    kept[...] = att[...]
    blocks, _, rows = att.shape
    part, width = rows // parts, weight.shape[1]
    value = jnp.concatenate([att[j].astype(f32) for j in range(blocks)], axis=0).T
    high, low = split_low(jnp.mean(value, axis=1, keepdims=True))
    centred = value - (high.astype(f32) + low.astype(f32))
    square = split_low(jnp.sum(centred * centred, axis=1, keepdims=True))
    gains = gain[...]
    row = lax.broadcasted_iota(jnp.int32, (16, gains.shape[1]), 0)
    gain_high, gain_low = (t.astype(f32) for t in split_low(gains))
    gain_rows = jnp.where(row == 0, gain_high, jnp.where(row == 1, gain_low, 0.0))
    left = jnp.concatenate([(centred * gains).astype(bf16), gain_rows.astype(bf16)], axis=0)
    total = dot(left, weight[...])
    folded = fold_row(total[rows : rows + 1] + total[rows + 1 : rows + 2], part)
    stats = lanes_of([high, low, *square], rows).astype(bf16)
    own[:, :width] = total[:part]
    own[:, width : width + 128] = stats[:part].astype(f32)
    own[:, width + 128 :] = folded.astype(f32)
    for k, piece in enumerate(pieces, 1):
        here = slice(k * part, (k + 1) * part)
        piece[:, :width] = total[here].astype(bf16)
        piece[:, width : width + 128] = stats[here]
        piece[:, width + 128 :] = folded


def middle_kernel(parts, head_width, own, *refs):
    got, (x, gain, x1, u, gain_row) = refs[: parts - 1], refs[parts - 1 :]
    part, width = x1.shape
    blocks = [own] + list(got)
    stats = [b[:, width : width + 128] for b in blocks]
    means = [pair_sum(b, 0) for b in stats]
    squares = [pair_sum(b, 2) for b in stats]
    rows = [unfold_row(b[:, width + 128 :]) for b in blocks]
    gain_row[...] = sum(rows)
    mean = sum(means) / parts
    spread = sum(squares) + head_width * sum((m - mean) * (m - mean) for m in means)
    scaling = lax.rsqrt(spread / width + eps)
    total = sum(b[:, :width].astype(f32) for b in blocks)
    for m, row in zip(means, rows):
        total = total + (m - mean) * row
    value = x[...].astype(f32) + total * scaling
    x1[...] = value
    normed, _ = norm_rows(value)
    u[:, :width] = (normed * gain[...]).astype(bf16)
    u[:, width:] = lanes_of([*split_low(mean), *split_low(scaling)], part).astype(bf16)


def grad_hidden_kernel(gy, weight, grad):
    grad[...] = dot_t(gy[...], weight[...])


def flip_kernel(weight, out):
    out[...] = weight[...].T


def up_kernel(parts, step, own, *refs):
    got, refs = refs[: parts - 1], refs[parts - 1 :]
    weight, grad, gain, act, slope, u, stats, tail, rows_u = refs
    part = own.shape[0]
    rows, width = rows_u.shape
    for k, block in enumerate([own] + list(got)):
        rows_u[k * part : (k + 1) * part, :] = block[:, :width]
        tail[k * part : (k + 1) * part, :] = block[:, width:].astype(f32)
    wide = u.shape[2]
    for j in range(u.shape[0]):
        u[j] = rows_u[:, j * wide : (j + 1) * wide]
    total = [jnp.zeros((rows, 128), f32)] * 4
    for i in range(0, weight.shape[1], step):
        here = slice(i, i + step)
        hidden = dot(rows_u[...], weight[:, here])
        cdf = 0.5 * (1.0 + lax.erf(hidden * (0.5**0.5)))
        value = hidden * cdf
        act[:, here] = value
        slope[:, here] = cdf + hidden * jnp.exp(-0.5 * hidden * hidden) * 0.3989422804014327
        grad_normed = grad[:, here] * gain[:, here]
        columns = [value, value * value, grad_normed, grad_normed * value]
        for n, column in enumerate(columns):
            for j in range(0, step, 128):
                total[n] = total[n] + column[:, j : j + 128]
    sums = lanes_of([jnp.sum(t, axis=1, keepdims=True) for t in total], rows)
    stats[...] = sums.T[:8, :]


def swap_lane_blocks(value, k, part):
    lanes = value.shape[1]
    lane = lax.broadcasted_iota(jnp.int32, value.shape, 1)
    distance = 1
    while distance <= k:
        if k & distance:
            move = distance * part
            value = jnp.where(
                (lane // move) % 2 == 0,
                pltpu.roll(value, lanes - move, 1),
                pltpu.roll(value, move, 1),
            )
        distance *= 2
    return value


def hidden_back_kernel(parts, full, step, own, *refs):
    got, refs = refs[: parts - 1], refs[parts - 1 :]
    act, slope, grad, gain, weight, gh, z2, own_out = refs[:8]
    pieces = refs[8:]
    rows = act.shape[0]
    part = rows // parts
    total = own[...]
    for k, block in enumerate(got, 1):
        total = total + swap_lane_blocks(block[...], k, part)
    mean = total[0:1] / full
    scaling = lax.rsqrt(total[1:2] / full - mean * mean + eps)
    first = total[2:3] / full
    cross = scaling * (total[3:4] / full - mean * first)
    row = lax.broadcasted_iota(jnp.int32, (rows, rows), 0)
    table = jnp.zeros((rows, rows), f32)
    for i, value in enumerate([mean, scaling, first, cross]):
        table = jnp.where(row == i, value, table)
    cols = table.T
    mean, scaling, first, cross = (cols[:, i : i + 1] for i in range(4))
    wide = z2.shape[2]
    for i in range(0, act.shape[1], step):
        here = slice(i, i + step)
        normed = (act[:, here] - mean) * scaling
        low = (normed * gain[:, here]).astype(bf16)
        for j in range(0, step, wide):
            z2[(i + j) // wide] = low[:, j : j + wide]
        value = scaling * (grad[:, here] * gain[:, here] - first - normed * cross) * slope[:, here]
        gh[:, here] = value.astype(bf16)
    width = weight.shape[1]
    for i in range(0, width, step):
        here = slice(i, i + step)
        result = dot(gh[...], weight[:, here])
        own_out[:, here] = result[:part]
        for k, piece in enumerate(pieces, 1):
            piece[:, here] = result[k * part : (k + 1) * part].astype(bf16)


def down_kernel(parts, step, z2, gh, weight, own_out, *refs):
    pieces, gh_out = refs[: parts - 1], refs[parts - 1]
    gh_out[...] = gh[...]
    wide = z2.shape[2]
    part = own_out.shape[0]
    for i in range(0, weight.shape[1], step):
        here = slice(i, i + step)
        result = sum(
            dot(z2[j], weight[j * wide : (j + 1) * wide, here]) for j in range(z2.shape[0])
        )
        own_out[:, here] = result[:part]
        for k, piece in enumerate(pieces, 1):
            piece[:, here] = result[k * part : (k + 1) * part].astype(bf16)


def middle_back_kernel(parts, own, *refs):
    got, refs = refs[: parts - 1], refs[parts - 1 :]
    gain_row, x, x1, gy, gain, gx1, gb = refs
    part, width = x1.shape
    grad = own[...]
    for block in got:
        grad = grad + block[...].astype(f32)
    value = x1[...]
    normed, scaling = norm_rows(value)
    result = gy[...].astype(f32) + norm_back(grad, gain[...], normed, scaling)
    gx1[...] = result
    low = result.astype(bf16)
    gb[:, :width] = low
    low = low.astype(f32)
    first = jnp.sum(low * gain_row[...], axis=1, keepdims=True) / width
    cross = jnp.sum(low * (value - x[...].astype(f32)), axis=1, keepdims=True) / width
    gb[:, width:] = lanes_of([*split_low(first), *split_low(cross)], part).astype(bf16)


def heads_back_kernel(parts, own, *refs):
    got, refs = refs[: parts - 1], refs[parts - 1 :]
    stats, att, gain, weight, sent, gb = refs
    blocks, _, rows = att.shape
    part, width = own.shape[0], gb.shape[1]
    for k, block in enumerate([own] + list(got)):
        gb[k * part : (k + 1) * part, :] = block[:, :width]
    columns = jnp.concatenate([b[:, width:].astype(f32) for b in [own] + list(got)], axis=0).T
    first = columns[0:1] + columns[1:2]
    cross = columns[2:3] + columns[3:4]
    columns = stats[...].T
    mean = columns[0:1] + columns[1:2]
    scaling = columns[2:3] + columns[3:4]
    grad = dot_t(weight[...], gb[...])
    value = jnp.concatenate([att[j].astype(f32) for j in range(blocks)], axis=0)
    normed = (value - mean) * scaling
    gain_col = jnp.broadcast_to(gain[...], (8, gain.shape[1])).T[:, 0:1]
    go = (scaling * (grad * gain_col - first - normed * cross)).astype(bf16)
    z = (normed * gain_col).astype(bf16)
    for j in range(blocks):
        sent[j, :HD, :] = go[j * HD : (j + 1) * HD]
        sent[j, HD:, :] = z[j * HD : (j + 1) * HD]


def hand_on_kernel(value, out):
    out[...] = value[...]


def turn_back(grad, table, base, j, inverse):
    here = [base[kind, :, j : j + 1] for kind in range(4)]
    cosine = table[0] * here[0] - table[1] * here[1]
    sine = table[1] * here[0] + table[0] * here[1]
    factor = table[3] * here[3] if inverse else table[2] * here[2]
    row = lax.broadcasted_iota(jnp.int32, grad.shape, 0)
    sine = jnp.where(row % 2 == 0, sine, -sine)
    return (grad * cosine + swap_pairs(grad, 0) * sine) * factor


def attend_back_kernel(parts, ids, got, grads, mixed, lse, inner, base, out, keys, values, ids_col, gk, gv):
    me = ids[0]
    blocks, _, rows = got.shape
    part = rows // parts
    gather_heads(got, keys, ids_col, values)
    gk[...] = jnp.zeros_like(gk)
    gv[...] = jnp.zeros_like(gv)
    table = []
    for kind in range(4):
        ordered = jnp.concatenate(
            [inner[kind, block_at(me, k, part), :] for k in range(parts)], axis=0
        )
        table.append(ordered.T[:HD])
    group = 2 if blocks % 2 == 0 else 1
    width = group * rows
    for i in range(blocks // group):
        mine = range(i * group, (i + 1) * group)
        query = jnp.concatenate([got[j, :HD, :] for j in mine], axis=1) * bf16(HD**-0.5)
        ids_row = jnp.concatenate([got[j, 3 * HD : 3 * HD + 1, :] for j in mine], axis=1).astype(f32)
        go = jnp.concatenate([grads[j, :HD, :] for j in mine], axis=1)
        span = slice(i * width, (i + 1) * width)
        delta = jnp.sum(go.astype(f32) * mixed[:, span], axis=0, keepdims=True)
        count = (i + 1) * width
        scores = dot(keys[0:count, :], query)
        allowed = visible_scores(me, part, scores, ids_col, ids_row, count, rows, width)
        probability = jnp.where(allowed, jnp.exp(jnp.minimum(scores - lse[:, span], 0.5)), 0.0)
        grad_prob = dot(values[0:count, :], go)
        grad_scores = (probability * (grad_prob - delta)).astype(bf16)
        gv[:, 0:count] += dot_t(go, probability.astype(bf16))
        gk[:, 0:count] += dot_t(query, grad_scores)
        key = jnp.concatenate([got[j, HD : 2 * HD, :] for j in range((i + 1) * group)], axis=1)
        gq = dot(key, grad_scores) * HD**-0.5
        for n, j in enumerate(mine):
            piece = turn_back(gq[:, n * rows : (n + 1) * rows], table, base, j, False)
            out[j, :HD, :] = piece.astype(bf16)
    for j in range(blocks):
        span = slice(j * rows, (j + 1) * rows)
        out[j, HD : 2 * HD, :] = turn_back(gk[:, span], table, base, j, True).astype(bf16)
        out[j, 2 * HD :, :] = gv[:, span].astype(bf16)


def input_back_kernel(parts, step, got, weight, own_out, *pieces):
    part, width = own_out.shape
    grads = []
    for c in range(3):
        here = slice(c * HD, (c + 1) * HD)
        grad = jnp.concatenate([got[j, here, :].astype(f32) for j in range(got.shape[0])], axis=0)
        grads.append(grad.T.astype(bf16))
    for i in range(0, width, step):
        here = slice(i, i + step)
        result = sum(dot_t(grads[c], weight[c, here, :]) for c in range(3))
        own_out[:, here] = result[:part]
        for k, piece in enumerate(pieces, 1):
            piece[:, here] = result[k * part : (k + 1) * part].astype(bf16)


def final_kernel(parts, own, *refs):
    got, refs = refs[: parts - 1], refs[parts - 1 :]
    x, gx1, gain, out = refs
    grad = own[...]
    for block in got:
        grad = grad + block[...].astype(f32)
    normed, scaling = norm_rows(x[...].astype(f32))
    out[...] = (gx1[...] + norm_back(grad, gain[...], normed, scaling)).astype(bf16)


def output_kernel(own, *refs):
    got, (x1, out) = refs[:-2], refs[-2:]
    total = own[...] + x1[...]
    for block in got:
        total = total + block[...].astype(f32)
    out[...] = total.astype(bf16)


def natural_kernel(ids, *refs):
    blocks, out = refs[:-1], refs[-1]
    part = blocks[0].shape[0]
    for k, block in enumerate(blocks):
        out[block_at(ids[0], k, part), :] = block[...]


def own_row(table, index):
    row = lax.broadcasted_iota(jnp.int32, table.shape, 0)
    return jnp.sum(jnp.where(row == index, table[...], 0.0), axis=0, keepdims=True)


def row_of(column, columns):
    return jnp.broadcast_to(column, (columns, 128)).T[:1, :]


def columns_grad_kernel(ids, left, right, weight, gain, out, gain_grad, left_all, sums):
    step = pl.program_id(0)

    @pl.when(step == 0)
    def _():
        rows = left.shape[1]
        for j in range(left.shape[0]):
            left_all[j * rows : (j + 1) * rows, :] = left[j]
        sums[...] = jnp.zeros_like(sums)

    grad = t_dot(left_all[...], right[...])
    out[...] = grad
    sums[...] += jnp.sum(grad * weight[...].astype(f32), axis=1, keepdims=True)

    @pl.when(step == pl.num_programs(0) - 1)
    def _():
        gain_grad[...] = row_of(sums[...], sums.shape[0]) / own_row(gain, ids[1])


def rows_grad_kernel(first, ids, left, right, weight, gain, out, gain_grad, sums):
    step = pl.program_id(0)

    @pl.when(step == 0)
    def _():
        sums[...] = jnp.zeros_like(sums)

    value = jnp.concatenate([left[j, first:, :] for j in range(left.shape[0])], axis=1)
    grad = dot(value, right[...])
    out[...] = grad
    sums[...] += jnp.sum(grad * weight[...].astype(f32), axis=1, keepdims=True)

    @pl.when(step == pl.num_programs(0) - 1)
    def _():
        gain_grad[...] = row_of(sums[...], sums.shape[0]) / own_row(gain, ids[1])


def grad_qkv_kernel(left, right, out):
    value = jnp.concatenate([left[j] for j in range(left.shape[0])], axis=1)
    out[0] = dot(value, right[...]).astype(bf16)


def grad_qkv_place_kernel(ids, got, weight, gain, up_gain, out, gain_grads):
    total = 0.0
    for c in range(3):
        value = jnp.concatenate(
            [got[j, c * HD : (c + 1) * HD, :].astype(f32) for j in range(got.shape[0])], axis=0
        ).T
        out[c] = value
        total = total + jnp.sum(value * weight[c].astype(f32), axis=1, keepdims=True)
    first = row_of(total, total.shape[0]) / own_row(gain, ids[1])
    row = lax.broadcasted_iota(jnp.int32, gain_grads.shape, 0)
    gain_grads[...] = jnp.where(row == 0, first, up_gain[...])


def gain_sum_kernel(*refs):
    blocks, (first, second) = refs[:-2], refs[-2:]
    total = sum(b[...] for b in blocks)
    first[...] = total[0:1]
    second[...] = total[1:2]


def body(
    layer_input,
    segment_ids,
    qkv_weight,
    out_weight,
    up_weight,
    down_weight,
    input_gain,
    heads_gain,
    middle_gain,
    hidden_gain,
    cotangent,
):
    rows, row_count, width = layer_input.shape
    T, C = lax.axis_size("tp"), lax.axis_size("cp")
    part = rows // T
    head_width = qkv_weight.shape[2]
    if head_width // HD != C or row_count != 1 or rows != 128 or 64 * part != width:
        return body_general(
            layer_input, segment_ids, qkv_weight, out_weight, up_weight, down_weight,
            input_gain, heads_gain, middle_gain, hidden_gain, cotangent,
        )
    tokens = rows * C
    hidden = up_weight.shape[1]
    wide = width // C
    high = hidden // C
    ids = jnp.stack([lax.axis_index("tp"), lax.axis_index("cp")]).astype(jnp.int32)
    x = layer_input.reshape(rows, width)
    gy = cotangent.reshape(rows, width)
    weight3 = jnp.transpose(qkv_weight, (1, 0, 2))
    gain_in, gain_mid = input_gain.reshape(1, -1), middle_gain.reshape(1, -1)
    gain_heads, gain_hid = heads_gain.reshape(1, -1), hidden_gain.reshape(1, -1)
    inner, base = tables(rows, C)
    inner2 = jnp.asarray(np.concatenate([inner, inner], axis=2))
    base2 = jnp.asarray(np.concatenate([base, base], axis=2))
    base_t = np.zeros((4, HD, 128), np.float32)
    base_t[:, :, :C] = np.transpose(base, (0, 2, 1))
    base_t = jnp.asarray(base_t)
    wide_part = width + 128
    step = 512

    def piece_shapes(columns):
        return [shape((part, columns), f32)] + [shape((part, columns), bf16)] * (T - 1)

    def exchange(pieces):
        return [swap_tp(piece, k) for k, piece in enumerate(pieces, 1)]

    def spread(block):
        return [swap_tp(block, k) for k in range(1, T)]

    def to_cp(value):
        return lax.all_to_all(value, "cp", 0, 0, tiled=True)

    def entire(value):
        return (value, value.shape, None)

    def own_rows(value):
        return (value, (part, width), lambda ids: (block_at(ids[0], 0, part), slice(None)))

    cols, first_rows = lambda i, *_: (0, i), lambda i, *_: (i, 0)
    origin2, origin3 = lambda i, *_: (0, 0), lambda i, *_: (0, 0, 0)

    a, gy_x, sent = call(
        functools.partial(project_kernel, T),
        [Pin(shape((rows, width), bf16)), Pin(shape((rows, width), bf16)), Pin(shape((C, 3 * HD + 16, rows), bf16))],
        [ids, Pin(x), Pin(gy), Pin(segment_ids.reshape(1, rows)), Pin(gain_in), Pin(weight3), Pin(inner2), Pin(base2)],
        [scalars(), fixed((rows, width)), fixed((rows, width)), fixed((1, rows)), fixed((1, width)),
         pl.BlockSpec((1, width, head_width), lambda i: (i, 0, 0)), fixed((4, rows, 128)), fixed((4, C, 128))],
        [fixed((rows, width)), fixed((rows, width)), fixed((C, 3 * HD + 16, rows))],
        grid=(3,), scratch=[pltpu.VMEM((4, rows, 128), f32)], mb=14,
    )
    got = to_cp(sent)
    near_up, near_out, near_x, near_gy, near_mid, near_heads, near_hid, near_in = bring(
        [entire(up_weight), entire(out_weight), own_rows(x), own_rows(gy), entire(gain_mid), entire(gain_heads),
         entire(gain_hid), entire(gain_in)],
        ids, after=[Pin(sent)],
    )
    back, mixed, lse, near_got, gy_x = call(
        functools.partial(attend_kernel, T),
        [Far(shape((C, HD, rows), bf16)), Near(shape((HD, tokens), f32)), Near(shape((1, tokens), f32)),
         Near(shape((C, 3 * HD + 16, rows), bf16))],
        [ids, got], [scalars(), whole()],
        scratch=[pltpu.VMEM((tokens, HD), bf16), pltpu.VMEM((tokens, 16), f32)],
        mb=10, after=[near_heads], carry=[gy_x],
    )
    att = to_cp(back)
    gy_all = cp_gather(gy_x)

    own, *pieces, near_att, a = call(
        functools.partial(out_kernel, T),
        piece_shapes(width + 256) + [Near(shape((C, HD, rows), bf16))],
        [att, near_heads, near_out], carry=[a],
    )
    a_all = cp_gather(a)
    grad_hid, near_token = call(
        lambda gy_ref, weight, grad, token: (
            grad_hidden_kernel(gy_ref, weight, grad), hand_on_kernel(jnp.zeros((8, 128), f32), token)),
        [Near(shape((rows, hidden), f32)), shape((8, 128), f32)],
        [Pin(gy_x), Pin(down_weight)],
        [fixed((rows, width)), pl.BlockSpec((step, width), first_rows)],
        [pl.BlockSpec((rows, step), cols), fixed((8, 128))],
        grid=(hidden // step,), after=[own], mb=10,
    )
    x1, u_own, gain_row = call(
        functools.partial(middle_kernel, T, head_width),
        [Near(shape((part, width), f32)), shape((part, wide_part), bf16), Near(shape((1, width), f32))],
        [own, *exchange(pieces), near_x, near_mid], after=[near_token],
    )
    u_blocks = [u_own] + spread(u_own)
    (near_down,) = bring([entire(down_weight)], ids, after=[u_own])
    (near_flip,) = call(flip_kernel, [Near(shape((hidden, width), bf16))], [near_up], after=[u_own], mb=16)

    act, slope, u_cols, stats, near_tail = call(
        functools.partial(up_kernel, T, step),
        [Near(shape((rows, hidden), f32)), Near(shape((rows, hidden), f32)), Near(shape((C, rows, wide), bf16)),
         shape((8, rows), f32), Near(shape((rows, 128), f32))],
        [*u_blocks, near_up, grad_hid, near_hid],
        scratch=[pltpu.VMEM((rows, width), bf16)], mb=8, after=[near_flip, near_down],
    )
    gh, z2, own, *pieces = call(
        functools.partial(hidden_back_kernel, T, FF, step),
        [Near(shape((rows, hidden), bf16)), Near(shape((C, rows, high), bf16))] + piece_shapes(width),
        [stats, *spread(stats), act, slope, grad_hid, near_hid, near_flip], mb=8,
    )
    gu_got = exchange(pieces)
    (z2_sent,) = call(hand_on_kernel, [Far(shape(z2.shape, bf16))], [z2], after=[own])
    z2_got = to_cp(z2_sent)
    y_own, *y_pieces, gh_out, u_sent = call(
        lambda z2_ref, gh_ref, w_ref, u_ref, *outs: (
            down_kernel(T, step, z2_ref, gh_ref, w_ref, *outs[:-1]), hand_on_kernel(u_ref, outs[-1])),
        [Near(t) for t in piece_shapes(width)] + [Far(shape((rows, hidden), bf16)), Far(shape(u_cols.shape, bf16))],
        [z2, gh, near_down, u_cols], after=[own, Pin(z2_sent)],
    )
    gh_all = cp_gather(gh_out)
    u_got = to_cp(u_sent)
    gx1, gb_own = call(
        functools.partial(middle_back_kernel, T),
        [Near(shape((part, width), f32)), shape((part, wide_part), bf16)],
        [own, *gu_got, gain_row, near_x, x1, near_gy, near_mid], after=[Pin(gh_out)],
    )
    gb_blocks = [gb_own] + spread(gb_own)

    def columns_grad(left, right, weight, gain, after):
        own_columns = left.shape[2]
        return call(
            columns_grad_kernel,
            [Pin(shape((own_columns, right.shape[1]), f32)), shape((1, own_columns), f32)],
            [ids, Pin(left), Pin(right), Pin(weight), gain.reshape(C, -1)],
            [scalars(), pl.BlockSpec(left.shape, origin3), pl.BlockSpec((tokens, step), cols),
             pl.BlockSpec((own_columns, step), lambda i, ids: (ids[1], i)), pl.BlockSpec((C, own_columns), origin2)],
            [pl.BlockSpec((own_columns, step), cols), pl.BlockSpec((1, own_columns), origin2)],
            grid=(right.shape[1] // step,),
            scratch=[pltpu.VMEM((tokens, own_columns), bf16), pltpu.VMEM((own_columns, 1), f32)],
            after=after, prefetch=1, mb=10,
        )

    grad_down, hidden_gain_grad = columns_grad(z2_got, gy_all, down_weight, hidden_gain, [gb_own])
    near_three, near_inner, near_base = bring(
        [entire(weight3), entire(inner2), entire(base_t)], ids, after=[Pin(grad_down)]
    )
    sent, gb, *y_pieces = call(
        functools.partial(heads_back_kernel, T),
        [Far(shape((C, 2 * HD, rows), bf16)), Near(shape((rows, width), bf16))],
        [*gb_blocks, near_tail, near_att, near_heads, near_out], after=[near_base], carry=y_pieces,
    )
    y_got = exchange(y_pieces)
    grads = to_cp(sent)
    (gb_out,) = call(hand_on_kernel, [Far(shape((rows, width), bf16))], [gb], after=[Pin(sent)])
    gb_all = cp_gather(gb_out)
    (gq_sent,) = call(
        functools.partial(attend_back_kernel, T), [Far(shape((C, 3 * HD, rows), bf16))],
        [ids, near_got, grads, mixed, lse, near_inner, near_base], [scalars()] + [whole()] * 6,
        scratch=[pltpu.VMEM((tokens, HD), bf16), pltpu.VMEM((tokens, HD), bf16), pltpu.VMEM((tokens, 16), f32),
                 pltpu.VMEM((HD, tokens), f32), pltpu.VMEM((HD, tokens), f32)],
        mb=12, after=[Pin(gb_out), y_got[0]],
    )
    gq = to_cp(gq_sent)
    (y_low,) = call(output_kernel, [shape((part, width), bf16)], [y_own, *y_got, x1], after=[Pin(gq_sent)])
    y_blocks = [y_low] + spread(y_low)
    (grad_qkv,) = call(
        grad_qkv_kernel, [Pin(shape((C, 3 * HD, wide), bf16))], [Pin(gq_sent), Pin(a_all)],
        [fixed(gq_sent.shape), pl.BlockSpec((tokens, wide), cols)],
        [pl.BlockSpec((1, 3 * HD, wide), lambda i: (i, 0, 0))], grid=(C,), after=[y_low],
    )
    own, *pieces, grad_qkv = call(
        functools.partial(input_back_kernel, T, step), piece_shapes(width), [gq, near_three], carry=[grad_qkv],
    )
    ga_got = exchange(pieces)
    grad_qkv_got = to_cp(grad_qkv)
    grad_up, up_gain = columns_grad(u_got, gh_all, up_weight, middle_gain, [own])
    (layer_output,) = call(
        natural_kernel, [Far(shape((rows, width), bf16))], [ids, *y_blocks], [scalars()] + [whole()] * T, after=[own]
    )
    (grad_in,) = call(
        functools.partial(final_kernel, T),
        [shape((part, width), bf16)],
        [own, *ga_got, near_x, gx1, near_in], after=[Pin(layer_output), Pin(grad_up)],
    )
    grad_blocks = [grad_in] + spread(grad_in)

    own_wide = lambda ids: (slice(None), pl.ds(pl.multiple_of(ids[1] * wide, wide), wide), slice(None))
    grad_out, heads_gain_grad = call(
        functools.partial(rows_grad_kernel, HD),
        [Pin(shape((HD, width), f32)), shape((1, HD), f32)],
        [ids, Pin(grads), Pin(gb_all), Pin(out_weight), heads_gain.reshape(C, -1)],
        [scalars(), pl.BlockSpec(grads.shape, origin3), pl.BlockSpec((tokens, step), cols),
         pl.BlockSpec((HD, step), lambda i, ids: (ids[1], i)), pl.BlockSpec((C, HD), origin2)],
        [pl.BlockSpec((HD, step), cols), pl.BlockSpec((1, HD), origin2)], grid=(width // step,),
        scratch=[pltpu.VMEM((HD, 1), f32)], after=[grad_in], prefetch=1,
    )
    grad_qkv, gains = call(
        grad_qkv_place_kernel,
        [Far(shape((3, wide, head_width), f32)), shape((8, wide), f32)],
        [ids, grad_qkv_got, Far(weight3, (3, wide, head_width), own_wide), input_gain.reshape(C, -1), up_gain],
        [scalars()] + [whole()] * 4, after=[Pin(grad_out)],
    )
    (grad_input,) = call(
        natural_kernel, [Far(shape((rows, width), bf16))], [ids, *grad_blocks], [scalars()] + [whole()] * T,
        after=[Pin(grad_qkv)],
    )
    input_gain_grad, middle_gain_grad = call(
        gain_sum_kernel, [shape((1, wide), f32), shape((1, wide), f32)], [gains, *spread(gains)]
    )
    return (
        layer_output.reshape(layer_input.shape),
        grad_input.reshape(layer_input.shape),
        jnp.transpose(grad_qkv, (1, 0, 2)),
        grad_out,
        grad_up,
        grad_down,
        input_gain_grad.reshape(-1),
        heads_gain_grad.reshape(-1),
        middle_gain_grad.reshape(-1),
        hidden_gain_grad.reshape(-1),
    )


def solution(mesh):
    placed = (
        P("cp", None, None),
        P("cp", None),
        P(None, None, "tp"),
        P("tp", None),
        P(None, "tp"),
        P("tp", None),
        P(),
        P("tp"),
        P(),
        P("tp"),
        P("cp", None, None),
    )
    return jax.shard_map(
        body,
        mesh=mesh,
        in_specs=placed,
        out_specs=(
            P("cp", None, None),
            P("cp", None, None),
            P("cp", None, "tp"),
            P(("tp", "cp"), None),
            P("cp", "tp"),
            P(("tp", "cp"), None),
            P("cp"),
            P(("tp", "cp")),
            P("cp"),
            P(("tp", "cp")),
        ),
        check_vma=False,
    )
```

```python
import functools

import jax
import jax.numpy as jnp
import numpy as np
from jax import lax
from jax.experimental import pallas as pl
from jax.experimental.pallas import tpu as pltpu
from jax.sharding import PartitionSpec as P

HD = 64
D = 2048
FF = 8192

eps = 1e-05
scale_base = 512.0
masked_score = -1e30
f32 = jnp.float32
bf16 = jnp.bfloat16


def dot(a, b):
    return jnp.dot(a, b, preferred_element_type=f32)


def dot_t(a, b):
    return lax.dot_general(a, b, (((1,), (1,)), ((), ())), preferred_element_type=f32)


def t_dot(a, b):
    return lax.dot_general(a, b, (((0,), (0,)), ((), ())), preferred_element_type=f32)


def pairs(count, k):
    return [(i, i ^ k) for i in range(count)]


def swap_tp(value, k):
    return lax.ppermute(value, "tp", pairs(lax.axis_size("tp"), k))


def tp_order(value):
    count, me = lax.axis_size("tp"), lax.axis_index("tp")
    part = value.shape[0] // count
    return jnp.concatenate(
        [lax.dynamic_slice_in_dim(value, (me ^ k) * part, part, 0) for k in range(count)], axis=0
    )


def tp_scatter_sum(partial_sum):
    count = lax.axis_size("tp")
    part = partial_sum.shape[0] // count
    low = partial_sum.astype(bf16)
    total = partial_sum[:part]
    for k in range(1, count):
        total = total + swap_tp(low[k * part : (k + 1) * part], k).astype(f32)
    return total


def tp_gather(block):
    count = lax.axis_size("tp")
    return jnp.concatenate([block] + [swap_tp(block, k) for k in range(1, count)], axis=0)


def tp_sum(value):
    total = value
    for k in range(1, lax.axis_size("tp")):
        total = total + swap_tp(value, k)
    return total


def tp_token_sum(value):
    count = lax.axis_size("tp")
    blocks = value.reshape(value.shape[0], count, -1)
    total = blocks
    for k in range(1, count):
        got = swap_tp(blocks, k)
        total = total + jnp.stack([got[:, j ^ k] for j in range(count)], axis=1)
    return total.reshape(value.shape)


def cp_columns(value):
    return lax.all_to_all(value, "cp", split_axis=1, concat_axis=0, tiled=True)


def cp_gather(value):
    return lax.all_gather(value, "cp", axis=0, tiled=True)


def xpos_tables(positions):
    column = jnp.arange(HD // 2, dtype=f32)
    frequency = 10000.0 ** (-column / (HD // 2))
    zeta = (2.0 * column + 0.4 * HD) / (1.4 * HD)
    places = positions.astype(f32)[:, None]
    angle = places * frequency
    return (jnp.cos(angle), jnp.sin(angle), zeta ** (places / scale_base))


def turn(vector, cosine, sine, factor):
    paired = vector.reshape(vector.shape[:-1] + (HD // 2, 2))
    first, second = paired[..., 0], paired[..., 1]
    cosine, sine, factor = cosine[:, None], sine[:, None], factor[:, None]
    turned = jnp.stack(
        [(first * cosine - second * sine) * factor, (first * sine + second * cosine) * factor],
        axis=-1,
    )
    return turned.reshape(vector.shape)


def norm_rows(vector):
    center = jnp.mean(vector, axis=-1, keepdims=True)
    shifted = vector - center
    scaling = lax.rsqrt(jnp.mean(shifted * shifted, axis=-1, keepdims=True) + eps)
    return (shifted * scaling, scaling)


def norm_back(grad_result, gain, normed, scaling):
    grad_normed = grad_result * gain
    first = jnp.mean(grad_normed, axis=-1, keepdims=True)
    cross = jnp.mean(grad_normed * normed, axis=-1, keepdims=True)
    return scaling * (grad_normed - first - normed * cross)


def attend(queries, keys, values, allowed):
    scores = jnp.einsum("qhd,khd->hqk", queries, keys, preferred_element_type=f32) * HD**-0.5
    scores = jnp.where(allowed[None], scores, masked_score)
    top = jnp.max(scores, axis=-1, keepdims=True)
    exponent = jnp.where(allowed[None], jnp.exp(scores - top), 0.0)
    total = jnp.sum(exponent, axis=-1, keepdims=True)
    probability = (exponent / total).astype(bf16)
    mixed = jnp.einsum("hqk,khd->qhd", probability, values, preferred_element_type=f32)
    return (mixed, top + jnp.log(total))


def attend_back(queries, keys, values, allowed, lse, grad, delta):
    scores = jnp.einsum("qhd,khd->hqk", queries, keys, preferred_element_type=f32) * HD**-0.5
    probability = jnp.where(allowed[None], jnp.exp(scores - lse), 0.0)
    grad_prob = jnp.einsum("qhd,khd->hqk", grad, values, preferred_element_type=f32)
    grad_scores = (probability * (grad_prob - delta.T[:, :, None])).astype(bf16)
    grad_q = jnp.einsum("hqk,khd->qhd", grad_scores, keys, preferred_element_type=f32) * HD**-0.5
    grad_k = jnp.einsum("hqk,qhd->khd", grad_scores, queries, preferred_element_type=f32) * HD**-0.5
    grad_v = jnp.einsum(
        "hqk,qhd->khd", probability.astype(bf16), grad, preferred_element_type=f32
    )
    return (grad_q, grad_k, grad_v)


def body_general(
    layer_input,
    segment_ids,
    qkv_weight,
    out_weight,
    up_weight,
    down_weight,
    input_gain,
    heads_gain,
    middle_gain,
    hidden_gain,
    cotangent,
):
    local_len, row_count, width = layer_input.shape
    tp_count, cp_count = lax.axis_size("tp"), lax.axis_size("cp")
    me_tp, me_cp = lax.axis_index("tp"), lax.axis_index("cp")
    part = local_len // tp_count
    head_width = qkv_weight.shape[2]
    heads = head_width // HD
    by_head = heads % cp_count == 0
    own_heads = heads // cp_count if by_head else heads
    weight3 = jnp.transpose(qkv_weight, (1, 0, 2))

    x = tp_order(layer_input.reshape(local_len, width))
    gy = tp_order(cotangent.reshape(local_len, width))
    seg = tp_order(segment_ids)[:, 0]
    natural = tp_order(jnp.arange(local_len, dtype=jnp.int32))
    position = me_cp * local_len + natural
    position_all = (jnp.arange(cp_count, dtype=jnp.int32)[:, None] * local_len + natural).reshape(-1)

    stream = x.astype(f32)
    normed_one, scaling_one = norm_rows(stream)
    a = (normed_one * input_gain).astype(bf16)
    a_all = cp_gather(a)
    cosine, sine, factor = xpos_tables(position)
    raw_q = dot(a, weight3[0]).reshape(local_len, heads, HD)
    raw_k = dot(a, weight3[1]).reshape(local_len, heads, HD)
    raw_v = dot(a, weight3[2]).reshape(local_len, heads, HD)
    q = turn(raw_q, cosine, sine, factor).astype(bf16)
    k = turn(raw_k, cosine, sine, 1.0 / factor).astype(bf16)
    v = raw_v.astype(bf16)
    if by_head:
        extra = jnp.broadcast_to(seg.astype(bf16)[:, None, None], (local_len, cp_count, 16))
        sent = jnp.concatenate(
            [t.reshape(local_len, cp_count, own_heads * HD) for t in (q, k, v)] + [extra], axis=-1
        )
        got = lax.all_to_all(sent, "cp", split_axis=1, concat_axis=0, tiled=True)[:, 0]
        span = own_heads * HD
        q_all, k_all, v_all = (
            got[:, i * span : (i + 1) * span].reshape(-1, own_heads, HD) for i in range(3)
        )
        seg_all = got[:, 3 * span]
        seg_q, position_q = seg_all, position_all
    else:
        q_all, k_all, v_all = q, cp_gather(k), cp_gather(v)
        seg_all = cp_gather(seg.astype(bf16))
        seg_q, position_q = seg.astype(bf16), position
    allowed = (position_all[None, :] <= position_q[:, None]) & (seg_q[:, None] == seg_all[None, :])
    mixed, lse = attend(q_all, k_all, v_all, allowed)
    if by_head:
        attended = lax.all_to_all(
            mixed.astype(bf16).reshape(cp_count * local_len, own_heads * HD),
            "cp", split_axis=0, concat_axis=1, tiled=True,
        ).astype(f32)
    else:
        attended = mixed.reshape(local_len, head_width)

    sums = tp_token_sum(jnp.stack([jnp.sum(attended, axis=1), jnp.sum(attended * attended, axis=1)]))
    center = sums[0] / width
    scaling_h = lax.rsqrt(sums[1] / width - center * center + eps)[:, None]
    normed_h = (attended - center[:, None]) * scaling_h
    z = (normed_h * heads_gain).astype(bf16)
    gain_row = tp_sum(jnp.dot(heads_gain, out_weight.astype(f32)))
    branch = tp_scatter_sum(dot(z, out_weight))
    x1 = stream[:part] + branch
    normed_two, scaling_two = norm_rows(x1)
    u = tp_gather((normed_two * middle_gain).astype(bf16))

    grad_hid = dot_t(gy, down_weight)
    grad_normed = grad_hid * hidden_gain
    hidden = dot(u, up_weight)
    cdf = 0.5 * (1.0 + lax.erf(hidden * (0.5**0.5)))
    act = hidden * cdf
    slope = cdf + hidden * jnp.exp(-0.5 * hidden * hidden) * 0.3989422804014327
    sums = tp_token_sum(
        jnp.stack(
            [
                jnp.sum(act, axis=1),
                jnp.sum(act * act, axis=1),
                jnp.sum(grad_normed, axis=1),
                jnp.sum(grad_normed * act, axis=1),
            ]
        )
    )
    center = sums[0] / FF
    scaling_f = lax.rsqrt(sums[1] / FF - center * center + eps)
    first = sums[2] / FF
    cross = scaling_f * (sums[3] / FF - center * first)
    normed_f = (act - center[:, None]) * scaling_f[:, None]
    z2 = (normed_f * hidden_gain).astype(bf16)
    grad_act = scaling_f[:, None] * (grad_normed - first[:, None] - normed_f * cross[:, None])
    gh = (grad_act * slope).astype(bf16)
    hidden_gain_sum = jnp.sum(grad_hid * normed_f, axis=0)
    gu = tp_scatter_sum(dot_t(gh, up_weight))
    gx1 = gy[:part].astype(f32) + norm_back(gu, middle_gain, normed_two, scaling_two)
    middle_gain_sum = jnp.sum(gu * normed_two, axis=0)
    gb_own = gx1.astype(bf16)
    gb_f = gb_own.astype(f32)
    first = jnp.sum(gb_f * gain_row, axis=1) / width
    cross = jnp.sum(gb_f * branch, axis=1) / width
    gb = tp_gather(gb_own)
    stats = tp_gather(jnp.stack([first, cross], axis=1))

    gz = dot_t(gb, out_weight)
    heads_gain_sum = jnp.sum(gz * normed_h, axis=0)
    go = (scaling_h * (gz * heads_gain - stats[:, :1] - normed_h * stats[:, 1:])).astype(bf16)
    if by_head:
        grad_mixed = cp_columns(go).reshape(-1, own_heads, HD)
    else:
        grad_mixed = go.reshape(local_len, heads, HD)
    delta = jnp.sum(grad_mixed.astype(f32) * mixed, axis=-1)
    gq, gk, gv = attend_back(q_all, k_all, v_all, allowed, lse, grad_mixed, delta)
    if by_head:
        cos_all, sin_all, factor_all = xpos_tables(position_all)
    else:
        cos_all, sin_all, factor_all = cosine, sine, factor
        gk = lax.psum_scatter(gk.astype(bf16), "cp", scatter_dimension=0, tiled=True).astype(f32)
        gv = lax.psum_scatter(gv.astype(bf16), "cp", scatter_dimension=0, tiled=True).astype(f32)
    gq = turn(gq, cos_all, -sin_all, factor_all)
    gk = turn(gk, cos_all, -sin_all, 1.0 / factor_all)
    grads = jnp.stack([gq, gk, gv], axis=1).astype(bf16)
    if by_head:
        grads_own = grads.reshape(-1, 3 * own_heads * HD)
        grads = lax.all_to_all(
            grads.reshape(-1, 3, own_heads * HD), "cp", split_axis=0, concat_axis=2, tiled=True
        )
    else:
        grads = grads.reshape(local_len, 3, head_width)
        grads_own = lax.all_to_all(grads, "cp", split_axis=2, concat_axis=0, tiled=True)
        grads_own = grads_own.reshape(-1, 3 * head_width // cp_count)
    ga = (
        dot_t(grads[:, 0], weight3[0]) + dot_t(grads[:, 1], weight3[1]) + dot_t(grads[:, 2], weight3[2])
    )
    ga = tp_scatter_sum(ga)
    input_gain_sum = jnp.sum(ga * normed_one[:part], axis=0)
    grad_in = gx1 + norm_back(ga, input_gain, normed_one[:part], scaling_one[:part])

    y = (x1 + tp_scatter_sum(dot(z2, down_weight))).astype(bf16)
    layer_output = tp_order(tp_gather(y)).reshape(layer_input.shape)
    grad_input = tp_order(tp_gather(grad_in.astype(bf16))).reshape(layer_input.shape)

    grad_down = t_dot(cp_columns(z2), cp_gather(gy))
    grad_up = t_dot(cp_columns(u), cp_gather(gh))
    grad_out = t_dot(cp_columns(z), cp_gather(gb))
    grad_qkv = t_dot(a_all, grads_own).astype(bf16)
    grad_qkv = lax.all_to_all(
        grad_qkv.reshape(width, 3, head_width // cp_count), "cp", split_axis=0, concat_axis=2, tiled=True
    ).astype(f32)

    def cp_sum_own(vector):
        return jnp.sum(lax.all_to_all(vector.reshape(cp_count, -1), "cp", 0, 0, tiled=True), axis=0)

    def both_sum_own(vector):
        return tp_sum(cp_sum_own(vector))

    return (
        layer_output,
        grad_input,
        grad_qkv,
        grad_out,
        grad_up,
        grad_down,
        both_sum_own(input_gain_sum),
        cp_sum_own(heads_gain_sum),
        both_sum_own(middle_gain_sum),
        cp_sum_own(hidden_gain_sum),
    )


INTERPRET = False


def params(megabytes):
    return pltpu.CompilerParams(vmem_limit_bytes=megabytes * 1024 * 1024)


def shape(dims, kind):
    return jax.ShapeDtypeStruct(dims, kind)


def whole():
    return pl.BlockSpec(memory_space=pltpu.VMEM)


def scalars():
    return pl.BlockSpec(memory_space=pltpu.SMEM)


class Pin:
    def __init__(self, value):
        self.value = value


class Far(Pin):
    def __init__(self, value, dims=None, block=None):
        super().__init__(value)
        self.dims = tuple(value.shape) if dims is None else dims
        self.block = block


class Near:
    def __init__(self, value):
        self.value = value


class Fetched:
    def __init__(self, ref, copy):
        self.ref, self.copy, self.shape = ref, copy, ref.shape

    def ready(self):
        if self.copy is not None:
            self.copy.wait()
            self.copy = None

    def __getitem__(self, index):
        self.ready()
        return self.ref[index]


class Stored:
    def __init__(self, ref, copy):
        self.ref, self.copy, self.shape, self.sent = ref, copy, ref.shape, False

    def send(self):
        if not self.sent:
            self.copy.start()
            self.sent = True

    def __getitem__(self, index):
        return self.ref[index]

    def __setitem__(self, index, value):
        self.ref[index] = value


def plain(value):
    return value.value if isinstance(value, (Pin, Near)) else value


def pinned(value):
    return value if INTERPRET else pltpu.with_memory_space_constraint(value, pltpu.HBM)


def call(
    kernel, outs, args, specs=None, out_specs=None, grid=None, scratch=(), mb=8, cost=0.3, after=(), carry=(), prefetch=0
):
    specs = list(specs) if specs is not None else [whole() for _ in args]
    out_specs = list(out_specs) if out_specs is not None else [whole() for _ in outs]
    count, extra, kept, made = len(args), len(after), len(carry), len(outs)
    anywhere = pl.BlockSpec(memory_space=pl.ANY)
    far_in = [i for i, t in enumerate(args) if isinstance(t, Far)]
    far_out = [i for i, t in enumerate(outs) if isinstance(t, Far)]
    for i in far_in:
        specs[i] = anywhere
    for i in far_out:
        out_specs[i] = anywhere
    moving = [pltpu.VMEM(args[i].dims, args[i].value.dtype) for i in far_in]
    moving += [pltpu.VMEM(outs[i].dims, outs[i].value.dtype) for i in far_out]
    moving += [pltpu.SemaphoreType.DMA] * (len(far_in) + len(far_out))
    own_scratch = len(scratch)

    def run(*refs):
        ins = list(refs[:count])
        results = refs[count + extra + kept :]
        products = list(results[:made])
        rest = results[made + kept :]
        slots, sems = rest[own_scratch : own_scratch + len(far_in) + len(far_out)], rest[own_scratch + len(far_in) + len(far_out) :]
        for i, slot, sem in zip(far_in, slots, sems):
            source = refs[i]
            if args[i].block is not None:
                source = source.at[args[i].block(refs[0])]
            copy = pltpu.make_async_copy(source, slot, sem)
            copy.start()
            ins[i] = Fetched(slot, copy)
        stored = [
            Stored(slot, pltpu.make_async_copy(slot, results[i], sem))
            for i, slot, sem in zip(far_out, slots[len(far_in) :], sems[len(far_in) :])
        ]
        for i, product in zip(far_out, stored):
            products[i] = product
        kernel(*ins, *products, *rest[:own_scratch])
        for i in far_in:
            ins[i].ready()
        for product in stored:
            product.send()
        for product in stored:
            product.copy.wait()

    def result(value):
        dims = plain(value)
        if INTERPRET or value is dims:
            return dims
        return (pltpu.HBM if isinstance(value, Pin) else pltpu.VMEM)(dims.shape, dims.dtype)

    where = dict(
        in_specs=specs + [anywhere] * (extra + kept),
        out_specs=tuple(out_specs + [anywhere] * kept),
        scratch_shapes=list(scratch) + moving,
    )
    if prefetch:
        where["in_specs"] = where["in_specs"][prefetch:]
        where = {"grid_spec": pltpu.PrefetchScalarGridSpec(num_scalar_prefetch=prefetch, grid=grid, **where)}
    elif grid is not None:
        where["grid"] = grid
    return pl.pallas_call(
        run,
        out_shape=tuple(result(t) for t in outs) + tuple(result(Pin(shape(t.shape, t.dtype))) for t in carry),
        input_output_aliases={count + extra + i: made + i for i in range(kept)},
        compiler_params=params(mb),
        cost_estimate=pl.CostEstimate(flops=int(cost * 1e9), bytes_accessed=0, transcendentals=0),
        interpret=INTERPRET,
        **where,
    )(*[pinned(t.value) if isinstance(t, Pin) else t for t in list(args) + list(after)], *[pinned(t) for t in carry])


def bring(items, ids, after=(), carry=(), cost=0.3):
    def kernel(ids, *refs):
        sources, slots, sems = refs[: len(items)], refs[len(items) : 2 * len(items)], refs[2 * len(items) :]
        copies = []
        for (_, _, block), source, slot, sem in zip(items, sources, slots, sems):
            copies.append(pltpu.make_async_copy(source if block is None else source.at[block(ids)], slot, sem))
        for copy in copies:
            copy.start()
        for copy in copies:
            copy.wait()

    return call(
        kernel,
        [Near(shape(dims, array.dtype)) for array, dims, _ in items],
        [ids] + [Pin(array) for array, _, _ in items],
        [scalars()] + [pl.BlockSpec(memory_space=pl.ANY)] * len(items),
        scratch=[pltpu.SemaphoreType.DMA] * len(items), after=after, carry=carry, mb=2, cost=cost,
    )


def fixed(dims):
    return pl.BlockSpec(dims, lambda i: (0,) * len(dims))


def split_low(value):
    high = value.astype(bf16)
    return high, (value - high.astype(f32)).astype(bf16)


def lanes_of(columns, rows):
    lane = lax.broadcasted_iota(jnp.int32, (rows, 128), 1)
    out = jnp.zeros((rows, 128), f32)
    for i, column in enumerate(columns):
        out = jnp.where(lane == i, column.astype(f32), out)
    return out


def pair_sum(block, i):
    return block[:, i : i + 1].astype(f32) + block[:, i + 1 : i + 2].astype(f32)


def own_order(me, part, index):
    return ((index // part) ^ me) * part + index % part


def block_at(me, k, part):
    return pl.ds(pl.multiple_of((me ^ k) * part, part), part)


def swap_pairs(value, axis):
    size = value.shape[axis]
    place = lax.broadcasted_iota(jnp.int32, value.shape, axis)
    return jnp.where(
        place % 2 == 0, pltpu.roll(value, size - 1, axis), pltpu.roll(value, 1, axis)
    )


def tables(local_len, cp_count):
    column = np.arange(HD) // 2
    frequency = 10000.0 ** (-column / (HD // 2))
    zeta = (2.0 * column + 0.4 * HD) / (1.4 * HD)

    def of(places):
        angle = places[:, None] * frequency
        factor = zeta ** (places[:, None] / scale_base)
        return np.stack([np.cos(angle), np.sin(angle), factor, 1.0 / factor]).astype(np.float32)

    return of(np.arange(local_len)), of(np.arange(cp_count) * local_len)


def project_kernel(parts, ids, x, gain, inner, base, seg, w0, w1, w2, gy, pair, gy_out, out):
    me, mine = ids[0], ids[1]
    rows, width = pair.shape[1:]
    part = rows // parts
    heads = out.shape[0]
    x.ready()
    for k in range(parts):
        normed, _ = norm_rows(x.ref[block_at(me, k, part), :].astype(f32))
        pair[0, k * part : (k + 1) * part, :] = (normed * gain[...]).astype(bf16)
    inner.ready()
    here = [base[kind, pl.ds(mine, 1), :] for kind in range(4)]
    table = [
        jnp.concatenate([inner.ref[kind, block_at(me, k, part), :] for k in range(parts)], axis=0)
        for kind in range(4)
    ]
    cosine = table[0] * here[0] - table[1] * here[1]
    sine = table[1] * here[0] + table[0] * here[1]
    lane = lax.broadcasted_iota(jnp.int32, cosine.shape, 1)
    sine = jnp.where(lane % 2 == 0, -sine, sine)
    place = lax.broadcasted_iota(jnp.int32, (rows, rows), 1)
    source = lax.broadcasted_iota(jnp.int32, (rows, rows), 0)
    moved = (own_order(me, part, place) == source).astype(bf16)
    ids_row = jnp.broadcast_to(seg[...].astype(f32), (16, rows)).astype(bf16)
    ordered = dot(ids_row, moved).astype(bf16)
    for j in range(heads):
        out[j, 3 * HD : 3 * HD + 16, :] = ordered
    for c, weight in enumerate((w0, w1, w2)):
        acc = dot(pair[0], weight[0])
        factor = (table[2] * here[2], table[3] * here[3], None)[c]
        for i in range(acc.shape[1] // 128):
            piece = acc[:, i * 128 : (i + 1) * 128]
            if c < 2:
                piece = piece * (cosine * factor) + swap_pairs(piece, 1) * (sine * factor)
            turned = piece.T.astype(bf16)
            for h in range(128 // HD):
                out[i * (128 // HD) + h, c * HD : (c + 1) * HD, :] = turned[h * HD : (h + 1) * HD]
    out.send()
    gy.ready()
    for k in range(parts):
        block = gy.ref[block_at(me, k, part), :]
        pair[1, k * part : (k + 1) * part, :] = block
        gy_out[k * part : (k + 1) * part, :] = block


def gather_heads(got, keys, ids_col, values=None):
    for j in range(got.shape[0]):
        rows = slice(j * got.shape[2], (j + 1) * got.shape[2])
        both = jnp.concatenate([got[j, HD : 3 * HD, :].astype(f32)], axis=0).T
        keys[rows, :] = both[:, :HD].astype(bf16)
        if values is not None:
            values[rows, :] = both[:, HD:].astype(bf16)
        ids_col[rows, :] = got[j, 3 * HD : 3 * HD + 16, :].astype(f32).T


def visible_scores(me, part, scores, ids_col, ids_row, count, first, group):
    same = ids_col[0:count, 0:1] == ids_row
    length = group
    key = lax.broadcasted_iota(jnp.int32, (length, length), 0)
    query = lax.broadcasted_iota(jnp.int32, (length, length), 1)
    rows = first
    own = lambda index: (index // rows) * rows + own_order(me, part, index % rows)
    earlier = own(key) <= own(query)
    if count > length:
        earlier = jnp.concatenate([jnp.ones((count - length, length), jnp.bool_), earlier], axis=0)
    return same & earlier


def attend_kernel(parts, ids, got, out, mixed, lse, kept, keys, ids_col):
    me = ids[0]
    kept[...] = got[...]
    kept.send()
    blocks, _, rows = got.shape
    part = rows // parts
    gather_heads(got, keys, ids_col)
    group = 2 if blocks % 2 == 0 else 1
    width = group * rows
    for i in range(blocks // group):
        mine = range(i * group, (i + 1) * group)
        query = jnp.concatenate([got[j, :HD, :] for j in mine], axis=1) * bf16(HD**-0.5)
        ids_row = jnp.concatenate([got[j, 3 * HD : 3 * HD + 1, :] for j in mine], axis=1).astype(f32)
        count = (i + 1) * width
        scores = dot(keys[0:count, :], query)
        allowed = visible_scores(me, part, scores, ids_col, ids_row, count, rows, width)
        scores = jnp.where(allowed, scores, masked_score)
        top = jnp.max(scores, axis=0, keepdims=True)
        exponent = jnp.exp(scores - top)
        total = jnp.sum(exponent, axis=0, keepdims=True)
        value = jnp.concatenate([got[j, 2 * HD : 3 * HD, :] for j in range((i + 1) * group)], axis=1)
        result = dot(value, exponent.astype(bf16)) / total
        mixed[:, i * width : (i + 1) * width] = result
        lse[:, i * width : (i + 1) * width] = top + jnp.log(total)
        for n, j in enumerate(mine):
            out[j] = result[:, n * rows : (n + 1) * rows].astype(bf16)
    out.send()


def store_pieces(total, own, pieces, part, extra=None):
    own[:, : total.shape[1]] = total[:part]
    for k, piece in enumerate(pieces, 1):
        piece[:, : total.shape[1]] = total[k * part : (k + 1) * part].astype(bf16)
    if extra is not None:
        own[:, total.shape[1] :] = extra[:part]
        for k, piece in enumerate(pieces, 1):
            piece[:, total.shape[1] :] = extra[k * part : (k + 1) * part].astype(bf16)


def fold_row(row, part):
    block = jnp.concatenate([row[:, i : i + 128] for i in range(0, row.shape[1], 128)], axis=0)
    return jnp.concatenate(split_low(block), axis=0)


def unfold_row(block):
    half = block.shape[0] // 2
    total = block[:half].astype(f32) + block[half:].astype(f32)
    return jnp.concatenate([total[i : i + 1] for i in range(half)], axis=1)


def out_kernel(parts, att, gain, weight, own, *refs):
    pieces, kept = refs[:-1], refs[-1]
    kept[...] = att[...]
    blocks, _, rows = att.shape
    part, width = rows // parts, weight.shape[1]
    value = jnp.concatenate([att[j].astype(f32) for j in range(blocks)], axis=0).T
    high, low = split_low(jnp.mean(value, axis=1, keepdims=True))
    centred = value - (high.astype(f32) + low.astype(f32))
    square = split_low(jnp.sum(centred * centred, axis=1, keepdims=True))
    gains = gain[...]
    row = lax.broadcasted_iota(jnp.int32, (16, gains.shape[1]), 0)
    gain_high, gain_low = (t.astype(f32) for t in split_low(gains))
    gain_rows = jnp.where(row == 0, gain_high, jnp.where(row == 1, gain_low, 0.0))
    left = jnp.concatenate([(centred * gains).astype(bf16), gain_rows.astype(bf16)], axis=0)
    total = dot(left, weight[...])
    folded = fold_row(total[rows : rows + 1] + total[rows + 1 : rows + 2], part)
    stats = lanes_of([high, low, *square], rows).astype(bf16)
    own[:, :width] = total[:part]
    own[:, width : width + 128] = stats[:part].astype(f32)
    own[:, width + 128 :] = folded.astype(f32)
    for k, piece in enumerate(pieces, 1):
        here = slice(k * part, (k + 1) * part)
        piece[:, :width] = total[here].astype(bf16)
        piece[:, width : width + 128] = stats[here]
        piece[:, width + 128 :] = folded


def middle_kernel(parts, head_width, own, *refs):
    got, (x, gain, x1, u, gain_row) = refs[: parts - 1], refs[parts - 1 :]
    part, width = x1.shape
    blocks = [own] + list(got)
    stats = [b[:, width : width + 128] for b in blocks]
    means = [pair_sum(b, 0) for b in stats]
    squares = [pair_sum(b, 2) for b in stats]
    rows = [unfold_row(b[:, width + 128 :]) for b in blocks]
    gain_row[...] = sum(rows)
    mean = sum(means) / parts
    spread = sum(squares) + head_width * sum((m - mean) * (m - mean) for m in means)
    scaling = lax.rsqrt(spread / width + eps)
    total = sum(b[:, :width].astype(f32) for b in blocks)
    for m, row in zip(means, rows):
        total = total + (m - mean) * row
    value = x[...].astype(f32) + total * scaling
    x1[...] = value
    normed, _ = norm_rows(value)
    u[:, :width] = (normed * gain[...]).astype(bf16)
    u[:, width:] = lanes_of([*split_low(mean), *split_low(scaling)], part).astype(bf16)


def grad_hidden_kernel(gy, weight, grad):
    grad[...] = dot_t(gy[...], weight[...])


def prepare_kernel(step, up, down, near_up, flipped, near_down, up_sems, down_sem):
    chunks = [slice(i, i + step) for i in range(0, up.shape[0], step)]
    copies = [pltpu.make_async_copy(up.at[c, :], near_up.at[c, :], up_sems.at[i]) for i, c in enumerate(chunks)]
    last = pltpu.make_async_copy(down, near_down, down_sem)
    for copy in copies + [last]:
        copy.start()
    for copy, chunk in zip(copies, chunks):
        copy.wait()
        flipped[:, chunk] = near_up[chunk, :].T
    last.wait()


def up_kernel(parts, step, own, *refs):
    got, refs = refs[: parts - 1], refs[parts - 1 :]
    weight, grad, gain, act, slope, u, stats, tail, rows_u = refs
    part = own.shape[0]
    rows, width = rows_u.shape
    for k, block in enumerate([own] + list(got)):
        rows_u[k * part : (k + 1) * part, :] = block[:, :width]
        tail[k * part : (k + 1) * part, :] = block[:, width:].astype(f32)
    wide = u.shape[2]
    for j in range(u.shape[0]):
        u[j] = rows_u[:, j * wide : (j + 1) * wide]
    total = [jnp.zeros((rows, 128), f32)] * 4
    for i in range(0, weight.shape[1], step):
        here = slice(i, i + step)
        hidden = dot(rows_u[...], weight[:, here])
        cdf = 0.5 * (1.0 + lax.erf(hidden * (0.5**0.5)))
        value = hidden * cdf
        act[:, here] = value
        slope[:, here] = cdf + hidden * jnp.exp(-0.5 * hidden * hidden) * 0.3989422804014327
        grad_normed = grad[:, here] * gain[:, here]
        columns = [value, value * value, grad_normed, grad_normed * value]
        for n, column in enumerate(columns):
            for j in range(0, step, 128):
                total[n] = total[n] + column[:, j : j + 128]
    sums = lanes_of([jnp.sum(t, axis=1, keepdims=True) for t in total], rows)
    stats[...] = sums.T[:8, :]


def swap_lane_blocks(value, k, part):
    lanes = value.shape[1]
    lane = lax.broadcasted_iota(jnp.int32, value.shape, 1)
    distance = 1
    while distance <= k:
        if k & distance:
            move = distance * part
            value = jnp.where(
                (lane // move) % 2 == 0,
                pltpu.roll(value, lanes - move, 1),
                pltpu.roll(value, move, 1),
            )
        distance *= 2
    return value


def hidden_back_kernel(parts, full, step, own, *refs):
    got, refs = refs[: parts - 1], refs[parts - 1 :]
    act, slope, grad, gain, weight, gh, z2, own_out = refs[:8]
    pieces = refs[8:]
    rows = act.shape[0]
    part = rows // parts
    total = own[...]
    for k, block in enumerate(got, 1):
        total = total + swap_lane_blocks(block[...], k, part)
    mean = total[0:1] / full
    scaling = lax.rsqrt(total[1:2] / full - mean * mean + eps)
    first = total[2:3] / full
    cross = scaling * (total[3:4] / full - mean * first)
    row = lax.broadcasted_iota(jnp.int32, (rows, rows), 0)
    table = jnp.zeros((rows, rows), f32)
    for i, value in enumerate([mean, scaling, first, cross]):
        table = jnp.where(row == i, value, table)
    cols = table.T
    mean, scaling, first, cross = (cols[:, i : i + 1] for i in range(4))
    wide = z2.shape[2]
    for i in range(0, act.shape[1], step):
        here = slice(i, i + step)
        normed = (act[:, here] - mean) * scaling
        low = (normed * gain[:, here]).astype(bf16)
        for j in range(0, step, wide):
            z2[(i + j) // wide] = low[:, j : j + wide]
        value = scaling * (grad[:, here] * gain[:, here] - first - normed * cross) * slope[:, here]
        gh[:, here] = value.astype(bf16)
    width = weight.shape[1]
    for i in range(0, width, step):
        here = slice(i, i + step)
        result = dot(gh[...], weight[:, here])
        own_out[:, here] = result[:part]
        for k, piece in enumerate(pieces, 1):
            piece[:, here] = result[k * part : (k + 1) * part].astype(bf16)


def down_kernel(parts, step, z2, gh, u, weight, own_out, *refs):
    pieces, (both_out, gh_out) = refs[: parts - 1], refs[parts - 1 :]
    both_out[:, :, : u.shape[2]] = u[...]
    both_out[:, :, u.shape[2] :] = z2[...]
    both_out.send()
    gh_out[...] = gh[...]
    gh_out.send()
    wide = z2.shape[2]
    part = own_out.shape[0]
    for i in range(0, weight.shape[1], step):
        here = slice(i, i + step)
        result = sum(
            dot(z2[j], weight[j * wide : (j + 1) * wide, here]) for j in range(z2.shape[0])
        )
        own_out[:, here] = result[:part]
        for k, piece in enumerate(pieces, 1):
            piece[:, here] = result[k * part : (k + 1) * part].astype(bf16)


def middle_back_kernel(parts, own, *refs):
    got, refs = refs[: parts - 1], refs[parts - 1 :]
    gain_row, x, x1, gy, gain, gx1, gb = refs
    part, width = x1.shape
    grad = own[...]
    for block in got:
        grad = grad + block[...].astype(f32)
    value = x1[...]
    normed, scaling = norm_rows(value)
    result = gy[...].astype(f32) + norm_back(grad, gain[...], normed, scaling)
    gx1[...] = result
    low = result.astype(bf16)
    gb[:, :width] = low
    low = low.astype(f32)
    first = jnp.sum(low * gain_row[...], axis=1, keepdims=True) / width
    cross = jnp.sum(low * (value - x[...].astype(f32)), axis=1, keepdims=True) / width
    gb[:, width:] = lanes_of([*split_low(first), *split_low(cross)], part).astype(bf16)


def heads_back_kernel(parts, own, *refs):
    got, refs = refs[: parts - 1], refs[parts - 1 :]
    stats, att, gain, weight, sent, gb = refs
    blocks, _, rows = att.shape
    part, width = own.shape[0], gb.shape[1]
    for k, block in enumerate([own] + list(got)):
        gb[k * part : (k + 1) * part, :] = block[:, :width]
    gb.send()
    columns = jnp.concatenate([b[:, width:].astype(f32) for b in [own] + list(got)], axis=0).T
    first = columns[0:1] + columns[1:2]
    cross = columns[2:3] + columns[3:4]
    columns = stats[...].T
    mean = columns[0:1] + columns[1:2]
    scaling = columns[2:3] + columns[3:4]
    grad = dot_t(weight[...], gb[...])
    value = jnp.concatenate([att[j].astype(f32) for j in range(blocks)], axis=0)
    normed = (value - mean) * scaling
    gain_col = jnp.broadcast_to(gain[...], (8, gain.shape[1])).T[:, 0:1]
    go = (scaling * (grad * gain_col - first - normed * cross)).astype(bf16)
    z = (normed * gain_col).astype(bf16)
    for j in range(blocks):
        sent[j, :HD, :] = go[j * HD : (j + 1) * HD]
        sent[j, HD:, :] = z[j * HD : (j + 1) * HD]


def turn_back(grad, table, base, j, inverse):
    here = [base[kind, :, j : j + 1] for kind in range(4)]
    cosine = table[0] * here[0] - table[1] * here[1]
    sine = table[1] * here[0] + table[0] * here[1]
    factor = table[3] * here[3] if inverse else table[2] * here[2]
    row = lax.broadcasted_iota(jnp.int32, grad.shape, 0)
    sine = jnp.where(row % 2 == 0, sine, -sine)
    return (grad * cosine + swap_pairs(grad, 0) * sine) * factor


def attend_back_kernel(parts, ids, got, grads, mixed, lse, inner, base, out, z, keys, values, ids_col, gk, gv):
    me = ids[0]
    for j in range(grads.shape[0]):
        z[j] = grads[j, HD:, :]
    z.send()
    blocks, _, rows = got.shape
    part = rows // parts
    gather_heads(got, keys, ids_col, values)
    gk[...] = jnp.zeros_like(gk)
    gv[...] = jnp.zeros_like(gv)
    table = []
    for kind in range(4):
        ordered = jnp.concatenate(
            [inner[kind, block_at(me, k, part), :] for k in range(parts)], axis=0
        )
        table.append(ordered.T[:HD])
    group = 2 if blocks % 2 == 0 else 1
    width = group * rows
    for i in range(blocks // group):
        mine = range(i * group, (i + 1) * group)
        query = jnp.concatenate([got[j, :HD, :] for j in mine], axis=1) * bf16(HD**-0.5)
        ids_row = jnp.concatenate([got[j, 3 * HD : 3 * HD + 1, :] for j in mine], axis=1).astype(f32)
        go = jnp.concatenate([grads[j, :HD, :] for j in mine], axis=1)
        span = slice(i * width, (i + 1) * width)
        delta = jnp.sum(go.astype(f32) * mixed[:, span], axis=0, keepdims=True)
        count = (i + 1) * width
        scores = dot(keys[0:count, :], query)
        allowed = visible_scores(me, part, scores, ids_col, ids_row, count, rows, width)
        probability = jnp.where(allowed, jnp.exp(jnp.minimum(scores - lse[:, span], 0.5)), 0.0)
        grad_prob = dot(values[0:count, :], go)
        grad_scores = (probability * (grad_prob - delta)).astype(bf16)
        gv[:, 0:count] += dot_t(go, probability.astype(bf16))
        gk[:, 0:count] += dot_t(query, grad_scores)
        key = jnp.concatenate([got[j, HD : 2 * HD, :] for j in range((i + 1) * group)], axis=1)
        gq = dot(key, grad_scores) * HD**-0.5
        for n, j in enumerate(mine):
            piece = turn_back(gq[:, n * rows : (n + 1) * rows], table, base, j, False)
            out[j, :HD, :] = piece.astype(bf16)
    for j in range(blocks):
        span = slice(j * rows, (j + 1) * rows)
        out[j, HD : 2 * HD, :] = turn_back(gk[:, span], table, base, j, True).astype(bf16)
        out[j, 2 * HD :, :] = gv[:, span].astype(bf16)


def input_back_kernel(parts, step, got, w0, w1, w2, own_out, *pieces):
    part, width = own_out.shape
    grads = []
    for c in range(3):
        here = slice(c * HD, (c + 1) * HD)
        grad = jnp.concatenate([got[j, here, :].astype(f32) for j in range(got.shape[0])], axis=0)
        grads.append(grad.T.astype(bf16))
    result = dot_t(grads[0], w0[0]) + dot_t(grads[1], w1[0]) + dot_t(grads[2], w2[0])
    own_out[...] = result[:part]
    for k, piece in enumerate(pieces, 1):
        piece[...] = result[k * part : (k + 1) * part].astype(bf16)


def final_kernel(parts, own, *refs):
    got, refs = refs[: parts - 1], refs[parts - 1 :]
    x, gx1, gain, y_own = refs[:4]
    y_got, (x1, out) = refs[4 : parts + 3], refs[parts + 3 :]
    width = x.shape[1]
    grad = own[...]
    for block in got:
        grad = grad + block[...].astype(f32)
    normed, scaling = norm_rows(x[...].astype(f32))
    out[:, :width] = (gx1[...] + norm_back(grad, gain[...], normed, scaling)).astype(bf16)
    total = y_own[...] + x1[...]
    for block in y_got:
        total = total + block[...].astype(f32)
    out[:, width:] = total.astype(bf16)


def output_kernel(own, *refs):
    got, (x1, out) = refs[:-2], refs[-2:]
    total = own[...] + x1[...]
    for block in got:
        total = total + block[...].astype(f32)
    out[...] = total.astype(bf16)


def natural_kernel(ids, *refs):
    blocks, out = refs[:-1], refs[-1]
    part = blocks[0].shape[0]
    for k, block in enumerate(blocks):
        out[block_at(ids[0], k, part), :] = block[...]


def own_row(table, index):
    row = lax.broadcasted_iota(jnp.int32, table.shape, 0)
    return jnp.sum(jnp.where(row == index, table[...], 0.0), axis=0, keepdims=True)


def row_of(column, columns):
    return jnp.broadcast_to(column, (columns, 128)).T[:1, :]


def product_kernel(step, columns, which, offset, ids, left, right, *refs):
    count = left.shape[0]
    gains = len(refs) > 7
    if gains:
        (weight, gain, out, gain_grad), refs = refs[:4], refs[4:]
        (near_weight, weight_sem), refs = refs[-2:], refs[:-2]
    else:
        out, refs = refs[0], refs[1:]
    left_all, right_all, result, left_sems, right_sems, out_sems = refs
    rows, size = right.shape[-2:]
    own = result.shape[0]
    tokens = count * rows
    chunks = [slice(i, i + step) for i in range(0, size, step)]

    first = []
    for r in range(count):
        source = left.at[r]
        if columns:
            source, place = source.at[:, pl.ds(offset, own)], left_all.at[pl.ds(r * rows, rows), :]
        else:
            source, place = source.at[pl.ds(offset, own), :], left_all.at[r]
        first.append(pltpu.make_async_copy(source, place, left_sems.at[r]))
    side = right if which is None else right.at[:, which]
    later = [
        [pltpu.make_async_copy(side.at[:, :, c], right_all.at[:, :, c], right_sems.at[i])] for i, c in enumerate(chunks)
    ]
    for copy in first + later[0]:
        copy.start()
    if gains:
        fetch = pltpu.make_async_copy(
            weight.at[pl.ds(pl.multiple_of(ids[1] * own, own), own), :], near_weight, weight_sem
        )
        fetch.start()
    for copies in later[1:]:
        for copy in copies:
            copy.start()
    for copy in first:
        copy.wait()
    if not columns:
        value = jnp.concatenate([left_all[r] for r in range(count)], axis=1)
    sums = jnp.zeros((own, 128), f32)
    sent = []
    for i, (c, copies) in enumerate(zip(chunks, later)):
        for copy in copies:
            copy.wait()
        block = right_all[:, :, c].reshape(tokens, step)
        grad = t_dot(left_all[...], block) if columns else dot(value, block)
        result[:, c] = grad.astype(result.dtype)
        if gains:
            if i == 0:
                fetch.wait()
            product = grad * near_weight[:, c].astype(f32)
            for j in range(0, step, 128):
                sums = sums + product[:, j : j + 128]
            moves = [pltpu.make_async_copy(result.at[:, c], out.at[:, c], out_sems.at[i, 0])]
        else:
            wide = out.shape[2]
            moves = [
                pltpu.make_async_copy(
                    result.at[:, pl.ds(j, wide)], out.at[j // wide], out_sems.at[i, (j - c.start) // wide]
                )
                for j in range(c.start, c.stop, wide)
            ]
        for move in moves:
            move.start()
        sent.extend(moves)
    if gains:
        gain_grad[...] = row_of(jnp.sum(sums, axis=1, keepdims=True), own) / own_row(gain, ids[1])
    for copy in sent:
        copy.wait()


def grad_qkv_place_kernel(ids, got, weight, gain, up_gain, out, gain_grads):
    total = 0.0
    for c in range(3):
        value = jnp.concatenate(
            [got[j, c * HD : (c + 1) * HD, :].astype(f32) for j in range(got.shape[0])], axis=0
        ).T
        out[c] = value
        total = total + jnp.sum(value * weight[c].astype(f32), axis=1, keepdims=True)
    out.send()
    first = row_of(total, total.shape[0]) / own_row(gain, ids[1])
    row = lax.broadcasted_iota(jnp.int32, gain_grads.shape, 0)
    gain_grads[...] = jnp.where(row == 0, first, up_gain[...])


def outputs_kernel(parts, ids, *refs):
    blocks, gains, (out, y, first, second) = refs[:parts], refs[parts : 2 * parts], refs[2 * parts :]
    part, width = blocks[0].shape[0], out.shape[1]
    for k, block in enumerate(blocks):
        out[block_at(ids[0], k, part), :] = block[:, :width]
        y[block_at(ids[0], k, part), :] = block[:, width:]
    total = sum(b[...] for b in gains)
    first[...] = total[0:1]
    second[...] = total[1:2]


def body(
    layer_input,
    segment_ids,
    qkv_weight,
    out_weight,
    up_weight,
    down_weight,
    input_gain,
    heads_gain,
    middle_gain,
    hidden_gain,
    cotangent,
):
    rows, row_count, width = layer_input.shape
    T, C = lax.axis_size("tp"), lax.axis_size("cp")
    part = rows // T
    head_width = qkv_weight.shape[2]
    if head_width // HD != C or row_count != 1 or rows != 128 or 64 * part != width:
        return body_general(
            layer_input, segment_ids, qkv_weight, out_weight, up_weight, down_weight,
            input_gain, heads_gain, middle_gain, hidden_gain, cotangent,
        )
    tokens = rows * C
    hidden = up_weight.shape[1]
    wide = width // C
    high = hidden // C
    ids = jnp.stack([lax.axis_index("tp"), lax.axis_index("cp")]).astype(jnp.int32)
    x = layer_input.reshape(rows, width)
    gy = cotangent.reshape(rows, width)
    weight3 = jnp.transpose(qkv_weight, (1, 0, 2))
    gain_in, gain_mid = input_gain.reshape(1, -1), middle_gain.reshape(1, -1)
    gain_heads, gain_hid = heads_gain.reshape(1, -1), hidden_gain.reshape(1, -1)
    inner, base = tables(rows, C)
    inner2 = jnp.asarray(np.concatenate([inner, inner], axis=2))
    base2 = jnp.asarray(np.concatenate([base, base], axis=2))
    base_t = np.zeros((4, HD, 128), np.float32)
    base_t[:, :, :C] = np.transpose(base, (0, 2, 1))
    base_t = jnp.asarray(base_t)
    wide_part = width + 128
    step = 512

    def piece_shapes(columns):
        return [shape((part, columns), f32)] + [shape((part, columns), bf16)] * (T - 1)

    def exchange(pieces):
        return [swap_tp(piece, k) for k, piece in enumerate(pieces, 1)]

    def spread(block):
        return [swap_tp(block, k) for k in range(1, T)]

    def to_cp(value):
        return lax.all_to_all(value, "cp", 0, 0, tiled=True)

    def entire(value):
        return (value, value.shape, None)

    def own_rows(value):
        return (value, (part, width), lambda ids: (block_at(ids[0], 0, part), slice(None)))

    def third(c):
        return lambda ids: (pl.ds(c, 1), slice(None), slice(None))

    cols, first_rows = lambda i, *_: (0, i), lambda i, *_: (i, 0)
    origin2, origin3 = lambda i, *_: (0, 0), lambda i, *_: (0, 0, 0)
    weight_thirds = [Far(weight3, (1, width, head_width), third(c)) for c in range(3)]

    pair, gy_x, sent = call(
        functools.partial(project_kernel, T),
        [Far(shape((2, rows, width), bf16)), Far(shape((rows, width), bf16)), Far(shape((C, 3 * HD + 16, rows), bf16))],
        [ids, Far(x), Far(gain_in), Far(inner2), Far(base2), Far(segment_ids.reshape(1, rows)), *weight_thirds, Far(gy)],
        [scalars()] + [whole()] * 9, mb=14,
    )
    got = to_cp(sent)
    near_out, near_x, near_gy, near_mid, near_heads, near_hid, near_in = bring(
        [entire(out_weight), own_rows(x), own_rows(gy), entire(gain_mid), entire(gain_heads),
         entire(gain_hid), entire(gain_in)],
        ids, after=[Pin(sent)],
    )
    back, mixed, lse, far_got, pair = call(
        functools.partial(attend_kernel, T),
        [Far(shape((C, HD, rows), bf16)), Far(shape((HD, tokens), f32)), Far(shape((1, tokens), f32)),
         Far(shape((C, 3 * HD + 16, rows), bf16))],
        [ids, got], [scalars(), whole()],
        scratch=[pltpu.VMEM((tokens, HD), bf16), pltpu.VMEM((tokens, 16), f32)],
        mb=10, after=[near_heads], carry=[pair],
    )
    att = to_cp(back)
    early = lax.all_gather(pair, "cp", axis=0)

    own, *pieces, near_att = call(
        functools.partial(out_kernel, T),
        piece_shapes(width + 256) + [Near(shape((C, HD, rows), bf16))],
        [att, near_heads, near_out],
    )
    (grad_hid,) = call(
        grad_hidden_kernel, [Near(shape((rows, hidden), f32))],
        [Pin(gy_x), Pin(down_weight)],
        [fixed((rows, width)), pl.BlockSpec((step, width), first_rows)],
        [pl.BlockSpec((rows, step), cols)],
        grid=(hidden // step,), after=[own], mb=10, cost=3,
    )
    x1, u_own, gain_row = call(
        functools.partial(middle_kernel, T, head_width),
        [Near(shape((part, width), f32)), shape((part, wide_part), bf16), Near(shape((1, width), f32))],
        [own, *exchange(pieces), near_x, near_mid], after=[grad_hid],
    )
    u_blocks = [u_own] + spread(u_own)
    near_up, near_flip, near_down = call(
        functools.partial(prepare_kernel, 256),
        [Near(shape((width, hidden), bf16)), Near(shape((hidden, width), bf16)), Near(shape((hidden, width), bf16))],
        [Pin(up_weight), Pin(down_weight)], [pl.BlockSpec(memory_space=pl.ANY)] * 2,
        scratch=[pltpu.SemaphoreType.DMA((width // 256,)), pltpu.SemaphoreType.DMA], after=[u_own], mb=6,
    )

    act, slope, u_cols, stats, near_tail = call(
        functools.partial(up_kernel, T, step),
        [Near(shape((rows, hidden), f32)), Near(shape((rows, hidden), f32)), Near(shape((C, rows, wide), bf16)),
         shape((8, rows), f32), Near(shape((rows, 128), f32))],
        [*u_blocks, near_up, grad_hid, near_hid],
        scratch=[pltpu.VMEM((rows, width), bf16)], mb=8, after=[near_flip],
    )
    gh, z2, own, *pieces = call(
        functools.partial(hidden_back_kernel, T, FF, step),
        [Near(shape((rows, hidden), bf16)), Near(shape((C, rows, high), bf16))] + piece_shapes(width),
        [stats, *spread(stats), act, slope, grad_hid, near_hid, near_flip], mb=8,
    )
    gu_got = exchange(pieces)
    y_own, *y_pieces, both_sent, gh_out = call(
        functools.partial(down_kernel, T, step),
        [Far(t) for t in piece_shapes(width)]
        + [Far(shape((C, rows, wide + high), bf16)), Far(shape((rows, hidden), bf16))],
        [z2, gh, u_cols, near_down], after=[own], cost=20,
    )
    both_got = to_cp(both_sent)
    gh_all = lax.all_gather(gh_out, "cp", axis=0)
    gx1, gb_own = call(
        functools.partial(middle_back_kernel, T),
        [Near(shape((part, width), f32)), shape((part, wide_part), bf16)],
        [own, *gu_got, gain_row, near_x, x1, near_gy, near_mid], after=[Pin(gh_out)], cost=8,
    )
    gb_blocks = [gb_own] + spread(gb_own)
    (near_out,) = bring([entire(out_weight)], ids, after=[gb_own])

    def product(left, right, columns, which, offset, own, after, weight=None, gain=None, cost=20):
        anywhere = pl.BlockSpec(memory_space=pl.ANY)
        size = right.shape[-1]
        chunk = 2 * step
        left_dims = (tokens, own) if columns else (C, own, rows)
        if weight is not None:
            outs = [Pin(shape((own, size), f32)), shape((1, own), f32)]
            more, more_specs = [Pin(weight), gain.reshape(C, -1)], [anywhere, whole()]
            out_specs, extra = [anywhere, whole()], [pltpu.VMEM((own, size), bf16), pltpu.SemaphoreType.DMA]
        else:
            outs, out_specs = [Pin(shape((C, own, size // C), bf16))], [anywhere]
            more, more_specs, extra = [], [], []
        return call(
            functools.partial(product_kernel, chunk, columns, which, offset), outs,
            [ids, Pin(left), Pin(right), *more], [scalars()] + [anywhere] * 2 + more_specs, out_specs,
            scratch=[pltpu.VMEM(left_dims, bf16), pltpu.VMEM((C, rows, size), bf16),
                     pltpu.VMEM((own, size), plain(outs[0]).dtype),
                     pltpu.SemaphoreType.DMA((C,)), pltpu.SemaphoreType.DMA((size // chunk,)),
                     pltpu.SemaphoreType.DMA((size // chunk, chunk * C // size))] + extra,
            mb=14, after=after, cost=cost,
        )

    sent, gb, *kept = call(
        functools.partial(heads_back_kernel, T),
        [Far(shape((C, 2 * HD, rows), bf16)), Far(shape((rows, width), bf16))],
        [*gb_blocks, near_tail, near_att, near_heads, near_out], after=[Pin(both_got)], carry=y_pieces,
    )
    y_pieces = kept
    gb_all = lax.all_gather(gb, "cp", axis=0)
    y_got = exchange(y_pieces)
    grads = to_cp(sent)
    near_got, near_mixed, near_lse, near_inner, near_base = bring(
        [entire(far_got), entire(mixed), entire(lse), entire(inner2), entire(base_t)], ids, after=[Pin(sent)]
    )
    gq_sent, z = call(
        functools.partial(attend_back_kernel, T),
        [Far(shape((C, 3 * HD, rows), bf16)), Far(shape((C, HD, rows), bf16))],
        [ids, near_got, grads, near_mixed, near_lse, near_inner, near_base], [scalars()] + [whole()] * 6,
        scratch=[pltpu.VMEM((tokens, HD), bf16), pltpu.VMEM((tokens, HD), bf16), pltpu.VMEM((tokens, 16), f32),
                 pltpu.VMEM((HD, tokens), f32), pltpu.VMEM((HD, tokens), f32)],
        mb=12, cost=8,
    )
    gq = to_cp(gq_sent)
    (grad_qkv,) = product(gq_sent, early, False, 0, 0, 3 * HD, [Pin(gq_sent)])
    own, *pieces = call(
        functools.partial(input_back_kernel, T, step), piece_shapes(width), [gq, *weight_thirds], mb=10, carry=[grad_qkv],
    )
    pieces, grad_qkv = pieces[: T - 1], pieces[T - 1]
    ga_got = exchange(pieces)
    grad_qkv_got = to_cp(grad_qkv)
    grad_up, up_gain = product(both_got, gh_all, True, None, 0, wide, [own], up_weight, middle_gain)
    (final,) = call(
        functools.partial(final_kernel, T),
        [shape((part, 2 * width), bf16)],
        [own, *ga_got, near_x, gx1, near_in, Far(y_own), *y_got, x1], after=[Pin(grad_up)],
    )
    final_blocks = [final] + spread(final)
    own_wide = lambda ids: (slice(None), pl.ds(pl.multiple_of(ids[1] * wide, wide), wide), slice(None))
    grad_qkv, gains = call(
        grad_qkv_place_kernel,
        [Far(shape((3, wide, head_width), f32)), shape((8, wide), f32)],
        [ids, grad_qkv_got, Far(weight3, (3, wide, head_width), own_wide), input_gain.reshape(C, -1), up_gain],
        [scalars()] + [whole()] * 4, after=[final], cost=20,
    )
    gain_blocks = [gains] + spread(gains)
    grad_down, hidden_gain_grad = product(both_got, early, True, 1, wide, high, [gains], down_weight, hidden_gain)
    grad_out, heads_gain_grad = product(z, gb_all, False, None, 0, HD, [Pin(grad_down)], out_weight, heads_gain)
    grad_input, layer_output, input_gain_grad, middle_gain_grad = call(
        functools.partial(outputs_kernel, T),
        [Far(shape((rows, width), bf16))] * 2 + [shape((1, wide), f32), shape((1, wide), f32)],
        [ids, *final_blocks, *gain_blocks], [scalars()] + [whole()] * (2 * T), after=[Pin(grad_out)],
    )
    return (
        layer_output.reshape(layer_input.shape),
        grad_input.reshape(layer_input.shape),
        jnp.transpose(grad_qkv, (1, 0, 2)),
        grad_out,
        grad_up,
        grad_down,
        input_gain_grad.reshape(-1),
        heads_gain_grad.reshape(-1),
        middle_gain_grad.reshape(-1),
        hidden_gain_grad.reshape(-1),
    )


def solution(mesh):
    placed = (
        P("cp", None, None),
        P("cp", None),
        P(None, None, "tp"),
        P("tp", None),
        P(None, "tp"),
        P("tp", None),
        P(),
        P("tp"),
        P(),
        P("tp"),
        P("cp", None, None),
    )
    return jax.shard_map(
        body,
        mesh=mesh,
        in_specs=placed,
        out_specs=(
            P("cp", None, None),
            P("cp", None, None),
            P("cp", None, "tp"),
            P(("tp", "cp"), None),
            P("cp", "tp"),
            P(("tp", "cp"), None),
            P("cp"),
            P(("tp", "cp")),
            P("cp"),
            P(("tp", "cp")),
        ),
        check_vma=False,
    )
```

```python
import functools

import jax
import jax.numpy as jnp
import numpy as np
from jax import lax
from jax.experimental import pallas as pl
from jax.experimental.pallas import tpu as pltpu
from jax.sharding import PartitionSpec as P

HD = 64
D = 2048
FF = 8192

eps = 1e-05
scale_base = 512.0
masked_score = -1e30
f32 = jnp.float32
bf16 = jnp.bfloat16


def dot(a, b):
    return jnp.dot(a, b, preferred_element_type=f32)


def dot_t(a, b):
    return lax.dot_general(a, b, (((1,), (1,)), ((), ())), preferred_element_type=f32)


def t_dot(a, b):
    return lax.dot_general(a, b, (((0,), (0,)), ((), ())), preferred_element_type=f32)


def pairs(count, k):
    return [(i, i ^ k) for i in range(count)]


def swap_tp(value, k):
    return lax.ppermute(value, "tp", pairs(lax.axis_size("tp"), k))


def tp_order(value):
    count, me = lax.axis_size("tp"), lax.axis_index("tp")
    part = value.shape[0] // count
    return jnp.concatenate(
        [lax.dynamic_slice_in_dim(value, (me ^ k) * part, part, 0) for k in range(count)], axis=0
    )


def tp_scatter_sum(partial_sum):
    count = lax.axis_size("tp")
    part = partial_sum.shape[0] // count
    low = partial_sum.astype(bf16)
    total = partial_sum[:part]
    for k in range(1, count):
        total = total + swap_tp(low[k * part : (k + 1) * part], k).astype(f32)
    return total


def tp_gather(block):
    count = lax.axis_size("tp")
    return jnp.concatenate([block] + [swap_tp(block, k) for k in range(1, count)], axis=0)


def tp_sum(value):
    total = value
    for k in range(1, lax.axis_size("tp")):
        total = total + swap_tp(value, k)
    return total


def tp_token_sum(value):
    count = lax.axis_size("tp")
    blocks = value.reshape(value.shape[0], count, -1)
    total = blocks
    for k in range(1, count):
        got = swap_tp(blocks, k)
        total = total + jnp.stack([got[:, j ^ k] for j in range(count)], axis=1)
    return total.reshape(value.shape)


def cp_columns(value):
    return lax.all_to_all(value, "cp", split_axis=1, concat_axis=0, tiled=True)


def cp_gather(value):
    return lax.all_gather(value, "cp", axis=0, tiled=True)


def xpos_tables(positions):
    column = jnp.arange(HD // 2, dtype=f32)
    frequency = 10000.0 ** (-column / (HD // 2))
    zeta = (2.0 * column + 0.4 * HD) / (1.4 * HD)
    places = positions.astype(f32)[:, None]
    angle = places * frequency
    return (jnp.cos(angle), jnp.sin(angle), zeta ** (places / scale_base))


def turn(vector, cosine, sine, factor):
    paired = vector.reshape(vector.shape[:-1] + (HD // 2, 2))
    first, second = paired[..., 0], paired[..., 1]
    cosine, sine, factor = cosine[:, None], sine[:, None], factor[:, None]
    turned = jnp.stack(
        [(first * cosine - second * sine) * factor, (first * sine + second * cosine) * factor],
        axis=-1,
    )
    return turned.reshape(vector.shape)


def norm_rows(vector):
    center = jnp.mean(vector, axis=-1, keepdims=True)
    shifted = vector - center
    scaling = lax.rsqrt(jnp.mean(shifted * shifted, axis=-1, keepdims=True) + eps)
    return (shifted * scaling, scaling)


def norm_back(grad_result, gain, normed, scaling):
    grad_normed = grad_result * gain
    first = jnp.mean(grad_normed, axis=-1, keepdims=True)
    cross = jnp.mean(grad_normed * normed, axis=-1, keepdims=True)
    return scaling * (grad_normed - first - normed * cross)


def attend(queries, keys, values, allowed):
    scores = jnp.einsum("qhd,khd->hqk", queries, keys, preferred_element_type=f32) * HD**-0.5
    scores = jnp.where(allowed[None], scores, masked_score)
    top = jnp.max(scores, axis=-1, keepdims=True)
    exponent = jnp.where(allowed[None], jnp.exp(scores - top), 0.0)
    total = jnp.sum(exponent, axis=-1, keepdims=True)
    probability = (exponent / total).astype(bf16)
    mixed = jnp.einsum("hqk,khd->qhd", probability, values, preferred_element_type=f32)
    return (mixed, top + jnp.log(total))


def attend_back(queries, keys, values, allowed, lse, grad, delta):
    scores = jnp.einsum("qhd,khd->hqk", queries, keys, preferred_element_type=f32) * HD**-0.5
    probability = jnp.where(allowed[None], jnp.exp(scores - lse), 0.0)
    grad_prob = jnp.einsum("qhd,khd->hqk", grad, values, preferred_element_type=f32)
    grad_scores = (probability * (grad_prob - delta.T[:, :, None])).astype(bf16)
    grad_q = jnp.einsum("hqk,khd->qhd", grad_scores, keys, preferred_element_type=f32) * HD**-0.5
    grad_k = jnp.einsum("hqk,qhd->khd", grad_scores, queries, preferred_element_type=f32) * HD**-0.5
    grad_v = jnp.einsum(
        "hqk,qhd->khd", probability.astype(bf16), grad, preferred_element_type=f32
    )
    return (grad_q, grad_k, grad_v)


def body_general(
    layer_input,
    segment_ids,
    qkv_weight,
    out_weight,
    up_weight,
    down_weight,
    input_gain,
    heads_gain,
    middle_gain,
    hidden_gain,
    cotangent,
):
    local_len, row_count, width = layer_input.shape
    tp_count, cp_count = lax.axis_size("tp"), lax.axis_size("cp")
    me_tp, me_cp = lax.axis_index("tp"), lax.axis_index("cp")
    part = local_len // tp_count
    head_width = qkv_weight.shape[2]
    heads = head_width // HD
    by_head = heads % cp_count == 0
    own_heads = heads // cp_count if by_head else heads
    weight3 = jnp.transpose(qkv_weight, (1, 0, 2))

    x = tp_order(layer_input.reshape(local_len, width))
    gy = tp_order(cotangent.reshape(local_len, width))
    seg = tp_order(segment_ids)[:, 0]
    natural = tp_order(jnp.arange(local_len, dtype=jnp.int32))
    position = me_cp * local_len + natural
    position_all = (jnp.arange(cp_count, dtype=jnp.int32)[:, None] * local_len + natural).reshape(-1)

    stream = x.astype(f32)
    normed_one, scaling_one = norm_rows(stream)
    a = (normed_one * input_gain).astype(bf16)
    a_all = cp_gather(a)
    cosine, sine, factor = xpos_tables(position)
    raw_q = dot(a, weight3[0]).reshape(local_len, heads, HD)
    raw_k = dot(a, weight3[1]).reshape(local_len, heads, HD)
    raw_v = dot(a, weight3[2]).reshape(local_len, heads, HD)
    q = turn(raw_q, cosine, sine, factor).astype(bf16)
    k = turn(raw_k, cosine, sine, 1.0 / factor).astype(bf16)
    v = raw_v.astype(bf16)
    if by_head:
        extra = jnp.broadcast_to(seg.astype(bf16)[:, None, None], (local_len, cp_count, 16))
        sent = jnp.concatenate(
            [t.reshape(local_len, cp_count, own_heads * HD) for t in (q, k, v)] + [extra], axis=-1
        )
        got = lax.all_to_all(sent, "cp", split_axis=1, concat_axis=0, tiled=True)[:, 0]
        span = own_heads * HD
        q_all, k_all, v_all = (
            got[:, i * span : (i + 1) * span].reshape(-1, own_heads, HD) for i in range(3)
        )
        seg_all = got[:, 3 * span]
        seg_q, position_q = seg_all, position_all
    else:
        q_all, k_all, v_all = q, cp_gather(k), cp_gather(v)
        seg_all = cp_gather(seg.astype(bf16))
        seg_q, position_q = seg.astype(bf16), position
    allowed = (position_all[None, :] <= position_q[:, None]) & (seg_q[:, None] == seg_all[None, :])
    mixed, lse = attend(q_all, k_all, v_all, allowed)
    if by_head:
        attended = lax.all_to_all(
            mixed.astype(bf16).reshape(cp_count * local_len, own_heads * HD),
            "cp", split_axis=0, concat_axis=1, tiled=True,
        ).astype(f32)
    else:
        attended = mixed.reshape(local_len, head_width)

    sums = tp_token_sum(jnp.stack([jnp.sum(attended, axis=1), jnp.sum(attended * attended, axis=1)]))
    center = sums[0] / width
    scaling_h = lax.rsqrt(sums[1] / width - center * center + eps)[:, None]
    normed_h = (attended - center[:, None]) * scaling_h
    z = (normed_h * heads_gain).astype(bf16)
    gain_row = tp_sum(jnp.dot(heads_gain, out_weight.astype(f32)))
    branch = tp_scatter_sum(dot(z, out_weight))
    x1 = stream[:part] + branch
    normed_two, scaling_two = norm_rows(x1)
    u = tp_gather((normed_two * middle_gain).astype(bf16))

    grad_hid = dot_t(gy, down_weight)
    grad_normed = grad_hid * hidden_gain
    hidden = dot(u, up_weight)
    cdf = 0.5 * (1.0 + lax.erf(hidden * (0.5**0.5)))
    act = hidden * cdf
    slope = cdf + hidden * jnp.exp(-0.5 * hidden * hidden) * 0.3989422804014327
    sums = tp_token_sum(
        jnp.stack(
            [
                jnp.sum(act, axis=1),
                jnp.sum(act * act, axis=1),
                jnp.sum(grad_normed, axis=1),
                jnp.sum(grad_normed * act, axis=1),
            ]
        )
    )
    center = sums[0] / FF
    scaling_f = lax.rsqrt(sums[1] / FF - center * center + eps)
    first = sums[2] / FF
    cross = scaling_f * (sums[3] / FF - center * first)
    normed_f = (act - center[:, None]) * scaling_f[:, None]
    z2 = (normed_f * hidden_gain).astype(bf16)
    grad_act = scaling_f[:, None] * (grad_normed - first[:, None] - normed_f * cross[:, None])
    gh = (grad_act * slope).astype(bf16)
    hidden_gain_sum = jnp.sum(grad_hid * normed_f, axis=0)
    gu = tp_scatter_sum(dot_t(gh, up_weight))
    gx1 = gy[:part].astype(f32) + norm_back(gu, middle_gain, normed_two, scaling_two)
    middle_gain_sum = jnp.sum(gu * normed_two, axis=0)
    gb_own = gx1.astype(bf16)
    gb_f = gb_own.astype(f32)
    first = jnp.sum(gb_f * gain_row, axis=1) / width
    cross = jnp.sum(gb_f * branch, axis=1) / width
    gb = tp_gather(gb_own)
    stats = tp_gather(jnp.stack([first, cross], axis=1))

    gz = dot_t(gb, out_weight)
    heads_gain_sum = jnp.sum(gz * normed_h, axis=0)
    go = (scaling_h * (gz * heads_gain - stats[:, :1] - normed_h * stats[:, 1:])).astype(bf16)
    if by_head:
        grad_mixed = cp_columns(go).reshape(-1, own_heads, HD)
    else:
        grad_mixed = go.reshape(local_len, heads, HD)
    delta = jnp.sum(grad_mixed.astype(f32) * mixed, axis=-1)
    gq, gk, gv = attend_back(q_all, k_all, v_all, allowed, lse, grad_mixed, delta)
    if by_head:
        cos_all, sin_all, factor_all = xpos_tables(position_all)
    else:
        cos_all, sin_all, factor_all = cosine, sine, factor
        gk = lax.psum_scatter(gk.astype(bf16), "cp", scatter_dimension=0, tiled=True).astype(f32)
        gv = lax.psum_scatter(gv.astype(bf16), "cp", scatter_dimension=0, tiled=True).astype(f32)
    gq = turn(gq, cos_all, -sin_all, factor_all)
    gk = turn(gk, cos_all, -sin_all, 1.0 / factor_all)
    grads = jnp.stack([gq, gk, gv], axis=1).astype(bf16)
    if by_head:
        grads_own = grads.reshape(-1, 3 * own_heads * HD)
        grads = lax.all_to_all(
            grads.reshape(-1, 3, own_heads * HD), "cp", split_axis=0, concat_axis=2, tiled=True
        )
    else:
        grads = grads.reshape(local_len, 3, head_width)
        grads_own = lax.all_to_all(grads, "cp", split_axis=2, concat_axis=0, tiled=True)
        grads_own = grads_own.reshape(-1, 3 * head_width // cp_count)
    ga = (
        dot_t(grads[:, 0], weight3[0]) + dot_t(grads[:, 1], weight3[1]) + dot_t(grads[:, 2], weight3[2])
    )
    ga = tp_scatter_sum(ga)
    input_gain_sum = jnp.sum(ga * normed_one[:part], axis=0)
    grad_in = gx1 + norm_back(ga, input_gain, normed_one[:part], scaling_one[:part])

    y = (x1 + tp_scatter_sum(dot(z2, down_weight))).astype(bf16)
    layer_output = tp_order(tp_gather(y)).reshape(layer_input.shape)
    grad_input = tp_order(tp_gather(grad_in.astype(bf16))).reshape(layer_input.shape)

    grad_down = t_dot(cp_columns(z2), cp_gather(gy))
    grad_up = t_dot(cp_columns(u), cp_gather(gh))
    grad_out = t_dot(cp_columns(z), cp_gather(gb))
    grad_qkv = t_dot(a_all, grads_own).astype(bf16)
    grad_qkv = lax.all_to_all(
        grad_qkv.reshape(width, 3, head_width // cp_count), "cp", split_axis=0, concat_axis=2, tiled=True
    ).astype(f32)

    def cp_sum_own(vector):
        return jnp.sum(lax.all_to_all(vector.reshape(cp_count, -1), "cp", 0, 0, tiled=True), axis=0)

    def both_sum_own(vector):
        return tp_sum(cp_sum_own(vector))

    return (
        layer_output,
        grad_input,
        grad_qkv,
        grad_out,
        grad_up,
        grad_down,
        both_sum_own(input_gain_sum),
        cp_sum_own(heads_gain_sum),
        both_sum_own(middle_gain_sum),
        cp_sum_own(hidden_gain_sum),
    )


INTERPRET = False


def params(megabytes):
    return pltpu.CompilerParams(vmem_limit_bytes=megabytes * 1024 * 1024)


def shape(dims, kind):
    return jax.ShapeDtypeStruct(dims, kind)


def whole():
    return pl.BlockSpec(memory_space=pltpu.VMEM)


def scalars():
    return pl.BlockSpec(memory_space=pltpu.SMEM)


class Pin:
    def __init__(self, value):
        self.value = value


class Far(Pin):
    def __init__(self, value, dims=None, block=None):
        super().__init__(value)
        self.dims = tuple(value.shape) if dims is None else dims
        self.block = block


class Near:
    def __init__(self, value):
        self.value = value


class Fetched:
    def __init__(self, ref, copy):
        self.ref, self.copy, self.shape = ref, copy, ref.shape

    def ready(self):
        if self.copy is not None:
            self.copy.wait()
            self.copy = None

    def __getitem__(self, index):
        self.ready()
        return self.ref[index]


class Stored:
    def __init__(self, ref, copy):
        self.ref, self.copy, self.shape, self.sent = ref, copy, ref.shape, False

    def send(self):
        if not self.sent:
            self.copy.start()
            self.sent = True

    def __getitem__(self, index):
        return self.ref[index]

    def __setitem__(self, index, value):
        self.ref[index] = value

    @property
    def dtype(self):
        return self.ref.dtype


def plain(value):
    return value.value if isinstance(value, (Pin, Near)) else value


def pinned(value):
    return value if INTERPRET else pltpu.with_memory_space_constraint(value, pltpu.HBM)


def call(
    kernel, outs, args, specs=None, out_specs=None, grid=None, scratch=(), mb=8, cost=0.3, after=(), carry=(), prefetch=0
):
    specs = list(specs) if specs is not None else [whole() for _ in args]
    out_specs = list(out_specs) if out_specs is not None else [whole() for _ in outs]
    count, extra, kept, made = len(args), len(after), len(carry), len(outs)
    anywhere = pl.BlockSpec(memory_space=pl.ANY)
    far_in = [i for i, t in enumerate(args) if isinstance(t, Far)]
    far_out = [i for i, t in enumerate(outs) if isinstance(t, Far)]
    for i in far_in:
        specs[i] = anywhere
    for i in far_out:
        out_specs[i] = anywhere
    moving = [pltpu.VMEM(args[i].dims, args[i].value.dtype) for i in far_in]
    moving += [pltpu.VMEM(outs[i].dims, outs[i].value.dtype) for i in far_out]
    moving += [pltpu.SemaphoreType.DMA] * (len(far_in) + len(far_out))
    own_scratch = len(scratch)

    def run(*refs):
        ins = list(refs[:count])
        results = refs[count + extra + kept :]
        products = list(results[:made])
        rest = results[made + kept :]
        slots, sems = rest[own_scratch : own_scratch + len(far_in) + len(far_out)], rest[own_scratch + len(far_in) + len(far_out) :]
        for i, slot, sem in zip(far_in, slots, sems):
            source = refs[i]
            if args[i].block is not None:
                source = source.at[args[i].block(refs[0])]
            copy = pltpu.make_async_copy(source, slot, sem)
            copy.start()
            ins[i] = Fetched(slot, copy)
        stored = [
            Stored(slot, pltpu.make_async_copy(slot, results[i], sem))
            for i, slot, sem in zip(far_out, slots[len(far_in) :], sems[len(far_in) :])
        ]
        for i, product in zip(far_out, stored):
            products[i] = product
        kernel(*ins, *products, *rest[:own_scratch])
        for i in far_in:
            ins[i].ready()
        for product in stored:
            product.send()
        for product in stored:
            product.copy.wait()

    def result(value):
        dims = plain(value)
        if INTERPRET or value is dims:
            return dims
        return (pltpu.HBM if isinstance(value, Pin) else pltpu.VMEM)(dims.shape, dims.dtype)

    where = dict(
        in_specs=specs + [anywhere] * (extra + kept),
        out_specs=tuple(out_specs + [anywhere] * kept),
        scratch_shapes=list(scratch) + moving,
    )
    if prefetch:
        where["in_specs"] = where["in_specs"][prefetch:]
        where = {"grid_spec": pltpu.PrefetchScalarGridSpec(num_scalar_prefetch=prefetch, grid=grid, **where)}
    elif grid is not None:
        where["grid"] = grid
    return pl.pallas_call(
        run,
        out_shape=tuple(result(t) for t in outs) + tuple(result(Pin(shape(t.shape, t.dtype))) for t in carry),
        input_output_aliases={count + extra + i: made + i for i in range(kept)},
        compiler_params=params(mb),
        cost_estimate=pl.CostEstimate(flops=int(cost * 1e9), bytes_accessed=0, transcendentals=0),
        interpret=INTERPRET,
        **where,
    )(*[pinned(t.value) if isinstance(t, Pin) else t for t in list(args) + list(after)], *[pinned(t) for t in carry])


def bring(items, ids, after=(), carry=(), cost=0.3):
    def kernel(ids, *refs):
        sources, slots, sems = refs[: len(items)], refs[len(items) : 2 * len(items)], refs[2 * len(items) :]
        copies = []
        for (_, _, block), source, slot, sem in zip(items, sources, slots, sems):
            copies.append(pltpu.make_async_copy(source if block is None else source.at[block(ids)], slot, sem))
        for copy in copies:
            copy.start()
        for copy in copies:
            copy.wait()

    return call(
        kernel,
        [Near(shape(dims, array.dtype)) for array, dims, _ in items],
        [ids] + [Pin(array) for array, _, _ in items],
        [scalars()] + [pl.BlockSpec(memory_space=pl.ANY)] * len(items),
        scratch=[pltpu.SemaphoreType.DMA] * len(items), after=after, carry=carry, mb=2, cost=cost,
    )


def fixed(dims):
    return pl.BlockSpec(dims, lambda i: (0,) * len(dims))


def split_low(value):
    high = value.astype(bf16)
    return high, (value - high.astype(f32)).astype(bf16)


def lanes_of(columns, rows):
    lane = lax.broadcasted_iota(jnp.int32, (rows, 128), 1)
    out = jnp.zeros((rows, 128), f32)
    for i, column in enumerate(columns):
        out = jnp.where(lane == i, column.astype(f32), out)
    return out


def pair_sum(block, i):
    return block[:, i : i + 1].astype(f32) + block[:, i + 1 : i + 2].astype(f32)


def own_order(me, part, index):
    return ((index // part) ^ me) * part + index % part


def block_at(me, k, part):
    return pl.ds(pl.multiple_of((me ^ k) * part, part), part)


def swap_pairs(value, axis):
    size = value.shape[axis]
    place = lax.broadcasted_iota(jnp.int32, value.shape, axis)
    return jnp.where(
        place % 2 == 0, pltpu.roll(value, size - 1, axis), pltpu.roll(value, 1, axis)
    )


def tables(local_len, cp_count):
    column = np.arange(HD) // 2
    frequency = 10000.0 ** (-column / (HD // 2))
    zeta = (2.0 * column + 0.4 * HD) / (1.4 * HD)

    def of(places):
        angle = places[:, None] * frequency
        factor = zeta ** (places[:, None] / scale_base)
        return np.stack([np.cos(angle), np.sin(angle), factor, 1.0 / factor]).astype(np.float32)

    return of(np.arange(local_len)), of(np.arange(cp_count) * local_len)


def project_kernel(parts, ids, x, gain, inner, base, seg, w0, w1, w2, gy, pair, gy_out, out):
    me, mine = ids[0], ids[1]
    rows, width = pair.shape[1:]
    part = rows // parts
    heads = out.shape[0]
    x.ready()
    for k in range(parts):
        normed, _ = norm_rows(x.ref[block_at(me, k, part), :].astype(f32))
        pair[0, k * part : (k + 1) * part, :] = (normed * gain[...]).astype(bf16)
    inner.ready()
    here = [base[kind, pl.ds(mine, 1), :] for kind in range(4)]
    table = [
        jnp.concatenate([inner.ref[kind, block_at(me, k, part), :] for k in range(parts)], axis=0)
        for kind in range(4)
    ]
    cosine = table[0] * here[0] - table[1] * here[1]
    sine = table[1] * here[0] + table[0] * here[1]
    lane = lax.broadcasted_iota(jnp.int32, cosine.shape, 1)
    sine = jnp.where(lane % 2 == 0, -sine, sine)
    place = lax.broadcasted_iota(jnp.int32, (rows, rows), 1)
    source = lax.broadcasted_iota(jnp.int32, (rows, rows), 0)
    moved = (own_order(me, part, place) == source).astype(bf16)
    ids_row = jnp.broadcast_to(seg[...].astype(f32), (16, rows)).astype(bf16)
    ordered = dot(ids_row, moved).astype(bf16)
    for j in range(heads):
        out[j, 3 * HD : 3 * HD + 16, :] = ordered
    for c, weight in enumerate((w0, w1, w2)):
        acc = dot(pair[0], weight[0])
        factor = (table[2] * here[2], table[3] * here[3], None)[c]
        for i in range(acc.shape[1] // 128):
            piece = acc[:, i * 128 : (i + 1) * 128]
            if c < 2:
                piece = piece * (cosine * factor) + swap_pairs(piece, 1) * (sine * factor)
            turned = piece.T.astype(bf16)
            for h in range(128 // HD):
                out[i * (128 // HD) + h, c * HD : (c + 1) * HD, :] = turned[h * HD : (h + 1) * HD]
    out.send()
    gy.ready()
    for k in range(parts):
        block = gy.ref[block_at(me, k, part), :]
        pair[1, k * part : (k + 1) * part, :] = block
        gy_out[k * part : (k + 1) * part, :] = block


def gather_heads(got, keys, ids_col, values=None):
    for j in range(got.shape[0]):
        rows = slice(j * got.shape[2], (j + 1) * got.shape[2])
        both = jnp.concatenate([got[j, HD : 3 * HD, :].astype(f32)], axis=0).T
        keys[rows, :] = both[:, :HD].astype(bf16)
        if values is not None:
            values[rows, :] = both[:, HD:].astype(bf16)
        ids_col[rows, :] = got[j, 3 * HD : 3 * HD + 16, :].astype(f32).T


def visible_scores(me, part, scores, ids_col, ids_row, count, first, group):
    same = ids_col[0:count, 0:1] == ids_row
    length = group
    key = lax.broadcasted_iota(jnp.int32, (length, length), 0)
    query = lax.broadcasted_iota(jnp.int32, (length, length), 1)
    rows = first
    own = lambda index: (index // rows) * rows + own_order(me, part, index % rows)
    earlier = own(key) <= own(query)
    if count > length:
        earlier = jnp.concatenate([jnp.ones((count - length, length), jnp.bool_), earlier], axis=0)
    return same & earlier


def attend_kernel(parts, ids, got, out, mixed, lse, kept, keys, ids_col):
    me = ids[0]
    kept[...] = got[...]
    kept.send()
    blocks, _, rows = got.shape
    part = rows // parts
    gather_heads(got, keys, ids_col)
    group = 2 if blocks % 2 == 0 else 1
    width = group * rows
    for i in range(blocks // group):
        mine = range(i * group, (i + 1) * group)
        query = jnp.concatenate([got[j, :HD, :] for j in mine], axis=1) * bf16(HD**-0.5)
        ids_row = jnp.concatenate([got[j, 3 * HD : 3 * HD + 1, :] for j in mine], axis=1).astype(f32)
        count = (i + 1) * width
        scores = dot(keys[0:count, :], query)
        allowed = visible_scores(me, part, scores, ids_col, ids_row, count, rows, width)
        scores = jnp.where(allowed, scores, masked_score)
        top = jnp.max(scores, axis=0, keepdims=True)
        exponent = jnp.exp(scores - top)
        total = jnp.sum(exponent, axis=0, keepdims=True)
        value = jnp.concatenate([got[j, 2 * HD : 3 * HD, :] for j in range((i + 1) * group)], axis=1)
        result = dot(value, exponent.astype(bf16)) / total
        mixed[:, i * width : (i + 1) * width] = result
        lse[:, i * width : (i + 1) * width] = top + jnp.log(total)
        for n, j in enumerate(mine):
            out[j] = result[:, n * rows : (n + 1) * rows].astype(bf16)
    out.send()


def store_pieces(total, own, pieces, part, extra=None):
    own[:, : total.shape[1]] = total[:part]
    for k, piece in enumerate(pieces, 1):
        piece[:, : total.shape[1]] = total[k * part : (k + 1) * part].astype(bf16)
    if extra is not None:
        own[:, total.shape[1] :] = extra[:part]
        for k, piece in enumerate(pieces, 1):
            piece[:, total.shape[1] :] = extra[k * part : (k + 1) * part].astype(bf16)


def fold_row(row, part):
    block = jnp.concatenate([row[:, i : i + 128] for i in range(0, row.shape[1], 128)], axis=0)
    return jnp.concatenate(split_low(block), axis=0)


def unfold_row(block):
    half = block.shape[0] // 2
    total = block[:half].astype(f32) + block[half:].astype(f32)
    return jnp.concatenate([total[i : i + 1] for i in range(half)], axis=1)


def out_kernel(parts, att, gain, weight, own, *refs):
    pieces, kept = refs[:-1], refs[-1]
    kept[...] = att[...]
    blocks, _, rows = att.shape
    part, width = rows // parts, weight.shape[1]
    value = jnp.concatenate([att[j].astype(f32) for j in range(blocks)], axis=0).T
    high, low = split_low(jnp.mean(value, axis=1, keepdims=True))
    centred = value - (high.astype(f32) + low.astype(f32))
    square = split_low(jnp.sum(centred * centred, axis=1, keepdims=True))
    gains = gain[...]
    row = lax.broadcasted_iota(jnp.int32, (16, gains.shape[1]), 0)
    gain_high, gain_low = (t.astype(f32) for t in split_low(gains))
    gain_rows = jnp.where(row == 0, gain_high, jnp.where(row == 1, gain_low, 0.0))
    left = jnp.concatenate([(centred * gains).astype(bf16), gain_rows.astype(bf16)], axis=0)
    total = dot(left, weight[...])
    folded = fold_row(total[rows : rows + 1] + total[rows + 1 : rows + 2], part)
    stats = lanes_of([high, low, *square], rows).astype(bf16)
    own[:, :width] = total[:part]
    own[:, width : width + 128] = stats[:part].astype(f32)
    own[:, width + 128 :] = folded.astype(f32)
    for k, piece in enumerate(pieces, 1):
        here = slice(k * part, (k + 1) * part)
        piece[:, :width] = total[here].astype(bf16)
        piece[:, width : width + 128] = stats[here]
        piece[:, width + 128 :] = folded


def middle_kernel(parts, head_width, own, *refs):
    got, (x, gain, x1, u, gain_row) = refs[: parts - 1][::-1], refs[parts - 1 :]
    part, width = x1.shape
    blocks = [own] + list(got)
    stats = [b[:, width : width + 128] for b in blocks]
    means = [pair_sum(b, 0) for b in stats]
    squares = [pair_sum(b, 2) for b in stats]
    rows = [unfold_row(b[:, width + 128 :]) for b in blocks]
    gain_row[...] = sum(rows)
    mean = sum(means) / parts
    spread = sum(squares) + head_width * sum((m - mean) * (m - mean) for m in means)
    scaling = lax.rsqrt(spread / width + eps)
    total = sum(b[:, :width].astype(f32) for b in blocks)
    for m, row in zip(means, rows):
        total = total + (m - mean) * row
    value = x[...].astype(f32) + total * scaling
    x1[...] = value
    normed, _ = norm_rows(value)
    u[:, :width] = (normed * gain[...]).astype(bf16)
    u[:, width:] = lanes_of([*split_low(mean), *split_low(scaling)], part).astype(bf16)


def grad_hidden_kernel(gy, weight, grad):
    grad[...] = dot_t(gy[...], weight[...])


def prepare_kernel(step, up, near_up, flipped, up_sems):
    chunks = [slice(i, i + step) for i in range(0, up.shape[0], step)]
    copies = [pltpu.make_async_copy(up.at[c, :], near_up.at[c, :], up_sems.at[i]) for i, c in enumerate(chunks)]
    for copy in copies:
        copy.start()
    for copy, chunk in zip(copies, chunks):
        copy.wait()
        flipped[:, chunk] = near_up[chunk, :].T


def up_kernel(parts, step, own, *refs):
    got, refs = refs[: parts - 1][::-1], refs[parts - 1 :]
    weight, grad, gain, act, slope, u, stats, tail, rows_u = refs
    part = own.shape[0]
    rows, width = rows_u.shape
    for k, block in enumerate([own] + list(got)):
        rows_u[k * part : (k + 1) * part, :] = block[:, :width]
        tail[k * part : (k + 1) * part, :] = block[:, width:].astype(f32)
    wide = u.shape[2]
    for j in range(u.shape[0]):
        u[j] = rows_u[:, j * wide : (j + 1) * wide]
    total = [jnp.zeros((rows, 128), f32)] * 4
    for i in range(0, weight.shape[1], step):
        here = slice(i, i + step)
        hidden = dot(rows_u[...], weight[:, here])
        cdf = 0.5 * (1.0 + lax.erf(hidden * (0.5**0.5)))
        value = hidden * cdf
        act[:, here] = value
        slope[:, here] = cdf + hidden * jnp.exp(-0.5 * hidden * hidden) * 0.3989422804014327
        grad_normed = grad[:, here] * gain[:, here]
        columns = [value, value * value, grad_normed, grad_normed * value]
        for n, column in enumerate(columns):
            for j in range(0, step, 128):
                total[n] = total[n] + column[:, j : j + 128]
    sums = lanes_of([jnp.sum(t, axis=1, keepdims=True) for t in total], rows)
    stats[...] = sums.T[:8, :]


def swap_lane_blocks(value, k, part):
    lanes = value.shape[1]
    lane = lax.broadcasted_iota(jnp.int32, value.shape, 1)
    distance = 1
    while distance <= k:
        if k & distance:
            move = distance * part
            value = jnp.where(
                (lane // move) % 2 == 0,
                pltpu.roll(value, lanes - move, 1),
                pltpu.roll(value, move, 1),
            )
        distance *= 2
    return value


def hidden_back_kernel(parts, full, step, own, *refs):
    got, refs = refs[: parts - 1][::-1], refs[parts - 1 :]
    act, slope, grad, gain, weight, u, gh, both, own_out = refs[:9]
    pieces = refs[9:]
    first_wide = u.shape[2]
    both[:, :, :first_wide] = u[...]
    rows = act.shape[0]
    part = rows // parts
    total = own[...]
    for k, block in enumerate(got, 1):
        total = total + swap_lane_blocks(block[...], k, part)
    mean = total[0:1] / full
    scaling = lax.rsqrt(total[1:2] / full - mean * mean + eps)
    first = total[2:3] / full
    cross = scaling * (total[3:4] / full - mean * first)
    row = lax.broadcasted_iota(jnp.int32, (rows, rows), 0)
    table = jnp.zeros((rows, rows), f32)
    for i, value in enumerate([mean, scaling, first, cross]):
        table = jnp.where(row == i, value, table)
    cols = table.T
    mean, scaling, first, cross = (cols[:, i : i + 1] for i in range(4))
    wide = both.shape[2] - first_wide
    for i in range(0, act.shape[1], step):
        here = slice(i, i + step)
        normed = (act[:, here] - mean) * scaling
        low = (normed * gain[:, here]).astype(bf16)
        for j in range(0, step, wide):
            both[(i + j) // wide, :, first_wide:] = low[:, j : j + wide]
        value = scaling * (grad[:, here] * gain[:, here] - first - normed * cross) * slope[:, here]
        gh[:, here] = value.astype(bf16)
    both.send()
    gh.send()
    width = weight.shape[1]
    for i in range(0, width, step):
        here = slice(i, i + step)
        result = dot(gh[...], weight[:, here])
        own_out[:, here] = result[:part]
        for k, piece in enumerate(pieces, 1):
            piece[:, here] = result[k * part : (k + 1) * part].astype(bf16)


def down_kernel(parts, z2, *refs):
    count = len(refs) - parts
    weights, own_out, pieces = refs[:count], refs[count], refs[count + 1 :]
    blocks, _, wide = z2.shape
    part = own_out.shape[0]
    total = 0.0
    for i, weight in enumerate(weights):
        rows = weight.shape[0]
        left = jnp.concatenate([z2[j] for j in range(i * rows // wide, (i + 1) * rows // wide)], axis=1)
        total = total + dot(left, weight[...])
    own_out[...] = total[:part]
    for k, piece in enumerate(pieces, 1):
        piece[...] = total[k * part : (k + 1) * part].astype(bf16)


def middle_back_kernel(parts, own, *refs):
    got, refs = refs[: parts - 1][::-1], refs[parts - 1 :]
    gain_row, x, x1, gy, gain, gx1, gb = refs
    part, width = x1.shape
    grad = own[...]
    for block in got:
        grad = grad + block[...].astype(f32)
    value = x1[...]
    normed, scaling = norm_rows(value)
    result = gy[...].astype(f32) + norm_back(grad, gain[...], normed, scaling)
    gx1[...] = result
    low = result.astype(bf16)
    gb[:, :width] = low
    low = low.astype(f32)
    first = jnp.sum(low * gain_row[...], axis=1, keepdims=True) / width
    cross = jnp.sum(low * (value - x[...].astype(f32)), axis=1, keepdims=True) / width
    gb[:, width:] = lanes_of([*split_low(first), *split_low(cross)], part).astype(bf16)


def heads_back_kernel(parts, own, *refs):
    got, refs = refs[: parts - 1][::-1], refs[parts - 1 :]
    stats, att, gain, weight, sent, gb = refs
    blocks, _, rows = att.shape
    part, width = own.shape[0], gb.shape[1]
    for k, block in enumerate([own] + list(got)):
        gb[k * part : (k + 1) * part, :] = block[:, :width]
    gb.send()
    columns = jnp.concatenate([b[:, width:].astype(f32) for b in [own] + list(got)], axis=0).T
    first = columns[0:1] + columns[1:2]
    cross = columns[2:3] + columns[3:4]
    columns = stats[...].T
    mean = columns[0:1] + columns[1:2]
    scaling = columns[2:3] + columns[3:4]
    grad = dot_t(weight[...], gb[...])
    value = jnp.concatenate([att[j].astype(f32) for j in range(blocks)], axis=0)
    normed = (value - mean) * scaling
    gain_col = jnp.broadcast_to(gain[...], (8, gain.shape[1])).T[:, 0:1]
    go = (scaling * (grad * gain_col - first - normed * cross)).astype(bf16)
    z = (normed * gain_col).astype(bf16)
    for j in range(blocks):
        sent[j, :HD, :] = go[j * HD : (j + 1) * HD]
        sent[j, HD:, :] = z[j * HD : (j + 1) * HD]


def turn_back(grad, table, base, j, inverse):
    here = [base[kind, :, j : j + 1] for kind in range(4)]
    cosine = table[0] * here[0] - table[1] * here[1]
    sine = table[1] * here[0] + table[0] * here[1]
    factor = table[3] * here[3] if inverse else table[2] * here[2]
    row = lax.broadcasted_iota(jnp.int32, grad.shape, 0)
    sine = jnp.where(row % 2 == 0, sine, -sine)
    return (grad * cosine + swap_pairs(grad, 0) * sine) * factor


def attend_back_kernel(parts, ids, got, grads, mixed, lse, inner, base, out, z, keys, values, ids_col, gk, gv):
    me = ids[0]
    for j in range(grads.shape[0]):
        z[j] = grads[j, HD:, :]
    z.send()
    blocks, _, rows = got.shape
    part = rows // parts
    gather_heads(got, keys, ids_col, values)
    gk[...] = jnp.zeros_like(gk)
    gv[...] = jnp.zeros_like(gv)
    table = []
    for kind in range(4):
        ordered = jnp.concatenate(
            [inner[kind, block_at(me, k, part), :] for k in range(parts)], axis=0
        )
        table.append(ordered.T[:HD])
    group = 2 if blocks % 2 == 0 else 1
    width = group * rows
    for i in range(blocks // group):
        mine = range(i * group, (i + 1) * group)
        query = jnp.concatenate([got[j, :HD, :] for j in mine], axis=1) * bf16(HD**-0.5)
        ids_row = jnp.concatenate([got[j, 3 * HD : 3 * HD + 1, :] for j in mine], axis=1).astype(f32)
        go = jnp.concatenate([grads[j, :HD, :] for j in mine], axis=1)
        span = slice(i * width, (i + 1) * width)
        delta = jnp.sum(go.astype(f32) * mixed[:, span], axis=0, keepdims=True)
        count = (i + 1) * width
        scores = dot(keys[0:count, :], query)
        allowed = visible_scores(me, part, scores, ids_col, ids_row, count, rows, width)
        probability = jnp.where(allowed, jnp.exp(jnp.minimum(scores - lse[:, span], 0.5)), 0.0)
        grad_prob = dot(values[0:count, :], go)
        grad_scores = (probability * (grad_prob - delta)).astype(bf16)
        gv[:, 0:count] += dot_t(go, probability.astype(bf16))
        gk[:, 0:count] += dot_t(query, grad_scores)
        key = jnp.concatenate([got[j, HD : 2 * HD, :] for j in range((i + 1) * group)], axis=1)
        gq = dot(key, grad_scores) * HD**-0.5
        for n, j in enumerate(mine):
            piece = turn_back(gq[:, n * rows : (n + 1) * rows], table, base, j, False)
            out[j, :HD, :] = piece.astype(bf16)
    for j in range(blocks):
        span = slice(j * rows, (j + 1) * rows)
        out[j, HD : 2 * HD, :] = turn_back(gk[:, span], table, base, j, True).astype(bf16)
        out[j, 2 * HD :, :] = gv[:, span].astype(bf16)


def input_back_kernel(parts, step, got, w0, w1, w2, own_out, *pieces):
    part, width = own_out.shape
    grads = []
    for c in range(3):
        here = slice(c * HD, (c + 1) * HD)
        grad = jnp.concatenate([got[j, here, :].astype(f32) for j in range(got.shape[0])], axis=0)
        grads.append(grad.T.astype(bf16))
    result = dot_t(grads[0], w0[0]) + dot_t(grads[1], w1[0]) + dot_t(grads[2], w2[0])
    own_out[...] = result[:part]
    for k, piece in enumerate(pieces, 1):
        piece[...] = result[k * part : (k + 1) * part].astype(bf16)


def final_kernel(parts, own, *refs):
    got, (x, gx1, gain, out) = refs[: parts - 1][::-1], refs[parts - 1 :]
    grad = own[...]
    for block in got:
        grad = grad + block[...].astype(f32)
    normed, scaling = norm_rows(x[...].astype(f32))
    out[...] = (gx1[...] + norm_back(grad, gain[...], normed, scaling)).astype(bf16)


def output_kernel(own, *refs):
    got, (x1, out) = refs[:-2], refs[-2:]
    total = own[...] + x1[...]
    for block in got:
        total = total + block[...].astype(f32)
    out[...] = total.astype(bf16)


def natural_kernel(ids, *refs):
    blocks, out = refs[:-1], refs[-1]
    part = blocks[0].shape[0]
    for k, block in enumerate(blocks):
        out[block_at(ids[0], k, part), :] = block[...]


def own_row(gain, index, own):
    total = jnp.zeros((1, own), f32)
    for j in range(gain.shape[1] // own):
        total = jnp.where(index == j, gain[:, j * own : (j + 1) * own], total)
    return total


def row_of(column, columns):
    return jnp.broadcast_to(column, (columns, 128)).T[:1, :]


def product_kernel(step, columns, which, offset, ids, left, right, *refs):
    count = left.shape[0]
    gains = len(refs) > 7
    if gains:
        (weight, gain, out, gain_grad), refs = refs[:4], refs[4:]
        (near_weight, weight_sem), refs = refs[-2:], refs[:-2]
    else:
        out, refs = refs[0], refs[1:]
    left_all, right_all, result, left_sems, right_sems, out_sems = refs
    rows, size = right.shape[-2:]
    own = result.shape[0]
    tokens = count * rows
    chunks = [slice(i, i + step) for i in range(0, size, step)]

    first = []
    for r in range(count):
        source = left.at[r]
        if columns:
            source, place = source.at[:, pl.ds(offset, own)], left_all.at[pl.ds(r * rows, rows), :]
        else:
            source, place = source.at[pl.ds(offset, own), :], left_all.at[r]
        first.append(pltpu.make_async_copy(source, place, left_sems.at[r]))
    side = right if which is None else right.at[:, which]
    later = [
        [pltpu.make_async_copy(side.at[:, :, c], right_all.at[:, :, c], right_sems.at[i])] for i, c in enumerate(chunks)
    ]
    for copy in first + later[0]:
        copy.start()
    if gains:
        fetch = pltpu.make_async_copy(
            weight.at[pl.ds(pl.multiple_of(ids[1] * own, own), own), :], near_weight, weight_sem
        )
        fetch.start()
    for copies in later[1:]:
        for copy in copies:
            copy.start()
    for copy in first:
        copy.wait()
    if not columns:
        value = jnp.concatenate([left_all[r] for r in range(count)], axis=1)
    sums = jnp.zeros((own, 128), f32)
    sent = []
    for i, (c, copies) in enumerate(zip(chunks, later)):
        for copy in copies:
            copy.wait()
        block = right_all[:, :, c].reshape(tokens, step)
        grad = t_dot(left_all[...], block) if columns else dot(value, block)
        result[:, c] = grad.astype(result.dtype)
        if gains:
            if i == 0:
                fetch.wait()
            product = grad * near_weight[:, c].astype(f32)
            for j in range(0, step, 128):
                sums = sums + product[:, j : j + 128]
            moves = [pltpu.make_async_copy(result.at[:, c], out.at[:, c], out_sems.at[i, 0])]
        else:
            wide = out.shape[2]
            moves = [
                pltpu.make_async_copy(
                    result.at[:, pl.ds(j, wide)], out.at[j // wide], out_sems.at[i, (j - c.start) // wide]
                )
                for j in range(c.start, c.stop, wide)
            ]
        for move in moves:
            move.start()
        sent.extend(moves)
    if gains:
        gain_grad[...] = row_of(jnp.sum(sums, axis=1, keepdims=True), own) / own_row(gain, ids[1], own)
    for copy in sent:
        copy.wait()


def grad_qkv_place_kernel(ids, got, weight, gain, up_gain, out, gain_grads):
    total = 0.0
    for c in range(3):
        value = jnp.concatenate(
            [got[j, c * HD : (c + 1) * HD, :].astype(f32) for j in range(got.shape[0])], axis=0
        ).T
        out[c] = value
        total = total + jnp.sum(value * weight[c].astype(f32), axis=1, keepdims=True)
    out.send()
    first = row_of(total, total.shape[0]) / own_row(gain, ids[1], total.shape[0])
    row = lax.broadcasted_iota(jnp.int32, gain_grads.shape, 0)
    gain_grads[...] = jnp.where(row == 0, first, up_gain[...])


def outputs_kernel(parts, ids, *refs):
    blocks, y_blocks, gains = (refs[i * parts : (i + 1) * parts] for i in range(3))
    out, y, first, second = refs[3 * parts :]
    part = blocks[0].shape[0]
    for k in range(parts):
        out[block_at(ids[0], k, part), :] = blocks[-k % parts][...]
        y[block_at(ids[0], k, part), :] = y_blocks[-k % parts][...]
    out.send()
    y.send()
    total = sum(b[...] for b in gains)
    first[...] = total[0:1]
    second[...] = total[1:2]


def body(
    layer_input,
    segment_ids,
    qkv_weight,
    out_weight,
    up_weight,
    down_weight,
    input_gain,
    heads_gain,
    middle_gain,
    hidden_gain,
    cotangent,
):
    rows, row_count, width = layer_input.shape
    T, C = lax.axis_size("tp"), lax.axis_size("cp")
    part = rows // T
    head_width = qkv_weight.shape[2]
    if head_width // HD != C or row_count != 1 or rows != 128 or 64 * part != width:
        return body_general(
            layer_input, segment_ids, qkv_weight, out_weight, up_weight, down_weight,
            input_gain, heads_gain, middle_gain, hidden_gain, cotangent,
        )
    tokens = rows * C
    hidden = up_weight.shape[1]
    wide = width // C
    high = hidden // C
    ids = jnp.stack([lax.axis_index("tp"), lax.axis_index("cp")]).astype(jnp.int32)
    x = layer_input.reshape(rows, width)
    gy = cotangent.reshape(rows, width)
    weight3 = jnp.transpose(qkv_weight, (1, 0, 2))
    gain_in, gain_mid = input_gain.reshape(1, -1), middle_gain.reshape(1, -1)
    gain_heads, gain_hid = heads_gain.reshape(1, -1), hidden_gain.reshape(1, -1)
    inner, base = tables(rows, C)
    inner2 = jnp.asarray(np.concatenate([inner, inner], axis=2))
    base2 = jnp.asarray(np.concatenate([base, base], axis=2))
    base_t = np.zeros((4, HD, 128), np.float32)
    base_t[:, :, :C] = np.transpose(base, (0, 2, 1))
    base_t = jnp.asarray(base_t)
    wide_part = width + 128
    step = 512

    def piece_shapes(columns):
        return [shape((part, columns), f32)] + [shape((part, columns), bf16)] * (T - 1)

    def exchange(pieces):
        return [swap_tp(pieces[k - 1], k) for k in range(T - 1, 0, -1)]

    def spread(block):
        return exchange([block] * (T - 1))

    def to_cp(value):
        return lax.all_to_all(value, "cp", 0, 0, tiled=True)

    def entire(value):
        return (value, value.shape, None)

    def own_rows(value):
        return (value, (part, width), lambda ids: (block_at(ids[0], 0, part), slice(None)))

    def third(c):
        return lambda ids: (pl.ds(c, 1), slice(None), slice(None))

    cols, first_rows = lambda i, *_: (0, i), lambda i, *_: (i, 0)
    origin2, origin3 = lambda i, *_: (0, 0), lambda i, *_: (0, 0, 0)
    weight_thirds = [Far(weight3, (1, width, head_width), third(c)) for c in range(3)]

    pair, gy_x, sent = call(
        functools.partial(project_kernel, T),
        [Far(shape((2, rows, width), bf16)), Far(shape((rows, width), bf16)), Far(shape((C, 3 * HD + 16, rows), bf16))],
        [ids, Far(x), Far(gain_in), Far(inner2), Far(base2), Far(segment_ids.reshape(1, rows)), *weight_thirds, Far(gy)],
        [scalars()] + [whole()] * 9, mb=14,
    )
    got = to_cp(sent)
    near_out, near_x, near_gy, near_mid, near_heads, near_hid, near_in = bring(
        [entire(out_weight), own_rows(x), own_rows(gy), entire(gain_mid), entire(gain_heads),
         entire(gain_hid), entire(gain_in)],
        ids, after=[Pin(sent)],
    )
    back, mixed, lse, far_got, pair = call(
        functools.partial(attend_kernel, T),
        [Far(shape((C, HD, rows), bf16)), Far(shape((HD, tokens), f32)), Far(shape((1, tokens), f32)),
         Far(shape((C, 3 * HD + 16, rows), bf16))],
        [ids, got], [scalars(), whole()],
        scratch=[pltpu.VMEM((tokens, HD), bf16), pltpu.VMEM((tokens, 16), f32)],
        mb=10, after=[near_heads], carry=[pair],
    )
    att = to_cp(back)
    early = lax.all_gather(pair, "cp", axis=0)

    own, *pieces, near_att = call(
        functools.partial(out_kernel, T),
        piece_shapes(width + 256) + [Near(shape((C, HD, rows), bf16))],
        [att, near_heads, near_out],
    )
    (grad_hid,) = call(
        grad_hidden_kernel, [Near(shape((rows, hidden), f32))],
        [Pin(gy_x), Pin(down_weight)],
        [fixed((rows, width)), pl.BlockSpec((step, width), first_rows)],
        [pl.BlockSpec((rows, step), cols)],
        grid=(hidden // step,), after=[own], mb=10, cost=3,
    )
    x1, u_own, gain_row = call(
        functools.partial(middle_kernel, T, head_width),
        [Near(shape((part, width), f32)), shape((part, wide_part), bf16), Near(shape((1, width), f32))],
        [own, *exchange(pieces), near_x, near_mid], after=[grad_hid],
    )
    u_blocks = [u_own] + spread(u_own)
    near_up, near_flip = call(
        functools.partial(prepare_kernel, 256),
        [Near(shape((width, hidden), bf16)), Near(shape((hidden, width), bf16))],
        [Pin(up_weight)], [pl.BlockSpec(memory_space=pl.ANY)],
        scratch=[pltpu.SemaphoreType.DMA((width // 256,))], after=[u_own], mb=6,
    )

    act, slope, u_cols, stats, near_tail = call(
        functools.partial(up_kernel, T, step),
        [Near(shape((rows, hidden), f32)), Near(shape((rows, hidden), f32)), Near(shape((C, rows, wide), bf16)),
         shape((8, rows), f32), Near(shape((rows, 128), f32))],
        [*u_blocks, near_up, grad_hid, near_hid],
        scratch=[pltpu.VMEM((rows, width), bf16)], mb=8, after=[near_flip],
    )
    gh, both, own, *pieces = call(
        functools.partial(hidden_back_kernel, T, FF, step),
        [Far(shape((rows, hidden), bf16)), Far(shape((C, rows, wide + high), bf16))] + piece_shapes(width),
        [stats, *spread(stats), act, slope, grad_hid, near_hid, near_flip, u_cols], mb=10,
    )
    gu_got = exchange(pieces)
    both_got = to_cp(both)
    gh_all = lax.all_gather(gh, "cp", axis=0)
    down_parts = [
        Far(down_weight, (step, width), (lambda at: lambda ids: (pl.ds(at, step), slice(None)))(i))
        for i in range(0, hidden, step)
    ]
    y_own, *y_pieces = call(
        functools.partial(down_kernel, T),
        [Far(t) for t in piece_shapes(width)],
        [Far(both, (C, rows, high), lambda ids: (slice(None), slice(None), pl.ds(wide, high))), *down_parts],
        after=[own], cost=20, mb=14,
    )
    gx1, gb_own = call(
        functools.partial(middle_back_kernel, T),
        [Near(shape((part, width), f32)), shape((part, wide_part), bf16)],
        [own, *gu_got, gain_row, near_x, x1, near_gy, near_mid], after=[Pin(y_own)], cost=8,
    )
    gb_blocks = [gb_own] + spread(gb_own)
    (near_out,) = bring([entire(out_weight)], ids, after=[gb_own])

    def product(left, right, columns, which, offset, own, after, weight=None, gain=None, cost=20):
        anywhere = pl.BlockSpec(memory_space=pl.ANY)
        size = right.shape[-1]
        chunk = 2 * step
        left_dims = (tokens, own) if columns else (C, own, rows)
        if weight is not None:
            outs = [Pin(shape((own, size), f32)), shape((1, own), f32)]
            more, more_specs = [Pin(weight), gain], [anywhere, whole()]
            out_specs, extra = [anywhere, whole()], [pltpu.VMEM((own, size), bf16), pltpu.SemaphoreType.DMA]
        else:
            outs, out_specs = [Pin(shape((C, own, size // C), bf16))], [anywhere]
            more, more_specs, extra = [], [], []
        return call(
            functools.partial(product_kernel, chunk, columns, which, offset), outs,
            [ids, Pin(left), Pin(right), *more], [scalars()] + [anywhere] * 2 + more_specs, out_specs,
            scratch=[pltpu.VMEM(left_dims, bf16), pltpu.VMEM((C, rows, size), bf16),
                     pltpu.VMEM((own, size), plain(outs[0]).dtype),
                     pltpu.SemaphoreType.DMA((C,)), pltpu.SemaphoreType.DMA((size // chunk,)),
                     pltpu.SemaphoreType.DMA((size // chunk, chunk * C // size))] + extra,
            mb=14, after=after, cost=cost,
        )


    sent, gb, *kept = call(
        functools.partial(heads_back_kernel, T),
        [Far(shape((C, 2 * HD, rows), bf16)), Far(shape((rows, width), bf16))],
        [*gb_blocks, near_tail, near_att, near_heads, near_out], after=[Pin(both_got)], carry=y_pieces,
    )
    y_pieces = kept
    gb_all = lax.all_gather(gb, "cp", axis=0)
    y_got = exchange(y_pieces)
    grads = to_cp(sent)
    near_got, near_mixed, near_lse, near_inner, near_base = bring(
        [entire(far_got), entire(mixed), entire(lse), entire(inner2), entire(base_t)], ids, after=[Pin(sent)]
    )
    grad_down, hidden_gain_grad = product(both_got, early, True, 1, wide, high, [Pin(sent)], down_weight, gain_hid)
    gq_sent, z = call(
        functools.partial(attend_back_kernel, T),
        [Far(shape((C, 3 * HD, rows), bf16)), Far(shape((C, HD, rows), bf16))],
        [ids, near_got, grads, near_mixed, near_lse, near_inner, near_base], [scalars()] + [whole()] * 6,
        scratch=[pltpu.VMEM((tokens, HD), bf16), pltpu.VMEM((tokens, HD), bf16), pltpu.VMEM((tokens, 16), f32),
                 pltpu.VMEM((HD, tokens), f32), pltpu.VMEM((HD, tokens), f32)],
        mb=12, cost=8, after=[Pin(grad_down)],
    )
    gq = to_cp(gq_sent)
    (y_low,) = call(
        output_kernel, [shape((part, width), bf16)], [Far(y_own), *y_got, x1], after=[Pin(gq_sent)]
    )
    y_blocks = [y_low] + spread(y_low)
    (grad_qkv,) = product(gq_sent, early, False, 0, 0, 3 * HD, [y_low])
    own, *pieces = call(
        functools.partial(input_back_kernel, T, step), piece_shapes(width), [gq, *weight_thirds], mb=10, cost=10,
    )
    ga_got = exchange(pieces)
    grad_qkv_got = to_cp(grad_qkv)
    grad_up, up_gain = product(both_got, gh_all, True, None, 0, wide, [own], up_weight, gain_mid)
    (final,) = call(
        functools.partial(final_kernel, T),
        [shape((part, width), bf16)],
        [own, *ga_got, near_x, gx1, near_in], after=[Pin(grad_up)],
    )
    final_blocks = [final] + spread(final)
    own_wide = lambda ids: (slice(None), pl.ds(pl.multiple_of(ids[1] * wide, wide), wide), slice(None))
    grad_qkv, gains = call(
        grad_qkv_place_kernel,
        [Far(shape((3, wide, head_width), f32)), shape((8, wide), f32)],
        [ids, grad_qkv_got, Far(weight3, (3, wide, head_width), own_wide), gain_in, up_gain],
        [scalars()] + [whole()] * 4, after=[final], cost=20,
    )
    gain_blocks = [gains] + spread(gains)
    grad_out, heads_gain_grad = product(z, gb_all, False, None, 0, HD, [gains], out_weight, gain_heads)
    grad_input, layer_output, input_gain_grad, middle_gain_grad = call(
        functools.partial(outputs_kernel, T),
        [Far(shape((rows, width), bf16))] * 2 + [shape((1, wide), f32), shape((1, wide), f32)],
        [ids, *final_blocks, *y_blocks, *gain_blocks], [scalars()] + [whole()] * (3 * T), after=[Pin(grad_out)],
    )
    return (
        layer_output.reshape(layer_input.shape),
        grad_input.reshape(layer_input.shape),
        jnp.transpose(grad_qkv, (1, 0, 2)),
        grad_out,
        grad_up,
        grad_down,
        input_gain_grad.reshape(-1),
        heads_gain_grad.reshape(-1),
        middle_gain_grad.reshape(-1),
        hidden_gain_grad.reshape(-1),
    )


def solution(mesh):
    placed = (
        P("cp", None, None),
        P("cp", None),
        P(None, None, "tp"),
        P("tp", None),
        P(None, "tp"),
        P("tp", None),
        P(),
        P("tp"),
        P(),
        P("tp"),
        P("cp", None, None),
    )
    return jax.shard_map(
        body,
        mesh=mesh,
        in_specs=placed,
        out_specs=(
            P("cp", None, None),
            P("cp", None, None),
            P("cp", None, "tp"),
            P(("tp", "cp"), None),
            P("cp", "tp"),
            P(("tp", "cp"), None),
            P("cp"),
            P(("tp", "cp")),
            P("cp"),
            P(("tp", "cp")),
        ),
        check_vma=False,
    )
```

```python
import functools

import jax
import jax.numpy as jnp
import numpy as np
from jax import lax
from jax.experimental import pallas as pl
from jax.experimental.pallas import tpu as pltpu
from jax.sharding import PartitionSpec as P

HD = 64
D = 2048
FF = 8192

eps = 1e-05
scale_base = 512.0
masked_score = -1e30
f32 = jnp.float32
bf16 = jnp.bfloat16


def dot(a, b):
    return jnp.dot(a, b, preferred_element_type=f32)


def dot_t(a, b):
    return lax.dot_general(a, b, (((1,), (1,)), ((), ())), preferred_element_type=f32)


def t_dot(a, b):
    return lax.dot_general(a, b, (((0,), (0,)), ((), ())), preferred_element_type=f32)


def pairs(count, k):
    return [(i, i ^ k) for i in range(count)]


def swap_tp(value, k):
    return lax.ppermute(value, "tp", pairs(lax.axis_size("tp"), k))


def tp_order(value):
    count, me = lax.axis_size("tp"), lax.axis_index("tp")
    part = value.shape[0] // count
    return jnp.concatenate(
        [lax.dynamic_slice_in_dim(value, (me ^ k) * part, part, 0) for k in range(count)], axis=0
    )


def tp_scatter_sum(partial_sum):
    count = lax.axis_size("tp")
    part = partial_sum.shape[0] // count
    low = partial_sum.astype(bf16)
    total = partial_sum[:part]
    for k in range(1, count):
        total = total + swap_tp(low[k * part : (k + 1) * part], k).astype(f32)
    return total


def tp_gather(block):
    count = lax.axis_size("tp")
    return jnp.concatenate([block] + [swap_tp(block, k) for k in range(1, count)], axis=0)


def tp_sum(value):
    total = value
    for k in range(1, lax.axis_size("tp")):
        total = total + swap_tp(value, k)
    return total


def tp_token_sum(value):
    count = lax.axis_size("tp")
    blocks = value.reshape(value.shape[0], count, -1)
    total = blocks
    for k in range(1, count):
        got = swap_tp(blocks, k)
        total = total + jnp.stack([got[:, j ^ k] for j in range(count)], axis=1)
    return total.reshape(value.shape)


def cp_columns(value):
    return lax.all_to_all(value, "cp", split_axis=1, concat_axis=0, tiled=True)


def cp_gather(value):
    return lax.all_gather(value, "cp", axis=0, tiled=True)


def xpos_tables(positions):
    column = jnp.arange(HD // 2, dtype=f32)
    frequency = 10000.0 ** (-column / (HD // 2))
    zeta = (2.0 * column + 0.4 * HD) / (1.4 * HD)
    places = positions.astype(f32)[:, None]
    angle = places * frequency
    return (jnp.cos(angle), jnp.sin(angle), zeta ** (places / scale_base))


def turn(vector, cosine, sine, factor):
    paired = vector.reshape(vector.shape[:-1] + (HD // 2, 2))
    first, second = paired[..., 0], paired[..., 1]
    cosine, sine, factor = cosine[:, None], sine[:, None], factor[:, None]
    turned = jnp.stack(
        [(first * cosine - second * sine) * factor, (first * sine + second * cosine) * factor],
        axis=-1,
    )
    return turned.reshape(vector.shape)


def norm_rows(vector):
    center = jnp.mean(vector, axis=-1, keepdims=True)
    shifted = vector - center
    scaling = lax.rsqrt(jnp.mean(shifted * shifted, axis=-1, keepdims=True) + eps)
    return (shifted * scaling, scaling)


def norm_back(grad_result, gain, normed, scaling):
    grad_normed = grad_result * gain
    first = jnp.mean(grad_normed, axis=-1, keepdims=True)
    cross = jnp.mean(grad_normed * normed, axis=-1, keepdims=True)
    return scaling * (grad_normed - first - normed * cross)


def attend(queries, keys, values, allowed):
    scores = jnp.einsum("qhd,khd->hqk", queries, keys, preferred_element_type=f32) * HD**-0.5
    scores = jnp.where(allowed[None], scores, masked_score)
    top = jnp.max(scores, axis=-1, keepdims=True)
    exponent = jnp.where(allowed[None], jnp.exp(scores - top), 0.0)
    total = jnp.sum(exponent, axis=-1, keepdims=True)
    probability = (exponent / total).astype(bf16)
    mixed = jnp.einsum("hqk,khd->qhd", probability, values, preferred_element_type=f32)
    return (mixed, top + jnp.log(total))


def attend_back(queries, keys, values, allowed, lse, grad, delta):
    scores = jnp.einsum("qhd,khd->hqk", queries, keys, preferred_element_type=f32) * HD**-0.5
    probability = jnp.where(allowed[None], jnp.exp(scores - lse), 0.0)
    grad_prob = jnp.einsum("qhd,khd->hqk", grad, values, preferred_element_type=f32)
    grad_scores = (probability * (grad_prob - delta.T[:, :, None])).astype(bf16)
    grad_q = jnp.einsum("hqk,khd->qhd", grad_scores, keys, preferred_element_type=f32) * HD**-0.5
    grad_k = jnp.einsum("hqk,qhd->khd", grad_scores, queries, preferred_element_type=f32) * HD**-0.5
    grad_v = jnp.einsum(
        "hqk,qhd->khd", probability.astype(bf16), grad, preferred_element_type=f32
    )
    return (grad_q, grad_k, grad_v)


def body_general(
    layer_input,
    segment_ids,
    qkv_weight,
    out_weight,
    up_weight,
    down_weight,
    input_gain,
    heads_gain,
    middle_gain,
    hidden_gain,
    cotangent,
):
    local_len, row_count, width = layer_input.shape
    tp_count, cp_count = lax.axis_size("tp"), lax.axis_size("cp")
    me_tp, me_cp = lax.axis_index("tp"), lax.axis_index("cp")
    part = local_len // tp_count
    head_width = qkv_weight.shape[2]
    heads = head_width // HD
    by_head = heads % cp_count == 0
    own_heads = heads // cp_count if by_head else heads
    weight3 = jnp.transpose(qkv_weight, (1, 0, 2))

    x = tp_order(layer_input.reshape(local_len, width))
    gy = tp_order(cotangent.reshape(local_len, width))
    seg = tp_order(segment_ids)[:, 0]
    natural = tp_order(jnp.arange(local_len, dtype=jnp.int32))
    position = me_cp * local_len + natural
    position_all = (jnp.arange(cp_count, dtype=jnp.int32)[:, None] * local_len + natural).reshape(-1)

    stream = x.astype(f32)
    normed_one, scaling_one = norm_rows(stream)
    a = (normed_one * input_gain).astype(bf16)
    a_all = cp_gather(a)
    cosine, sine, factor = xpos_tables(position)
    raw_q = dot(a, weight3[0]).reshape(local_len, heads, HD)
    raw_k = dot(a, weight3[1]).reshape(local_len, heads, HD)
    raw_v = dot(a, weight3[2]).reshape(local_len, heads, HD)
    q = turn(raw_q, cosine, sine, factor).astype(bf16)
    k = turn(raw_k, cosine, sine, 1.0 / factor).astype(bf16)
    v = raw_v.astype(bf16)
    if by_head:
        extra = jnp.broadcast_to(seg.astype(bf16)[:, None, None], (local_len, cp_count, 16))
        sent = jnp.concatenate(
            [t.reshape(local_len, cp_count, own_heads * HD) for t in (q, k, v)] + [extra], axis=-1
        )
        got = lax.all_to_all(sent, "cp", split_axis=1, concat_axis=0, tiled=True)[:, 0]
        span = own_heads * HD
        q_all, k_all, v_all = (
            got[:, i * span : (i + 1) * span].reshape(-1, own_heads, HD) for i in range(3)
        )
        seg_all = got[:, 3 * span]
        seg_q, position_q = seg_all, position_all
    else:
        q_all, k_all, v_all = q, cp_gather(k), cp_gather(v)
        seg_all = cp_gather(seg.astype(bf16))
        seg_q, position_q = seg.astype(bf16), position
    allowed = (position_all[None, :] <= position_q[:, None]) & (seg_q[:, None] == seg_all[None, :])
    mixed, lse = attend(q_all, k_all, v_all, allowed)
    if by_head:
        attended = lax.all_to_all(
            mixed.astype(bf16).reshape(cp_count * local_len, own_heads * HD),
            "cp", split_axis=0, concat_axis=1, tiled=True,
        ).astype(f32)
    else:
        attended = mixed.reshape(local_len, head_width)

    sums = tp_token_sum(jnp.stack([jnp.sum(attended, axis=1), jnp.sum(attended * attended, axis=1)]))
    center = sums[0] / width
    scaling_h = lax.rsqrt(sums[1] / width - center * center + eps)[:, None]
    normed_h = (attended - center[:, None]) * scaling_h
    z = (normed_h * heads_gain).astype(bf16)
    gain_row = tp_sum(jnp.dot(heads_gain, out_weight.astype(f32)))
    branch = tp_scatter_sum(dot(z, out_weight))
    x1 = stream[:part] + branch
    normed_two, scaling_two = norm_rows(x1)
    u = tp_gather((normed_two * middle_gain).astype(bf16))

    grad_hid = dot_t(gy, down_weight)
    grad_normed = grad_hid * hidden_gain
    hidden = dot(u, up_weight)
    cdf = 0.5 * (1.0 + lax.erf(hidden * (0.5**0.5)))
    act = hidden * cdf
    slope = cdf + hidden * jnp.exp(-0.5 * hidden * hidden) * 0.3989422804014327
    sums = tp_token_sum(
        jnp.stack(
            [
                jnp.sum(act, axis=1),
                jnp.sum(act * act, axis=1),
                jnp.sum(grad_normed, axis=1),
                jnp.sum(grad_normed * act, axis=1),
            ]
        )
    )
    center = sums[0] / FF
    scaling_f = lax.rsqrt(sums[1] / FF - center * center + eps)
    first = sums[2] / FF
    cross = scaling_f * (sums[3] / FF - center * first)
    normed_f = (act - center[:, None]) * scaling_f[:, None]
    z2 = (normed_f * hidden_gain).astype(bf16)
    grad_act = scaling_f[:, None] * (grad_normed - first[:, None] - normed_f * cross[:, None])
    gh = (grad_act * slope).astype(bf16)
    hidden_gain_sum = jnp.sum(grad_hid * normed_f, axis=0)
    gu = tp_scatter_sum(dot_t(gh, up_weight))
    gx1 = gy[:part].astype(f32) + norm_back(gu, middle_gain, normed_two, scaling_two)
    middle_gain_sum = jnp.sum(gu * normed_two, axis=0)
    gb_own = gx1.astype(bf16)
    gb_f = gb_own.astype(f32)
    first = jnp.sum(gb_f * gain_row, axis=1) / width
    cross = jnp.sum(gb_f * branch, axis=1) / width
    gb = tp_gather(gb_own)
    stats = tp_gather(jnp.stack([first, cross], axis=1))

    gz = dot_t(gb, out_weight)
    heads_gain_sum = jnp.sum(gz * normed_h, axis=0)
    go = (scaling_h * (gz * heads_gain - stats[:, :1] - normed_h * stats[:, 1:])).astype(bf16)
    if by_head:
        grad_mixed = cp_columns(go).reshape(-1, own_heads, HD)
    else:
        grad_mixed = go.reshape(local_len, heads, HD)
    delta = jnp.sum(grad_mixed.astype(f32) * mixed, axis=-1)
    gq, gk, gv = attend_back(q_all, k_all, v_all, allowed, lse, grad_mixed, delta)
    if by_head:
        cos_all, sin_all, factor_all = xpos_tables(position_all)
    else:
        cos_all, sin_all, factor_all = cosine, sine, factor
        gk = lax.psum_scatter(gk.astype(bf16), "cp", scatter_dimension=0, tiled=True).astype(f32)
        gv = lax.psum_scatter(gv.astype(bf16), "cp", scatter_dimension=0, tiled=True).astype(f32)
    gq = turn(gq, cos_all, -sin_all, factor_all)
    gk = turn(gk, cos_all, -sin_all, 1.0 / factor_all)
    grads = jnp.stack([gq, gk, gv], axis=1).astype(bf16)
    if by_head:
        grads_own = grads.reshape(-1, 3 * own_heads * HD)
        grads = lax.all_to_all(
            grads.reshape(-1, 3, own_heads * HD), "cp", split_axis=0, concat_axis=2, tiled=True
        )
    else:
        grads = grads.reshape(local_len, 3, head_width)
        grads_own = lax.all_to_all(grads, "cp", split_axis=2, concat_axis=0, tiled=True)
        grads_own = grads_own.reshape(-1, 3 * head_width // cp_count)
    ga = (
        dot_t(grads[:, 0], weight3[0]) + dot_t(grads[:, 1], weight3[1]) + dot_t(grads[:, 2], weight3[2])
    )
    ga = tp_scatter_sum(ga)
    input_gain_sum = jnp.sum(ga * normed_one[:part], axis=0)
    grad_in = gx1 + norm_back(ga, input_gain, normed_one[:part], scaling_one[:part])

    y = (x1 + tp_scatter_sum(dot(z2, down_weight))).astype(bf16)
    layer_output = tp_order(tp_gather(y)).reshape(layer_input.shape)
    grad_input = tp_order(tp_gather(grad_in.astype(bf16))).reshape(layer_input.shape)

    grad_down = t_dot(cp_columns(z2), cp_gather(gy))
    grad_up = t_dot(cp_columns(u), cp_gather(gh))
    grad_out = t_dot(cp_columns(z), cp_gather(gb))
    grad_qkv = t_dot(a_all, grads_own).astype(bf16)
    grad_qkv = lax.all_to_all(
        grad_qkv.reshape(width, 3, head_width // cp_count), "cp", split_axis=0, concat_axis=2, tiled=True
    ).astype(f32)

    def cp_sum_own(vector):
        return jnp.sum(lax.all_to_all(vector.reshape(cp_count, -1), "cp", 0, 0, tiled=True), axis=0)

    def both_sum_own(vector):
        return tp_sum(cp_sum_own(vector))

    return (
        layer_output,
        grad_input,
        grad_qkv,
        grad_out,
        grad_up,
        grad_down,
        both_sum_own(input_gain_sum),
        cp_sum_own(heads_gain_sum),
        both_sum_own(middle_gain_sum),
        cp_sum_own(hidden_gain_sum),
    )


INTERPRET = False


def params(megabytes):
    return pltpu.CompilerParams(vmem_limit_bytes=megabytes * 1024 * 1024)


def shape(dims, kind):
    return jax.ShapeDtypeStruct(dims, kind)


def whole():
    return pl.BlockSpec(memory_space=pltpu.VMEM)


def scalars():
    return pl.BlockSpec(memory_space=pltpu.SMEM)


class Pin:
    def __init__(self, value):
        self.value = value


class Far(Pin):
    def __init__(self, value, dims=None, block=None):
        super().__init__(value)
        self.dims = tuple(value.shape) if dims is None else dims
        self.block = block


class Near:
    def __init__(self, value):
        self.value = value


class Fetched:
    def __init__(self, ref, copy):
        self.ref, self.copy, self.shape = ref, copy, ref.shape

    def ready(self):
        if self.copy is not None:
            self.copy.wait()
            self.copy = None

    def __getitem__(self, index):
        self.ready()
        return self.ref[index]


class Stored:
    def __init__(self, ref, copy):
        self.ref, self.copy, self.shape, self.sent = ref, copy, ref.shape, False

    def send(self):
        if not self.sent:
            self.copy.start()
            self.sent = True

    def __getitem__(self, index):
        return self.ref[index]

    def __setitem__(self, index, value):
        self.ref[index] = value

    @property
    def dtype(self):
        return self.ref.dtype


def plain(value):
    return value.value if isinstance(value, (Pin, Near)) else value


def pinned(value):
    return value if INTERPRET else pltpu.with_memory_space_constraint(value, pltpu.HBM)


def call(
    kernel, outs, args, specs=None, out_specs=None, grid=None, scratch=(), mb=8, cost=0.3, after=(), carry=(), prefetch=0
):
    specs = list(specs) if specs is not None else [whole() for _ in args]
    out_specs = list(out_specs) if out_specs is not None else [whole() for _ in outs]
    count, extra, kept, made = len(args), len(after), len(carry), len(outs)
    anywhere = pl.BlockSpec(memory_space=pl.ANY)
    far_in = [i for i, t in enumerate(args) if isinstance(t, Far)]
    far_out = [i for i, t in enumerate(outs) if isinstance(t, Far)]
    for i in far_in:
        specs[i] = anywhere
    for i in far_out:
        out_specs[i] = anywhere
    moving = [pltpu.VMEM(args[i].dims, args[i].value.dtype) for i in far_in]
    moving += [pltpu.VMEM(outs[i].dims, outs[i].value.dtype) for i in far_out]
    moving += [pltpu.SemaphoreType.DMA] * (len(far_in) + len(far_out))
    own_scratch = len(scratch)

    def run(*refs):
        ins = list(refs[:count])
        results = refs[count + extra + kept :]
        products = list(results[:made])
        rest = results[made + kept :]
        slots, sems = rest[own_scratch : own_scratch + len(far_in) + len(far_out)], rest[own_scratch + len(far_in) + len(far_out) :]
        for i, slot, sem in zip(far_in, slots, sems):
            source = refs[i]
            if args[i].block is not None:
                source = source.at[args[i].block(refs[0])]
            copy = pltpu.make_async_copy(source, slot, sem)
            copy.start()
            ins[i] = Fetched(slot, copy)
        stored = [
            Stored(slot, pltpu.make_async_copy(slot, results[i], sem))
            for i, slot, sem in zip(far_out, slots[len(far_in) :], sems[len(far_in) :])
        ]
        for i, product in zip(far_out, stored):
            products[i] = product
        kernel(*ins, *products, *rest[:own_scratch])
        for i in far_in:
            ins[i].ready()
        for product in stored:
            product.send()
        for product in stored:
            product.copy.wait()

    def result(value):
        dims = plain(value)
        if INTERPRET or value is dims:
            return dims
        return (pltpu.HBM if isinstance(value, Pin) else pltpu.VMEM)(dims.shape, dims.dtype)

    where = dict(
        in_specs=specs + [anywhere] * (extra + kept),
        out_specs=tuple(out_specs + [anywhere] * kept),
        scratch_shapes=list(scratch) + moving,
    )
    if prefetch:
        where["in_specs"] = where["in_specs"][prefetch:]
        where = {"grid_spec": pltpu.PrefetchScalarGridSpec(num_scalar_prefetch=prefetch, grid=grid, **where)}
    elif grid is not None:
        where["grid"] = grid
    return pl.pallas_call(
        run,
        out_shape=tuple(result(t) for t in outs) + tuple(result(Pin(shape(t.shape, t.dtype))) for t in carry),
        input_output_aliases={count + extra + i: made + i for i in range(kept)},
        compiler_params=params(mb),
        cost_estimate=pl.CostEstimate(flops=int(cost * 1e9), bytes_accessed=0, transcendentals=0),
        interpret=INTERPRET,
        **where,
    )(*[pinned(t.value) if isinstance(t, Pin) else t for t in list(args) + list(after)], *[pinned(t) for t in carry])


def bring(items, ids, after=(), carry=(), cost=0.3):
    def kernel(ids, *refs):
        sources, slots, sems = refs[: len(items)], refs[len(items) : 2 * len(items)], refs[2 * len(items) :]
        copies = []
        for (_, _, block), source, slot, sem in zip(items, sources, slots, sems):
            copies.append(pltpu.make_async_copy(source if block is None else source.at[block(ids)], slot, sem))
        for copy in copies:
            copy.start()
        for copy in copies:
            copy.wait()

    return call(
        kernel,
        [Near(shape(dims, array.dtype)) for array, dims, _ in items],
        [ids] + [Pin(array) for array, _, _ in items],
        [scalars()] + [pl.BlockSpec(memory_space=pl.ANY)] * len(items),
        scratch=[pltpu.SemaphoreType.DMA] * len(items), after=after, carry=carry, mb=2, cost=cost,
    )


def fixed(dims):
    return pl.BlockSpec(dims, lambda i: (0,) * len(dims))


def split_low(value):
    high = value.astype(bf16)
    return high, (value - high.astype(f32)).astype(bf16)


def lanes_of(columns, rows):
    lane = lax.broadcasted_iota(jnp.int32, (rows, 128), 1)
    out = jnp.zeros((rows, 128), f32)
    for i, column in enumerate(columns):
        out = jnp.where(lane == i, column.astype(f32), out)
    return out


def pair_sum(block, i):
    return block[:, i : i + 1].astype(f32) + block[:, i + 1 : i + 2].astype(f32)


def own_order(me, part, index):
    return ((index // part) ^ me) * part + index % part


def block_at(me, k, part):
    return pl.ds(pl.multiple_of((me ^ k) * part, part), part)


def swap_pairs(value, axis):
    size = value.shape[axis]
    place = lax.broadcasted_iota(jnp.int32, value.shape, axis)
    return jnp.where(
        place % 2 == 0, pltpu.roll(value, size - 1, axis), pltpu.roll(value, 1, axis)
    )


def tables(local_len, cp_count):
    column = np.arange(HD) // 2
    frequency = 10000.0 ** (-column / (HD // 2))
    zeta = (2.0 * column + 0.4 * HD) / (1.4 * HD)

    def of(places):
        angle = places[:, None] * frequency
        factor = zeta ** (places[:, None] / scale_base)
        return np.stack([np.cos(angle), np.sin(angle), factor, 1.0 / factor]).astype(np.float32)

    return of(np.arange(local_len)), of(np.arange(cp_count) * local_len)


def project_kernel(parts, ids, x, gain, gy, inner, base, seg, w0, w1, w2, pair, gy_out, out):
    me, mine = ids[0], ids[1]
    rows, width = pair.shape[1:]
    part = rows // parts
    heads = out.shape[0]
    x.ready()
    for k in range(parts):
        normed, _ = norm_rows(x.ref[block_at(me, k, part), :].astype(f32))
        pair[0, k * part : (k + 1) * part, :] = (normed * gain[...]).astype(bf16)
    gy.ready()
    for k in range(parts):
        block = gy.ref[block_at(me, k, part), :]
        pair[1, k * part : (k + 1) * part, :] = block
        gy_out[k * part : (k + 1) * part, :] = block
    pair.send()
    gy_out.send()
    inner.ready()
    here = [base[kind, pl.ds(mine, 1), :] for kind in range(4)]
    table = [
        jnp.concatenate([inner.ref[kind, block_at(me, k, part), :] for k in range(parts)], axis=0)
        for kind in range(4)
    ]
    cosine = table[0] * here[0] - table[1] * here[1]
    sine = table[1] * here[0] + table[0] * here[1]
    lane = lax.broadcasted_iota(jnp.int32, cosine.shape, 1)
    sine = jnp.where(lane % 2 == 0, -sine, sine)
    place = lax.broadcasted_iota(jnp.int32, (rows, rows), 1)
    source = lax.broadcasted_iota(jnp.int32, (rows, rows), 0)
    moved = (own_order(me, part, place) == source).astype(bf16)
    ids_row = jnp.broadcast_to(seg[...].astype(f32), (16, rows)).astype(bf16)
    ordered = dot(ids_row, moved).astype(bf16)
    for j in range(heads):
        out[j, 3 * HD : 3 * HD + 16, :] = ordered
    for c, weight in enumerate((w0, w1, w2)):
        acc = dot(pair[0], weight[0])
        factor = (table[2] * here[2], table[3] * here[3], None)[c]
        for i in range(acc.shape[1] // 128):
            piece = acc[:, i * 128 : (i + 1) * 128]
            if c < 2:
                piece = piece * (cosine * factor) + swap_pairs(piece, 1) * (sine * factor)
            turned = piece.T.astype(bf16)
            for h in range(128 // HD):
                out[i * (128 // HD) + h, c * HD : (c + 1) * HD, :] = turned[h * HD : (h + 1) * HD]
    out.send()


def gather_heads(got, keys, ids_col, values=None):
    for j in range(got.shape[0]):
        rows = slice(j * got.shape[2], (j + 1) * got.shape[2])
        both = jnp.concatenate([got[j, HD : 3 * HD, :].astype(f32)], axis=0).T
        keys[rows, :] = both[:, :HD].astype(bf16)
        if values is not None:
            values[rows, :] = both[:, HD:].astype(bf16)
        ids_col[rows, :] = got[j, 3 * HD : 3 * HD + 16, :].astype(f32).T


def visible_scores(me, part, scores, ids_col, ids_row, count, first, group):
    same = ids_col[0:count, 0:1] == ids_row
    length = group
    key = lax.broadcasted_iota(jnp.int32, (length, length), 0)
    query = lax.broadcasted_iota(jnp.int32, (length, length), 1)
    rows = first
    own = lambda index: (index // rows) * rows + own_order(me, part, index % rows)
    earlier = own(key) <= own(query)
    if count > length:
        earlier = jnp.concatenate([jnp.ones((count - length, length), jnp.bool_), earlier], axis=0)
    return same & earlier


def attend_kernel(parts, ids, got, out, mixed, lse, kept, keys, ids_col):
    me = ids[0]
    kept[...] = got[...]
    kept.send()
    blocks, _, rows = got.shape
    part = rows // parts
    gather_heads(got, keys, ids_col)
    group = 2 if blocks % 2 == 0 else 1
    width = group * rows
    for i in range(blocks // group):
        mine = range(i * group, (i + 1) * group)
        query = jnp.concatenate([got[j, :HD, :] for j in mine], axis=1) * bf16(HD**-0.5)
        ids_row = jnp.concatenate([got[j, 3 * HD : 3 * HD + 1, :] for j in mine], axis=1).astype(f32)
        count = (i + 1) * width
        scores = dot(keys[0:count, :], query)
        allowed = visible_scores(me, part, scores, ids_col, ids_row, count, rows, width)
        scores = jnp.where(allowed, scores, masked_score)
        top = jnp.max(scores, axis=0, keepdims=True)
        exponent = jnp.exp(scores - top)
        total = jnp.sum(exponent, axis=0, keepdims=True)
        value = jnp.concatenate([got[j, 2 * HD : 3 * HD, :] for j in range((i + 1) * group)], axis=1)
        result = dot(value, exponent.astype(bf16)) / total
        mixed[:, i * width : (i + 1) * width] = result
        lse[:, i * width : (i + 1) * width] = top + jnp.log(total)
        for n, j in enumerate(mine):
            out[j] = result[:, n * rows : (n + 1) * rows].astype(bf16)
    out.send()


def store_pieces(total, own, pieces, part, extra=None):
    own[:, : total.shape[1]] = total[:part]
    for k, piece in enumerate(pieces, 1):
        piece[:, : total.shape[1]] = total[k * part : (k + 1) * part].astype(bf16)
    if extra is not None:
        own[:, total.shape[1] :] = extra[:part]
        for k, piece in enumerate(pieces, 1):
            piece[:, total.shape[1] :] = extra[k * part : (k + 1) * part].astype(bf16)


def fold_row(row, part):
    block = jnp.concatenate([row[:, i : i + 128] for i in range(0, row.shape[1], 128)], axis=0)
    return jnp.concatenate(split_low(block), axis=0)


def unfold_row(block):
    half = block.shape[0] // 2
    total = block[:half].astype(f32) + block[half:].astype(f32)
    return jnp.concatenate([total[i : i + 1] for i in range(half)], axis=1)


def out_kernel(parts, att, gain, weight, own, *refs):
    pieces, kept = refs[:-1], refs[-1]
    kept[...] = att[...]
    blocks, _, rows = att.shape
    part, width = rows // parts, weight.shape[1]
    value = jnp.concatenate([att[j].astype(f32) for j in range(blocks)], axis=0).T
    high, low = split_low(jnp.mean(value, axis=1, keepdims=True))
    centred = value - (high.astype(f32) + low.astype(f32))
    square = split_low(jnp.sum(centred * centred, axis=1, keepdims=True))
    gains = gain[...]
    row = lax.broadcasted_iota(jnp.int32, (16, gains.shape[1]), 0)
    gain_high, gain_low = (t.astype(f32) for t in split_low(gains))
    gain_rows = jnp.where(row == 0, gain_high, jnp.where(row == 1, gain_low, 0.0))
    left = jnp.concatenate([(centred * gains).astype(bf16), gain_rows.astype(bf16)], axis=0)
    total = dot(left, weight[...])
    folded = fold_row(total[rows : rows + 1] + total[rows + 1 : rows + 2], part)
    stats = lanes_of([high, low, *square], rows).astype(bf16)
    own[:, :width] = total[:part]
    own[:, width : width + 128] = stats[:part].astype(f32)
    own[:, width + 128 :] = folded.astype(f32)
    for k, piece in enumerate(pieces, 1):
        here = slice(k * part, (k + 1) * part)
        piece[:, :width] = total[here].astype(bf16)
        piece[:, width : width + 128] = stats[here]
        piece[:, width + 128 :] = folded


def middle_kernel(parts, head_width, own, *refs):
    got, (x, gain, x1, u, gain_row) = refs[: parts - 1][::-1], refs[parts - 1 :]
    part, width = x1.shape
    blocks = [own] + list(got)
    stats = [b[:, width : width + 128] for b in blocks]
    means = [pair_sum(b, 0) for b in stats]
    squares = [pair_sum(b, 2) for b in stats]
    rows = [unfold_row(b[:, width + 128 :]) for b in blocks]
    gain_row[...] = sum(rows)
    mean = sum(means) / parts
    spread = sum(squares) + head_width * sum((m - mean) * (m - mean) for m in means)
    scaling = lax.rsqrt(spread / width + eps)
    total = sum(b[:, :width].astype(f32) for b in blocks)
    for m, row in zip(means, rows):
        total = total + (m - mean) * row
    value = x[...].astype(f32) + total * scaling
    x1[...] = value
    normed, _ = norm_rows(value)
    u[:, :width] = (normed * gain[...]).astype(bf16)
    u[:, width:] = lanes_of([*split_low(mean), *split_low(scaling)], part).astype(bf16)


def grad_hidden_kernel(gy, weight, grad):
    grad[...] = dot_t(gy[...], weight[...])


def prepare_kernel(step, up, near_up, flipped, up_sems):
    chunks = [slice(i, i + step) for i in range(0, up.shape[0], step)]
    copies = [pltpu.make_async_copy(up.at[c, :], near_up.at[c, :], up_sems.at[i]) for i, c in enumerate(chunks)]
    for copy in copies:
        copy.start()
    for copy, chunk in zip(copies, chunks):
        copy.wait()
        flipped[:, chunk] = near_up[chunk, :].T


def up_kernel(parts, step, own, *refs):
    got, refs = refs[: parts - 1][::-1], refs[parts - 1 :]
    weight, grad, gain, act, slope, u, stats, tail, rows_u = refs
    part = own.shape[0]
    rows, width = rows_u.shape
    for k, block in enumerate([own] + list(got)):
        rows_u[k * part : (k + 1) * part, :] = block[:, :width]
        tail[k * part : (k + 1) * part, :] = block[:, width:].astype(f32)
    wide = u.shape[2]
    for j in range(u.shape[0]):
        u[j] = rows_u[:, j * wide : (j + 1) * wide]
    total = [jnp.zeros((rows, 128), f32)] * 4
    for i in range(0, weight.shape[1], step):
        here = slice(i, i + step)
        hidden = dot(rows_u[...], weight[:, here])
        cdf = 0.5 * (1.0 + lax.erf(hidden * (0.5**0.5)))
        value = hidden * cdf
        act[:, here] = value
        slope[:, here] = cdf + hidden * jnp.exp(-0.5 * hidden * hidden) * 0.3989422804014327
        grad_normed = grad[:, here] * gain[:, here]
        columns = [value, value * value, grad_normed, grad_normed * value]
        for n, column in enumerate(columns):
            for j in range(0, step, 128):
                total[n] = total[n] + column[:, j : j + 128]
    sums = lanes_of([jnp.sum(t, axis=1, keepdims=True) for t in total], rows)
    stats[...] = sums.T[:8, :]


def swap_lane_blocks(value, k, part):
    lanes = value.shape[1]
    lane = lax.broadcasted_iota(jnp.int32, value.shape, 1)
    distance = 1
    while distance <= k:
        if k & distance:
            move = distance * part
            value = jnp.where(
                (lane // move) % 2 == 0,
                pltpu.roll(value, lanes - move, 1),
                pltpu.roll(value, move, 1),
            )
        distance *= 2
    return value


def hidden_back_kernel(parts, full, step, own, *refs):
    got, refs = refs[: parts - 1][::-1], refs[parts - 1 :]
    act, slope, grad, gain, weight, u, gh, both, own_out = refs[:9]
    pieces = refs[9:]
    first_wide = u.shape[2]
    both[:, :, :first_wide] = u[...]
    rows = act.shape[0]
    part = rows // parts
    total = own[...]
    for k, block in enumerate(got, 1):
        total = total + swap_lane_blocks(block[...], k, part)
    mean = total[0:1] / full
    scaling = lax.rsqrt(total[1:2] / full - mean * mean + eps)
    first = total[2:3] / full
    cross = scaling * (total[3:4] / full - mean * first)
    row = lax.broadcasted_iota(jnp.int32, (rows, rows), 0)
    table = jnp.zeros((rows, rows), f32)
    for i, value in enumerate([mean, scaling, first, cross]):
        table = jnp.where(row == i, value, table)
    cols = table.T
    mean, scaling, first, cross = (cols[:, i : i + 1] for i in range(4))
    wide = both.shape[2] - first_wide
    for i in range(0, act.shape[1], step):
        here = slice(i, i + step)
        normed = (act[:, here] - mean) * scaling
        low = (normed * gain[:, here]).astype(bf16)
        for j in range(0, step, wide):
            both[(i + j) // wide, :, first_wide:] = low[:, j : j + wide]
        value = scaling * (grad[:, here] * gain[:, here] - first - normed * cross) * slope[:, here]
        gh[:, here] = value.astype(bf16)
    both.send()
    gh.send()
    width = weight.shape[1]
    for i in range(0, width, step):
        here = slice(i, i + step)
        result = dot(gh[...], weight[:, here])
        own_out[:, here] = result[:part]
        for k, piece in enumerate(pieces, 1):
            piece[:, here] = result[k * part : (k + 1) * part].astype(bf16)


def down_kernel(z2, *refs):
    weights, (own, second, odd) = refs[:-3], refs[-3:]
    _, _, wide = z2.shape
    part = own.shape[0]
    total = 0.0
    for i, weight in enumerate(weights):
        rows = weight.shape[0]
        left = jnp.concatenate([z2[j] for j in range(i * rows // wide, (i + 1) * rows // wide)], axis=1)
        total = total + dot(left, weight[...])
    own[...] = total[:part]
    second[...] = total[2 * part : 3 * part]
    odd[:part, :] = total[part : 2 * part].astype(bf16)
    odd[part:, :] = total[3 * part :].astype(bf16)


def half_kernel(second, got, out):
    part = second.shape[0]
    out[...] = (second[...] + got[part:, :].astype(f32)).astype(bf16)


def join_kernel(first, second, out):
    part = first.shape[0]
    out[:part, :] = first[...]
    out[part:, :] = second[...]


def middle_back_kernel(parts, own, *refs):
    got, refs = refs[: parts - 1][::-1], refs[parts - 1 :]
    gain_row, x, x1, gy, gain, gx1, gb = refs
    part, width = x1.shape
    grad = own[...]
    for block in got:
        grad = grad + block[...].astype(f32)
    value = x1[...]
    normed, scaling = norm_rows(value)
    result = gy[...].astype(f32) + norm_back(grad, gain[...], normed, scaling)
    gx1[...] = result
    low = result.astype(bf16)
    gb[:, :width] = low
    low = low.astype(f32)
    first = jnp.sum(low * gain_row[...], axis=1, keepdims=True) / width
    cross = jnp.sum(low * (value - x[...].astype(f32)), axis=1, keepdims=True) / width
    gb[:, width:] = lanes_of([*split_low(first), *split_low(cross)], part).astype(bf16)


def heads_back_kernel(parts, own, *refs):
    got, refs = refs[: parts - 1][::-1], refs[parts - 1 :]
    stats, att, gain, weight, sent, gb = refs
    blocks, _, rows = att.shape
    part, width = own.shape[0], gb.shape[1]
    for k, block in enumerate([own] + list(got)):
        gb[k * part : (k + 1) * part, :] = block[:, :width]
    gb.send()
    columns = jnp.concatenate([b[:, width:].astype(f32) for b in [own] + list(got)], axis=0).T
    first = columns[0:1] + columns[1:2]
    cross = columns[2:3] + columns[3:4]
    columns = stats[...].T
    mean = columns[0:1] + columns[1:2]
    scaling = columns[2:3] + columns[3:4]
    grad = dot_t(weight[...], gb[...])
    value = jnp.concatenate([att[j].astype(f32) for j in range(blocks)], axis=0)
    normed = (value - mean) * scaling
    gain_col = jnp.broadcast_to(gain[...], (8, gain.shape[1])).T[:, 0:1]
    go = (scaling * (grad * gain_col - first - normed * cross)).astype(bf16)
    z = (normed * gain_col).astype(bf16)
    for j in range(blocks):
        sent[j, :HD, :] = go[j * HD : (j + 1) * HD]
        sent[j, HD:, :] = z[j * HD : (j + 1) * HD]


def turn_back(grad, table, base, j, inverse):
    here = [base[kind, :, j : j + 1] for kind in range(4)]
    cosine = table[0] * here[0] - table[1] * here[1]
    sine = table[1] * here[0] + table[0] * here[1]
    factor = table[3] * here[3] if inverse else table[2] * here[2]
    row = lax.broadcasted_iota(jnp.int32, grad.shape, 0)
    sine = jnp.where(row % 2 == 0, sine, -sine)
    return (grad * cosine + swap_pairs(grad, 0) * sine) * factor


def attend_back_kernel(parts, ids, got, grads, mixed, lse, inner, base, out, z, keys, values, ids_col, gk, gv):
    me = ids[0]
    for j in range(grads.shape[0]):
        z[j] = grads[j, HD:, :]
    z.send()
    blocks, _, rows = got.shape
    part = rows // parts
    gather_heads(got, keys, ids_col, values)
    gk[...] = jnp.zeros_like(gk)
    gv[...] = jnp.zeros_like(gv)
    table = []
    for kind in range(4):
        ordered = jnp.concatenate(
            [inner[kind, block_at(me, k, part), :] for k in range(parts)], axis=0
        )
        table.append(ordered.T[:HD])
    group = 2 if blocks % 2 == 0 else 1
    width = group * rows
    for i in range(blocks // group):
        mine = range(i * group, (i + 1) * group)
        query = jnp.concatenate([got[j, :HD, :] for j in mine], axis=1) * bf16(HD**-0.5)
        ids_row = jnp.concatenate([got[j, 3 * HD : 3 * HD + 1, :] for j in mine], axis=1).astype(f32)
        go = jnp.concatenate([grads[j, :HD, :] for j in mine], axis=1)
        span = slice(i * width, (i + 1) * width)
        delta = jnp.sum(go.astype(f32) * mixed[:, span], axis=0, keepdims=True)
        count = (i + 1) * width
        scores = dot(keys[0:count, :], query)
        allowed = visible_scores(me, part, scores, ids_col, ids_row, count, rows, width)
        probability = jnp.where(allowed, jnp.exp(jnp.minimum(scores - lse[:, span], 0.5)), 0.0)
        grad_prob = dot(values[0:count, :], go)
        grad_scores = (probability * (grad_prob - delta)).astype(bf16)
        gv[:, 0:count] += dot_t(go, probability.astype(bf16))
        gk[:, 0:count] += dot_t(query, grad_scores)
        key = jnp.concatenate([got[j, HD : 2 * HD, :] for j in range((i + 1) * group)], axis=1)
        gq = dot(key, grad_scores) * HD**-0.5
        for n, j in enumerate(mine):
            piece = turn_back(gq[:, n * rows : (n + 1) * rows], table, base, j, False)
            out[j, :HD, :] = piece.astype(bf16)
    for j in range(blocks):
        span = slice(j * rows, (j + 1) * rows)
        out[j, HD : 2 * HD, :] = turn_back(gk[:, span], table, base, j, True).astype(bf16)
        out[j, 2 * HD :, :] = gv[:, span].astype(bf16)


def input_back_kernel(parts, step, got, w0, w1, w2, own_out, *pieces):
    part, width = own_out.shape
    grads = []
    for c in range(3):
        here = slice(c * HD, (c + 1) * HD)
        grad = jnp.concatenate([got[j, here, :].astype(f32) for j in range(got.shape[0])], axis=0)
        grads.append(grad.T.astype(bf16))
    result = dot_t(grads[0], w0[0]) + dot_t(grads[1], w1[0]) + dot_t(grads[2], w2[0])
    own_out[...] = result[:part]
    for k, piece in enumerate(pieces, 1):
        piece[...] = result[k * part : (k + 1) * part].astype(bf16)


def final_kernel(parts, own, *refs):
    got, (x, gx1, gain, gains, out) = refs[: parts - 1][::-1], refs[parts - 1 :]
    part, width = gx1.shape
    grad = own[...]
    for block in got:
        grad = grad + block[...].astype(f32)
    normed, scaling = norm_rows(x[...].astype(f32))
    out[:, :width] = (gx1[...] + norm_back(grad, gain[...], normed, scaling)).astype(bf16)
    rows = gains[0:2]
    pieces = [rows[n : n + 1, i : i + 128] for n in range(2) for i in range(0, rows.shape[1], 128)]
    high, low = split_low(jnp.concatenate(pieces, axis=0))
    empty = jnp.zeros((part - 2 * len(pieces), 128), f32)
    tail = jnp.concatenate([high.astype(f32), low.astype(f32), empty], axis=0)
    out[:, width:] = tail.astype(bf16)


def output_kernel(own, got, last, x1, out):
    total = own[...] + x1[...] + got[: out.shape[0], :].astype(f32)
    out[...] = (total + last[...].astype(f32)).astype(bf16)


def natural_kernel(ids, *refs):
    blocks, out = refs[:-1], refs[-1]
    part = blocks[0].shape[0]
    for k, block in enumerate(blocks):
        out[block_at(ids[0], k, part), :] = block[...]


def own_row(gain, index, own):
    total = jnp.zeros((1, own), f32)
    for j in range(gain.shape[1] // own):
        total = jnp.where(index == j, gain[:, j * own : (j + 1) * own], total)
    return total


def row_of(column, columns):
    return jnp.broadcast_to(column, (columns, 128)).T[:1, :]


def product_kernel(step, columns, which, offset, ids, left, right, *refs):
    count = left.shape[0]
    gains = len(refs) > 7
    if gains:
        (weight, gain, out, gain_grad), refs = refs[:4], refs[4:]
        (near_weight, weight_sem), refs = refs[-2:], refs[:-2]
    else:
        out, refs = refs[0], refs[1:]
    left_all, right_all, result, left_sems, right_sems, out_sems = refs
    rows, size = right.shape[-2:]
    own = result.shape[0]
    tokens = count * rows
    chunks = [slice(i, i + step) for i in range(0, size, step)]

    first = []
    for r in range(count):
        source = left.at[r]
        if columns:
            source, place = source.at[:, pl.ds(offset, own)], left_all.at[pl.ds(r * rows, rows), :]
        else:
            source, place = source.at[pl.ds(offset, own), :], left_all.at[r]
        first.append(pltpu.make_async_copy(source, place, left_sems.at[r]))
    side = right if which is None else right.at[:, which]
    later = [
        [pltpu.make_async_copy(side.at[:, :, c], right_all.at[:, :, c], right_sems.at[i])] for i, c in enumerate(chunks)
    ]
    for copy in first + later[0]:
        copy.start()
    if gains:
        fetch = pltpu.make_async_copy(
            weight.at[pl.ds(pl.multiple_of(ids[1] * own, own), own), :], near_weight, weight_sem
        )
        fetch.start()
    for copies in later[1:]:
        for copy in copies:
            copy.start()
    for copy in first:
        copy.wait()
    if not columns:
        value = jnp.concatenate([left_all[r] for r in range(count)], axis=1)
    sums = jnp.zeros((own, 128), f32)
    sent = []
    for i, (c, copies) in enumerate(zip(chunks, later)):
        for copy in copies:
            copy.wait()
        block = right_all[:, :, c].reshape(tokens, step)
        grad = t_dot(left_all[...], block) if columns else dot(value, block)
        result[:, c] = grad.astype(result.dtype)
        if gains:
            if i == 0:
                fetch.wait()
            product = grad * near_weight[:, c].astype(f32)
            for j in range(0, step, 128):
                sums = sums + product[:, j : j + 128]
            moves = [pltpu.make_async_copy(result.at[:, c], out.at[:, c], out_sems.at[i, 0])]
        else:
            wide = out.shape[2]
            moves = [
                pltpu.make_async_copy(
                    result.at[:, pl.ds(j, wide)], out.at[j // wide], out_sems.at[i, (j - c.start) // wide]
                )
                for j in range(c.start, c.stop, wide)
            ]
        for move in moves:
            move.start()
        sent.extend(moves)
    if gains:
        gain_grad[...] = row_of(jnp.sum(sums, axis=1, keepdims=True), own) / own_row(gain, ids[1], own)
    for copy in sent:
        copy.wait()


def grad_qkv_place_kernel(ids, got, weight, gain, up_gain, out, gain_grads):
    total = 0.0
    for c in range(3):
        value = jnp.concatenate(
            [got[j, c * HD : (c + 1) * HD, :].astype(f32) for j in range(got.shape[0])], axis=0
        ).T
        out[c] = value
        total = total + jnp.sum(value * weight[c].astype(f32), axis=1, keepdims=True)
    out.send()
    first = row_of(total, total.shape[0]) / own_row(gain, ids[1], total.shape[0])
    row = lax.broadcasted_iota(jnp.int32, gain_grads.shape, 0)
    gain_grads[...] = jnp.where(row == 0, first, up_gain[...])


def outputs_kernel(parts, ids, *refs):
    blocks, (y_even, y_odd, out, y, first, second) = refs[:parts], refs[parts:]
    part, width = blocks[0].shape[0], out.shape[1]
    for k in range(parts):
        out[block_at(ids[0], k, part), :] = blocks[-k % parts][:, :width]
        both = y_odd if k % 2 else y_even
        y[block_at(ids[0], k, part), :] = both[k // 2 * part : (k // 2 + 1) * part, :]
    out.send()
    y.send()
    count = first.shape[1] // 128
    total = sum(b[:, width:].astype(f32) for b in blocks)
    total = total[: 2 * count] + total[2 * count : 4 * count]
    for i in range(count):
        first[:, i * 128 : (i + 1) * 128] = total[i : i + 1]
        second[:, i * 128 : (i + 1) * 128] = total[count + i : count + i + 1]


def body(
    layer_input,
    segment_ids,
    qkv_weight,
    out_weight,
    up_weight,
    down_weight,
    input_gain,
    heads_gain,
    middle_gain,
    hidden_gain,
    cotangent,
):
    rows, row_count, width = layer_input.shape
    T, C = lax.axis_size("tp"), lax.axis_size("cp")
    part = rows // T
    head_width = qkv_weight.shape[2]
    if head_width // HD != C or row_count != 1 or rows != 128 or T != 4 or 64 * part != width:
        return body_general(
            layer_input, segment_ids, qkv_weight, out_weight, up_weight, down_weight,
            input_gain, heads_gain, middle_gain, hidden_gain, cotangent,
        )
    tokens = rows * C
    hidden = up_weight.shape[1]
    wide = width // C
    high = hidden // C
    ids = jnp.stack([lax.axis_index("tp"), lax.axis_index("cp")]).astype(jnp.int32)
    x = layer_input.reshape(rows, width)
    gy = cotangent.reshape(rows, width)
    weight3 = jnp.transpose(qkv_weight, (1, 0, 2))
    gain_in, gain_mid = input_gain.reshape(1, -1), middle_gain.reshape(1, -1)
    gain_heads, gain_hid = heads_gain.reshape(1, -1), hidden_gain.reshape(1, -1)
    inner, base = tables(rows, C)
    inner2 = jnp.asarray(np.concatenate([inner, inner], axis=2))
    base2 = jnp.asarray(np.concatenate([base, base], axis=2))
    base_t = np.zeros((4, HD, 128), np.float32)
    base_t[:, :, :C] = np.transpose(base, (0, 2, 1))
    base_t = jnp.asarray(base_t)
    wide_part = width + 128
    step = 512

    def piece_shapes(columns):
        return [shape((part, columns), f32)] + [shape((part, columns), bf16)] * (T - 1)

    def exchange(pieces):
        return [swap_tp(pieces[k - 1], k) for k in range(T - 1, 0, -1)]

    def spread(block):
        return exchange([block] * (T - 1))

    def to_cp(value):
        return lax.all_to_all(value, "cp", 0, 0, tiled=True)

    def entire(value):
        return (value, value.shape, None)

    def own_rows(value):
        return (value, (part, width), lambda ids: (block_at(ids[0], 0, part), slice(None)))

    def third(c):
        return lambda ids: (pl.ds(c, 1), slice(None), slice(None))

    cols, first_rows = lambda i, *_: (0, i), lambda i, *_: (i, 0)
    origin2, origin3 = lambda i, *_: (0, 0), lambda i, *_: (0, 0, 0)
    weight_thirds = [Far(weight3, (1, width, head_width), third(c)) for c in range(3)]

    pair, gy_x, sent = call(
        functools.partial(project_kernel, T),
        [Far(shape((2, rows, width), bf16)), Far(shape((rows, width), bf16)), Far(shape((C, 3 * HD + 16, rows), bf16))],
        [ids, Far(x), Far(gain_in), Far(gy), Far(inner2), Far(base2), Far(segment_ids.reshape(1, rows)), *weight_thirds],
        [scalars()] + [whole()] * 9, mb=14,
    )
    got = to_cp(sent)
    near_out, near_x, near_gy, near_mid, near_heads, near_hid, near_in = bring(
        [entire(out_weight), own_rows(x), own_rows(gy), entire(gain_mid), entire(gain_heads),
         entire(gain_hid), entire(gain_in)],
        ids, after=[Pin(sent)],
    )
    back, mixed, lse, far_got, pair = call(
        functools.partial(attend_kernel, T),
        [Far(shape((C, HD, rows), bf16)), Far(shape((HD, tokens), f32)), Far(shape((1, tokens), f32)),
         Far(shape((C, 3 * HD + 16, rows), bf16))],
        [ids, got], [scalars(), whole()],
        scratch=[pltpu.VMEM((tokens, HD), bf16), pltpu.VMEM((tokens, 16), f32)],
        mb=10, after=[near_heads], carry=[pair],
    )
    att = to_cp(back)
    early = lax.all_gather(pair, "cp", axis=0)

    own, *pieces, near_att = call(
        functools.partial(out_kernel, T),
        piece_shapes(width + 256) + [Near(shape((C, HD, rows), bf16))],
        [att, near_heads, near_out],
    )
    (grad_hid,) = call(
        grad_hidden_kernel, [Near(shape((rows, hidden), f32))],
        [Pin(gy_x), Pin(down_weight)],
        [fixed((rows, width)), pl.BlockSpec((step, width), first_rows)],
        [pl.BlockSpec((rows, step), cols)],
        grid=(hidden // step,), after=[own], mb=10, cost=3,
    )
    x1, u_own, gain_row = call(
        functools.partial(middle_kernel, T, head_width),
        [Near(shape((part, width), f32)), shape((part, wide_part), bf16), Near(shape((1, width), f32))],
        [own, *exchange(pieces), near_x, near_mid], after=[grad_hid],
    )
    u_blocks = [u_own] + spread(u_own)
    near_up, near_flip = call(
        functools.partial(prepare_kernel, 256),
        [Near(shape((width, hidden), bf16)), Near(shape((hidden, width), bf16))],
        [Pin(up_weight)], [pl.BlockSpec(memory_space=pl.ANY)],
        scratch=[pltpu.SemaphoreType.DMA((width // 256,))], after=[u_own], mb=6,
    )

    act, slope, u_cols, stats, near_tail = call(
        functools.partial(up_kernel, T, step),
        [Near(shape((rows, hidden), f32)), Near(shape((rows, hidden), f32)), Near(shape((C, rows, wide), bf16)),
         shape((8, rows), f32), Near(shape((rows, 128), f32))],
        [*u_blocks, near_up, grad_hid, near_hid],
        scratch=[pltpu.VMEM((rows, width), bf16)], mb=8, after=[near_flip],
    )
    gh, both, own, *pieces = call(
        functools.partial(hidden_back_kernel, T, FF, step),
        [Far(shape((rows, hidden), bf16)), Far(shape((C, rows, wide + high), bf16))] + piece_shapes(width),
        [stats, *spread(stats), act, slope, grad_hid, near_hid, near_flip, u_cols], mb=10,
    )
    gu_got = exchange(pieces)
    both_got = to_cp(both)
    gh_all = lax.all_gather(gh, "cp", axis=0)
    down_parts = [
        Far(down_weight, (step, width), (lambda at: lambda ids: (pl.ds(at, step), slice(None)))(i))
        for i in range(0, hidden, step)
    ]
    gx1, gb_own = call(
        functools.partial(middle_back_kernel, T),
        [Near(shape((part, width), f32)), shape((part, wide_part), bf16)],
        [own, *gu_got, gain_row, near_x, x1, near_gy, near_mid], cost=8,
    )
    gb_blocks = [gb_own] + spread(gb_own)
    y_own, y_second, y_odd = call(
        down_kernel,
        [Far(shape((part, width), f32)), Far(shape((part, width), f32)), Far(shape((2 * part, width), bf16))],
        [Far(both, (C, rows, high), lambda ids: (slice(None), slice(None), pl.ds(wide, high))), *down_parts],
        after=[gb_own], cost=20, mb=14,
    )
    (near_out,) = bring([entire(out_weight)], ids, after=[gb_own])

    def product(left, right, columns, which, offset, own, after, weight=None, gain=None, cost=20):
        anywhere = pl.BlockSpec(memory_space=pl.ANY)
        size = right.shape[-1]
        chunk = 2 * step
        left_dims = (tokens, own) if columns else (C, own, rows)
        if weight is not None:
            outs = [Pin(shape((own, size), f32)), shape((1, own), f32)]
            more, more_specs = [Pin(weight), gain], [anywhere, whole()]
            out_specs, extra = [anywhere, whole()], [pltpu.VMEM((own, size), bf16), pltpu.SemaphoreType.DMA]
        else:
            outs, out_specs = [Pin(shape((C, own, size // C), bf16))], [anywhere]
            more, more_specs, extra = [], [], []
        return call(
            functools.partial(product_kernel, chunk, columns, which, offset), outs,
            [ids, Pin(left), Pin(right), *more], [scalars()] + [anywhere] * 2 + more_specs, out_specs,
            scratch=[pltpu.VMEM(left_dims, bf16), pltpu.VMEM((C, rows, size), bf16),
                     pltpu.VMEM((own, size), plain(outs[0]).dtype),
                     pltpu.SemaphoreType.DMA((C,)), pltpu.SemaphoreType.DMA((size // chunk,)),
                     pltpu.SemaphoreType.DMA((size // chunk, chunk * C // size))] + extra,
            mb=14, after=after, cost=cost,
        )


    sent, gb, y_odd = call(
        functools.partial(heads_back_kernel, T),
        [Far(shape((C, 2 * HD, rows), bf16)), Far(shape((rows, width), bf16))],
        [*gb_blocks, near_tail, near_att, near_heads, near_out], after=[Pin(both_got)], carry=[y_odd],
    )
    y_got = swap_tp(y_odd, 1)
    gb_all = lax.all_gather(gb, "cp", axis=0)
    grads = to_cp(sent)
    near_got, near_mixed, near_lse, near_inner, near_base = bring(
        [entire(far_got), entire(mixed), entire(lse), entire(inner2), entire(base_t)], ids, after=[Pin(sent)]
    )
    grad_down, hidden_gain_grad = product(both_got, early, True, 1, wide, high, [Pin(sent)], down_weight, gain_hid)
    (y_half,) = call(half_kernel, [shape((part, width), bf16)], [Far(y_second), y_got], after=[Pin(sent)])
    y_last = swap_tp(y_half, 2)
    gq_sent, z = call(
        functools.partial(attend_back_kernel, T),
        [Far(shape((C, 3 * HD, rows), bf16)), Far(shape((C, HD, rows), bf16))],
        [ids, near_got, grads, near_mixed, near_lse, near_inner, near_base], [scalars()] + [whole()] * 6,
        scratch=[pltpu.VMEM((tokens, HD), bf16), pltpu.VMEM((tokens, HD), bf16), pltpu.VMEM((tokens, 16), f32),
                 pltpu.VMEM((HD, tokens), f32), pltpu.VMEM((HD, tokens), f32)],
        mb=12, cost=8, after=[Pin(grad_down), y_half],
    )
    gq = to_cp(gq_sent)
    (y_low,) = call(
        output_kernel, [shape((part, width), bf16)], [Far(y_own), y_got, y_last, x1], after=[Pin(gq_sent)]
    )
    y_even = swap_tp(y_low, 2)
    (grad_qkv,) = product(gq_sent, early, False, 0, 0, 3 * HD, [y_low])
    own, *pieces = call(
        functools.partial(input_back_kernel, T, step), piece_shapes(width), [gq, *weight_thirds], mb=10, cost=10,
    )
    ga_got = exchange(pieces)
    (y_even,) = call(join_kernel, [shape((2 * part, width), bf16)], [y_low, y_even], after=[own])
    y_odd = swap_tp(y_even, 1)
    grad_qkv_got = to_cp(grad_qkv)
    grad_up, up_gain = product(both_got, gh_all, True, None, 0, wide, [own], up_weight, gain_mid)
    own_wide = lambda ids: (slice(None), pl.ds(pl.multiple_of(ids[1] * wide, wide), wide), slice(None))
    grad_qkv, gains = call(
        grad_qkv_place_kernel,
        [Far(shape((3, wide, head_width), f32)), shape((8, wide), f32)],
        [ids, grad_qkv_got, Far(weight3, (3, wide, head_width), own_wide), gain_in, up_gain],
        [scalars()] + [whole()] * 4, after=[own], cost=20,
    )
    (final,) = call(
        functools.partial(final_kernel, T),
        [shape((part, wide_part), bf16)],
        [own, *ga_got, near_x, gx1, near_in, gains], after=[Pin(grad_up)],
    )
    final_blocks = [final] + spread(final)
    grad_out, heads_gain_grad = product(z, gb_all, False, None, 0, HD, [final], out_weight, gain_heads)
    grad_input, layer_output, input_gain_grad, middle_gain_grad = call(
        functools.partial(outputs_kernel, T),
        [Far(shape((rows, width), bf16))] * 2 + [shape((1, wide), f32), shape((1, wide), f32)],
        [ids, *final_blocks, y_even, y_odd], [scalars()] + [whole()] * (T + 2), after=[Pin(grad_out)],
    )
    return (
        layer_output.reshape(layer_input.shape),
        grad_input.reshape(layer_input.shape),
        jnp.transpose(grad_qkv, (1, 0, 2)),
        grad_out,
        grad_up,
        grad_down,
        input_gain_grad.reshape(-1),
        heads_gain_grad.reshape(-1),
        middle_gain_grad.reshape(-1),
        hidden_gain_grad.reshape(-1),
    )


def solution(mesh):
    placed = (
        P("cp", None, None),
        P("cp", None),
        P(None, None, "tp"),
        P("tp", None),
        P(None, "tp"),
        P("tp", None),
        P(),
        P("tp"),
        P(),
        P("tp"),
        P("cp", None, None),
    )
    return jax.shard_map(
        body,
        mesh=mesh,
        in_specs=placed,
        out_specs=(
            P("cp", None, None),
            P("cp", None, None),
            P("cp", None, "tp"),
            P(("tp", "cp"), None),
            P("cp", "tp"),
            P(("tp", "cp"), None),
            P("cp"),
            P(("tp", "cp")),
            P("cp"),
            P(("tp", "cp")),
        ),
        check_vma=False,
    )
```

```python
import functools

import jax
import jax.numpy as jnp
import numpy as np
from jax import lax
from jax.experimental import pallas as pl
from jax.experimental.pallas import tpu as pltpu
from jax.sharding import PartitionSpec as P

HD = 64
D = 2048
FF = 8192

eps = 1e-05
scale_base = 512.0
masked_score = -1e30
f32 = jnp.float32
bf16 = jnp.bfloat16


def dot(a, b):
    return jnp.dot(a, b, preferred_element_type=f32)


def dot_t(a, b):
    return lax.dot_general(a, b, (((1,), (1,)), ((), ())), preferred_element_type=f32)


def t_dot(a, b):
    return lax.dot_general(a, b, (((0,), (0,)), ((), ())), preferred_element_type=f32)


def pairs(count, k):
    return [(i, i ^ k) for i in range(count)]


def swap_tp(value, k):
    return lax.ppermute(value, "tp", pairs(lax.axis_size("tp"), k))


def tp_order(value):
    count, me = lax.axis_size("tp"), lax.axis_index("tp")
    part = value.shape[0] // count
    return jnp.concatenate(
        [lax.dynamic_slice_in_dim(value, (me ^ k) * part, part, 0) for k in range(count)], axis=0
    )


def tp_scatter_sum(partial_sum):
    count = lax.axis_size("tp")
    part = partial_sum.shape[0] // count
    low = partial_sum.astype(bf16)
    total = partial_sum[:part]
    for k in range(1, count):
        total = total + swap_tp(low[k * part : (k + 1) * part], k).astype(f32)
    return total


def tp_gather(block):
    count = lax.axis_size("tp")
    return jnp.concatenate([block] + [swap_tp(block, k) for k in range(1, count)], axis=0)


def tp_sum(value):
    total = value
    for k in range(1, lax.axis_size("tp")):
        total = total + swap_tp(value, k)
    return total


def tp_token_sum(value):
    count = lax.axis_size("tp")
    blocks = value.reshape(value.shape[0], count, -1)
    total = blocks
    for k in range(1, count):
        got = swap_tp(blocks, k)
        total = total + jnp.stack([got[:, j ^ k] for j in range(count)], axis=1)
    return total.reshape(value.shape)


def cp_columns(value):
    return lax.all_to_all(value, "cp", split_axis=1, concat_axis=0, tiled=True)


def cp_gather(value):
    return lax.all_gather(value, "cp", axis=0, tiled=True)


def xpos_tables(positions):
    column = jnp.arange(HD // 2, dtype=f32)
    frequency = 10000.0 ** (-column / (HD // 2))
    zeta = (2.0 * column + 0.4 * HD) / (1.4 * HD)
    places = positions.astype(f32)[:, None]
    angle = places * frequency
    return (jnp.cos(angle), jnp.sin(angle), zeta ** (places / scale_base))


def turn(vector, cosine, sine, factor):
    paired = vector.reshape(vector.shape[:-1] + (HD // 2, 2))
    first, second = paired[..., 0], paired[..., 1]
    cosine, sine, factor = cosine[:, None], sine[:, None], factor[:, None]
    turned = jnp.stack(
        [(first * cosine - second * sine) * factor, (first * sine + second * cosine) * factor],
        axis=-1,
    )
    return turned.reshape(vector.shape)


def norm_rows(vector):
    center = jnp.mean(vector, axis=-1, keepdims=True)
    shifted = vector - center
    scaling = lax.rsqrt(jnp.mean(shifted * shifted, axis=-1, keepdims=True) + eps)
    return (shifted * scaling, scaling)


def norm_back(grad_result, gain, normed, scaling):
    grad_normed = grad_result * gain
    first = jnp.mean(grad_normed, axis=-1, keepdims=True)
    cross = jnp.mean(grad_normed * normed, axis=-1, keepdims=True)
    return scaling * (grad_normed - first - normed * cross)


def attend(queries, keys, values, allowed):
    scores = jnp.einsum("qhd,khd->hqk", queries, keys, preferred_element_type=f32) * HD**-0.5
    scores = jnp.where(allowed[None], scores, masked_score)
    top = jnp.max(scores, axis=-1, keepdims=True)
    exponent = jnp.where(allowed[None], jnp.exp(scores - top), 0.0)
    total = jnp.sum(exponent, axis=-1, keepdims=True)
    probability = (exponent / total).astype(bf16)
    mixed = jnp.einsum("hqk,khd->qhd", probability, values, preferred_element_type=f32)
    return (mixed, top + jnp.log(total))


def attend_back(queries, keys, values, allowed, lse, grad, delta):
    scores = jnp.einsum("qhd,khd->hqk", queries, keys, preferred_element_type=f32) * HD**-0.5
    probability = jnp.where(allowed[None], jnp.exp(scores - lse), 0.0)
    grad_prob = jnp.einsum("qhd,khd->hqk", grad, values, preferred_element_type=f32)
    grad_scores = (probability * (grad_prob - delta.T[:, :, None])).astype(bf16)
    grad_q = jnp.einsum("hqk,khd->qhd", grad_scores, keys, preferred_element_type=f32) * HD**-0.5
    grad_k = jnp.einsum("hqk,qhd->khd", grad_scores, queries, preferred_element_type=f32) * HD**-0.5
    grad_v = jnp.einsum(
        "hqk,qhd->khd", probability.astype(bf16), grad, preferred_element_type=f32
    )
    return (grad_q, grad_k, grad_v)


def body_general(
    layer_input,
    segment_ids,
    qkv_weight,
    out_weight,
    up_weight,
    down_weight,
    input_gain,
    heads_gain,
    middle_gain,
    hidden_gain,
    cotangent,
):
    local_len, row_count, width = layer_input.shape
    tp_count, cp_count = lax.axis_size("tp"), lax.axis_size("cp")
    me_tp, me_cp = lax.axis_index("tp"), lax.axis_index("cp")
    part = local_len // tp_count
    head_width = qkv_weight.shape[2]
    heads = head_width // HD
    by_head = heads % cp_count == 0
    own_heads = heads // cp_count if by_head else heads
    weight3 = jnp.transpose(qkv_weight, (1, 0, 2))

    x = tp_order(layer_input.reshape(local_len, width))
    gy = tp_order(cotangent.reshape(local_len, width))
    seg = tp_order(segment_ids)[:, 0]
    natural = tp_order(jnp.arange(local_len, dtype=jnp.int32))
    position = me_cp * local_len + natural
    position_all = (jnp.arange(cp_count, dtype=jnp.int32)[:, None] * local_len + natural).reshape(-1)

    stream = x.astype(f32)
    normed_one, scaling_one = norm_rows(stream)
    a = (normed_one * input_gain).astype(bf16)
    a_all = cp_gather(a)
    cosine, sine, factor = xpos_tables(position)
    raw_q = dot(a, weight3[0]).reshape(local_len, heads, HD)
    raw_k = dot(a, weight3[1]).reshape(local_len, heads, HD)
    raw_v = dot(a, weight3[2]).reshape(local_len, heads, HD)
    q = turn(raw_q, cosine, sine, factor).astype(bf16)
    k = turn(raw_k, cosine, sine, 1.0 / factor).astype(bf16)
    v = raw_v.astype(bf16)
    if by_head:
        extra = jnp.broadcast_to(seg.astype(bf16)[:, None, None], (local_len, cp_count, 16))
        sent = jnp.concatenate(
            [t.reshape(local_len, cp_count, own_heads * HD) for t in (q, k, v)] + [extra], axis=-1
        )
        got = lax.all_to_all(sent, "cp", split_axis=1, concat_axis=0, tiled=True)[:, 0]
        span = own_heads * HD
        q_all, k_all, v_all = (
            got[:, i * span : (i + 1) * span].reshape(-1, own_heads, HD) for i in range(3)
        )
        seg_all = got[:, 3 * span]
        seg_q, position_q = seg_all, position_all
    else:
        q_all, k_all, v_all = q, cp_gather(k), cp_gather(v)
        seg_all = cp_gather(seg.astype(bf16))
        seg_q, position_q = seg.astype(bf16), position
    allowed = (position_all[None, :] <= position_q[:, None]) & (seg_q[:, None] == seg_all[None, :])
    mixed, lse = attend(q_all, k_all, v_all, allowed)
    if by_head:
        attended = lax.all_to_all(
            mixed.astype(bf16).reshape(cp_count * local_len, own_heads * HD),
            "cp", split_axis=0, concat_axis=1, tiled=True,
        ).astype(f32)
    else:
        attended = mixed.reshape(local_len, head_width)

    sums = tp_token_sum(jnp.stack([jnp.sum(attended, axis=1), jnp.sum(attended * attended, axis=1)]))
    center = sums[0] / width
    scaling_h = lax.rsqrt(sums[1] / width - center * center + eps)[:, None]
    normed_h = (attended - center[:, None]) * scaling_h
    z = (normed_h * heads_gain).astype(bf16)
    gain_row = tp_sum(jnp.dot(heads_gain, out_weight.astype(f32)))
    branch = tp_scatter_sum(dot(z, out_weight))
    x1 = stream[:part] + branch
    normed_two, scaling_two = norm_rows(x1)
    u = tp_gather((normed_two * middle_gain).astype(bf16))

    grad_hid = dot_t(gy, down_weight)
    grad_normed = grad_hid * hidden_gain
    hidden = dot(u, up_weight)
    cdf = 0.5 * (1.0 + lax.erf(hidden * (0.5**0.5)))
    act = hidden * cdf
    slope = cdf + hidden * jnp.exp(-0.5 * hidden * hidden) * 0.3989422804014327
    sums = tp_token_sum(
        jnp.stack(
            [
                jnp.sum(act, axis=1),
                jnp.sum(act * act, axis=1),
                jnp.sum(grad_normed, axis=1),
                jnp.sum(grad_normed * act, axis=1),
            ]
        )
    )
    center = sums[0] / FF
    scaling_f = lax.rsqrt(sums[1] / FF - center * center + eps)
    first = sums[2] / FF
    cross = scaling_f * (sums[3] / FF - center * first)
    normed_f = (act - center[:, None]) * scaling_f[:, None]
    z2 = (normed_f * hidden_gain).astype(bf16)
    grad_act = scaling_f[:, None] * (grad_normed - first[:, None] - normed_f * cross[:, None])
    gh = (grad_act * slope).astype(bf16)
    hidden_gain_sum = jnp.sum(grad_hid * normed_f, axis=0)
    gu = tp_scatter_sum(dot_t(gh, up_weight))
    gx1 = gy[:part].astype(f32) + norm_back(gu, middle_gain, normed_two, scaling_two)
    middle_gain_sum = jnp.sum(gu * normed_two, axis=0)
    gb_own = gx1.astype(bf16)
    gb_f = gb_own.astype(f32)
    first = jnp.sum(gb_f * gain_row, axis=1) / width
    cross = jnp.sum(gb_f * branch, axis=1) / width
    gb = tp_gather(gb_own)
    stats = tp_gather(jnp.stack([first, cross], axis=1))

    gz = dot_t(gb, out_weight)
    heads_gain_sum = jnp.sum(gz * normed_h, axis=0)
    go = (scaling_h * (gz * heads_gain - stats[:, :1] - normed_h * stats[:, 1:])).astype(bf16)
    if by_head:
        grad_mixed = cp_columns(go).reshape(-1, own_heads, HD)
    else:
        grad_mixed = go.reshape(local_len, heads, HD)
    delta = jnp.sum(grad_mixed.astype(f32) * mixed, axis=-1)
    gq, gk, gv = attend_back(q_all, k_all, v_all, allowed, lse, grad_mixed, delta)
    if by_head:
        cos_all, sin_all, factor_all = xpos_tables(position_all)
    else:
        cos_all, sin_all, factor_all = cosine, sine, factor
        gk = lax.psum_scatter(gk.astype(bf16), "cp", scatter_dimension=0, tiled=True).astype(f32)
        gv = lax.psum_scatter(gv.astype(bf16), "cp", scatter_dimension=0, tiled=True).astype(f32)
    gq = turn(gq, cos_all, -sin_all, factor_all)
    gk = turn(gk, cos_all, -sin_all, 1.0 / factor_all)
    grads = jnp.stack([gq, gk, gv], axis=1).astype(bf16)
    if by_head:
        grads_own = grads.reshape(-1, 3 * own_heads * HD)
        grads = lax.all_to_all(
            grads.reshape(-1, 3, own_heads * HD), "cp", split_axis=0, concat_axis=2, tiled=True
        )
    else:
        grads = grads.reshape(local_len, 3, head_width)
        grads_own = lax.all_to_all(grads, "cp", split_axis=2, concat_axis=0, tiled=True)
        grads_own = grads_own.reshape(-1, 3 * head_width // cp_count)
    ga = (
        dot_t(grads[:, 0], weight3[0]) + dot_t(grads[:, 1], weight3[1]) + dot_t(grads[:, 2], weight3[2])
    )
    ga = tp_scatter_sum(ga)
    input_gain_sum = jnp.sum(ga * normed_one[:part], axis=0)
    grad_in = gx1 + norm_back(ga, input_gain, normed_one[:part], scaling_one[:part])

    y = (x1 + tp_scatter_sum(dot(z2, down_weight))).astype(bf16)
    layer_output = tp_order(tp_gather(y)).reshape(layer_input.shape)
    grad_input = tp_order(tp_gather(grad_in.astype(bf16))).reshape(layer_input.shape)

    grad_down = t_dot(cp_columns(z2), cp_gather(gy))
    grad_up = t_dot(cp_columns(u), cp_gather(gh))
    grad_out = t_dot(cp_columns(z), cp_gather(gb))
    grad_qkv = t_dot(a_all, grads_own).astype(bf16)
    grad_qkv = lax.all_to_all(
        grad_qkv.reshape(width, 3, head_width // cp_count), "cp", split_axis=0, concat_axis=2, tiled=True
    ).astype(f32)

    def cp_sum_own(vector):
        return jnp.sum(lax.all_to_all(vector.reshape(cp_count, -1), "cp", 0, 0, tiled=True), axis=0)

    def both_sum_own(vector):
        return tp_sum(cp_sum_own(vector))

    return (
        layer_output,
        grad_input,
        grad_qkv,
        grad_out,
        grad_up,
        grad_down,
        both_sum_own(input_gain_sum),
        cp_sum_own(heads_gain_sum),
        both_sum_own(middle_gain_sum),
        cp_sum_own(hidden_gain_sum),
    )


INTERPRET = False


def params(megabytes):
    return pltpu.CompilerParams(vmem_limit_bytes=megabytes * 1024 * 1024)


def shape(dims, kind):
    return jax.ShapeDtypeStruct(dims, kind)


def whole():
    return pl.BlockSpec(memory_space=pltpu.VMEM)


def scalars():
    return pl.BlockSpec(memory_space=pltpu.SMEM)


class Pin:
    def __init__(self, value):
        self.value = value


class Far(Pin):
    def __init__(self, value, dims=None, block=None):
        super().__init__(value)
        self.dims = tuple(value.shape) if dims is None else dims
        self.block = block


class Near:
    def __init__(self, value):
        self.value = value


class Fetched:
    def __init__(self, ref, copy):
        self.ref, self.copy, self.shape = ref, copy, ref.shape

    def ready(self):
        if self.copy is not None:
            self.copy.wait()
            self.copy = None

    def __getitem__(self, index):
        self.ready()
        return self.ref[index]


class Stored:
    def __init__(self, ref, copy):
        self.ref, self.copy, self.shape, self.sent = ref, copy, ref.shape, False

    def send(self):
        if not self.sent:
            self.copy.start()
            self.sent = True

    def __getitem__(self, index):
        return self.ref[index]

    def __setitem__(self, index, value):
        self.ref[index] = value

    @property
    def dtype(self):
        return self.ref.dtype


def plain(value):
    return value.value if isinstance(value, (Pin, Near)) else value


def pinned(value):
    return value if INTERPRET else pltpu.with_memory_space_constraint(value, pltpu.HBM)


def call(
    kernel, outs, args, specs=None, out_specs=None, grid=None, scratch=(), mb=8, cost=0.3, after=(), carry=(), prefetch=0
):
    specs = list(specs) if specs is not None else [whole() for _ in args]
    out_specs = list(out_specs) if out_specs is not None else [whole() for _ in outs]
    count, extra, kept, made = len(args), len(after), len(carry), len(outs)
    anywhere = pl.BlockSpec(memory_space=pl.ANY)
    far_in = [i for i, t in enumerate(args) if isinstance(t, Far)]
    far_out = [i for i, t in enumerate(outs) if isinstance(t, Far)]
    for i in far_in:
        specs[i] = anywhere
    for i in far_out:
        out_specs[i] = anywhere
    moving = [pltpu.VMEM(args[i].dims, args[i].value.dtype) for i in far_in]
    moving += [pltpu.VMEM(outs[i].dims, outs[i].value.dtype) for i in far_out]
    moving += [pltpu.SemaphoreType.DMA] * (len(far_in) + len(far_out))
    own_scratch = len(scratch)

    def run(*refs):
        ins = list(refs[:count])
        results = refs[count + extra + kept :]
        products = list(results[:made])
        rest = results[made + kept :]
        slots, sems = rest[own_scratch : own_scratch + len(far_in) + len(far_out)], rest[own_scratch + len(far_in) + len(far_out) :]
        for i, slot, sem in zip(far_in, slots, sems):
            source = refs[i]
            if args[i].block is not None:
                source = source.at[args[i].block(refs[0])]
            copy = pltpu.make_async_copy(source, slot, sem)
            copy.start()
            ins[i] = Fetched(slot, copy)
        stored = [
            Stored(slot, pltpu.make_async_copy(slot, results[i], sem))
            for i, slot, sem in zip(far_out, slots[len(far_in) :], sems[len(far_in) :])
        ]
        for i, product in zip(far_out, stored):
            products[i] = product
        kernel(*ins, *products, *rest[:own_scratch])
        for i in far_in:
            ins[i].ready()
        for product in stored:
            product.send()
        for product in stored:
            product.copy.wait()

    def result(value):
        dims = plain(value)
        if INTERPRET or value is dims:
            return dims
        return (pltpu.HBM if isinstance(value, Pin) else pltpu.VMEM)(dims.shape, dims.dtype)

    where = dict(
        in_specs=specs + [anywhere] * (extra + kept),
        out_specs=tuple(out_specs + [anywhere] * kept),
        scratch_shapes=list(scratch) + moving,
    )
    if prefetch:
        where["in_specs"] = where["in_specs"][prefetch:]
        where = {"grid_spec": pltpu.PrefetchScalarGridSpec(num_scalar_prefetch=prefetch, grid=grid, **where)}
    elif grid is not None:
        where["grid"] = grid
    return pl.pallas_call(
        run,
        out_shape=tuple(result(t) for t in outs) + tuple(result(Pin(shape(t.shape, t.dtype))) for t in carry),
        input_output_aliases={count + extra + i: made + i for i in range(kept)},
        compiler_params=params(mb),
        cost_estimate=pl.CostEstimate(flops=int(cost * 1e9), bytes_accessed=0, transcendentals=0),
        interpret=INTERPRET,
        **where,
    )(*[pinned(t.value) if isinstance(t, Pin) else t for t in list(args) + list(after)], *[pinned(t) for t in carry])


def bring(items, ids, after=(), carry=(), cost=0.3):
    def kernel(ids, *refs):
        sources, slots, sems = refs[: len(items)], refs[len(items) : 2 * len(items)], refs[2 * len(items) :]
        copies = []
        for (_, _, block), source, slot, sem in zip(items, sources, slots, sems):
            copies.append(pltpu.make_async_copy(source if block is None else source.at[block(ids)], slot, sem))
        for copy in copies:
            copy.start()
        for copy in copies:
            copy.wait()

    return call(
        kernel,
        [Near(shape(dims, array.dtype)) for array, dims, _ in items],
        [ids] + [Pin(array) for array, _, _ in items],
        [scalars()] + [pl.BlockSpec(memory_space=pl.ANY)] * len(items),
        scratch=[pltpu.SemaphoreType.DMA] * len(items), after=after, carry=carry, mb=2, cost=cost,
    )


def fixed(dims):
    return pl.BlockSpec(dims, lambda i: (0,) * len(dims))


def split_low(value):
    high = value.astype(bf16)
    return high, (value - high.astype(f32)).astype(bf16)


def lanes_of(columns, rows):
    lane = lax.broadcasted_iota(jnp.int32, (rows, 128), 1)
    out = jnp.zeros((rows, 128), f32)
    for i, column in enumerate(columns):
        out = jnp.where(lane == i, column.astype(f32), out)
    return out


def pair_sum(block, i):
    return block[:, i : i + 1].astype(f32) + block[:, i + 1 : i + 2].astype(f32)


def own_order(me, part, index):
    return ((index // part) ^ me) * part + index % part


def block_at(me, k, part):
    return pl.ds(pl.multiple_of((me ^ k) * part, part), part)


def swap_pairs(value, axis):
    size = value.shape[axis]
    place = lax.broadcasted_iota(jnp.int32, value.shape, axis)
    return jnp.where(
        place % 2 == 0, pltpu.roll(value, size - 1, axis), pltpu.roll(value, 1, axis)
    )


def tables(local_len, cp_count):
    column = np.arange(HD) // 2
    frequency = 10000.0 ** (-column / (HD // 2))
    zeta = (2.0 * column + 0.4 * HD) / (1.4 * HD)

    def of(places):
        angle = places[:, None] * frequency
        factor = zeta ** (places[:, None] / scale_base)
        return np.stack([np.cos(angle), np.sin(angle), factor, 1.0 / factor]).astype(np.float32)

    return of(np.arange(local_len)), of(np.arange(cp_count) * local_len)


def project_kernel(parts, ids, x, gain, gy, inner, base, seg, w0, w1, w2, pair, gy_out, out):
    me, mine = ids[0], ids[1]
    rows, width = pair.shape[1:]
    part = rows // parts
    heads = out.shape[0]
    x.ready()
    for k in range(parts):
        normed, _ = norm_rows(x.ref[block_at(me, k, part), :].astype(f32))
        pair[0, k * part : (k + 1) * part, :] = (normed * gain[...]).astype(bf16)
    gy.ready()
    for k in range(parts):
        block = gy.ref[block_at(me, k, part), :]
        pair[1, k * part : (k + 1) * part, :] = block
        gy_out[k * part : (k + 1) * part, :] = block
    pair.send()
    gy_out.send()
    inner.ready()
    here = [base[kind, pl.ds(mine, 1), :] for kind in range(4)]
    table = [
        jnp.concatenate([inner.ref[kind, block_at(me, k, part), :] for k in range(parts)], axis=0)
        for kind in range(4)
    ]
    cosine = table[0] * here[0] - table[1] * here[1]
    sine = table[1] * here[0] + table[0] * here[1]
    lane = lax.broadcasted_iota(jnp.int32, cosine.shape, 1)
    sine = jnp.where(lane % 2 == 0, -sine, sine)
    place = lax.broadcasted_iota(jnp.int32, (rows, rows), 1)
    source = lax.broadcasted_iota(jnp.int32, (rows, rows), 0)
    moved = (own_order(me, part, place) == source).astype(bf16)
    ids_row = jnp.broadcast_to(seg[...].astype(f32), (16, rows)).astype(bf16)
    ordered = dot(ids_row, moved).astype(bf16)
    for j in range(heads):
        out[j, 3 * HD : 3 * HD + 16, :] = ordered
    for c, weight in enumerate((w0, w1, w2)):
        acc = dot(pair[0], weight[0])
        factor = (table[2] * here[2], table[3] * here[3], None)[c]
        for i in range(acc.shape[1] // 128):
            piece = acc[:, i * 128 : (i + 1) * 128]
            if c < 2:
                piece = piece * (cosine * factor) + swap_pairs(piece, 1) * (sine * factor)
            turned = piece.T.astype(bf16)
            for h in range(128 // HD):
                out[i * (128 // HD) + h, c * HD : (c + 1) * HD, :] = turned[h * HD : (h + 1) * HD]
    out.send()


def gather_heads(got, keys, ids_col, values=None):
    for j in range(got.shape[0]):
        rows = slice(j * got.shape[2], (j + 1) * got.shape[2])
        both = jnp.concatenate([got[j, HD : 3 * HD, :].astype(f32)], axis=0).T
        keys[rows, :] = both[:, :HD].astype(bf16)
        if values is not None:
            values[rows, :] = both[:, HD:].astype(bf16)
        ids_col[rows, :] = got[j, 3 * HD : 3 * HD + 16, :].astype(f32).T


def visible_scores(me, part, scores, ids_col, ids_row, count, first, group):
    same = ids_col[0:count, 0:1] == ids_row
    length = group
    key = lax.broadcasted_iota(jnp.int32, (length, length), 0)
    query = lax.broadcasted_iota(jnp.int32, (length, length), 1)
    rows = first
    own = lambda index: (index // rows) * rows + own_order(me, part, index % rows)
    earlier = own(key) <= own(query)
    if count > length:
        earlier = jnp.concatenate([jnp.ones((count - length, length), jnp.bool_), earlier], axis=0)
    return same & earlier


def attend_kernel(parts, ids, got, out, mixed, lse, kept, keys, ids_col):
    me = ids[0]
    kept[...] = got[...]
    kept.send()
    blocks, _, rows = got.shape
    part = rows // parts
    gather_heads(got, keys, ids_col)
    group = 4 if blocks % 4 == 0 else 1
    width = group * rows
    for i in range(blocks // group):
        mine = range(i * group, (i + 1) * group)
        query = jnp.concatenate([got[j, :HD, :] for j in mine], axis=1) * bf16(HD**-0.5)
        ids_row = jnp.concatenate([got[j, 3 * HD : 3 * HD + 16, :].astype(f32)[:1] for j in mine], axis=1)
        count = (i + 1) * width
        scores = dot(keys[0:count, :], query)
        allowed = visible_scores(me, part, scores, ids_col, ids_row, count, rows, width)
        scores = jnp.where(allowed, scores, masked_score)
        top = jnp.max(scores, axis=0, keepdims=True)
        exponent = jnp.exp(scores - top)
        total = jnp.sum(exponent, axis=0, keepdims=True)
        value = jnp.concatenate([got[j, 2 * HD : 3 * HD, :] for j in range((i + 1) * group)], axis=1)
        result = dot(value, exponent.astype(bf16)) / total
        mixed[:, i * width : (i + 1) * width] = result
        lse[:, i * width : (i + 1) * width] = top + jnp.log(total)
        for n, j in enumerate(mine):
            out[j] = result[:, n * rows : (n + 1) * rows].astype(bf16)
    out.send()


def store_pieces(total, own, pieces, part, extra=None):
    own[:, : total.shape[1]] = total[:part]
    for k, piece in enumerate(pieces, 1):
        piece[:, : total.shape[1]] = total[k * part : (k + 1) * part].astype(bf16)
    if extra is not None:
        own[:, total.shape[1] :] = extra[:part]
        for k, piece in enumerate(pieces, 1):
            piece[:, total.shape[1] :] = extra[k * part : (k + 1) * part].astype(bf16)


def out_kernel(parts, att, gain, weight, own, *refs):
    pieces, kept = refs[:-1], refs[-1]
    kept[...] = att[...]
    blocks, _, rows = att.shape
    part, width = rows // parts, weight.shape[1]
    value = jnp.concatenate([att[j].astype(f32) for j in range(blocks)], axis=0).T
    high, low = split_low(jnp.mean(value, axis=1, keepdims=True))
    centred = value - (high.astype(f32) + low.astype(f32))
    square = split_low(jnp.sum(centred * centred, axis=1, keepdims=True))
    gains = gain[...]
    row = lax.broadcasted_iota(jnp.int32, (16, gains.shape[1]), 0)
    gain_high, gain_low = (t.astype(f32) for t in split_low(gains))
    gain_rows = jnp.where(row == 0, gain_high, jnp.where(row == 1, gain_low, 0.0))
    left = jnp.concatenate([(centred * gains).astype(bf16), gain_rows.astype(bf16)], axis=0)
    total = dot(left, weight[...])
    gain_row = total[rows : rows + 1] + total[rows + 1 : rows + 2]
    gain_block = jnp.concatenate([gain_row[:, i : i + 128] for i in range(0, width, 128)], axis=0)
    stats = lanes_of([high, low, *square], rows).T
    empty = jnp.zeros((part - gain_block.shape[0] - 1, 128), f32)

    def extra(k):
        row = jnp.concatenate([stats[i : i + 1, k * part : (k + 1) * part] for i in range(4)], axis=1)
        return jnp.concatenate([gain_block, row, empty], axis=0).astype(bf16)

    own[:, :width] = total[:part]
    own[:, width:] = extra(0).astype(f32)
    for k, piece in enumerate(pieces, 1):
        here = slice(k * part, (k + 1) * part)
        piece[:, :width] = total[here].astype(bf16)
        piece[:, width:] = extra(k)


def middle_kernel(parts, head_width, own, *refs):
    got, (x, gain, x1, u, gain_row, norms) = refs[: parts - 1][::-1], refs[parts - 1 :]
    part, width = x1.shape
    blocks = [own] + list(got)
    extras = [b[:, width:].astype(f32) for b in blocks]
    count = width // 128
    rows = [jnp.concatenate([e[i : i + 1] for i in range(count)], axis=1) for e in extras]
    columns = [jnp.broadcast_to(e[count : count + 1], (128, 128)).T[:, 0:1] for e in extras]
    means = [c[:part] + c[part : 2 * part] for c in columns]
    squares = [c[2 * part : 3 * part] + c[3 * part :] for c in columns]
    gain_row[...] = sum(rows)
    mean = sum(means) / parts
    spread = sum(squares) + head_width * sum((m - mean) * (m - mean) for m in means)
    scaling = lax.rsqrt(spread / width + eps)
    total = sum(b[:, :width].astype(f32) for b in blocks)
    for m, row in zip(means, rows):
        total = total + (m - mean) * row
    value = x[...].astype(f32) + total * scaling
    x1[...] = value
    normed, _ = norm_rows(value)
    u[...] = (normed * gain[...]).astype(bf16)
    norms[...] = jnp.zeros_like(norms)
    norms[0:2, :part] = lanes_of([mean, scaling], part).T[0:2, :]


def grad_hidden_kernel(gy, weight, grad):
    grad[...] = dot_t(gy[...], weight[...])


def prepare_kernel(step, up, near_up, flipped, up_sems):
    chunks = [slice(i, i + step) for i in range(0, up.shape[0], step)]
    copies = [pltpu.make_async_copy(up.at[c, :], near_up.at[c, :], up_sems.at[i]) for i, c in enumerate(chunks)]
    for copy in copies:
        copy.start()
    for copy, chunk in zip(copies, chunks):
        copy.wait()
        flipped[:, chunk] = near_up[chunk, :].T


def up_kernel(parts, step, own, *refs):
    got, refs = refs[: parts - 1][::-1], refs[parts - 1 :]
    weight, grad, gain, norms, act, slope, u, stats, rows_u = refs
    part = own.shape[0]
    rows, width = rows_u.shape
    for k, block in enumerate([own] + list(got)):
        rows_u[k * part : (k + 1) * part, :] = block[...]
    wide = u.shape[2]
    for j in range(u.shape[0]):
        u[j] = rows_u[:, j * wide : (j + 1) * wide]
    total = [jnp.zeros((rows, 128), f32)] * 4
    for i in range(0, weight.shape[1], step):
        here = slice(i, i + step)
        hidden = dot(rows_u[...], weight[:, here])
        cdf = 0.5 * (1.0 + lax.erf(hidden * (0.5**0.5)))
        value = hidden * cdf
        act[:, here] = value
        slope[:, here] = cdf + hidden * jnp.exp(-0.5 * hidden * hidden) * 0.3989422804014327
        grad_normed = grad[:, here] * gain[:, here]
        columns = [value, value * value, grad_normed, grad_normed * value]
        for n, column in enumerate(columns):
            for j in range(0, step, 128):
                total[n] = total[n] + column[:, j : j + 128]
    sums = lanes_of([jnp.sum(t, axis=1, keepdims=True) for t in total], rows)
    stats[...] = sums.T[:8, :]
    stats[4:6, :] = norms[0:2, :]


def swap_lane_blocks(value, k, part):
    lanes = value.shape[1]
    lane = lax.broadcasted_iota(jnp.int32, value.shape, 1)
    distance = 1
    while distance <= k:
        if k & distance:
            move = distance * part
            value = jnp.where(
                (lane // move) % 2 == 0,
                pltpu.roll(value, lanes - move, 1),
                pltpu.roll(value, move, 1),
            )
        distance *= 2
    return value


def hidden_back_kernel(parts, full, step, own, *refs):
    got, refs = refs[: parts - 1][::-1], refs[parts - 1 :]
    act, slope, grad, gain, weight, u, gh, both, norms, own_out = refs[:10]
    pieces = refs[10:]
    first_wide = u.shape[2]
    both[:, :, :first_wide] = u[...]
    rows = act.shape[0]
    part = rows // parts
    total = own[...]
    for k, block in enumerate(got, 1):
        total = total + swap_lane_blocks(block[...], k, part)
    norms[...] = jnp.zeros_like(norms)
    for k, block in enumerate([own] + list(got)):
        norms[0:2, k * part : (k + 1) * part] = block[4:6, :part]
    mean = total[0:1] / full
    scaling = lax.rsqrt(total[1:2] / full - mean * mean + eps)
    first = total[2:3] / full
    cross = scaling * (total[3:4] / full - mean * first)
    row = lax.broadcasted_iota(jnp.int32, (rows, rows), 0)
    table = jnp.zeros((rows, rows), f32)
    for i, value in enumerate([mean, scaling, first, cross]):
        table = jnp.where(row == i, value, table)
    cols = table.T
    mean, scaling, first, cross = (cols[:, i : i + 1] for i in range(4))
    wide = both.shape[2] - first_wide
    for i in range(0, act.shape[1], step):
        here = slice(i, i + step)
        normed = (act[:, here] - mean) * scaling
        low = (normed * gain[:, here]).astype(bf16)
        for j in range(0, step, wide):
            both[(i + j) // wide, :, first_wide:] = low[:, j : j + wide]
        value = scaling * (grad[:, here] * gain[:, here] - first - normed * cross) * slope[:, here]
        gh[:, here] = value.astype(bf16)
    both.send()
    gh.send()
    width = weight.shape[1]
    for i in range(0, width, step):
        here = slice(i, i + step)
        result = dot(gh[...], weight[:, here])
        own_out[:, here] = result[:part]
        for k, piece in enumerate(pieces, 1):
            piece[:, here] = result[k * part : (k + 1) * part].astype(bf16)


def down_kernel(z2, *refs):
    weights, (own, second, odd) = refs[:-3], refs[-3:]
    _, _, wide = z2.shape
    part = own.shape[0]
    total = 0.0
    for i, weight in enumerate(weights):
        rows = weight.shape[0]
        left = jnp.concatenate([z2[j] for j in range(i * rows // wide, (i + 1) * rows // wide)], axis=1)
        total = total + dot(left, weight[...])
    own[...] = total[:part]
    second[...] = total[2 * part : 3 * part]
    odd[:part, :] = total[part : 2 * part].astype(bf16)
    odd[part:, :] = total[3 * part :].astype(bf16)


def half_kernel(second, got, out):
    part = second.shape[0]
    out[...] = (second[...] + got[part:, :].astype(f32)).astype(bf16)


def join_kernel(first, second, out):
    part = first.shape[0]
    out[:part, :] = first[...]
    out[part:, :] = second[...]


def middle_back_kernel(parts, own, *refs):
    got, refs = refs[: parts - 1][::-1], refs[parts - 1 :]
    gain_row, x, x1, gy, gain, gx1, gb = refs
    part, width = x1.shape
    grad = own[...]
    for block in got:
        grad = grad + block[...].astype(f32)
    value = x1[...]
    normed, scaling = norm_rows(value)
    result = gy[...].astype(f32) + norm_back(grad, gain[...], normed, scaling)
    gx1[...] = result
    low = result.astype(bf16)
    gb[:, :width] = low
    low = low.astype(f32)
    first = jnp.sum(low * gain_row[...], axis=1, keepdims=True) / width
    cross = jnp.sum(low * (value - x[...].astype(f32)), axis=1, keepdims=True) / width
    gb[:, width:] = lanes_of([*split_low(first), *split_low(cross)], part).astype(bf16)


def heads_back_kernel(parts, own, *refs):
    got, refs = refs[: parts - 1][::-1], refs[parts - 1 :]
    stats, att, gain, weight, sent, gb = refs
    blocks, _, rows = att.shape
    part, width = own.shape[0], gb.shape[1]
    for k, block in enumerate([own] + list(got)):
        gb[k * part : (k + 1) * part, :] = block[:, :width]
    gb.send()
    columns = jnp.concatenate([b[:, width:].astype(f32) for b in [own] + list(got)], axis=0).T
    first = columns[0:1] + columns[1:2]
    cross = columns[2:3] + columns[3:4]
    mean, scaling = stats[0:1], stats[1:2]
    grad = dot_t(weight[...], gb[...])
    value = jnp.concatenate([att[j].astype(f32) for j in range(blocks)], axis=0)
    normed = (value - mean) * scaling
    gain_col = jnp.broadcast_to(gain[...], (8, gain.shape[1])).T[:, 0:1]
    go = (scaling * (grad * gain_col - first - normed * cross)).astype(bf16)
    z = (normed * gain_col).astype(bf16)
    for j in range(blocks):
        sent[j, :HD, :] = go[j * HD : (j + 1) * HD]
        sent[j, HD:, :] = z[j * HD : (j + 1) * HD]


def turn_back(grad, table, base, j, inverse):
    here = [base[kind, :, j : j + 1] for kind in range(4)]
    cosine = table[0] * here[0] - table[1] * here[1]
    sine = table[1] * here[0] + table[0] * here[1]
    factor = table[3] * here[3] if inverse else table[2] * here[2]
    row = lax.broadcasted_iota(jnp.int32, grad.shape, 0)
    sine = jnp.where(row % 2 == 0, sine, -sine)
    return (grad * cosine + swap_pairs(grad, 0) * sine) * factor


def attend_back_kernel(parts, ids, got, grads, mixed, lse, inner, base, out, z, keys, values, ids_col, gk, gv):
    me = ids[0]
    for j in range(grads.shape[0]):
        z[j] = grads[j, HD:, :]
    z.send()
    blocks, _, rows = got.shape
    part = rows // parts
    gather_heads(got, keys, ids_col, values)
    gk[...] = jnp.zeros_like(gk)
    gv[...] = jnp.zeros_like(gv)
    table = []
    for kind in range(4):
        ordered = jnp.concatenate(
            [inner[kind, block_at(me, k, part), :] for k in range(parts)], axis=0
        )
        table.append(ordered.T[:HD])
    group = 2 if blocks % 2 == 0 else 1
    width = group * rows
    for i in range(blocks // group):
        mine = range(i * group, (i + 1) * group)
        query = jnp.concatenate([got[j, :HD, :] for j in mine], axis=1) * bf16(HD**-0.5)
        ids_row = jnp.concatenate([got[j, 3 * HD : 3 * HD + 16, :].astype(f32)[:1] for j in mine], axis=1)
        go = jnp.concatenate([grads[j, :HD, :] for j in mine], axis=1)
        span = slice(i * width, (i + 1) * width)
        delta = jnp.sum(go.astype(f32) * mixed[:, span], axis=0, keepdims=True)
        count = (i + 1) * width
        scores = dot(keys[0:count, :], query)
        allowed = visible_scores(me, part, scores, ids_col, ids_row, count, rows, width)
        probability = jnp.where(allowed, jnp.exp(jnp.minimum(scores - lse[:, span], 0.5)), 0.0)
        grad_prob = dot(values[0:count, :], go)
        grad_scores = (probability * (grad_prob - delta)).astype(bf16)
        gv[:, 0:count] += dot_t(go, probability.astype(bf16))
        gk[:, 0:count] += dot_t(query, grad_scores)
        key = jnp.concatenate([got[j, HD : 2 * HD, :] for j in range((i + 1) * group)], axis=1)
        gq = dot(key, grad_scores) * HD**-0.5
        for n, j in enumerate(mine):
            piece = turn_back(gq[:, n * rows : (n + 1) * rows], table, base, j, False)
            out[j, :HD, :] = piece.astype(bf16)
    for j in range(blocks):
        span = slice(j * rows, (j + 1) * rows)
        out[j, HD : 2 * HD, :] = turn_back(gk[:, span], table, base, j, True).astype(bf16)
        out[j, 2 * HD :, :] = gv[:, span].astype(bf16)


def input_back_kernel(parts, got, *refs):
    weights, own_out, pieces = refs[:6], refs[6], refs[7:]
    part, width = own_out.shape
    half = width // 2
    grads = []
    for c in range(3):
        here = slice(c * HD, (c + 1) * HD)
        grad = jnp.concatenate([got[j, here, :].astype(f32) for j in range(got.shape[0])], axis=0)
        grads.append(grad.T.astype(bf16))
    totals = [0.0, 0.0]
    for n, weight in enumerate(weights):
        totals[n % 2] = totals[n % 2] + dot_t(grads[n // 2], weight[0])
    for h, result in enumerate(totals):
        here = slice(h * half, (h + 1) * half)
        own_out[:, here] = result[:part]
        for k, piece in enumerate(pieces, 1):
            piece[:, here] = result[k * part : (k + 1) * part].astype(bf16)


def final_kernel(parts, own, *refs):
    got, (x, gx1, gain, gains, out) = refs[: parts - 1][::-1], refs[parts - 1 :]
    part, width = gx1.shape
    grad = own[...]
    for block in got:
        grad = grad + block[...].astype(f32)
    normed, scaling = norm_rows(x[...].astype(f32))
    out[:, :width] = (gx1[...] + norm_back(grad, gain[...], normed, scaling)).astype(bf16)
    rows = gains[0:2]
    pieces = [rows[n : n + 1, i : i + 128] for n in range(2) for i in range(0, rows.shape[1], 128)]
    high, low = split_low(jnp.concatenate(pieces, axis=0))
    empty = jnp.zeros((part - 2 * len(pieces), 128), f32)
    tail = jnp.concatenate([high.astype(f32), low.astype(f32), empty], axis=0)
    out[:, width:] = tail.astype(bf16)


def output_kernel(own, got, last, x1, out):
    total = own[...] + x1[...] + got[: out.shape[0], :].astype(f32)
    out[...] = (total + last[...].astype(f32)).astype(bf16)


def natural_kernel(ids, *refs):
    blocks, out = refs[:-1], refs[-1]
    part = blocks[0].shape[0]
    for k, block in enumerate(blocks):
        out[block_at(ids[0], k, part), :] = block[...]


def own_row(gain, index, own):
    total = jnp.zeros((1, own), f32)
    for j in range(gain.shape[1] // own):
        total = jnp.where(index == j, gain[:, j * own : (j + 1) * own], total)
    return total


def row_of(column, columns):
    return jnp.broadcast_to(column, (columns, 128)).T[:1, :]


def product_kernel(step, columns, which, offset, ids, left, right, *refs):
    count = left.shape[0]
    gains = len(refs) > 7
    if gains:
        (weight, gain, out, gain_grad), refs = refs[:4], refs[4:]
        (near_weight, weight_sem), refs = refs[-2:], refs[:-2]
    else:
        out, refs = refs[0], refs[1:]
    left_all, right_all, result, left_sems, right_sems, out_sems = refs
    rows, size = right.shape[-2:]
    own = result.shape[0]
    tokens = count * rows
    chunks = [slice(i, i + step) for i in range(0, size, step)]

    first = []
    for r in range(count):
        source = left.at[r]
        if columns:
            source, place = source.at[:, pl.ds(offset, own)], left_all.at[pl.ds(r * rows, rows), :]
        else:
            source, place = source.at[pl.ds(offset, own), :], left_all.at[r]
        first.append(pltpu.make_async_copy(source, place, left_sems.at[r]))
    side = right if which is None else right.at[:, which]
    later = [
        [pltpu.make_async_copy(side.at[:, :, c], right_all.at[:, :, c], right_sems.at[i])] for i, c in enumerate(chunks)
    ]
    for copy in first + later[0]:
        copy.start()
    if gains:
        fetch = pltpu.make_async_copy(
            weight.at[pl.ds(pl.multiple_of(ids[1] * own, own), own), :], near_weight, weight_sem
        )
        fetch.start()
    for copies in later[1:]:
        for copy in copies:
            copy.start()
    for copy in first:
        copy.wait()
    if not columns:
        value = jnp.concatenate([left_all[r] for r in range(count)], axis=1)
    sums = jnp.zeros((own, 128), f32)
    sent = []
    for i, (c, copies) in enumerate(zip(chunks, later)):
        for copy in copies:
            copy.wait()
        block = right_all[:, :, c].reshape(tokens, step)
        grad = t_dot(left_all[...], block) if columns else dot(value, block)
        result[:, c] = grad.astype(result.dtype)
        if gains:
            if i == 0:
                fetch.wait()
            product = grad * near_weight[:, c].astype(f32)
            for j in range(0, step, 128):
                sums = sums + product[:, j : j + 128]
            moves = [pltpu.make_async_copy(result.at[:, c], out.at[:, c], out_sems.at[i, 0])]
        else:
            wide = out.shape[2]
            moves = [
                pltpu.make_async_copy(
                    result.at[:, pl.ds(j, wide)], out.at[j // wide], out_sems.at[i, (j - c.start) // wide]
                )
                for j in range(c.start, c.stop, wide)
            ]
        for move in moves:
            move.start()
        sent.extend(moves)
    if gains:
        gain_grad[...] = row_of(jnp.sum(sums, axis=1, keepdims=True), own) / own_row(gain, ids[1], own)
    for copy in sent:
        copy.wait()


def grad_qkv_place_kernel(ids, got, weight, gain, up_gain, out, gain_grads):
    total = 0.0
    for c in range(3):
        value = jnp.concatenate(
            [got[j, c * HD : (c + 1) * HD, :].astype(f32) for j in range(got.shape[0])], axis=0
        ).T
        out[c] = value
        total = total + jnp.sum(value * weight[c].astype(f32), axis=1, keepdims=True)
    out.send()
    first = row_of(total, total.shape[0]) / own_row(gain, ids[1], total.shape[0])
    row = lax.broadcasted_iota(jnp.int32, gain_grads.shape, 0)
    gain_grads[...] = jnp.where(row == 0, first, up_gain[...])


def outputs_kernel(parts, ids, *refs):
    blocks, (out, first, second) = refs[:parts], refs[parts:]
    part, width = blocks[0].shape[0], out.shape[1]
    for k in range(parts):
        out[block_at(ids[0], k, part), :] = blocks[-k % parts][:, :width]
    out.send()
    count = first.shape[1] // 128
    total = sum(b[:, width:].astype(f32) for b in blocks)
    total = total[: 2 * count] + total[2 * count : 4 * count]
    for i in range(count):
        first[:, i * 128 : (i + 1) * 128] = total[i : i + 1]
        second[:, i * 128 : (i + 1) * 128] = total[count + i : count + i + 1]


def layer_output_kernel(ids, even, odd, out):
    part = even.shape[0] // 2
    for k in range(4):
        out[block_at(ids[0], k, part), :] = (odd if k % 2 else even)[k // 2 * part : (k // 2 + 1) * part, :]


def body(
    layer_input,
    segment_ids,
    qkv_weight,
    out_weight,
    up_weight,
    down_weight,
    input_gain,
    heads_gain,
    middle_gain,
    hidden_gain,
    cotangent,
):
    rows, row_count, width = layer_input.shape
    T, C = lax.axis_size("tp"), lax.axis_size("cp")
    part = rows // T
    head_width = qkv_weight.shape[2]
    if head_width // HD != C or row_count != 1 or rows != 128 or T != 4 or 64 * part != width:
        return body_general(
            layer_input, segment_ids, qkv_weight, out_weight, up_weight, down_weight,
            input_gain, heads_gain, middle_gain, hidden_gain, cotangent,
        )
    tokens = rows * C
    hidden = up_weight.shape[1]
    wide = width // C
    high = hidden // C
    ids = jnp.stack([lax.axis_index("tp"), lax.axis_index("cp")]).astype(jnp.int32)
    x = layer_input.reshape(rows, width)
    gy = cotangent.reshape(rows, width)
    weight3 = jnp.transpose(qkv_weight, (1, 0, 2))
    gain_in, gain_mid = input_gain.reshape(1, -1), middle_gain.reshape(1, -1)
    gain_heads, gain_hid = heads_gain.reshape(1, -1), hidden_gain.reshape(1, -1)
    inner, base = tables(rows, C)
    inner2 = jnp.asarray(np.concatenate([inner, inner], axis=2))
    base2 = jnp.asarray(np.concatenate([base, base], axis=2))
    base_t = np.zeros((4, HD, 128), np.float32)
    base_t[:, :, :C] = np.transpose(base, (0, 2, 1))
    base_t = jnp.asarray(base_t)
    wide_part = width + 128
    step = 512

    def piece_shapes(columns):
        return [shape((part, columns), f32)] + [shape((part, columns), bf16)] * (T - 1)

    def exchange(pieces):
        return [swap_tp(pieces[k - 1], k) for k in range(T - 1, 0, -1)]

    def spread(block):
        return exchange([block] * (T - 1))

    def to_cp(value):
        return lax.all_to_all(value, "cp", 0, 0, tiled=True)

    def entire(value):
        return (value, value.shape, None)

    def own_rows(value):
        return (value, (part, width), lambda ids: (block_at(ids[0], 0, part), slice(None)))

    def third(c):
        return lambda ids: (pl.ds(c, 1), slice(None), slice(None))

    cols, first_rows = lambda i, *_: (0, i), lambda i, *_: (i, 0)
    origin2, origin3 = lambda i, *_: (0, 0), lambda i, *_: (0, 0, 0)
    sixth = lambda c, h: lambda ids: (pl.ds(c, 1), pl.ds(h * width // 2, width // 2), slice(None))
    weight_sixths = [Far(weight3, (1, width // 2, head_width), sixth(c, h)) for c in range(3) for h in range(2)]
    weight_thirds = [Far(weight3, (1, width, head_width), third(c)) for c in range(3)]

    pair, gy_x, sent = call(
        functools.partial(project_kernel, T),
        [Far(shape((2, rows, width), bf16)), Far(shape((rows, width), bf16)), Far(shape((C, 3 * HD + 16, rows), bf16))],
        [ids, Far(x), Far(gain_in), Far(gy), Far(inner2), Far(base2), Far(segment_ids.reshape(1, rows)), *weight_thirds],
        [scalars()] + [whole()] * 9, mb=14,
    )
    got = to_cp(sent)
    near_out, near_x, near_gy, near_mid, near_heads, near_hid, near_in = bring(
        [entire(out_weight), own_rows(x), own_rows(gy), entire(gain_mid), entire(gain_heads),
         entire(gain_hid), entire(gain_in)],
        ids, after=[Pin(sent)],
    )
    back, mixed, lse, far_got, pair = call(
        functools.partial(attend_kernel, T),
        [Far(shape((C, HD, rows), bf16)), Far(shape((HD, tokens), f32)), Far(shape((1, tokens), f32)),
         Far(shape((C, 3 * HD + 16, rows), bf16))],
        [ids, got], [scalars(), whole()],
        scratch=[pltpu.VMEM((tokens, HD), bf16), pltpu.VMEM((tokens, 16), f32)],
        mb=10, after=[near_heads], carry=[pair],
    )
    att = to_cp(back)
    early = lax.all_gather(pair, "cp", axis=0)

    own, *pieces, near_att = call(
        functools.partial(out_kernel, T),
        piece_shapes(wide_part) + [Near(shape((C, HD, rows), bf16))],
        [att, near_heads, near_out],
    )
    (grad_hid,) = call(
        grad_hidden_kernel, [Near(shape((rows, hidden), f32))],
        [Pin(gy_x), Pin(down_weight)],
        [fixed((rows, width)), pl.BlockSpec((step, width), first_rows)],
        [pl.BlockSpec((rows, step), cols)],
        grid=(hidden // step,), after=[own], mb=10, cost=3,
    )
    x1, u_own, gain_row, norms = call(
        functools.partial(middle_kernel, T, head_width),
        [Near(shape((part, width), f32)), shape((part, width), bf16), Near(shape((1, width), f32)), Near(shape((8, 128), f32))],
        [own, *exchange(pieces), near_x, near_mid], after=[grad_hid],
    )
    u_blocks = [u_own] + spread(u_own)
    near_up, near_flip = call(
        functools.partial(prepare_kernel, 256),
        [Near(shape((width, hidden), bf16)), Near(shape((hidden, width), bf16))],
        [Pin(up_weight)], [pl.BlockSpec(memory_space=pl.ANY)],
        scratch=[pltpu.SemaphoreType.DMA((width // 256,))], after=[u_own], mb=6,
    )

    act, slope, u_cols, stats = call(
        functools.partial(up_kernel, T, step),
        [Near(shape((rows, hidden), f32)), Near(shape((rows, hidden), f32)), Near(shape((C, rows, wide), bf16)),
         shape((8, rows), f32)],
        [*u_blocks, near_up, grad_hid, near_hid, norms],
        scratch=[pltpu.VMEM((rows, width), bf16)], mb=8, after=[near_flip],
    )
    gh, both, norms, own, *pieces = call(
        functools.partial(hidden_back_kernel, T, FF, step),
        [Far(shape((rows, hidden), bf16)), Far(shape((C, rows, wide + high), bf16)), Near(shape((8, rows), f32))] + piece_shapes(width),
        [stats, *spread(stats), act, slope, grad_hid, near_hid, near_flip, u_cols], mb=10,
    )
    gu_got = exchange(pieces)
    both_got = to_cp(both)
    gh_all = lax.all_gather(gh, "cp", axis=0)
    down_parts = [
        Far(down_weight, (step, width), (lambda at: lambda ids: (pl.ds(at, step), slice(None)))(i))
        for i in range(0, hidden, step)
    ]
    gx1, gb_own = call(
        functools.partial(middle_back_kernel, T),
        [Near(shape((part, width), f32)), shape((part, wide_part), bf16)],
        [own, *gu_got, gain_row, near_x, x1, near_gy, near_mid], cost=8,
    )
    gb_blocks = [gb_own] + spread(gb_own)
    y_own, y_second, y_odd = call(
        down_kernel,
        [Far(shape((part, width), f32)), Far(shape((part, width), f32)), Far(shape((2 * part, width), bf16))],
        [Far(both, (C, rows, high), lambda ids: (slice(None), slice(None), pl.ds(wide, high))), *down_parts],
        after=[gb_own], cost=20, mb=14,
    )
    (near_out,) = bring([entire(out_weight)], ids, after=[gb_own])

    def product(left, right, columns, which, offset, own, after, weight=None, gain=None, cost=20):
        anywhere = pl.BlockSpec(memory_space=pl.ANY)
        size = right.shape[-1]
        chunk = 2 * step
        left_dims = (tokens, own) if columns else (C, own, rows)
        if weight is not None:
            outs = [Pin(shape((own, size), f32)), shape((1, own), f32)]
            more, more_specs = [Pin(weight), gain], [anywhere, whole()]
            out_specs, extra = [anywhere, whole()], [pltpu.VMEM((own, size), bf16), pltpu.SemaphoreType.DMA]
        else:
            outs, out_specs = [Pin(shape((C, own, size // C), bf16))], [anywhere]
            more, more_specs, extra = [], [], []
        return call(
            functools.partial(product_kernel, chunk, columns, which, offset), outs,
            [ids, Pin(left), Pin(right), *more], [scalars()] + [anywhere] * 2 + more_specs, out_specs,
            scratch=[pltpu.VMEM(left_dims, bf16), pltpu.VMEM((C, rows, size), bf16),
                     pltpu.VMEM((own, size), plain(outs[0]).dtype),
                     pltpu.SemaphoreType.DMA((C,)), pltpu.SemaphoreType.DMA((size // chunk,)),
                     pltpu.SemaphoreType.DMA((size // chunk, chunk * C // size))] + extra,
            mb=14, after=after, cost=cost,
        )


    sent, gb, y_odd = call(
        functools.partial(heads_back_kernel, T),
        [Far(shape((C, 2 * HD, rows), bf16)), Far(shape((rows, width), bf16))],
        [*gb_blocks, norms, near_att, near_heads, near_out], after=[Pin(both_got)], carry=[y_odd],
    )
    y_got = swap_tp(y_odd, 1)
    gb_all = lax.all_gather(gb, "cp", axis=0)
    grads = to_cp(sent)
    near_got, near_mixed, near_lse, near_inner, near_base = bring(
        [entire(far_got), entire(mixed), entire(lse), entire(inner2), entire(base_t)], ids, after=[Pin(sent)]
    )
    grad_down, hidden_gain_grad = product(both_got, early, True, 1, wide, high, [Pin(sent)], down_weight, gain_hid)
    (y_half,) = call(half_kernel, [shape((part, width), bf16)], [Far(y_second), y_got], after=[Pin(sent)])
    y_last = swap_tp(y_half, 2)
    gq_sent, z = call(
        functools.partial(attend_back_kernel, T),
        [Far(shape((C, 3 * HD, rows), bf16)), Far(shape((C, HD, rows), bf16))],
        [ids, near_got, grads, near_mixed, near_lse, near_inner, near_base], [scalars()] + [whole()] * 6,
        scratch=[pltpu.VMEM((tokens, HD), bf16), pltpu.VMEM((tokens, HD), bf16), pltpu.VMEM((tokens, 16), f32),
                 pltpu.VMEM((HD, tokens), f32), pltpu.VMEM((HD, tokens), f32)],
        mb=12, cost=8, after=[Pin(grad_down), y_half],
    )
    gq = to_cp(gq_sent)
    (y_low,) = call(
        output_kernel, [shape((part, width), bf16)], [Far(y_own), y_got, y_last, x1], after=[Pin(gq_sent)]
    )
    y_even = swap_tp(y_low, 2)
    (grad_qkv,) = product(gq_sent, early, False, 0, 0, 3 * HD, [y_low])
    own, *pieces = call(
        functools.partial(input_back_kernel, T), piece_shapes(width), [gq, *weight_sixths], mb=10, cost=10,
    )
    ga_got = exchange(pieces)
    (y_even,) = call(join_kernel, [shape((2 * part, width), bf16)], [y_low, y_even], after=[own])
    y_odd = swap_tp(y_even, 1)
    grad_qkv_got = to_cp(grad_qkv)
    grad_up, up_gain = product(both_got, gh_all, True, None, 0, wide, [own], up_weight, gain_mid)
    own_wide = lambda ids: (slice(None), pl.ds(pl.multiple_of(ids[1] * wide, wide), wide), slice(None))
    grad_qkv, gains = call(
        grad_qkv_place_kernel,
        [Far(shape((3, wide, head_width), f32)), shape((8, wide), f32)],
        [ids, grad_qkv_got, Far(weight3, (3, wide, head_width), own_wide), gain_in, up_gain],
        [scalars()] + [whole()] * 4, after=[own], cost=20,
    )
    (final,) = call(
        functools.partial(final_kernel, T),
        [shape((part, wide_part), bf16)],
        [own, *ga_got, near_x, gx1, near_in, gains], after=[Pin(grad_up)],
    )
    final_blocks = [final] + spread(final)
    grad_out, heads_gain_grad = product(z, gb_all, False, None, 0, HD, [final], out_weight, gain_heads)
    (layer_output,) = call(
        layer_output_kernel, [Far(shape((rows, width), bf16))], [ids, y_even, y_odd], [scalars(), whole(), whole()],
        after=[final],
    )
    grad_input, input_gain_grad, middle_gain_grad = call(
        functools.partial(outputs_kernel, T),
        [Far(shape((rows, width), bf16)), shape((1, wide), f32), shape((1, wide), f32)],
        [ids, *final_blocks], [scalars()] + [whole()] * T, after=[Pin(grad_out), Pin(layer_output)],
    )
    return (
        layer_output.reshape(layer_input.shape),
        grad_input.reshape(layer_input.shape),
        jnp.transpose(grad_qkv, (1, 0, 2)),
        grad_out,
        grad_up,
        grad_down,
        input_gain_grad.reshape(-1),
        heads_gain_grad.reshape(-1),
        middle_gain_grad.reshape(-1),
        hidden_gain_grad.reshape(-1),
    )


def solution(mesh):
    placed = (
        P("cp", None, None),
        P("cp", None),
        P(None, None, "tp"),
        P("tp", None),
        P(None, "tp"),
        P("tp", None),
        P(),
        P("tp"),
        P(),
        P("tp"),
        P("cp", None, None),
    )
    return jax.shard_map(
        body,
        mesh=mesh,
        in_specs=placed,
        out_specs=(
            P("cp", None, None),
            P("cp", None, None),
            P("cp", None, "tp"),
            P(("tp", "cp"), None),
            P("cp", "tp"),
            P(("tp", "cp"), None),
            P("cp"),
            P(("tp", "cp")),
            P("cp"),
            P(("tp", "cp")),
        ),
        check_vma=False,
    )
```

```python
import functools

import jax
import jax.numpy as jnp
import numpy as np
from jax import lax
from jax.experimental import pallas as pl
from jax.experimental.pallas import tpu as pltpu
from jax.sharding import PartitionSpec as P

HD = 64
D = 2048
FF = 8192

eps = 1e-05
scale_base = 512.0
masked_score = -1e30
f32 = jnp.float32
bf16 = jnp.bfloat16


def dot(a, b):
    return jnp.dot(a, b, preferred_element_type=f32)


def dot_t(a, b):
    return lax.dot_general(a, b, (((1,), (1,)), ((), ())), preferred_element_type=f32)


def t_dot(a, b):
    return lax.dot_general(a, b, (((0,), (0,)), ((), ())), preferred_element_type=f32)


def pairs(count, k):
    return [(i, i ^ k) for i in range(count)]


def swap_tp(value, k):
    return lax.ppermute(value, "tp", pairs(lax.axis_size("tp"), k))


def tp_order(value):
    count, me = lax.axis_size("tp"), lax.axis_index("tp")
    part = value.shape[0] // count
    return jnp.concatenate(
        [lax.dynamic_slice_in_dim(value, (me ^ k) * part, part, 0) for k in range(count)], axis=0
    )


def tp_scatter_sum(partial_sum):
    count = lax.axis_size("tp")
    part = partial_sum.shape[0] // count
    low = partial_sum.astype(bf16)
    total = partial_sum[:part]
    for k in range(1, count):
        total = total + swap_tp(low[k * part : (k + 1) * part], k).astype(f32)
    return total


def tp_gather(block):
    count = lax.axis_size("tp")
    return jnp.concatenate([block] + [swap_tp(block, k) for k in range(1, count)], axis=0)


def tp_sum(value):
    total = value
    for k in range(1, lax.axis_size("tp")):
        total = total + swap_tp(value, k)
    return total


def tp_token_sum(value):
    count = lax.axis_size("tp")
    blocks = value.reshape(value.shape[0], count, -1)
    total = blocks
    for k in range(1, count):
        got = swap_tp(blocks, k)
        total = total + jnp.stack([got[:, j ^ k] for j in range(count)], axis=1)
    return total.reshape(value.shape)


def cp_columns(value):
    return lax.all_to_all(value, "cp", split_axis=1, concat_axis=0, tiled=True)


def cp_gather(value):
    return lax.all_gather(value, "cp", axis=0, tiled=True)


def xpos_tables(positions):
    column = jnp.arange(HD // 2, dtype=f32)
    frequency = 10000.0 ** (-column / (HD // 2))
    zeta = (2.0 * column + 0.4 * HD) / (1.4 * HD)
    places = positions.astype(f32)[:, None]
    angle = places * frequency
    return (jnp.cos(angle), jnp.sin(angle), zeta ** (places / scale_base))


def turn(vector, cosine, sine, factor):
    paired = vector.reshape(vector.shape[:-1] + (HD // 2, 2))
    first, second = paired[..., 0], paired[..., 1]
    cosine, sine, factor = cosine[:, None], sine[:, None], factor[:, None]
    turned = jnp.stack(
        [(first * cosine - second * sine) * factor, (first * sine + second * cosine) * factor],
        axis=-1,
    )
    return turned.reshape(vector.shape)


def norm_rows(vector):
    center = jnp.mean(vector, axis=-1, keepdims=True)
    shifted = vector - center
    scaling = lax.rsqrt(jnp.mean(shifted * shifted, axis=-1, keepdims=True) + eps)
    return (shifted * scaling, scaling)


def norm_back(grad_result, gain, normed, scaling):
    grad_normed = grad_result * gain
    first = jnp.mean(grad_normed, axis=-1, keepdims=True)
    cross = jnp.mean(grad_normed * normed, axis=-1, keepdims=True)
    return scaling * (grad_normed - first - normed * cross)


def attend(queries, keys, values, allowed):
    scores = jnp.einsum("qhd,khd->hqk", queries, keys, preferred_element_type=f32) * HD**-0.5
    scores = jnp.where(allowed[None], scores, masked_score)
    top = jnp.max(scores, axis=-1, keepdims=True)
    exponent = jnp.where(allowed[None], jnp.exp(scores - top), 0.0)
    total = jnp.sum(exponent, axis=-1, keepdims=True)
    probability = (exponent / total).astype(bf16)
    mixed = jnp.einsum("hqk,khd->qhd", probability, values, preferred_element_type=f32)
    return (mixed, top + jnp.log(total))


def attend_back(queries, keys, values, allowed, lse, grad, delta):
    scores = jnp.einsum("qhd,khd->hqk", queries, keys, preferred_element_type=f32) * HD**-0.5
    probability = jnp.where(allowed[None], jnp.exp(scores - lse), 0.0)
    grad_prob = jnp.einsum("qhd,khd->hqk", grad, values, preferred_element_type=f32)
    grad_scores = (probability * (grad_prob - delta.T[:, :, None])).astype(bf16)
    grad_q = jnp.einsum("hqk,khd->qhd", grad_scores, keys, preferred_element_type=f32) * HD**-0.5
    grad_k = jnp.einsum("hqk,qhd->khd", grad_scores, queries, preferred_element_type=f32) * HD**-0.5
    grad_v = jnp.einsum(
        "hqk,qhd->khd", probability.astype(bf16), grad, preferred_element_type=f32
    )
    return (grad_q, grad_k, grad_v)


def body_general(
    layer_input,
    segment_ids,
    qkv_weight,
    out_weight,
    up_weight,
    down_weight,
    input_gain,
    heads_gain,
    middle_gain,
    hidden_gain,
    cotangent,
):
    local_len, row_count, width = layer_input.shape
    tp_count, cp_count = lax.axis_size("tp"), lax.axis_size("cp")
    me_tp, me_cp = lax.axis_index("tp"), lax.axis_index("cp")
    part = local_len // tp_count
    head_width = qkv_weight.shape[2]
    heads = head_width // HD
    by_head = heads % cp_count == 0
    own_heads = heads // cp_count if by_head else heads
    weight3 = jnp.transpose(qkv_weight, (1, 0, 2))

    x = tp_order(layer_input.reshape(local_len, width))
    gy = tp_order(cotangent.reshape(local_len, width))
    seg = tp_order(segment_ids)[:, 0]
    natural = tp_order(jnp.arange(local_len, dtype=jnp.int32))
    position = me_cp * local_len + natural
    position_all = (jnp.arange(cp_count, dtype=jnp.int32)[:, None] * local_len + natural).reshape(-1)

    stream = x.astype(f32)
    normed_one, scaling_one = norm_rows(stream)
    a = (normed_one * input_gain).astype(bf16)
    a_all = cp_gather(a)
    cosine, sine, factor = xpos_tables(position)
    raw_q = dot(a, weight3[0]).reshape(local_len, heads, HD)
    raw_k = dot(a, weight3[1]).reshape(local_len, heads, HD)
    raw_v = dot(a, weight3[2]).reshape(local_len, heads, HD)
    q = turn(raw_q, cosine, sine, factor).astype(bf16)
    k = turn(raw_k, cosine, sine, 1.0 / factor).astype(bf16)
    v = raw_v.astype(bf16)
    if by_head:
        extra = jnp.broadcast_to(seg.astype(bf16)[:, None, None], (local_len, cp_count, 16))
        sent = jnp.concatenate(
            [t.reshape(local_len, cp_count, own_heads * HD) for t in (q, k, v)] + [extra], axis=-1
        )
        got = lax.all_to_all(sent, "cp", split_axis=1, concat_axis=0, tiled=True)[:, 0]
        span = own_heads * HD
        q_all, k_all, v_all = (
            got[:, i * span : (i + 1) * span].reshape(-1, own_heads, HD) for i in range(3)
        )
        seg_all = got[:, 3 * span]
        seg_q, position_q = seg_all, position_all
    else:
        q_all, k_all, v_all = q, cp_gather(k), cp_gather(v)
        seg_all = cp_gather(seg.astype(bf16))
        seg_q, position_q = seg.astype(bf16), position
    allowed = (position_all[None, :] <= position_q[:, None]) & (seg_q[:, None] == seg_all[None, :])
    mixed, lse = attend(q_all, k_all, v_all, allowed)
    if by_head:
        attended = lax.all_to_all(
            mixed.astype(bf16).reshape(cp_count * local_len, own_heads * HD),
            "cp", split_axis=0, concat_axis=1, tiled=True,
        ).astype(f32)
    else:
        attended = mixed.reshape(local_len, head_width)

    sums = tp_token_sum(jnp.stack([jnp.sum(attended, axis=1), jnp.sum(attended * attended, axis=1)]))
    center = sums[0] / width
    scaling_h = lax.rsqrt(sums[1] / width - center * center + eps)[:, None]
    normed_h = (attended - center[:, None]) * scaling_h
    z = (normed_h * heads_gain).astype(bf16)
    gain_row = tp_sum(jnp.dot(heads_gain, out_weight.astype(f32)))
    branch = tp_scatter_sum(dot(z, out_weight))
    x1 = stream[:part] + branch
    normed_two, scaling_two = norm_rows(x1)
    u = tp_gather((normed_two * middle_gain).astype(bf16))

    grad_hid = dot_t(gy, down_weight)
    grad_normed = grad_hid * hidden_gain
    hidden = dot(u, up_weight)
    cdf = 0.5 * (1.0 + lax.erf(hidden * (0.5**0.5)))
    act = hidden * cdf
    slope = cdf + hidden * jnp.exp(-0.5 * hidden * hidden) * 0.3989422804014327
    sums = tp_token_sum(
        jnp.stack(
            [
                jnp.sum(act, axis=1),
                jnp.sum(act * act, axis=1),
                jnp.sum(grad_normed, axis=1),
                jnp.sum(grad_normed * act, axis=1),
            ]
        )
    )
    center = sums[0] / FF
    scaling_f = lax.rsqrt(sums[1] / FF - center * center + eps)
    first = sums[2] / FF
    cross = scaling_f * (sums[3] / FF - center * first)
    normed_f = (act - center[:, None]) * scaling_f[:, None]
    z2 = (normed_f * hidden_gain).astype(bf16)
    grad_act = scaling_f[:, None] * (grad_normed - first[:, None] - normed_f * cross[:, None])
    gh = (grad_act * slope).astype(bf16)
    hidden_gain_sum = jnp.sum(grad_hid * normed_f, axis=0)
    gu = tp_scatter_sum(dot_t(gh, up_weight))
    gx1 = gy[:part].astype(f32) + norm_back(gu, middle_gain, normed_two, scaling_two)
    middle_gain_sum = jnp.sum(gu * normed_two, axis=0)
    gb_own = gx1.astype(bf16)
    gb_f = gb_own.astype(f32)
    first = jnp.sum(gb_f * gain_row, axis=1) / width
    cross = jnp.sum(gb_f * branch, axis=1) / width
    gb = tp_gather(gb_own)
    stats = tp_gather(jnp.stack([first, cross], axis=1))

    gz = dot_t(gb, out_weight)
    heads_gain_sum = jnp.sum(gz * normed_h, axis=0)
    go = (scaling_h * (gz * heads_gain - stats[:, :1] - normed_h * stats[:, 1:])).astype(bf16)
    if by_head:
        grad_mixed = cp_columns(go).reshape(-1, own_heads, HD)
    else:
        grad_mixed = go.reshape(local_len, heads, HD)
    delta = jnp.sum(grad_mixed.astype(f32) * mixed, axis=-1)
    gq, gk, gv = attend_back(q_all, k_all, v_all, allowed, lse, grad_mixed, delta)
    if by_head:
        cos_all, sin_all, factor_all = xpos_tables(position_all)
    else:
        cos_all, sin_all, factor_all = cosine, sine, factor
        gk = lax.psum_scatter(gk.astype(bf16), "cp", scatter_dimension=0, tiled=True).astype(f32)
        gv = lax.psum_scatter(gv.astype(bf16), "cp", scatter_dimension=0, tiled=True).astype(f32)
    gq = turn(gq, cos_all, -sin_all, factor_all)
    gk = turn(gk, cos_all, -sin_all, 1.0 / factor_all)
    grads = jnp.stack([gq, gk, gv], axis=1).astype(bf16)
    if by_head:
        grads_own = grads.reshape(-1, 3 * own_heads * HD)
        grads = lax.all_to_all(
            grads.reshape(-1, 3, own_heads * HD), "cp", split_axis=0, concat_axis=2, tiled=True
        )
    else:
        grads = grads.reshape(local_len, 3, head_width)
        grads_own = lax.all_to_all(grads, "cp", split_axis=2, concat_axis=0, tiled=True)
        grads_own = grads_own.reshape(-1, 3 * head_width // cp_count)
    ga = (
        dot_t(grads[:, 0], weight3[0]) + dot_t(grads[:, 1], weight3[1]) + dot_t(grads[:, 2], weight3[2])
    )
    ga = tp_scatter_sum(ga)
    input_gain_sum = jnp.sum(ga * normed_one[:part], axis=0)
    grad_in = gx1 + norm_back(ga, input_gain, normed_one[:part], scaling_one[:part])

    y = (x1 + tp_scatter_sum(dot(z2, down_weight))).astype(bf16)
    layer_output = tp_order(tp_gather(y)).reshape(layer_input.shape)
    grad_input = tp_order(tp_gather(grad_in.astype(bf16))).reshape(layer_input.shape)

    grad_down = t_dot(cp_columns(z2), cp_gather(gy))
    grad_up = t_dot(cp_columns(u), cp_gather(gh))
    grad_out = t_dot(cp_columns(z), cp_gather(gb))
    grad_qkv = t_dot(a_all, grads_own).astype(bf16)
    grad_qkv = lax.all_to_all(
        grad_qkv.reshape(width, 3, head_width // cp_count), "cp", split_axis=0, concat_axis=2, tiled=True
    ).astype(f32)

    def cp_sum_own(vector):
        return jnp.sum(lax.all_to_all(vector.reshape(cp_count, -1), "cp", 0, 0, tiled=True), axis=0)

    def both_sum_own(vector):
        return tp_sum(cp_sum_own(vector))

    return (
        layer_output,
        grad_input,
        grad_qkv,
        grad_out,
        grad_up,
        grad_down,
        both_sum_own(input_gain_sum),
        cp_sum_own(heads_gain_sum),
        both_sum_own(middle_gain_sum),
        cp_sum_own(hidden_gain_sum),
    )


INTERPRET = False


def params(megabytes):
    return pltpu.CompilerParams(vmem_limit_bytes=megabytes * 1024 * 1024)


def shape(dims, kind):
    return jax.ShapeDtypeStruct(dims, kind)


def whole():
    return pl.BlockSpec(memory_space=pltpu.VMEM)


def scalars():
    return pl.BlockSpec(memory_space=pltpu.SMEM)


class Pin:
    def __init__(self, value):
        self.value = value


class Far(Pin):
    def __init__(self, value, dims=None, block=None):
        super().__init__(value)
        self.dims = tuple(value.shape) if dims is None else dims
        self.block = block


class Near:
    def __init__(self, value):
        self.value = value


class Fetched:
    def __init__(self, ref, copy):
        self.ref, self.copy, self.shape = ref, copy, ref.shape

    def ready(self):
        if self.copy is not None:
            self.copy.wait()
            self.copy = None

    def __getitem__(self, index):
        self.ready()
        return self.ref[index]


class Stored:
    def __init__(self, ref, copy):
        self.ref, self.copy, self.shape, self.sent = ref, copy, ref.shape, False

    def send(self):
        if not self.sent:
            self.copy.start()
            self.sent = True

    def __getitem__(self, index):
        return self.ref[index]

    def __setitem__(self, index, value):
        self.ref[index] = value

    @property
    def dtype(self):
        return self.ref.dtype


def plain(value):
    return value.value if isinstance(value, (Pin, Near)) else value


def pinned(value):
    return value if INTERPRET else pltpu.with_memory_space_constraint(value, pltpu.HBM)


def call(
    kernel, outs, args, specs=None, out_specs=None, grid=None, scratch=(), mb=8, cost=0.3, after=(), carry=(), prefetch=0
):
    specs = list(specs) if specs is not None else [whole() for _ in args]
    out_specs = list(out_specs) if out_specs is not None else [whole() for _ in outs]
    count, extra, kept, made = len(args), len(after), len(carry), len(outs)
    anywhere = pl.BlockSpec(memory_space=pl.ANY)
    far_in = [i for i, t in enumerate(args) if isinstance(t, Far)]
    far_out = [i for i, t in enumerate(outs) if isinstance(t, Far)]
    for i in far_in:
        specs[i] = anywhere
    for i in far_out:
        out_specs[i] = anywhere
    moving = [pltpu.VMEM(args[i].dims, args[i].value.dtype) for i in far_in]
    moving += [pltpu.VMEM(outs[i].dims, outs[i].value.dtype) for i in far_out]
    moving += [pltpu.SemaphoreType.DMA] * (len(far_in) + len(far_out))
    own_scratch = len(scratch)

    def run(*refs):
        ins = list(refs[:count])
        results = refs[count + extra + kept :]
        products = list(results[:made])
        rest = results[made + kept :]
        slots, sems = rest[own_scratch : own_scratch + len(far_in) + len(far_out)], rest[own_scratch + len(far_in) + len(far_out) :]
        for i, slot, sem in zip(far_in, slots, sems):
            source = refs[i]
            if args[i].block is not None:
                source = source.at[args[i].block(refs[0])]
            copy = pltpu.make_async_copy(source, slot, sem)
            copy.start()
            ins[i] = Fetched(slot, copy)
        stored = [
            Stored(slot, pltpu.make_async_copy(slot, results[i], sem))
            for i, slot, sem in zip(far_out, slots[len(far_in) :], sems[len(far_in) :])
        ]
        for i, product in zip(far_out, stored):
            products[i] = product
        kernel(*ins, *products, *rest[:own_scratch])
        for i in far_in:
            ins[i].ready()
        for product in stored:
            product.send()
        for product in stored:
            product.copy.wait()

    def result(value):
        dims = plain(value)
        if INTERPRET or value is dims:
            return dims
        return (pltpu.HBM if isinstance(value, Pin) else pltpu.VMEM)(dims.shape, dims.dtype)

    where = dict(
        in_specs=specs + [anywhere] * (extra + kept),
        out_specs=tuple(out_specs + [anywhere] * kept),
        scratch_shapes=list(scratch) + moving,
    )
    if prefetch:
        where["in_specs"] = where["in_specs"][prefetch:]
        where = {"grid_spec": pltpu.PrefetchScalarGridSpec(num_scalar_prefetch=prefetch, grid=grid, **where)}
    elif grid is not None:
        where["grid"] = grid
    return pl.pallas_call(
        run,
        out_shape=tuple(result(t) for t in outs) + tuple(result(Pin(shape(t.shape, t.dtype))) for t in carry),
        input_output_aliases={count + extra + i: made + i for i in range(kept)},
        compiler_params=params(mb),
        cost_estimate=pl.CostEstimate(flops=int(cost * 1e9), bytes_accessed=0, transcendentals=0),
        interpret=INTERPRET,
        **where,
    )(*[pinned(t.value) if isinstance(t, Pin) else t for t in list(args) + list(after)], *[pinned(t) for t in carry])


def bring(items, ids, after=(), carry=(), cost=0.3):
    def kernel(ids, *refs):
        sources, slots, sems = refs[: len(items)], refs[len(items) : 2 * len(items)], refs[2 * len(items) :]
        copies = []
        for (_, _, block), source, slot, sem in zip(items, sources, slots, sems):
            copies.append(pltpu.make_async_copy(source if block is None else source.at[block(ids)], slot, sem))
        for copy in copies:
            copy.start()
        for copy in copies:
            copy.wait()

    return call(
        kernel,
        [Near(shape(dims, array.dtype)) for array, dims, _ in items],
        [ids] + [Pin(array) for array, _, _ in items],
        [scalars()] + [pl.BlockSpec(memory_space=pl.ANY)] * len(items),
        scratch=[pltpu.SemaphoreType.DMA] * len(items), after=after, carry=carry, mb=2, cost=cost,
    )


def fixed(dims):
    return pl.BlockSpec(dims, lambda i: (0,) * len(dims))


def split_low(value):
    high = value.astype(bf16)
    return high, (value - high.astype(f32)).astype(bf16)


def lanes_of(columns, rows):
    lane = lax.broadcasted_iota(jnp.int32, (rows, 128), 1)
    out = jnp.zeros((rows, 128), f32)
    for i, column in enumerate(columns):
        out = jnp.where(lane == i, column.astype(f32), out)
    return out


def own_order(me, part, index):
    return ((index // part) ^ me) * part + index % part


def block_at(me, k, part):
    return pl.ds(pl.multiple_of((me ^ k) * part, part), part)


def swap_pairs(value, axis):
    size = value.shape[axis]
    place = lax.broadcasted_iota(jnp.int32, value.shape, axis)
    return jnp.where(
        place % 2 == 0, pltpu.roll(value, size - 1, axis), pltpu.roll(value, 1, axis)
    )


def tables(local_len, cp_count):
    column = np.arange(HD) // 2
    frequency = 10000.0 ** (-column / (HD // 2))
    zeta = (2.0 * column + 0.4 * HD) / (1.4 * HD)

    def of(places):
        angle = places[:, None] * frequency
        factor = zeta ** (places[:, None] / scale_base)
        return np.stack([np.cos(angle), np.sin(angle), factor, 1.0 / factor]).astype(np.float32)

    return of(np.arange(local_len)), of(np.arange(cp_count) * local_len)


def project_kernel(parts, ids, x, gain, gy, inner, base, seg, w0, w1, w2, pair, out):
    me, mine = ids[0], ids[1]
    rows, width = pair.shape[1:]
    part = rows // parts
    heads = out.shape[0]
    x.ready()
    for k in range(parts):
        normed, _ = norm_rows(x.ref[block_at(me, k, part), :].astype(f32))
        pair[0, k * part : (k + 1) * part, :] = (normed * gain[...]).astype(bf16)
    gy.ready()
    for k in range(parts):
        pair[1, k * part : (k + 1) * part, :] = gy.ref[block_at(me, k, part), :]
    pair.send()
    inner.ready()
    here = [base[kind, pl.ds(mine, 1), :] for kind in range(4)]
    table = [
        jnp.concatenate([inner.ref[kind, block_at(me, k, part), :] for k in range(parts)], axis=0)
        for kind in range(4)
    ]
    cosine = table[0] * here[0] - table[1] * here[1]
    sine = table[1] * here[0] + table[0] * here[1]
    lane = lax.broadcasted_iota(jnp.int32, cosine.shape, 1)
    sine = jnp.where(lane % 2 == 0, -sine, sine)
    place = lax.broadcasted_iota(jnp.int32, (rows, rows), 1)
    source = lax.broadcasted_iota(jnp.int32, (rows, rows), 0)
    moved = (own_order(me, part, place) == source).astype(bf16)
    ids_row = jnp.broadcast_to(seg[...].astype(f32), (16, rows)).astype(bf16)
    ordered = dot(ids_row, moved).astype(bf16)
    for j in range(heads):
        out[j, 3 * HD : 3 * HD + 16, :] = ordered
    for c, weight in enumerate((w0, w1, w2)):
        acc = dot(pair[0], weight[0])
        factor = (table[2] * here[2], table[3] * here[3], None)[c]
        for i in range(acc.shape[1] // 128):
            piece = acc[:, i * 128 : (i + 1) * 128]
            if c < 2:
                piece = piece * (cosine * factor) + swap_pairs(piece, 1) * (sine * factor)
            turned = piece.T.astype(bf16)
            for h in range(128 // HD):
                out[i * (128 // HD) + h, c * HD : (c + 1) * HD, :] = turned[h * HD : (h + 1) * HD]
    out.send()


def gather_heads(got, keys, ids_col, values=None):
    for j in range(got.shape[0]):
        rows = slice(j * got.shape[2], (j + 1) * got.shape[2])
        both = jnp.concatenate([got[j, HD : 3 * HD, :].astype(f32)], axis=0).T
        keys[rows, :] = both[:, :HD].astype(bf16)
        if values is not None:
            values[rows, :] = both[:, HD:].astype(bf16)
        ids_col[rows, :] = got[j, 3 * HD : 3 * HD + 16, :].astype(f32).T


def visible_scores(me, part, scores, ids_col, ids_row, count, first, group):
    same = ids_col[0:count, 0:1] == ids_row
    length = group
    key = lax.broadcasted_iota(jnp.int32, (length, length), 0)
    query = lax.broadcasted_iota(jnp.int32, (length, length), 1)
    rows = first
    own = lambda index: (index // rows) * rows + own_order(me, part, index % rows)
    earlier = own(key) <= own(query)
    if count > length:
        earlier = jnp.concatenate([jnp.ones((count - length, length), jnp.bool_), earlier], axis=0)
    return same & earlier


def attend_kernel(parts, ids, got, out, mixed, lse, kept, keys, ids_col):
    me = ids[0]
    kept[...] = got[...]
    kept.send()
    blocks, _, rows = got.shape
    part = rows // parts
    gather_heads(got, keys, ids_col)
    group = 4 if blocks % 4 == 0 else 1
    width = group * rows
    for i in range(blocks // group):
        mine = range(i * group, (i + 1) * group)
        query = jnp.concatenate([got[j, :HD, :] for j in mine], axis=1) * bf16(HD**-0.5)
        ids_row = jnp.concatenate([got[j, 3 * HD : 3 * HD + 16, :].astype(f32)[:1] for j in mine], axis=1)
        count = (i + 1) * width
        scores = dot(keys[0:count, :], query)
        allowed = visible_scores(me, part, scores, ids_col, ids_row, count, rows, width)
        scores = jnp.where(allowed, scores, masked_score)
        top = jnp.max(scores, axis=0, keepdims=True)
        exponent = jnp.exp(scores - top)
        total = jnp.sum(exponent, axis=0, keepdims=True)
        value = jnp.concatenate([got[j, 2 * HD : 3 * HD, :] for j in range((i + 1) * group)], axis=1)
        result = dot(value, exponent.astype(bf16)) / total
        mixed[:, i * width : (i + 1) * width] = result
        lse[:, i * width : (i + 1) * width] = top + jnp.log(total)
        for n, j in enumerate(mine):
            out[j] = result[:, n * rows : (n + 1) * rows].astype(bf16)
    out.send()


def out_kernel(parts, att, gain, weight, own, *refs):
    pieces, kept = refs[:-1], refs[-1]
    kept[...] = att[...]
    blocks, _, rows = att.shape
    part, width = rows // parts, weight.shape[1]
    value = jnp.concatenate([att[j].astype(f32) for j in range(blocks)], axis=0).T
    high, low = split_low(jnp.mean(value, axis=1, keepdims=True))
    centred = value - (high.astype(f32) + low.astype(f32))
    square = split_low(jnp.sum(centred * centred, axis=1, keepdims=True))
    gains = gain[...]
    row = lax.broadcasted_iota(jnp.int32, (16, gains.shape[1]), 0)
    gain_high, gain_low = (t.astype(f32) for t in split_low(gains))
    gain_rows = jnp.where(row == 0, gain_high, jnp.where(row == 1, gain_low, 0.0))
    left = jnp.concatenate([(centred * gains).astype(bf16), gain_rows.astype(bf16)], axis=0)
    total = dot(left, weight[...])
    gain_row = total[rows : rows + 1] + total[rows + 1 : rows + 2]
    gain_block = jnp.concatenate([gain_row[:, i : i + 128] for i in range(0, width, 128)], axis=0)
    stats = lanes_of([high, low, *square], rows).T
    empty = jnp.zeros((part - gain_block.shape[0] - 1, 128), f32)

    def extra(k):
        row = jnp.concatenate([stats[i : i + 1, k * part : (k + 1) * part] for i in range(4)], axis=1)
        return jnp.concatenate([gain_block, row, empty], axis=0).astype(bf16)

    own[:, :width] = total[:part]
    own[:, width:] = extra(0).astype(f32)
    for k, piece in enumerate(pieces, 1):
        here = slice(k * part, (k + 1) * part)
        piece[:, :width] = total[here].astype(bf16)
        piece[:, width:] = extra(k)


def middle_kernel(parts, head_width, own, *refs):
    got, (x, gain, x1, u, gain_row, norms) = refs[: parts - 1][::-1], refs[parts - 1 :]
    part, width = x1.shape
    blocks = [own] + list(got)
    extras = [b[:, width:].astype(f32) for b in blocks]
    count = width // 128
    rows = [jnp.concatenate([e[i : i + 1] for i in range(count)], axis=1) for e in extras]
    columns = [jnp.broadcast_to(e[count : count + 1], (128, 128)).T[:, 0:1] for e in extras]
    means = [c[:part] + c[part : 2 * part] for c in columns]
    squares = [c[2 * part : 3 * part] + c[3 * part :] for c in columns]
    gain_row[...] = sum(rows)
    mean = sum(means) / parts
    spread = sum(squares) + head_width * sum((m - mean) * (m - mean) for m in means)
    scaling = lax.rsqrt(spread / width + eps)
    total = sum(b[:, :width].astype(f32) for b in blocks)
    for m, row in zip(means, rows):
        total = total + (m - mean) * row
    value = x[...].astype(f32) + total * scaling
    x1[...] = value
    normed, _ = norm_rows(value)
    u[...] = (normed * gain[...]).astype(bf16)
    norms[...] = jnp.zeros_like(norms)
    norms[0:2, :part] = lanes_of([mean, scaling], part).T[0:2, :]


def grad_hidden_kernel(gy, weight, grad):
    grad[...] = dot_t(gy[0], weight[...])


def prepare_kernel(step, up, near_up, flipped, up_sems):
    chunks = [slice(i, i + step) for i in range(0, up.shape[0], step)]
    copies = [pltpu.make_async_copy(up.at[c, :], near_up.at[c, :], up_sems.at[i]) for i, c in enumerate(chunks)]
    for copy in copies:
        copy.start()
    for copy, chunk in zip(copies, chunks):
        copy.wait()
        flipped[:, chunk] = near_up[chunk, :].T


def up_kernel(parts, step, own, *refs):
    got, refs = refs[: parts - 1][::-1], refs[parts - 1 :]
    weight, grad, gain, norms, act, slope, u, stats, rows_u = refs
    part = own.shape[0]
    rows, width = rows_u.shape
    for k, block in enumerate([own] + list(got)):
        rows_u[k * part : (k + 1) * part, :] = block[...]
    wide = u.shape[2]
    for j in range(u.shape[0]):
        u[j] = rows_u[:, j * wide : (j + 1) * wide]
    total = [jnp.zeros((rows, 128), f32)] * 4
    for i in range(0, weight.shape[1], step):
        here = slice(i, i + step)
        hidden = dot(rows_u[...], weight[:, here])
        cdf = 0.5 * (1.0 + lax.erf(hidden * (0.5**0.5)))
        value = hidden * cdf
        act[:, here] = value
        slope[:, here] = cdf + hidden * jnp.exp(-0.5 * hidden * hidden) * 0.3989422804014327
        grad_normed = grad[:, here] * gain[:, here]
        columns = [value, value * value, grad_normed, grad_normed * value]
        for n, column in enumerate(columns):
            for j in range(0, step, 128):
                total[n] = total[n] + column[:, j : j + 128]
    sums = lanes_of([jnp.sum(t, axis=1, keepdims=True) for t in total], rows)
    stats[...] = sums.T[:8, :]
    stats[4:6, :] = norms[0:2, :]


def swap_lane_blocks(value, k, part):
    lanes = value.shape[1]
    lane = lax.broadcasted_iota(jnp.int32, value.shape, 1)
    distance = 1
    while distance <= k:
        if k & distance:
            move = distance * part
            value = jnp.where(
                (lane // move) % 2 == 0,
                pltpu.roll(value, lanes - move, 1),
                pltpu.roll(value, move, 1),
            )
        distance *= 2
    return value


def hidden_back_kernel(parts, full, step, own, *refs):
    got, refs = refs[: parts - 1][::-1], refs[parts - 1 :]
    act, slope, grad, gain, weight, u, gh, both, norms, own_out = refs[:10]
    pieces = refs[10:]
    first_wide = u.shape[2]
    both[:, :, :first_wide] = u[...]
    rows = act.shape[0]
    part = rows // parts
    total = own[...]
    for k, block in enumerate(got, 1):
        total = total + swap_lane_blocks(block[...], k, part)
    norms[...] = jnp.zeros_like(norms)
    for k, block in enumerate([own] + list(got)):
        norms[0:2, k * part : (k + 1) * part] = block[4:6, :part]
    mean = total[0:1] / full
    scaling = lax.rsqrt(total[1:2] / full - mean * mean + eps)
    first = total[2:3] / full
    cross = scaling * (total[3:4] / full - mean * first)
    row = lax.broadcasted_iota(jnp.int32, (rows, rows), 0)
    table = jnp.zeros((rows, rows), f32)
    for i, value in enumerate([mean, scaling, first, cross]):
        table = jnp.where(row == i, value, table)
    cols = table.T
    mean, scaling, first, cross = (cols[:, i : i + 1] for i in range(4))
    wide = both.shape[2] - first_wide
    for i in range(0, act.shape[1], step):
        here = slice(i, i + step)
        normed = (act[:, here] - mean) * scaling
        low = (normed * gain[:, here]).astype(bf16)
        for j in range(0, step, wide):
            both[(i + j) // wide, :, first_wide:] = low[:, j : j + wide]
        value = scaling * (grad[:, here] * gain[:, here] - first - normed * cross) * slope[:, here]
        gh[:, here] = value.astype(bf16)
    both.send()
    gh.send()
    width = weight.shape[1]
    for i in range(0, width, step):
        here = slice(i, i + step)
        result = dot(gh[...], weight[:, here])
        own_out[:, here] = result[:part]
        for k, piece in enumerate(pieces, 1):
            piece[:, here] = result[k * part : (k + 1) * part].astype(bf16)


def down_kernel(z2, *refs):
    weights, (own, second, odd) = refs[:-3], refs[-3:]
    _, _, wide = z2.shape
    part = own.shape[0]
    total = 0.0
    for i, weight in enumerate(weights):
        rows = weight.shape[0]
        left = jnp.concatenate([z2[j] for j in range(i * rows // wide, (i + 1) * rows // wide)], axis=1)
        total = total + dot(left, weight[...])
    own[...] = total[:part]
    second[...] = total[2 * part : 3 * part]
    odd[:part, :] = total[part : 2 * part].astype(bf16)
    odd[part:, :] = total[3 * part :].astype(bf16)


def half_kernel(second, got, out):
    part = second.shape[0]
    out[...] = (second[...] + got[part:, :].astype(f32)).astype(bf16)


def join_kernel(first, second, out):
    part = first.shape[0]
    out[:part, :] = first[...]
    out[part:, :] = second[...]


def middle_back_kernel(parts, own, *refs):
    got, refs = refs[: parts - 1][::-1], refs[parts - 1 :]
    gain_row, x, x1, gy, gain, gx1, gb = refs
    part, width = x1.shape
    grad = own[...]
    for block in got:
        grad = grad + block[...].astype(f32)
    value = x1[...]
    normed, scaling = norm_rows(value)
    result = gy[...].astype(f32) + norm_back(grad, gain[...], normed, scaling)
    gx1[...] = result
    low = result.astype(bf16)
    gb[:, :width] = low
    low = low.astype(f32)
    first = jnp.sum(low * gain_row[...], axis=1, keepdims=True) / width
    cross = jnp.sum(low * (value - x[...].astype(f32)), axis=1, keepdims=True) / width
    gb[:, width:] = lanes_of([*split_low(first), *split_low(cross)], part).astype(bf16)


def heads_back_kernel(parts, own, *refs):
    got, refs = refs[: parts - 1][::-1], refs[parts - 1 :]
    stats, att, gain, weight, sent, gb = refs
    blocks, _, rows = att.shape
    part, width = own.shape[0], gb.shape[1]
    for k, block in enumerate([own] + list(got)):
        gb[k * part : (k + 1) * part, :] = block[:, :width]
    gb.send()
    columns = jnp.concatenate([b[:, width:].astype(f32) for b in [own] + list(got)], axis=0).T
    first = columns[0:1] + columns[1:2]
    cross = columns[2:3] + columns[3:4]
    mean, scaling = stats[0:1], stats[1:2]
    grad = dot_t(weight[...], gb[...])
    value = jnp.concatenate([att[j].astype(f32) for j in range(blocks)], axis=0)
    normed = (value - mean) * scaling
    gain_col = jnp.broadcast_to(gain[...], (8, gain.shape[1])).T[:, 0:1]
    go = (scaling * (grad * gain_col - first - normed * cross)).astype(bf16)
    z = (normed * gain_col).astype(bf16)
    for j in range(blocks):
        sent[j, :HD, :] = go[j * HD : (j + 1) * HD]
        sent[j, HD:, :] = z[j * HD : (j + 1) * HD]


def turn_back(grad, table, base, j, inverse):
    here = [base[kind, :, j : j + 1] for kind in range(4)]
    cosine = table[0] * here[0] - table[1] * here[1]
    sine = table[1] * here[0] + table[0] * here[1]
    factor = table[3] * here[3] if inverse else table[2] * here[2]
    row = lax.broadcasted_iota(jnp.int32, grad.shape, 0)
    sine = jnp.where(row % 2 == 0, sine, -sine)
    return (grad * cosine + swap_pairs(grad, 0) * sine) * factor


def attend_back_kernel(parts, ids, got, grads, mixed, lse, inner, base, out, z, keys, values, ids_col, gk, gv):
    me = ids[0]
    for j in range(grads.shape[0]):
        z[j] = grads[j, HD:, :]
    z.send()
    blocks, _, rows = got.shape
    part = rows // parts
    gather_heads(got, keys, ids_col, values)
    gk[...] = jnp.zeros_like(gk)
    gv[...] = jnp.zeros_like(gv)
    table = []
    for kind in range(4):
        ordered = jnp.concatenate(
            [inner[kind, block_at(me, k, part), :] for k in range(parts)], axis=0
        )
        table.append(ordered.T[:HD])
    group = 2 if blocks % 2 == 0 else 1
    width = group * rows
    for i in range(blocks // group):
        mine = range(i * group, (i + 1) * group)
        query = jnp.concatenate([got[j, :HD, :] for j in mine], axis=1) * bf16(HD**-0.5)
        ids_row = jnp.concatenate([got[j, 3 * HD : 3 * HD + 16, :].astype(f32)[:1] for j in mine], axis=1)
        go = jnp.concatenate([grads[j, :HD, :] for j in mine], axis=1)
        span = slice(i * width, (i + 1) * width)
        delta = jnp.sum(go.astype(f32) * mixed[:, span], axis=0, keepdims=True)
        count = (i + 1) * width
        scores = dot(keys[0:count, :], query)
        allowed = visible_scores(me, part, scores, ids_col, ids_row, count, rows, width)
        probability = jnp.where(allowed, jnp.exp(jnp.minimum(scores - lse[:, span], 0.5)), 0.0)
        grad_prob = dot(values[0:count, :], go)
        grad_scores = (probability * (grad_prob - delta)).astype(bf16)
        gv[:, 0:count] += dot_t(go, probability.astype(bf16))
        gk[:, 0:count] += dot_t(query, grad_scores)
        key = jnp.concatenate([got[j, HD : 2 * HD, :] for j in range((i + 1) * group)], axis=1)
        gq = dot(key, grad_scores) * HD**-0.5
        for n, j in enumerate(mine):
            piece = turn_back(gq[:, n * rows : (n + 1) * rows], table, base, j, False)
            out[j, :HD, :] = piece.astype(bf16)
    for j in range(blocks):
        span = slice(j * rows, (j + 1) * rows)
        out[j, HD : 2 * HD, :] = turn_back(gk[:, span], table, base, j, True).astype(bf16)
        out[j, 2 * HD :, :] = gv[:, span].astype(bf16)


def input_back_kernel(parts, got, *refs):
    weights, own_out, pieces = refs[:6], refs[6], refs[7:]
    part, width = own_out.shape
    half = width // 2
    grads = []
    for c in range(3):
        here = slice(c * HD, (c + 1) * HD)
        grad = jnp.concatenate([got[j, here, :].astype(f32) for j in range(got.shape[0])], axis=0)
        grads.append(grad.T.astype(bf16))
    totals = [0.0, 0.0]
    for n, weight in enumerate(weights):
        totals[n % 2] = totals[n % 2] + dot_t(grads[n // 2], weight[0])
    for h, result in enumerate(totals):
        here = slice(h * half, (h + 1) * half)
        own_out[:, here] = result[:part]
        for k, piece in enumerate(pieces, 1):
            piece[:, here] = result[k * part : (k + 1) * part].astype(bf16)


def final_kernel(parts, own, *refs):
    got, (x, gx1, gain, gains, out) = refs[: parts - 1][::-1], refs[parts - 1 :]
    part, width = gx1.shape
    grad = own[...]
    for block in got:
        grad = grad + block[...].astype(f32)
    normed, scaling = norm_rows(x[...].astype(f32))
    out[:, :width] = (gx1[...] + norm_back(grad, gain[...], normed, scaling)).astype(bf16)
    rows = gains[0:2]
    pieces = [rows[n : n + 1, i : i + 128] for n in range(2) for i in range(0, rows.shape[1], 128)]
    high, low = split_low(jnp.concatenate(pieces, axis=0))
    empty = jnp.zeros((part - 2 * len(pieces), 128), f32)
    tail = jnp.concatenate([high.astype(f32), low.astype(f32), empty], axis=0)
    out[:, width:] = tail.astype(bf16)


def output_kernel(own, got, last, x1, out):
    total = own[...] + x1[...] + got[: out.shape[0], :].astype(f32)
    out[...] = (total + last[...].astype(f32)).astype(bf16)


def own_row(gain, index, own):
    total = jnp.zeros((1, own), f32)
    for j in range(gain.shape[1] // own):
        total = jnp.where(index == j, gain[:, j * own : (j + 1) * own], total)
    return total


def row_of(column, columns):
    return jnp.broadcast_to(column, (columns, 128)).T[:1, :]


def product_kernel(step, columns, which, offset, ids, left, right, *refs):
    count = left.shape[0]
    gains = len(refs) > 7
    if gains:
        (weight, gain, out, gain_grad), refs = refs[:4], refs[4:]
        (near_weight, weight_sem), refs = refs[-2:], refs[:-2]
    else:
        out, refs = refs[0], refs[1:]
    left_all, right_all, result, left_sems, right_sems, out_sems = refs
    rows, size = right.shape[-2:]
    own = result.shape[0]
    tokens = count * rows
    chunks = [slice(i, i + step) for i in range(0, size, step)]

    first = []
    for r in range(count):
        source = left.at[r]
        if columns:
            source, place = source.at[:, pl.ds(offset, own)], left_all.at[pl.ds(r * rows, rows), :]
        else:
            source, place = source.at[pl.ds(offset, own), :], left_all.at[r]
        first.append(pltpu.make_async_copy(source, place, left_sems.at[r]))
    side = right if which is None else right.at[:, which]
    later = [
        [pltpu.make_async_copy(side.at[:, :, c], right_all.at[:, :, c], right_sems.at[i])] for i, c in enumerate(chunks)
    ]
    for copy in first + later[0]:
        copy.start()
    if gains:
        fetch = pltpu.make_async_copy(
            weight.at[pl.ds(pl.multiple_of(ids[1] * own, own), own), :], near_weight, weight_sem
        )
        fetch.start()
    for copies in later[1:]:
        for copy in copies:
            copy.start()
    for copy in first:
        copy.wait()
    if not columns:
        value = jnp.concatenate([left_all[r] for r in range(count)], axis=1)
    sums = jnp.zeros((own, 128), f32)
    sent = []
    for i, (c, copies) in enumerate(zip(chunks, later)):
        for copy in copies:
            copy.wait()
        block = right_all[:, :, c].reshape(tokens, step)
        grad = t_dot(left_all[...], block) if columns else dot(value, block)
        result[:, c] = grad.astype(result.dtype)
        if gains:
            if i == 0:
                fetch.wait()
            product = grad * near_weight[:, c].astype(f32)
            for j in range(0, step, 128):
                sums = sums + product[:, j : j + 128]
            moves = [pltpu.make_async_copy(result.at[:, c], out.at[:, c], out_sems.at[i, 0])]
        else:
            wide = out.shape[2]
            moves = [
                pltpu.make_async_copy(
                    result.at[:, pl.ds(j, wide)], out.at[j // wide], out_sems.at[i, (j - c.start) // wide]
                )
                for j in range(c.start, c.stop, wide)
            ]
        for move in moves:
            move.start()
        sent.extend(moves)
    if gains:
        gain_grad[...] = row_of(jnp.sum(sums, axis=1, keepdims=True), own) / own_row(gain, ids[1], own)
    for copy in sent:
        copy.wait()


def grad_qkv_place_kernel(ids, got, weight, gain, up_gain, out, gain_grads):
    total = 0.0
    for c in range(3):
        value = jnp.concatenate(
            [got[j, c * HD : (c + 1) * HD, :].astype(f32) for j in range(got.shape[0])], axis=0
        ).T
        out[c] = value
        total = total + jnp.sum(value * weight[c].astype(f32), axis=1, keepdims=True)
    out.send()
    first = row_of(total, total.shape[0]) / own_row(gain, ids[1], total.shape[0])
    row = lax.broadcasted_iota(jnp.int32, gain_grads.shape, 0)
    gain_grads[...] = jnp.where(row == 0, first, up_gain[...])


def outputs_kernel(parts, ids, *refs):
    blocks, (out, first, second) = refs[:parts], refs[parts:]
    part, width = blocks[0].shape[0], out.shape[1]
    for k in range(parts):
        out[block_at(ids[0], k, part), :] = blocks[-k % parts][:, :width]
    out.send()
    count = first.shape[1] // 128
    total = sum(b[:, width:].astype(f32) for b in blocks)
    total = total[: 2 * count] + total[2 * count : 4 * count]
    for i in range(count):
        first[:, i * 128 : (i + 1) * 128] = total[i : i + 1]
        second[:, i * 128 : (i + 1) * 128] = total[count + i : count + i + 1]


def layer_output_kernel(ids, even, odd, out):
    part = even.shape[0] // 2
    for k in range(4):
        out[block_at(ids[0], k, part), :] = (odd if k % 2 else even)[k // 2 * part : (k // 2 + 1) * part, :]


def body(
    layer_input,
    segment_ids,
    qkv_weight,
    out_weight,
    up_weight,
    down_weight,
    input_gain,
    heads_gain,
    middle_gain,
    hidden_gain,
    cotangent,
):
    rows, row_count, width = layer_input.shape
    T, C = lax.axis_size("tp"), lax.axis_size("cp")
    part = rows // T
    head_width = qkv_weight.shape[2]
    if head_width // HD != C or row_count != 1 or rows != 128 or T != 4 or 64 * part != width:
        return body_general(
            layer_input, segment_ids, qkv_weight, out_weight, up_weight, down_weight,
            input_gain, heads_gain, middle_gain, hidden_gain, cotangent,
        )
    tokens = rows * C
    hidden = up_weight.shape[1]
    wide = width // C
    high = hidden // C
    ids = jnp.stack([lax.axis_index("tp"), lax.axis_index("cp")]).astype(jnp.int32)
    x = layer_input.reshape(rows, width)
    gy = cotangent.reshape(rows, width)
    weight3 = jnp.transpose(qkv_weight, (1, 0, 2))
    gain_in, gain_mid = input_gain.reshape(1, -1), middle_gain.reshape(1, -1)
    gain_heads, gain_hid = heads_gain.reshape(1, -1), hidden_gain.reshape(1, -1)
    inner, base = tables(rows, C)
    inner2 = jnp.asarray(np.concatenate([inner, inner], axis=2))
    base2 = jnp.asarray(np.concatenate([base, base], axis=2))
    base_t = np.zeros((4, HD, 128), np.float32)
    base_t[:, :, :C] = np.transpose(base, (0, 2, 1))
    base_t = jnp.asarray(base_t)
    wide_part = width + 128
    step = 512

    def piece_shapes(columns):
        return [shape((part, columns), f32)] + [shape((part, columns), bf16)] * (T - 1)

    def exchange(pieces):
        return [swap_tp(pieces[k - 1], k) for k in range(T - 1, 0, -1)]

    def spread(block):
        return exchange([block] * (T - 1))

    def to_cp(value):
        return lax.all_to_all(value, "cp", 0, 0, tiled=True)

    def entire(value):
        return (value, value.shape, None)

    def own_rows(value):
        return (value, (part, width), lambda ids: (block_at(ids[0], 0, part), slice(None)))

    def third(c):
        return lambda ids: (pl.ds(c, 1), slice(None), slice(None))

    cols, first_rows = lambda i, *_: (0, i), lambda i, *_: (i, 0)
    origin2, origin3 = lambda i, *_: (0, 0), lambda i, *_: (0, 0, 0)
    sixth = lambda c, h: lambda ids: (pl.ds(c, 1), pl.ds(h * width // 2, width // 2), slice(None))
    weight_sixths = [Far(weight3, (1, width // 2, head_width), sixth(c, h)) for c in range(3) for h in range(2)]
    weight_thirds = [Far(weight3, (1, width, head_width), third(c)) for c in range(3)]

    pair, sent = call(
        functools.partial(project_kernel, T),
        [Far(shape((2, rows, width), bf16)), Far(shape((C, 3 * HD + 16, rows), bf16))],
        [ids, Far(x), Far(gain_in), Far(gy), Far(inner2), Far(base2), Far(segment_ids.reshape(1, rows)), *weight_thirds],
        [scalars()] + [whole()] * 9, mb=14,
    )
    got = to_cp(sent)
    near_out, near_x, near_gy, near_mid, near_heads, near_hid, near_in = bring(
        [entire(out_weight), own_rows(x), own_rows(gy), entire(gain_mid), entire(gain_heads),
         entire(gain_hid), entire(gain_in)],
        ids, after=[Pin(sent)],
    )
    back, mixed, lse, far_got, pair = call(
        functools.partial(attend_kernel, T),
        [Far(shape((C, HD, rows), bf16)), Far(shape((HD, tokens), f32)), Far(shape((1, tokens), f32)),
         Far(shape((C, 3 * HD + 16, rows), bf16))],
        [ids, got], [scalars(), whole()],
        scratch=[pltpu.VMEM((tokens, HD), bf16), pltpu.VMEM((tokens, 16), f32)],
        mb=10, after=[near_heads], carry=[pair],
    )
    att = to_cp(back)
    early = lax.all_gather(pair, "cp", axis=0)

    own, *pieces, near_att = call(
        functools.partial(out_kernel, T),
        piece_shapes(wide_part) + [Near(shape((C, HD, rows), bf16))],
        [att, near_heads, near_out],
    )
    (grad_hid,) = call(
        grad_hidden_kernel, [Near(shape((rows, hidden), f32))],
        [Pin(pair), Pin(down_weight)],
        [pl.BlockSpec((1, rows, width), lambda i: (1, 0, 0)), pl.BlockSpec((step, width), first_rows)],
        [pl.BlockSpec((rows, step), cols)],
        grid=(hidden // step,), after=[own], mb=10, cost=3,
    )
    x1, u_own, gain_row, norms = call(
        functools.partial(middle_kernel, T, head_width),
        [Near(shape((part, width), f32)), shape((part, width), bf16), Near(shape((1, width), f32)), Near(shape((8, 128), f32))],
        [own, *exchange(pieces), near_x, near_mid], after=[grad_hid],
    )
    u_blocks = [u_own] + spread(u_own)
    near_up, near_flip = call(
        functools.partial(prepare_kernel, 256),
        [Near(shape((width, hidden), bf16)), Near(shape((hidden, width), bf16))],
        [Pin(up_weight)], [pl.BlockSpec(memory_space=pl.ANY)],
        scratch=[pltpu.SemaphoreType.DMA((width // 256,))], after=[u_own], mb=6,
    )

    act, slope, u_cols, stats = call(
        functools.partial(up_kernel, T, step),
        [Near(shape((rows, hidden), f32)), Near(shape((rows, hidden), f32)), Near(shape((C, rows, wide), bf16)),
         shape((8, rows), f32)],
        [*u_blocks, near_up, grad_hid, near_hid, norms],
        scratch=[pltpu.VMEM((rows, width), bf16)], mb=8, after=[near_flip],
    )
    gh, both, norms, own, *pieces = call(
        functools.partial(hidden_back_kernel, T, FF, step),
        [Far(shape((rows, hidden), bf16)), Far(shape((C, rows, wide + high), bf16)), Near(shape((8, rows), f32))] + piece_shapes(width),
        [stats, *spread(stats), act, slope, grad_hid, near_hid, near_flip, u_cols], mb=10,
    )
    gu_got = exchange(pieces)
    both_got = to_cp(both)
    gh_all = lax.all_gather(gh, "cp", axis=0)
    down_parts = [
        Far(down_weight, (step, width), (lambda at: lambda ids: (pl.ds(at, step), slice(None)))(i))
        for i in range(0, hidden, step)
    ]
    gx1, gb_own = call(
        functools.partial(middle_back_kernel, T),
        [Near(shape((part, width), f32)), shape((part, wide_part), bf16)],
        [own, *gu_got, gain_row, near_x, x1, near_gy, near_mid], cost=8,
    )
    gb_blocks = [gb_own] + spread(gb_own)
    y_own, y_second, y_odd = call(
        down_kernel,
        [Far(shape((part, width), f32)), Far(shape((part, width), f32)), Far(shape((2 * part, width), bf16))],
        [Far(both, (C, rows, high), lambda ids: (slice(None), slice(None), pl.ds(wide, high))), *down_parts],
        after=[gb_own], cost=20, mb=14,
    )
    (near_out,) = bring([entire(out_weight)], ids, after=[gb_own])

    def product(left, right, columns, which, offset, own, after, weight=None, gain=None, cost=20):
        anywhere = pl.BlockSpec(memory_space=pl.ANY)
        size = right.shape[-1]
        chunk = 2 * step
        left_dims = (tokens, own) if columns else (C, own, rows)
        if weight is not None:
            outs = [Pin(shape((own, size), f32)), shape((1, own), f32)]
            more, more_specs = [Pin(weight), gain], [anywhere, whole()]
            out_specs, extra = [anywhere, whole()], [pltpu.VMEM((own, size), bf16), pltpu.SemaphoreType.DMA]
        else:
            outs, out_specs = [Pin(shape((C, own, size // C), bf16))], [anywhere]
            more, more_specs, extra = [], [], []
        return call(
            functools.partial(product_kernel, chunk, columns, which, offset), outs,
            [ids, Pin(left), Pin(right), *more], [scalars()] + [anywhere] * 2 + more_specs, out_specs,
            scratch=[pltpu.VMEM(left_dims, bf16), pltpu.VMEM((C, rows, size), bf16),
                     pltpu.VMEM((own, size), plain(outs[0]).dtype),
                     pltpu.SemaphoreType.DMA((C,)), pltpu.SemaphoreType.DMA((size // chunk,)),
                     pltpu.SemaphoreType.DMA((size // chunk, chunk * C // size))] + extra,
            mb=14, after=after, cost=cost,
        )


    sent, gb, y_odd = call(
        functools.partial(heads_back_kernel, T),
        [Far(shape((C, 2 * HD, rows), bf16)), Far(shape((rows, width), bf16))],
        [*gb_blocks, norms, near_att, near_heads, near_out], after=[Pin(both_got)], carry=[y_odd],
    )
    y_got = swap_tp(y_odd, 1)
    gb_all = lax.all_gather(gb, "cp", axis=0)
    grads = to_cp(sent)
    near_got, near_mixed, near_lse, near_inner, near_base = bring(
        [entire(far_got), entire(mixed), entire(lse), entire(inner2), entire(base_t)], ids, after=[Pin(sent)]
    )
    grad_down, hidden_gain_grad = product(both_got, early, True, 1, wide, high, [Pin(sent)], down_weight, gain_hid)
    (y_half,) = call(half_kernel, [shape((part, width), bf16)], [Far(y_second), y_got], after=[Pin(sent)])
    y_last = swap_tp(y_half, 2)
    gq_sent, z = call(
        functools.partial(attend_back_kernel, T),
        [Far(shape((C, 3 * HD, rows), bf16)), Far(shape((C, HD, rows), bf16))],
        [ids, near_got, grads, near_mixed, near_lse, near_inner, near_base], [scalars()] + [whole()] * 6,
        scratch=[pltpu.VMEM((tokens, HD), bf16), pltpu.VMEM((tokens, HD), bf16), pltpu.VMEM((tokens, 16), f32),
                 pltpu.VMEM((HD, tokens), f32), pltpu.VMEM((HD, tokens), f32)],
        mb=12, cost=8, after=[Pin(grad_down), y_half],
    )
    gq = to_cp(gq_sent)
    (y_low,) = call(
        output_kernel, [shape((part, width), bf16)], [Far(y_own), y_got, y_last, x1], after=[Pin(gq_sent)]
    )
    y_even = swap_tp(y_low, 2)
    (grad_qkv,) = product(gq_sent, early, False, 0, 0, 3 * HD, [y_low])
    own, *pieces = call(
        functools.partial(input_back_kernel, T), piece_shapes(width), [gq, *weight_sixths], mb=10, cost=10,
    )
    ga_got = exchange(pieces)
    (y_even,) = call(join_kernel, [shape((2 * part, width), bf16)], [y_low, y_even], after=[own])
    y_odd = swap_tp(y_even, 1)
    grad_qkv_got = to_cp(grad_qkv)
    grad_up, up_gain = product(both_got, gh_all, True, None, 0, wide, [own], up_weight, gain_mid)
    own_wide = lambda ids: (slice(None), pl.ds(pl.multiple_of(ids[1] * wide, wide), wide), slice(None))
    grad_qkv, gains = call(
        grad_qkv_place_kernel,
        [Far(shape((3, wide, head_width), f32)), shape((8, wide), f32)],
        [ids, grad_qkv_got, Far(weight3, (3, wide, head_width), own_wide), gain_in, up_gain],
        [scalars()] + [whole()] * 4, after=[own], cost=20,
    )
    (final,) = call(
        functools.partial(final_kernel, T),
        [shape((part, wide_part), bf16)],
        [own, *ga_got, near_x, gx1, near_in, gains], after=[Pin(grad_up)],
    )
    final_blocks = [final] + spread(final)
    grad_out, heads_gain_grad = product(z, gb_all, False, None, 0, HD, [final], out_weight, gain_heads)
    (layer_output,) = call(
        layer_output_kernel, [Far(shape((rows, width), bf16))], [ids, y_even, y_odd], [scalars(), whole(), whole()],
        after=[final],
    )
    grad_input, input_gain_grad, middle_gain_grad = call(
        functools.partial(outputs_kernel, T),
        [Far(shape((rows, width), bf16)), shape((1, wide), f32), shape((1, wide), f32)],
        [ids, *final_blocks], [scalars()] + [whole()] * T, after=[Pin(grad_out), Pin(layer_output)],
    )
    return (
        layer_output.reshape(layer_input.shape),
        grad_input.reshape(layer_input.shape),
        jnp.transpose(grad_qkv, (1, 0, 2)),
        grad_out,
        grad_up,
        grad_down,
        input_gain_grad.reshape(-1),
        heads_gain_grad.reshape(-1),
        middle_gain_grad.reshape(-1),
        hidden_gain_grad.reshape(-1),
    )


def solution(mesh):
    placed = (
        P("cp", None, None),
        P("cp", None),
        P(None, None, "tp"),
        P("tp", None),
        P(None, "tp"),
        P("tp", None),
        P(),
        P("tp"),
        P(),
        P("tp"),
        P("cp", None, None),
    )
    return jax.shard_map(
        body,
        mesh=mesh,
        in_specs=placed,
        out_specs=(
            P("cp", None, None),
            P("cp", None, None),
            P("cp", None, "tp"),
            P(("tp", "cp"), None),
            P("cp", "tp"),
            P(("tp", "cp"), None),
            P("cp"),
            P(("tp", "cp")),
            P("cp"),
            P(("tp", "cp")),
        ),
        check_vma=False,
    )
```

```python
import functools

import jax
import jax.numpy as jnp
import numpy as np
from jax import lax
from jax.experimental import pallas as pl
from jax.experimental.pallas import tpu as pltpu
from jax.sharding import PartitionSpec as P

HD = 64
D = 2048
FF = 8192

eps = 1e-05
scale_base = 512.0
masked_score = -1e30
f32 = jnp.float32
bf16 = jnp.bfloat16


def dot(a, b):
    return jnp.dot(a, b, preferred_element_type=f32)


def dot_t(a, b):
    return lax.dot_general(a, b, (((1,), (1,)), ((), ())), preferred_element_type=f32)


def t_dot(a, b):
    return lax.dot_general(a, b, (((0,), (0,)), ((), ())), preferred_element_type=f32)


def pairs(count, k):
    return [(i, i ^ k) for i in range(count)]


def swap_tp(value, k):
    return lax.ppermute(value, "tp", pairs(lax.axis_size("tp"), k))


def tp_order(value):
    count, me = lax.axis_size("tp"), lax.axis_index("tp")
    part = value.shape[0] // count
    return jnp.concatenate(
        [lax.dynamic_slice_in_dim(value, (me ^ k) * part, part, 0) for k in range(count)], axis=0
    )


def tp_scatter_sum(partial_sum):
    count = lax.axis_size("tp")
    part = partial_sum.shape[0] // count
    low = partial_sum.astype(bf16)
    total = partial_sum[:part]
    for k in range(1, count):
        total = total + swap_tp(low[k * part : (k + 1) * part], k).astype(f32)
    return total


def tp_gather(block):
    count = lax.axis_size("tp")
    return jnp.concatenate([block] + [swap_tp(block, k) for k in range(1, count)], axis=0)


def tp_sum(value):
    total = value
    for k in range(1, lax.axis_size("tp")):
        total = total + swap_tp(value, k)
    return total


def tp_token_sum(value):
    count = lax.axis_size("tp")
    blocks = value.reshape(value.shape[0], count, -1)
    total = blocks
    for k in range(1, count):
        got = swap_tp(blocks, k)
        total = total + jnp.stack([got[:, j ^ k] for j in range(count)], axis=1)
    return total.reshape(value.shape)


def cp_columns(value):
    return lax.all_to_all(value, "cp", split_axis=1, concat_axis=0, tiled=True)


def cp_gather(value):
    return lax.all_gather(value, "cp", axis=0, tiled=True)


def xpos_tables(positions):
    column = jnp.arange(HD // 2, dtype=f32)
    frequency = 10000.0 ** (-column / (HD // 2))
    zeta = (2.0 * column + 0.4 * HD) / (1.4 * HD)
    places = positions.astype(f32)[:, None]
    angle = places * frequency
    return (jnp.cos(angle), jnp.sin(angle), zeta ** (places / scale_base))


def turn(vector, cosine, sine, factor):
    paired = vector.reshape(vector.shape[:-1] + (HD // 2, 2))
    first, second = paired[..., 0], paired[..., 1]
    cosine, sine, factor = cosine[:, None], sine[:, None], factor[:, None]
    turned = jnp.stack(
        [(first * cosine - second * sine) * factor, (first * sine + second * cosine) * factor],
        axis=-1,
    )
    return turned.reshape(vector.shape)


def norm_rows(vector):
    center = jnp.mean(vector, axis=-1, keepdims=True)
    shifted = vector - center
    scaling = lax.rsqrt(jnp.mean(shifted * shifted, axis=-1, keepdims=True) + eps)
    return (shifted * scaling, scaling)


def norm_back(grad_result, gain, normed, scaling):
    grad_normed = grad_result * gain
    first = jnp.mean(grad_normed, axis=-1, keepdims=True)
    cross = jnp.mean(grad_normed * normed, axis=-1, keepdims=True)
    return scaling * (grad_normed - first - normed * cross)


def attend(queries, keys, values, allowed):
    scores = jnp.einsum("qhd,khd->hqk", queries, keys, preferred_element_type=f32) * HD**-0.5
    scores = jnp.where(allowed[None], scores, masked_score)
    top = jnp.max(scores, axis=-1, keepdims=True)
    exponent = jnp.where(allowed[None], jnp.exp(scores - top), 0.0)
    total = jnp.sum(exponent, axis=-1, keepdims=True)
    probability = (exponent / total).astype(bf16)
    mixed = jnp.einsum("hqk,khd->qhd", probability, values, preferred_element_type=f32)
    return (mixed, top + jnp.log(total))


def attend_back(queries, keys, values, allowed, lse, grad, delta):
    scores = jnp.einsum("qhd,khd->hqk", queries, keys, preferred_element_type=f32) * HD**-0.5
    probability = jnp.where(allowed[None], jnp.exp(scores - lse), 0.0)
    grad_prob = jnp.einsum("qhd,khd->hqk", grad, values, preferred_element_type=f32)
    grad_scores = (probability * (grad_prob - delta.T[:, :, None])).astype(bf16)
    grad_q = jnp.einsum("hqk,khd->qhd", grad_scores, keys, preferred_element_type=f32) * HD**-0.5
    grad_k = jnp.einsum("hqk,qhd->khd", grad_scores, queries, preferred_element_type=f32) * HD**-0.5
    grad_v = jnp.einsum(
        "hqk,qhd->khd", probability.astype(bf16), grad, preferred_element_type=f32
    )
    return (grad_q, grad_k, grad_v)


def body_general(
    layer_input,
    segment_ids,
    qkv_weight,
    out_weight,
    up_weight,
    down_weight,
    input_gain,
    heads_gain,
    middle_gain,
    hidden_gain,
    cotangent,
):
    local_len, row_count, width = layer_input.shape
    tp_count, cp_count = lax.axis_size("tp"), lax.axis_size("cp")
    me_tp, me_cp = lax.axis_index("tp"), lax.axis_index("cp")
    part = local_len // tp_count
    head_width = qkv_weight.shape[2]
    heads = head_width // HD
    by_head = heads % cp_count == 0
    own_heads = heads // cp_count if by_head else heads
    weight3 = jnp.transpose(qkv_weight, (1, 0, 2))

    x = tp_order(layer_input.reshape(local_len, width))
    gy = tp_order(cotangent.reshape(local_len, width))
    seg = tp_order(segment_ids)[:, 0]
    natural = tp_order(jnp.arange(local_len, dtype=jnp.int32))
    position = me_cp * local_len + natural
    position_all = (jnp.arange(cp_count, dtype=jnp.int32)[:, None] * local_len + natural).reshape(-1)

    stream = x.astype(f32)
    normed_one, scaling_one = norm_rows(stream)
    a = (normed_one * input_gain).astype(bf16)
    a_all = cp_gather(a)
    cosine, sine, factor = xpos_tables(position)
    raw_q = dot(a, weight3[0]).reshape(local_len, heads, HD)
    raw_k = dot(a, weight3[1]).reshape(local_len, heads, HD)
    raw_v = dot(a, weight3[2]).reshape(local_len, heads, HD)
    q = turn(raw_q, cosine, sine, factor).astype(bf16)
    k = turn(raw_k, cosine, sine, 1.0 / factor).astype(bf16)
    v = raw_v.astype(bf16)
    if by_head:
        extra = jnp.broadcast_to(seg.astype(bf16)[:, None, None], (local_len, cp_count, 16))
        sent = jnp.concatenate(
            [t.reshape(local_len, cp_count, own_heads * HD) for t in (q, k, v)] + [extra], axis=-1
        )
        got = lax.all_to_all(sent, "cp", split_axis=1, concat_axis=0, tiled=True)[:, 0]
        span = own_heads * HD
        q_all, k_all, v_all = (
            got[:, i * span : (i + 1) * span].reshape(-1, own_heads, HD) for i in range(3)
        )
        seg_all = got[:, 3 * span]
        seg_q, position_q = seg_all, position_all
    else:
        q_all, k_all, v_all = q, cp_gather(k), cp_gather(v)
        seg_all = cp_gather(seg.astype(bf16))
        seg_q, position_q = seg.astype(bf16), position
    allowed = (position_all[None, :] <= position_q[:, None]) & (seg_q[:, None] == seg_all[None, :])
    mixed, lse = attend(q_all, k_all, v_all, allowed)
    if by_head:
        attended = lax.all_to_all(
            mixed.astype(bf16).reshape(cp_count * local_len, own_heads * HD),
            "cp", split_axis=0, concat_axis=1, tiled=True,
        ).astype(f32)
    else:
        attended = mixed.reshape(local_len, head_width)

    sums = tp_token_sum(jnp.stack([jnp.sum(attended, axis=1), jnp.sum(attended * attended, axis=1)]))
    center = sums[0] / width
    scaling_h = lax.rsqrt(sums[1] / width - center * center + eps)[:, None]
    normed_h = (attended - center[:, None]) * scaling_h
    z = (normed_h * heads_gain).astype(bf16)
    gain_row = tp_sum(jnp.dot(heads_gain, out_weight.astype(f32)))
    branch = tp_scatter_sum(dot(z, out_weight))
    x1 = stream[:part] + branch
    normed_two, scaling_two = norm_rows(x1)
    u = tp_gather((normed_two * middle_gain).astype(bf16))

    grad_hid = dot_t(gy, down_weight)
    grad_normed = grad_hid * hidden_gain
    hidden = dot(u, up_weight)
    cdf = 0.5 * (1.0 + lax.erf(hidden * (0.5**0.5)))
    act = hidden * cdf
    slope = cdf + hidden * jnp.exp(-0.5 * hidden * hidden) * 0.3989422804014327
    sums = tp_token_sum(
        jnp.stack(
            [
                jnp.sum(act, axis=1),
                jnp.sum(act * act, axis=1),
                jnp.sum(grad_normed, axis=1),
                jnp.sum(grad_normed * act, axis=1),
            ]
        )
    )
    center = sums[0] / FF
    scaling_f = lax.rsqrt(sums[1] / FF - center * center + eps)
    first = sums[2] / FF
    cross = scaling_f * (sums[3] / FF - center * first)
    normed_f = (act - center[:, None]) * scaling_f[:, None]
    z2 = (normed_f * hidden_gain).astype(bf16)
    grad_act = scaling_f[:, None] * (grad_normed - first[:, None] - normed_f * cross[:, None])
    gh = (grad_act * slope).astype(bf16)
    hidden_gain_sum = jnp.sum(grad_hid * normed_f, axis=0)
    gu = tp_scatter_sum(dot_t(gh, up_weight))
    gx1 = gy[:part].astype(f32) + norm_back(gu, middle_gain, normed_two, scaling_two)
    middle_gain_sum = jnp.sum(gu * normed_two, axis=0)
    gb_own = gx1.astype(bf16)
    gb_f = gb_own.astype(f32)
    first = jnp.sum(gb_f * gain_row, axis=1) / width
    cross = jnp.sum(gb_f * branch, axis=1) / width
    gb = tp_gather(gb_own)
    stats = tp_gather(jnp.stack([first, cross], axis=1))

    gz = dot_t(gb, out_weight)
    heads_gain_sum = jnp.sum(gz * normed_h, axis=0)
    go = (scaling_h * (gz * heads_gain - stats[:, :1] - normed_h * stats[:, 1:])).astype(bf16)
    if by_head:
        grad_mixed = cp_columns(go).reshape(-1, own_heads, HD)
    else:
        grad_mixed = go.reshape(local_len, heads, HD)
    delta = jnp.sum(grad_mixed.astype(f32) * mixed, axis=-1)
    gq, gk, gv = attend_back(q_all, k_all, v_all, allowed, lse, grad_mixed, delta)
    if by_head:
        cos_all, sin_all, factor_all = xpos_tables(position_all)
    else:
        cos_all, sin_all, factor_all = cosine, sine, factor
        gk = lax.psum_scatter(gk.astype(bf16), "cp", scatter_dimension=0, tiled=True).astype(f32)
        gv = lax.psum_scatter(gv.astype(bf16), "cp", scatter_dimension=0, tiled=True).astype(f32)
    gq = turn(gq, cos_all, -sin_all, factor_all)
    gk = turn(gk, cos_all, -sin_all, 1.0 / factor_all)
    grads = jnp.stack([gq, gk, gv], axis=1).astype(bf16)
    if by_head:
        grads_own = grads.reshape(-1, 3 * own_heads * HD)
        grads = lax.all_to_all(
            grads.reshape(-1, 3, own_heads * HD), "cp", split_axis=0, concat_axis=2, tiled=True
        )
    else:
        grads = grads.reshape(local_len, 3, head_width)
        grads_own = lax.all_to_all(grads, "cp", split_axis=2, concat_axis=0, tiled=True)
        grads_own = grads_own.reshape(-1, 3 * head_width // cp_count)
    ga = (
        dot_t(grads[:, 0], weight3[0]) + dot_t(grads[:, 1], weight3[1]) + dot_t(grads[:, 2], weight3[2])
    )
    ga = tp_scatter_sum(ga)
    input_gain_sum = jnp.sum(ga * normed_one[:part], axis=0)
    grad_in = gx1 + norm_back(ga, input_gain, normed_one[:part], scaling_one[:part])

    y = (x1 + tp_scatter_sum(dot(z2, down_weight))).astype(bf16)
    layer_output = tp_order(tp_gather(y)).reshape(layer_input.shape)
    grad_input = tp_order(tp_gather(grad_in.astype(bf16))).reshape(layer_input.shape)

    grad_down = t_dot(cp_columns(z2), cp_gather(gy))
    grad_up = t_dot(cp_columns(u), cp_gather(gh))
    grad_out = t_dot(cp_columns(z), cp_gather(gb))
    grad_qkv = t_dot(a_all, grads_own).astype(bf16)
    grad_qkv = lax.all_to_all(
        grad_qkv.reshape(width, 3, head_width // cp_count), "cp", split_axis=0, concat_axis=2, tiled=True
    ).astype(f32)

    def cp_sum_own(vector):
        return jnp.sum(lax.all_to_all(vector.reshape(cp_count, -1), "cp", 0, 0, tiled=True), axis=0)

    def both_sum_own(vector):
        return tp_sum(cp_sum_own(vector))

    return (
        layer_output,
        grad_input,
        grad_qkv,
        grad_out,
        grad_up,
        grad_down,
        both_sum_own(input_gain_sum),
        cp_sum_own(heads_gain_sum),
        both_sum_own(middle_gain_sum),
        cp_sum_own(hidden_gain_sum),
    )


INTERPRET = False


def params(megabytes):
    return pltpu.CompilerParams(vmem_limit_bytes=megabytes * 1024 * 1024)


def shape(dims, kind):
    return jax.ShapeDtypeStruct(dims, kind)


def whole():
    return pl.BlockSpec(memory_space=pltpu.VMEM)


def scalars():
    return pl.BlockSpec(memory_space=pltpu.SMEM)


class Pin:
    def __init__(self, value):
        self.value = value


class Far(Pin):
    def __init__(self, value, dims=None, block=None):
        super().__init__(value)
        self.dims = tuple(value.shape) if dims is None else dims
        self.block = block


class Near:
    def __init__(self, value):
        self.value = value


class Fetched:
    def __init__(self, ref, copy):
        self.ref, self.copy, self.shape = ref, copy, ref.shape

    def ready(self):
        if self.copy is not None:
            self.copy.wait()
            self.copy = None

    def __getitem__(self, index):
        self.ready()
        return self.ref[index]


class Stored:
    def __init__(self, ref, copy):
        self.ref, self.copy, self.shape, self.sent = ref, copy, ref.shape, False

    def send(self):
        if not self.sent:
            self.copy.start()
            self.sent = True

    def __getitem__(self, index):
        return self.ref[index]

    def __setitem__(self, index, value):
        self.ref[index] = value

    @property
    def dtype(self):
        return self.ref.dtype


def plain(value):
    return value.value if isinstance(value, (Pin, Near)) else value


def pinned(value):
    return value if INTERPRET else pltpu.with_memory_space_constraint(value, pltpu.HBM)


def call(
    kernel, outs, args, specs=None, out_specs=None, grid=None, scratch=(), mb=8, cost=0.3, after=(), carry=(), prefetch=0
):
    specs = list(specs) if specs is not None else [whole() for _ in args]
    out_specs = list(out_specs) if out_specs is not None else [whole() for _ in outs]
    count, extra, kept, made = len(args), len(after), len(carry), len(outs)
    anywhere = pl.BlockSpec(memory_space=pl.ANY)
    far_in = [i for i, t in enumerate(args) if isinstance(t, Far)]
    far_out = [i for i, t in enumerate(outs) if isinstance(t, Far)]
    for i in far_in:
        specs[i] = anywhere
    for i in far_out:
        out_specs[i] = anywhere
    moving = [pltpu.VMEM(args[i].dims, args[i].value.dtype) for i in far_in]
    moving += [pltpu.VMEM(outs[i].dims, outs[i].value.dtype) for i in far_out]
    moving += [pltpu.SemaphoreType.DMA] * (len(far_in) + len(far_out))
    own_scratch = len(scratch)

    def run(*refs):
        ins = list(refs[:count])
        results = refs[count + extra + kept :]
        products = list(results[:made])
        rest = results[made + kept :]
        slots, sems = rest[own_scratch : own_scratch + len(far_in) + len(far_out)], rest[own_scratch + len(far_in) + len(far_out) :]
        for i, slot, sem in zip(far_in, slots, sems):
            source = refs[i]
            if args[i].block is not None:
                source = source.at[args[i].block(refs[0])]
            copy = pltpu.make_async_copy(source, slot, sem)
            copy.start()
            ins[i] = Fetched(slot, copy)
        stored = [
            Stored(slot, pltpu.make_async_copy(slot, results[i], sem))
            for i, slot, sem in zip(far_out, slots[len(far_in) :], sems[len(far_in) :])
        ]
        for i, product in zip(far_out, stored):
            products[i] = product
        kernel(*ins, *products, *rest[:own_scratch])
        for i in far_in:
            ins[i].ready()
        for product in stored:
            product.send()
        for product in stored:
            product.copy.wait()

    def result(value):
        dims = plain(value)
        if INTERPRET or value is dims:
            return dims
        return (pltpu.HBM if isinstance(value, Pin) else pltpu.VMEM)(dims.shape, dims.dtype)

    where = dict(
        in_specs=specs + [anywhere] * (extra + kept),
        out_specs=tuple(out_specs + [anywhere] * kept),
        scratch_shapes=list(scratch) + moving,
    )
    if prefetch:
        where["in_specs"] = where["in_specs"][prefetch:]
        where = {"grid_spec": pltpu.PrefetchScalarGridSpec(num_scalar_prefetch=prefetch, grid=grid, **where)}
    elif grid is not None:
        where["grid"] = grid
    return pl.pallas_call(
        run,
        out_shape=tuple(result(t) for t in outs) + tuple(result(Pin(shape(t.shape, t.dtype))) for t in carry),
        input_output_aliases={count + extra + i: made + i for i in range(kept)},
        compiler_params=params(mb),
        cost_estimate=pl.CostEstimate(flops=int(cost * 1e9), bytes_accessed=0, transcendentals=0),
        interpret=INTERPRET,
        **where,
    )(*[pinned(t.value) if isinstance(t, Pin) else t for t in list(args) + list(after)], *[pinned(t) for t in carry])


def bring(items, ids, after=(), carry=(), cost=0.3):
    def kernel(ids, *refs):
        sources, slots, sems = refs[: len(items)], refs[len(items) : 2 * len(items)], refs[2 * len(items) :]
        copies = []
        for (_, _, block), source, slot, sem in zip(items, sources, slots, sems):
            copies.append(pltpu.make_async_copy(source if block is None else source.at[block(ids)], slot, sem))
        for copy in copies:
            copy.start()
        for copy in copies:
            copy.wait()

    return call(
        kernel,
        [Near(shape(dims, array.dtype)) for array, dims, _ in items],
        [ids] + [Pin(array) for array, _, _ in items],
        [scalars()] + [pl.BlockSpec(memory_space=pl.ANY)] * len(items),
        scratch=[pltpu.SemaphoreType.DMA] * len(items), after=after, carry=carry, mb=2, cost=cost,
    )


def in_hbm():
    return pl.BlockSpec(memory_space=pl.ANY)


def started(source, to, sem):
    copy = pltpu.make_async_copy(source, to, sem)
    copy.start()
    return copy


def fixed(dims):
    return pl.BlockSpec(dims, lambda i: (0,) * len(dims))


def split_low(value):
    high = value.astype(bf16)
    return high, (value - high.astype(f32)).astype(bf16)


def lanes_of(columns, rows):
    lane = lax.broadcasted_iota(jnp.int32, (rows, 128), 1)
    out = jnp.zeros((rows, 128), f32)
    for i, column in enumerate(columns):
        out = jnp.where(lane == i, column.astype(f32), out)
    return out


def own_order(me, part, index):
    return ((index // part) ^ me) * part + index % part


def block_at(me, k, part):
    return pl.ds(pl.multiple_of((me ^ k) * part, part), part)


def swap_pairs(value, axis):
    size = value.shape[axis]
    place = lax.broadcasted_iota(jnp.int32, value.shape, axis)
    return jnp.where(
        place % 2 == 0, pltpu.roll(value, size - 1, axis), pltpu.roll(value, 1, axis)
    )


def tables(local_len, cp_count):
    column = np.arange(HD) // 2
    frequency = 10000.0 ** (-column / (HD // 2))
    zeta = (2.0 * column + 0.4 * HD) / (1.4 * HD)

    def of(places):
        angle = places[:, None] * frequency
        factor = zeta ** (places[:, None] / scale_base)
        return np.stack([np.cos(angle), np.sin(angle), factor, 1.0 / factor]).astype(np.float32)

    return of(np.arange(local_len)), of(np.arange(cp_count) * local_len)


def project_kernel(parts, ids, x, gain, gy, inner, base, seg, w0, w1, w2, pair, out):
    me, mine = ids[0], ids[1]
    rows, width = pair.shape[1:]
    part = rows // parts
    heads = out.shape[0]
    x.ready()
    for k in range(parts):
        normed, _ = norm_rows(x.ref[block_at(me, k, part), :].astype(f32))
        pair[0, k * part : (k + 1) * part, :] = (normed * gain[...]).astype(bf16)
    gy.ready()
    for k in range(parts):
        pair[1, k * part : (k + 1) * part, :] = gy.ref[block_at(me, k, part), :]
    pair.send()
    inner.ready()
    here = [base[kind, pl.ds(mine, 1), :] for kind in range(4)]
    table = [
        jnp.concatenate([inner.ref[kind, block_at(me, k, part), :] for k in range(parts)], axis=0)
        for kind in range(4)
    ]
    cosine = table[0] * here[0] - table[1] * here[1]
    sine = table[1] * here[0] + table[0] * here[1]
    lane = lax.broadcasted_iota(jnp.int32, cosine.shape, 1)
    sine = jnp.where(lane % 2 == 0, -sine, sine)
    place = lax.broadcasted_iota(jnp.int32, (rows, rows), 1)
    source = lax.broadcasted_iota(jnp.int32, (rows, rows), 0)
    moved = (own_order(me, part, place) == source).astype(bf16)
    ids_row = jnp.broadcast_to(seg[...].astype(f32), (16, rows)).astype(bf16)
    ordered = dot(ids_row, moved).astype(bf16)
    for j in range(heads):
        out[j, 3 * HD : 3 * HD + 16, :] = ordered
    for c, weight in enumerate((w0, w1, w2)):
        acc = dot(pair[0], weight[0])
        factor = (table[2] * here[2], table[3] * here[3], None)[c]
        for i in range(acc.shape[1] // 128):
            piece = acc[:, i * 128 : (i + 1) * 128]
            if c < 2:
                piece = piece * (cosine * factor) + swap_pairs(piece, 1) * (sine * factor)
            turned = piece.T.astype(bf16)
            for h in range(128 // HD):
                out[i * (128 // HD) + h, c * HD : (c + 1) * HD, :] = turned[h * HD : (h + 1) * HD]
    out.send()


def gather_heads(got, keys, ids_col, values=None):
    for j in range(got.shape[0]):
        rows = slice(j * got.shape[2], (j + 1) * got.shape[2])
        both = jnp.concatenate([got[j, HD : 3 * HD, :].astype(f32)], axis=0).T
        keys[rows, :] = both[:, :HD].astype(bf16)
        if values is not None:
            values[rows, :] = both[:, HD:].astype(bf16)
        ids_col[rows, :] = got[j, 3 * HD : 3 * HD + 16, :].astype(f32).T


def visible_scores(me, part, scores, ids_col, ids_row, count, first, group):
    same = ids_col[0:count, 0:1] == ids_row
    length = group
    key = lax.broadcasted_iota(jnp.int32, (length, length), 0)
    query = lax.broadcasted_iota(jnp.int32, (length, length), 1)
    rows = first
    own = lambda index: (index // rows) * rows + own_order(me, part, index % rows)
    earlier = own(key) <= own(query)
    if count > length:
        earlier = jnp.concatenate([jnp.ones((count - length, length), jnp.bool_), earlier], axis=0)
    return same & earlier


def attend_kernel(parts, ids, got, out, mixed, lse, kept, keys, ids_col, kept_sem):
    me = ids[0]
    keep = started(got, kept, kept_sem)
    blocks, _, rows = got.shape
    part = rows // parts
    gather_heads(got, keys, ids_col)
    group = 4 if blocks % 4 == 0 else 1
    width = group * rows
    for i in range(blocks // group):
        mine = range(i * group, (i + 1) * group)
        query = jnp.concatenate([got[j, :HD, :] for j in mine], axis=1) * bf16(HD**-0.5)
        ids_row = jnp.concatenate([got[j, 3 * HD : 3 * HD + 16, :].astype(f32)[:1] for j in mine], axis=1)
        count = (i + 1) * width
        scores = dot(keys[0:count, :], query)
        allowed = visible_scores(me, part, scores, ids_col, ids_row, count, rows, width)
        scores = jnp.where(allowed, scores, masked_score)
        top = jnp.max(scores, axis=0, keepdims=True)
        exponent = jnp.exp(scores - top)
        total = jnp.sum(exponent, axis=0, keepdims=True)
        value = jnp.concatenate([got[j, 2 * HD : 3 * HD, :] for j in range((i + 1) * group)], axis=1)
        result = dot(value, exponent.astype(bf16)) / total
        mixed[:, i * width : (i + 1) * width] = result
        lse[:, i * width : (i + 1) * width] = top + jnp.log(total)
        for n, j in enumerate(mine):
            out[j] = result[:, n * rows : (n + 1) * rows].astype(bf16)
    out.send()
    keep.wait()


def out_kernel(parts, att, gain, weight, own, *refs):
    pieces, kept = refs[:-1], refs[-1]
    kept[...] = att[...]
    blocks, _, rows = att.shape
    part, width = rows // parts, weight.shape[1]
    value = jnp.concatenate([att[j].astype(f32) for j in range(blocks)], axis=0).T
    high, low = split_low(jnp.mean(value, axis=1, keepdims=True))
    centred = value - (high.astype(f32) + low.astype(f32))
    square = split_low(jnp.sum(centred * centred, axis=1, keepdims=True))
    gains = gain[...]
    row = lax.broadcasted_iota(jnp.int32, (16, gains.shape[1]), 0)
    gain_high, gain_low = (t.astype(f32) for t in split_low(gains))
    gain_rows = jnp.where(row == 0, gain_high, jnp.where(row == 1, gain_low, 0.0))
    left = jnp.concatenate([(centred * gains).astype(bf16), gain_rows.astype(bf16)], axis=0)
    total = dot(left, weight[...])
    gain_row = total[rows : rows + 1] + total[rows + 1 : rows + 2]
    gain_block = jnp.concatenate([gain_row[:, i : i + 128] for i in range(0, width, 128)], axis=0)
    stats = lanes_of([high, low, *square], rows).T
    empty = jnp.zeros((part - gain_block.shape[0] - 1, 128), f32)

    def extra(k):
        row = jnp.concatenate([stats[i : i + 1, k * part : (k + 1) * part] for i in range(4)], axis=1)
        return jnp.concatenate([gain_block, row, empty], axis=0).astype(bf16)

    own[:, :width] = total[:part]
    own[:, width:] = extra(0).astype(f32)
    for k, piece in enumerate(pieces, 1):
        here = slice(k * part, (k + 1) * part)
        piece[:, :width] = total[here].astype(bf16)
        piece[:, width:] = extra(k)


def middle_kernel(parts, head_width, own, *refs):
    got, (x, gain, x1, u, gain_row, norms) = refs[: parts - 1][::-1], refs[parts - 1 :]
    part, width = x1.shape
    blocks = [own] + list(got)
    extras = [b[:, width:].astype(f32) for b in blocks]
    count = width // 128
    rows = [jnp.concatenate([e[i : i + 1] for i in range(count)], axis=1) for e in extras]
    columns = [jnp.broadcast_to(e[count : count + 1], (128, 128)).T[:, 0:1] for e in extras]
    means = [c[:part] + c[part : 2 * part] for c in columns]
    squares = [c[2 * part : 3 * part] + c[3 * part :] for c in columns]
    gain_row[...] = sum(rows)
    mean = sum(means) / parts
    spread = sum(squares) + head_width * sum((m - mean) * (m - mean) for m in means)
    scaling = lax.rsqrt(spread / width + eps)
    total = sum(b[:, :width].astype(f32) for b in blocks)
    for m, row in zip(means, rows):
        total = total + (m - mean) * row
    value = x[...].astype(f32) + total * scaling
    x1[...] = value
    normed, _ = norm_rows(value)
    u[...] = (normed * gain[...]).astype(bf16)
    norms[...] = jnp.zeros_like(norms)
    norms[0:2, :part] = lanes_of([mean, scaling], part).T[0:2, :]


def grad_hidden_kernel(gy, weight, grad):
    grad[...] = dot_t(gy[0], weight[...])


def prepare_kernel(step, up, near_up, flipped, up_sems):
    chunks = [slice(i, i + step) for i in range(0, up.shape[0], step)]
    copies = [pltpu.make_async_copy(up.at[c, :], near_up.at[c, :], up_sems.at[i]) for i, c in enumerate(chunks)]
    for copy in copies:
        copy.start()
    for copy, chunk in zip(copies, chunks):
        copy.wait()
        flipped[:, chunk] = near_up[chunk, :].T


def up_kernel(parts, step, own, *refs):
    got, refs = refs[: parts - 1][::-1], refs[parts - 1 :]
    weight, grad, gain, norms, act, slope, u, stats, rows_u = refs
    part = own.shape[0]
    rows, width = rows_u.shape
    for k, block in enumerate([own] + list(got)):
        rows_u[k * part : (k + 1) * part, :] = block[...]
    wide = u.shape[2]
    for j in range(u.shape[0]):
        u[j] = rows_u[:, j * wide : (j + 1) * wide]
    total = [jnp.zeros((rows, 128), f32)] * 4
    for i in range(0, weight.shape[1], step):
        here = slice(i, i + step)
        hidden = dot(rows_u[...], weight[:, here])
        cdf = 0.5 * (1.0 + lax.erf(hidden * (0.5**0.5)))
        value = hidden * cdf
        act[:, here] = value
        slope[:, here] = cdf + hidden * jnp.exp(-0.5 * hidden * hidden) * 0.3989422804014327
        grad_normed = grad[:, here] * gain[:, here]
        columns = [value, value * value, grad_normed, grad_normed * value]
        for n, column in enumerate(columns):
            for j in range(0, step, 128):
                total[n] = total[n] + column[:, j : j + 128]
    sums = lanes_of([jnp.sum(t, axis=1, keepdims=True) for t in total], rows)
    stats[...] = sums.T[:8, :]
    stats[4:6, :] = norms[0:2, :]


def swap_lane_blocks(value, k, part):
    lanes = value.shape[1]
    lane = lax.broadcasted_iota(jnp.int32, value.shape, 1)
    distance = 1
    while distance <= k:
        if k & distance:
            move = distance * part
            value = jnp.where(
                (lane // move) % 2 == 0,
                pltpu.roll(value, lanes - move, 1),
                pltpu.roll(value, move, 1),
            )
        distance *= 2
    return value


def hidden_back_kernel(parts, full, step, own, *refs):
    got, refs = refs[: parts - 1][::-1], refs[parts - 1 :]
    act, slope, grad, gain, weight, u, gh, both, norms, own_out = refs[:10]
    pieces, (low_all, u_sem, low_sem) = refs[10 : 9 + parts], refs[9 + parts :]
    first_wide, wide = u.shape[2], low_all.shape[2]
    copies = [started(u, both.at[:, :, pl.ds(0, first_wide)], u_sem)]
    rows = act.shape[0]
    part = rows // parts
    total = own[...]
    for k, block in enumerate(got, 1):
        total = total + swap_lane_blocks(block[...], k, part)
    norms[...] = jnp.zeros_like(norms)
    for k, block in enumerate([own] + list(got)):
        norms[0:2, k * part : (k + 1) * part] = block[4:6, :part]
    mean = total[0:1] / full
    scaling = lax.rsqrt(total[1:2] / full - mean * mean + eps)
    first = total[2:3] / full
    cross = scaling * (total[3:4] / full - mean * first)
    row = lax.broadcasted_iota(jnp.int32, (rows, rows), 0)
    table = jnp.zeros((rows, rows), f32)
    for i, value in enumerate([mean, scaling, first, cross]):
        table = jnp.where(row == i, value, table)
    cols = table.T
    mean, scaling, first, cross = (cols[:, i : i + 1] for i in range(4))
    for i in range(0, act.shape[1], step):
        here = slice(i, i + step)
        normed = (act[:, here] - mean) * scaling
        low = (normed * gain[:, here]).astype(bf16)
        for j in range(0, step, wide):
            low_all[(i + j) // wide] = low[:, j : j + wide]
        value = scaling * (grad[:, here] * gain[:, here] - first - normed * cross) * slope[:, here]
        gh[:, here] = value.astype(bf16)
    copies.append(started(low_all, both.at[:, :, pl.ds(first_wide, wide)], low_sem))
    gh.send()
    width = weight.shape[1]
    for i in range(0, width, step):
        here = slice(i, i + step)
        result = dot(gh[...], weight[:, here])
        own_out[:, here] = result[:part]
        for k, piece in enumerate(pieces, 1):
            piece[:, here] = result[k * part : (k + 1) * part].astype(bf16)
    for copy in copies:
        copy.wait()


def down_kernel(z2, *refs):
    weights, (own, second, odd) = refs[:-3], refs[-3:]
    _, _, wide = z2.shape
    part = own.shape[0]
    total = 0.0
    for i, weight in enumerate(weights):
        rows = weight.shape[0]
        left = jnp.concatenate([z2[j] for j in range(i * rows // wide, (i + 1) * rows // wide)], axis=1)
        total = total + dot(left, weight[...])
    own[...] = total[:part]
    second[...] = total[2 * part : 3 * part]
    odd[:part, :] = total[part : 2 * part].astype(bf16)
    odd[part:, :] = total[3 * part :].astype(bf16)


def half_kernel(second, got, out):
    part = second.shape[0]
    out[...] = (second[...] + got[part:, :].astype(f32)).astype(bf16)


def join_kernel(first, second, out):
    part = first.shape[0]
    out[:part, :] = first[...]
    out[part:, :] = second[...]


def middle_back_kernel(parts, own, *refs):
    got, refs = refs[: parts - 1][::-1], refs[parts - 1 :]
    gain_row, x, x1, gy, gain, gx1, gb = refs
    part, width = x1.shape
    grad = own[...]
    for block in got:
        grad = grad + block[...].astype(f32)
    value = x1[...]
    normed, scaling = norm_rows(value)
    result = gy[...].astype(f32) + norm_back(grad, gain[...], normed, scaling)
    gx1[...] = result
    low = result.astype(bf16)
    gb[:, :width] = low
    low = low.astype(f32)
    first = jnp.sum(low * gain_row[...], axis=1, keepdims=True) / width
    cross = jnp.sum(low * (value - x[...].astype(f32)), axis=1, keepdims=True) / width
    gb[:, width:] = lanes_of([*split_low(first), *split_low(cross)], part).astype(bf16)


def heads_back_kernel(parts, own, *refs):
    got, refs = refs[: parts - 1][::-1], refs[parts - 1 :]
    stats, att, gain, weight, sent, gb = refs
    blocks, _, rows = att.shape
    part, width = own.shape[0], gb.shape[1]
    for k, block in enumerate([own] + list(got)):
        gb[k * part : (k + 1) * part, :] = block[:, :width]
    gb.send()
    columns = jnp.concatenate([b[:, width:].astype(f32) for b in [own] + list(got)], axis=0).T
    first = columns[0:1] + columns[1:2]
    cross = columns[2:3] + columns[3:4]
    mean, scaling = stats[0:1], stats[1:2]
    grad = dot_t(weight[...], gb[...])
    value = jnp.concatenate([att[j].astype(f32) for j in range(blocks)], axis=0)
    normed = (value - mean) * scaling
    gain_col = jnp.broadcast_to(gain[...], (8, gain.shape[1])).T[:, 0:1]
    go = (scaling * (grad * gain_col - first - normed * cross)).astype(bf16)
    z = (normed * gain_col).astype(bf16)
    for j in range(blocks):
        sent[j, :HD, :] = go[j * HD : (j + 1) * HD]
        sent[j, HD:, :] = z[j * HD : (j + 1) * HD]


def turn_back(grad, table, base, j, inverse):
    here = [base[kind, :, j : j + 1] for kind in range(4)]
    cosine = table[0] * here[0] - table[1] * here[1]
    sine = table[1] * here[0] + table[0] * here[1]
    factor = table[3] * here[3] if inverse else table[2] * here[2]
    row = lax.broadcasted_iota(jnp.int32, grad.shape, 0)
    sine = jnp.where(row % 2 == 0, sine, -sine)
    return (grad * cosine + swap_pairs(grad, 0) * sine) * factor


def attend_back_kernel(parts, ids, got, grads, mixed, lse, inner, base, out, z, keys, values, ids_col, gk, gv, z_sem):
    me = ids[0]
    send_z = started(grads.at[:, pl.ds(HD, HD), :], z, z_sem)
    blocks, _, rows = got.shape
    part = rows // parts
    gather_heads(got, keys, ids_col, values)
    gk[...] = jnp.zeros_like(gk)
    gv[...] = jnp.zeros_like(gv)
    table = []
    for kind in range(4):
        ordered = jnp.concatenate(
            [inner[kind, block_at(me, k, part), :] for k in range(parts)], axis=0
        )
        table.append(ordered.T[:HD])
    group = 2 if blocks % 2 == 0 else 1
    width = group * rows
    for i in range(blocks // group):
        mine = range(i * group, (i + 1) * group)
        query = jnp.concatenate([got[j, :HD, :] for j in mine], axis=1) * bf16(HD**-0.5)
        ids_row = jnp.concatenate([got[j, 3 * HD : 3 * HD + 16, :].astype(f32)[:1] for j in mine], axis=1)
        go = jnp.concatenate([grads[j, :HD, :] for j in mine], axis=1)
        span = slice(i * width, (i + 1) * width)
        delta = jnp.sum(go.astype(f32) * mixed[:, span], axis=0, keepdims=True)
        count = (i + 1) * width
        scores = dot(keys[0:count, :], query)
        allowed = visible_scores(me, part, scores, ids_col, ids_row, count, rows, width)
        probability = jnp.where(allowed, jnp.exp(jnp.minimum(scores - lse[:, span], 0.5)), 0.0)
        grad_prob = dot(values[0:count, :], go)
        grad_scores = (probability * (grad_prob - delta)).astype(bf16)
        gv[:, 0:count] += dot_t(go, probability.astype(bf16))
        gk[:, 0:count] += dot_t(query, grad_scores)
        key = jnp.concatenate([got[j, HD : 2 * HD, :] for j in range((i + 1) * group)], axis=1)
        gq = dot(key, grad_scores) * HD**-0.5
        for n, j in enumerate(mine):
            piece = turn_back(gq[:, n * rows : (n + 1) * rows], table, base, j, False)
            out[j, :HD, :] = piece.astype(bf16)
    for j in range(blocks):
        span = slice(j * rows, (j + 1) * rows)
        out[j, HD : 2 * HD, :] = turn_back(gk[:, span], table, base, j, True).astype(bf16)
        out[j, 2 * HD :, :] = gv[:, span].astype(bf16)
    send_z.wait()


def input_back_kernel(parts, got, *refs):
    weights, own_out, pieces = refs[:6], refs[6], refs[7:]
    part, width = own_out.shape
    half = width // 2
    grads = []
    for c in range(3):
        here = slice(c * HD, (c + 1) * HD)
        grad = jnp.concatenate([got[j, here, :].astype(f32) for j in range(got.shape[0])], axis=0)
        grads.append(grad.T.astype(bf16))
    totals = [0.0, 0.0]
    for n, weight in enumerate(weights):
        totals[n % 2] = totals[n % 2] + dot_t(grads[n // 2], weight[0])
    for h, result in enumerate(totals):
        here = slice(h * half, (h + 1) * half)
        own_out[:, here] = result[:part]
        for k, piece in enumerate(pieces, 1):
            piece[:, here] = result[k * part : (k + 1) * part].astype(bf16)


def final_kernel(parts, own, *refs):
    got, (x, gx1, gain, gains, out) = refs[: parts - 1][::-1], refs[parts - 1 :]
    part, width = gx1.shape
    grad = own[...]
    for block in got:
        grad = grad + block[...].astype(f32)
    normed, scaling = norm_rows(x[...].astype(f32))
    out[:, :width] = (gx1[...] + norm_back(grad, gain[...], normed, scaling)).astype(bf16)
    rows = gains[0:2]
    pieces = [rows[n : n + 1, i : i + 128] for n in range(2) for i in range(0, rows.shape[1], 128)]
    high, low = split_low(jnp.concatenate(pieces, axis=0))
    empty = jnp.zeros((part - 2 * len(pieces), 128), f32)
    tail = jnp.concatenate([high.astype(f32), low.astype(f32), empty], axis=0)
    out[:, width:] = tail.astype(bf16)


def output_kernel(own, got, last, x1, out):
    total = own[...] + x1[...] + got[: out.shape[0], :].astype(f32)
    out[...] = (total + last[...].astype(f32)).astype(bf16)


def own_row(gain, index, own):
    total = jnp.zeros((1, own), f32)
    for j in range(gain.shape[1] // own):
        total = jnp.where(index == j, gain[:, j * own : (j + 1) * own], total)
    return total


def row_of(column, columns):
    return jnp.broadcast_to(column, (columns, 128)).T[:1, :]


def product_kernel(step, columns, which, offset, ids, left, right, *refs):
    count = left.shape[0]
    gains = len(refs) > 7
    if gains:
        (weight, gain, out, gain_grad), refs = refs[:4], refs[4:]
        (near_weight, weight_sem), refs = refs[-2:], refs[:-2]
    else:
        out, refs = refs[0], refs[1:]
    left_all, right_all, result, left_sems, right_sems, out_sems = refs
    rows, size = right.shape[-2:]
    own = result.shape[0]
    tokens = count * rows
    chunks = [slice(i, i + step) for i in range(0, size, step)]

    first = []
    for r in range(count):
        source = left.at[r]
        if columns:
            source, place = source.at[:, pl.ds(offset, own)], left_all.at[pl.ds(r * rows, rows), :]
        else:
            source, place = source.at[pl.ds(offset, own), :], left_all.at[r]
        first.append(pltpu.make_async_copy(source, place, left_sems.at[r]))
    side = right if which is None else right.at[:, which]
    later = [
        [pltpu.make_async_copy(side.at[:, :, c], right_all.at[:, :, c], right_sems.at[i])] for i, c in enumerate(chunks)
    ]
    for copy in first + later[0]:
        copy.start()
    if gains:
        fetch = pltpu.make_async_copy(
            weight.at[pl.ds(pl.multiple_of(ids[1] * own, own), own), :], near_weight, weight_sem
        )
        fetch.start()
    for copies in later[1:]:
        for copy in copies:
            copy.start()
    for copy in first:
        copy.wait()
    if not columns:
        value = jnp.concatenate([left_all[r] for r in range(count)], axis=1)
    sums = jnp.zeros((own, 128), f32)
    sent = []
    for i, (c, copies) in enumerate(zip(chunks, later)):
        for copy in copies:
            copy.wait()
        block = right_all[:, :, c].reshape(tokens, step)
        grad = t_dot(left_all[...], block) if columns else dot(value, block)
        result[:, c] = grad.astype(result.dtype)
        if gains:
            if i == 0:
                fetch.wait()
            product = grad * near_weight[:, c].astype(f32)
            for j in range(0, step, 128):
                sums = sums + product[:, j : j + 128]
            moves = [pltpu.make_async_copy(result.at[:, c], out.at[:, c], out_sems.at[i, 0])]
        else:
            wide = out.shape[2]
            moves = [
                pltpu.make_async_copy(
                    result.at[:, pl.ds(j, wide)], out.at[j // wide], out_sems.at[i, (j - c.start) // wide]
                )
                for j in range(c.start, c.stop, wide)
            ]
        for move in moves:
            move.start()
        sent.extend(moves)
    if gains:
        gain_grad[...] = row_of(jnp.sum(sums, axis=1, keepdims=True), own) / own_row(gain, ids[1], own)
    for copy in sent:
        copy.wait()


def grad_qkv_place_kernel(ids, got, weight, gain, up_gain, out, gain_grads):
    total = 0.0
    for c in range(3):
        value = jnp.concatenate(
            [got[j, c * HD : (c + 1) * HD, :].astype(f32) for j in range(got.shape[0])], axis=0
        ).T
        out[c] = value
        total = total + jnp.sum(value * weight[c].astype(f32), axis=1, keepdims=True)
    out.send()
    first = row_of(total, total.shape[0]) / own_row(gain, ids[1], total.shape[0])
    row = lax.broadcasted_iota(jnp.int32, gain_grads.shape, 0)
    gain_grads[...] = jnp.where(row == 0, first, up_gain[...])


def outputs_kernel(parts, ids, *refs):
    blocks, (out, first, second, sems) = refs[:parts], refs[parts:]
    part, width = blocks[0].shape[0], out.shape[1]
    copies = [
        started(blocks[-k % parts].at[:, pl.ds(0, width)], out.at[block_at(ids[0], k, part), :], sems.at[k])
        for k in range(parts)
    ]
    count = first.shape[1] // 128
    total = sum(b[:, width:].astype(f32) for b in blocks)
    total = total[: 2 * count] + total[2 * count : 4 * count]
    for i in range(count):
        first[:, i * 128 : (i + 1) * 128] = total[i : i + 1]
        second[:, i * 128 : (i + 1) * 128] = total[count + i : count + i + 1]
    for copy in copies:
        copy.wait()


def layer_output_kernel(ids, even, odd, out, sems):
    part = even.shape[0] // 2
    copies = []
    for k in range(4):
        source = (odd if k % 2 else even).at[pl.ds(k // 2 * part, part), :]
        copies.append(started(source, out.at[block_at(ids[0], k, part), :], sems.at[k]))
    for copy in copies:
        copy.wait()


def body(
    layer_input,
    segment_ids,
    qkv_weight,
    out_weight,
    up_weight,
    down_weight,
    input_gain,
    heads_gain,
    middle_gain,
    hidden_gain,
    cotangent,
):
    rows, row_count, width = layer_input.shape
    T, C = lax.axis_size("tp"), lax.axis_size("cp")
    part = rows // T
    head_width = qkv_weight.shape[2]
    if head_width // HD != C or row_count != 1 or rows != 128 or T != 4 or 64 * part != width:
        return body_general(
            layer_input, segment_ids, qkv_weight, out_weight, up_weight, down_weight,
            input_gain, heads_gain, middle_gain, hidden_gain, cotangent,
        )
    tokens = rows * C
    hidden = up_weight.shape[1]
    wide = width // C
    high = hidden // C
    ids = jnp.stack([lax.axis_index("tp"), lax.axis_index("cp")]).astype(jnp.int32)
    x = layer_input.reshape(rows, width)
    gy = cotangent.reshape(rows, width)
    weight3 = jnp.transpose(qkv_weight, (1, 0, 2))
    gain_in, gain_mid = input_gain.reshape(1, -1), middle_gain.reshape(1, -1)
    gain_heads, gain_hid = heads_gain.reshape(1, -1), hidden_gain.reshape(1, -1)
    inner, base = tables(rows, C)
    inner2 = jnp.asarray(np.concatenate([inner, inner], axis=2))
    base2 = jnp.asarray(np.concatenate([base, base], axis=2))
    base_t = np.zeros((4, HD, 128), np.float32)
    base_t[:, :, :C] = np.transpose(base, (0, 2, 1))
    base_t = jnp.asarray(base_t)
    wide_part = width + 128
    step = 512

    def piece_shapes(columns):
        return [shape((part, columns), f32)] + [shape((part, columns), bf16)] * (T - 1)

    def exchange(pieces):
        return [swap_tp(pieces[k - 1], k) for k in range(T - 1, 0, -1)]

    def spread(block):
        return exchange([block] * (T - 1))

    def to_cp(value):
        return lax.all_to_all(value, "cp", 0, 0, tiled=True)

    def entire(value):
        return (value, value.shape, None)

    def own_rows(value):
        return (value, (part, width), lambda ids: (block_at(ids[0], 0, part), slice(None)))

    def third(c):
        return lambda ids: (pl.ds(c, 1), slice(None), slice(None))

    cols, first_rows = lambda i, *_: (0, i), lambda i, *_: (i, 0)
    origin2, origin3 = lambda i, *_: (0, 0), lambda i, *_: (0, 0, 0)
    sixth = lambda c, h: lambda ids: (pl.ds(c, 1), pl.ds(h * width // 2, width // 2), slice(None))
    weight_sixths = [Far(weight3, (1, width // 2, head_width), sixth(c, h)) for c in range(3) for h in range(2)]
    weight_thirds = [Far(weight3, (1, width, head_width), third(c)) for c in range(3)]

    pair, sent = call(
        functools.partial(project_kernel, T),
        [Far(shape((2, rows, width), bf16)), Far(shape((C, 3 * HD + 16, rows), bf16))],
        [ids, Far(x), Far(gain_in), Far(gy), Far(inner2), Far(base2), Far(segment_ids.reshape(1, rows)), *weight_thirds],
        [scalars()] + [whole()] * 9, mb=14,
    )
    got = to_cp(sent)
    near_out, near_x, near_gy, near_mid, near_heads, near_hid, near_in = bring(
        [entire(out_weight), own_rows(x), own_rows(gy), entire(gain_mid), entire(gain_heads),
         entire(gain_hid), entire(gain_in)],
        ids, after=[Pin(sent)],
    )
    back, mixed, lse, far_got, pair = call(
        functools.partial(attend_kernel, T),
        [Far(shape((C, HD, rows), bf16)), Far(shape((HD, tokens), f32)), Far(shape((1, tokens), f32)),
         Pin(shape((C, 3 * HD + 16, rows), bf16))],
        [ids, got], [scalars(), whole()], [whole()] * 3 + [in_hbm()],
        scratch=[pltpu.VMEM((tokens, HD), bf16), pltpu.VMEM((tokens, 16), f32), pltpu.SemaphoreType.DMA],
        mb=10, after=[near_heads], carry=[pair],
    )
    att = to_cp(back)
    early = lax.all_gather(pair, "cp", axis=0)

    own, *pieces, near_att = call(
        functools.partial(out_kernel, T),
        piece_shapes(wide_part) + [Near(shape((C, HD, rows), bf16))],
        [att, near_heads, near_out],
    )
    (grad_hid,) = call(
        grad_hidden_kernel, [Near(shape((rows, hidden), f32))],
        [Pin(pair), Pin(down_weight)],
        [pl.BlockSpec((1, rows, width), lambda i: (1, 0, 0)), pl.BlockSpec((step, width), first_rows)],
        [pl.BlockSpec((rows, step), cols)],
        grid=(hidden // step,), after=[own], mb=10, cost=3,
    )
    x1, u_own, gain_row, norms = call(
        functools.partial(middle_kernel, T, head_width),
        [Near(shape((part, width), f32)), shape((part, width), bf16), Near(shape((1, width), f32)), Near(shape((8, 128), f32))],
        [own, *exchange(pieces), near_x, near_mid], after=[grad_hid],
    )
    u_blocks = [u_own] + spread(u_own)
    near_up, near_flip = call(
        functools.partial(prepare_kernel, 256),
        [Near(shape((width, hidden), bf16)), Near(shape((hidden, width), bf16))],
        [Pin(up_weight)], [pl.BlockSpec(memory_space=pl.ANY)],
        scratch=[pltpu.SemaphoreType.DMA((width // 256,))], after=[u_own], mb=6,
    )

    act, slope, u_cols, stats = call(
        functools.partial(up_kernel, T, step),
        [Near(shape((rows, hidden), f32)), Near(shape((rows, hidden), f32)), Near(shape((C, rows, wide), bf16)),
         shape((8, rows), f32)],
        [*u_blocks, near_up, grad_hid, near_hid, norms],
        scratch=[pltpu.VMEM((rows, width), bf16)], mb=8, after=[near_flip],
    )
    gh, both, norms, own, *pieces = call(
        functools.partial(hidden_back_kernel, T, FF, step),
        [Far(shape((rows, hidden), bf16)), Pin(shape((C, rows, wide + high), bf16)), Near(shape((8, rows), f32))] + piece_shapes(width),
        [stats, *spread(stats), act, slope, grad_hid, near_hid, near_flip, u_cols], mb=10,
        out_specs=[whole(), in_hbm()] + [whole()] * (T + 1),
        scratch=[pltpu.VMEM((C, rows, high), bf16), pltpu.SemaphoreType.DMA, pltpu.SemaphoreType.DMA],
    )
    gu_got = exchange(pieces)
    both_got = to_cp(both)
    gh_all = lax.all_gather(gh, "cp", axis=0)
    down_parts = [
        Far(down_weight, (step, width), (lambda at: lambda ids: (pl.ds(at, step), slice(None)))(i))
        for i in range(0, hidden, step)
    ]
    gx1, gb_own = call(
        functools.partial(middle_back_kernel, T),
        [Near(shape((part, width), f32)), shape((part, wide_part), bf16)],
        [own, *gu_got, gain_row, near_x, x1, near_gy, near_mid], cost=8,
    )
    gb_blocks = [gb_own] + spread(gb_own)
    y_own, y_second, y_odd = call(
        down_kernel,
        [Far(shape((part, width), f32)), Far(shape((part, width), f32)), Far(shape((2 * part, width), bf16))],
        [Far(both, (C, rows, high), lambda ids: (slice(None), slice(None), pl.ds(wide, high))), *down_parts],
        after=[gb_own], cost=20, mb=14,
    )
    (near_out,) = bring([entire(out_weight)], ids, after=[gb_own])

    def product(left, right, columns, which, offset, own, after, weight=None, gain=None, cost=20):
        anywhere = pl.BlockSpec(memory_space=pl.ANY)
        size = right.shape[-1]
        chunk = 2 * step
        left_dims = (tokens, own) if columns else (C, own, rows)
        if weight is not None:
            outs = [Pin(shape((own, size), f32)), shape((1, own), f32)]
            more, more_specs = [Pin(weight), gain], [anywhere, whole()]
            out_specs, extra = [anywhere, whole()], [pltpu.VMEM((own, size), bf16), pltpu.SemaphoreType.DMA]
        else:
            outs, out_specs = [Pin(shape((C, own, size // C), bf16))], [anywhere]
            more, more_specs, extra = [], [], []
        return call(
            functools.partial(product_kernel, chunk, columns, which, offset), outs,
            [ids, Pin(left), Pin(right), *more], [scalars()] + [anywhere] * 2 + more_specs, out_specs,
            scratch=[pltpu.VMEM(left_dims, bf16), pltpu.VMEM((C, rows, size), bf16),
                     pltpu.VMEM((own, size), plain(outs[0]).dtype),
                     pltpu.SemaphoreType.DMA((C,)), pltpu.SemaphoreType.DMA((size // chunk,)),
                     pltpu.SemaphoreType.DMA((size // chunk, chunk * C // size))] + extra,
            mb=14, after=after, cost=cost,
        )


    sent, gb, y_odd = call(
        functools.partial(heads_back_kernel, T),
        [Far(shape((C, 2 * HD, rows), bf16)), Far(shape((rows, width), bf16))],
        [*gb_blocks, norms, near_att, near_heads, near_out], after=[Pin(both_got)], carry=[y_odd],
    )
    y_got = swap_tp(y_odd, 1)
    gb_all = lax.all_gather(gb, "cp", axis=0)
    grads = to_cp(sent)
    near_got, near_mixed, near_lse, near_inner, near_base = bring(
        [entire(far_got), entire(mixed), entire(lse), entire(inner2), entire(base_t)], ids, after=[Pin(sent)]
    )
    grad_down, hidden_gain_grad = product(both_got, early, True, 1, wide, high, [Pin(sent)], down_weight, gain_hid)
    (y_half,) = call(half_kernel, [shape((part, width), bf16)], [Far(y_second), y_got], after=[Pin(sent)])
    y_last = swap_tp(y_half, 2)
    gq_sent, z = call(
        functools.partial(attend_back_kernel, T),
        [Far(shape((C, 3 * HD, rows), bf16)), Pin(shape((C, HD, rows), bf16))],
        [ids, near_got, grads, near_mixed, near_lse, near_inner, near_base], [scalars()] + [whole()] * 6,
        [whole(), in_hbm()],
        scratch=[pltpu.VMEM((tokens, HD), bf16), pltpu.VMEM((tokens, HD), bf16), pltpu.VMEM((tokens, 16), f32),
                 pltpu.VMEM((HD, tokens), f32), pltpu.VMEM((HD, tokens), f32), pltpu.SemaphoreType.DMA],
        mb=12, cost=8, after=[Pin(grad_down), y_half],
    )
    gq = to_cp(gq_sent)
    (y_low,) = call(
        output_kernel, [shape((part, width), bf16)], [Far(y_own), y_got, y_last, x1], after=[Pin(gq_sent)]
    )
    y_even = swap_tp(y_low, 2)
    (grad_qkv,) = product(gq_sent, early, False, 0, 0, 3 * HD, [y_low])
    own, *pieces = call(
        functools.partial(input_back_kernel, T), piece_shapes(width), [gq, *weight_sixths], mb=10, cost=10,
    )
    ga_got = exchange(pieces)
    (y_even,) = call(join_kernel, [shape((2 * part, width), bf16)], [y_low, y_even], after=[own])
    y_odd = swap_tp(y_even, 1)
    grad_qkv_got = to_cp(grad_qkv)
    grad_up, up_gain = product(both_got, gh_all, True, None, 0, wide, [own], up_weight, gain_mid)
    own_wide = lambda ids: (slice(None), pl.ds(pl.multiple_of(ids[1] * wide, wide), wide), slice(None))
    grad_qkv, gains = call(
        grad_qkv_place_kernel,
        [Far(shape((3, wide, head_width), f32)), shape((8, wide), f32)],
        [ids, grad_qkv_got, Far(weight3, (3, wide, head_width), own_wide), gain_in, up_gain],
        [scalars()] + [whole()] * 4, after=[own], cost=20,
    )
    (final,) = call(
        functools.partial(final_kernel, T),
        [shape((part, wide_part), bf16)],
        [own, *ga_got, near_x, gx1, near_in, gains], after=[Pin(grad_up)],
    )
    final_blocks = [final] + spread(final)
    grad_out, heads_gain_grad = product(z, gb_all, False, None, 0, HD, [final], out_weight, gain_heads)
    (layer_output,) = call(
        layer_output_kernel, [Pin(shape((rows, width), bf16))], [ids, y_even, y_odd], [scalars(), whole(), whole()],
        [in_hbm()], scratch=[pltpu.SemaphoreType.DMA((T,))],
        after=[final],
    )
    grad_input, input_gain_grad, middle_gain_grad = call(
        functools.partial(outputs_kernel, T),
        [Pin(shape((rows, width), bf16)), shape((1, wide), f32), shape((1, wide), f32)],
        [ids, *final_blocks], [scalars()] + [whole()] * T, [in_hbm(), whole(), whole()],
        scratch=[pltpu.SemaphoreType.DMA((T,))], after=[Pin(grad_out), Pin(layer_output)],
    )
    return (
        layer_output.reshape(layer_input.shape),
        grad_input.reshape(layer_input.shape),
        jnp.transpose(grad_qkv, (1, 0, 2)),
        grad_out,
        grad_up,
        grad_down,
        input_gain_grad.reshape(-1),
        heads_gain_grad.reshape(-1),
        middle_gain_grad.reshape(-1),
        hidden_gain_grad.reshape(-1),
    )


def solution(mesh):
    placed = (
        P("cp", None, None),
        P("cp", None),
        P(None, None, "tp"),
        P("tp", None),
        P(None, "tp"),
        P("tp", None),
        P(),
        P("tp"),
        P(),
        P("tp"),
        P("cp", None, None),
    )
    return jax.shard_map(
        body,
        mesh=mesh,
        in_specs=placed,
        out_specs=(
            P("cp", None, None),
            P("cp", None, None),
            P("cp", None, "tp"),
            P(("tp", "cp"), None),
            P("cp", "tp"),
            P(("tp", "cp"), None),
            P("cp"),
            P(("tp", "cp")),
            P("cp"),
            P(("tp", "cp")),
        ),
        check_vma=False,
    )
```
